32 devices in a mesh: parts: 2 (over x), dp: 8 (over z, y), tp: 2 (over core).
Axes of the slice: x: 2, y: 2, z: 4, core: 2. Of those that a mesh axis runs over, the one named last changes fastest.
Arguments:
- hidden: bfloat16 [768, 4, 5120], P(('parts', 'dp'), None, 'tp'), parts along dimension 0, may hold values from -6 to 6
- base_weight: bfloat16 [5120, 2, 4, 128], P('tp'), may hold values from -0.078125 to 0.078125
- factor_a: bfloat16 [10240, 64], P(('parts', 'tp'), 'dp'), parts along dimension 0, may hold values from -0.078125 to 0.078125
- factor_b: bfloat16 [128, 2, 4, 128], P(('parts', 'dp')), parts along dimension 0, may hold values from -0.75 to 0.75
- queries: bfloat16 [768, 4, 32, 128], P(('parts', 'dp'), None, 'tp'), parts along dimension 0, may hold values from -144 to 144
- cache: bfloat16 [768, 128, 2, 4, 128], P(('parts', 'dp'), None, None, 'tp'), parts along dimension 0, may hold values from -6 to 6
- lengths: int32 [768], P(('parts', 'dp')), parts along dimension 0, may hold values from 8 to 128, as said below
Outputs:
- fresh: bfloat16 [768, 4, 2, 4, 128], P(('parts', 'dp'), None, None, 'tp'), parts along dimension 0
- context: bfloat16 [768, 4, 32, 128], P(('parts', 'dp'), None, 'tp'), parts along dimension 0
The draws below stay inside these ranges and needn't reach their ends.
There are 2 independent parts, one for each index of `parts`. The reference program is written for one: setup_inputs(seed, part) draws one part's arguments, and reference() takes and returns one part's arrays. A program takes and returns all parts, laid end to end along the dimension named above; an argument that names none is the same for every part. Nothing has to cross between parts.
Inputs may be any that keep to these rules, and one draw needn't show every extreme that they name: `lengths`: some row has exactly 128 live slots.
All inputs are finite; a program needn't handle non-finite values.
Results may differ from the reference program's by a relative error of at most 0.0054.
Values may be sent and summed in bfloat16 or wider, within the bound.
No kernel may reach another device: no remote copies, remote signals or barrier semaphores. Data moves between devices by JAX's collectives and lax.ppermute only.
A program may use at most 64 MiB of HBM per device.

```python
import jax
import jax.numpy as jnp
from jax import lax

D = 5120
HD = 128
KVH = 4
R = 64
STEPS = 4
CACHE = 128
ROWS = 384
HEADS = 32


def shared_cache(key):
    raw = jnp.clip(jax.random.normal(key, (ROWS, CACHE, 2, KVH, HD), jnp.float32), -6.0, 6.0)
    return raw


def draw_cache(key, part):
    raw = shared_cache(key)
    return raw.astype(jnp.bfloat16)


def draw_queries(key, part):
    own = jax.random.fold_in(key, 5)
    shape = (ROWS, STEPS, HEADS, HD)
    values = jnp.clip(jax.random.normal(own, shape, jnp.float32), -6.0, 6.0)
    return values.astype(jnp.bfloat16)


def draw_lengths(key, part):
    key = jax.random.fold_in(key, 3)
    drawn = jax.random.randint(key, (ROWS,), 8, CACHE + 1)
    longest = jax.random.randint(jax.random.fold_in(key, 1), (), 0, ROWS)
    return jnp.where(jnp.arange(ROWS) == longest, CACHE, drawn).astype(jnp.int32)


def shard_levels(own_key, dims, shards, low, top_value):
    def one(axis_at, parts):
        draws = jax.random.uniform(jax.random.fold_in(jax.random.fold_in(own_key, 6), axis_at), (parts,), jnp.float32, low / len(shards), top_value / len(shards))
        return jnp.repeat(jnp.exp(draws), dims[axis_at] // parts).reshape((-1,) + (1,) * (len(dims) - axis_at - 1))

    loudness = one(*shards[0])
    for cut in shards[1:]:
        loudness = loudness * one(*cut)
    return loudness


def normal_values(own_key, extent, scale, reach, pieces=(), held_as=jnp.bfloat16):
    values = jax.random.normal(own_key, extent, jnp.float32) * scale
    if len(pieces) > 0:
        values = shard_levels(own_key, extent, pieces, -0.22, 0.18) * values
    return jnp.clip(values, min=-reach, max=reach).astype(held_as)


def setup_inputs(seed: int = 0, part: int = 0) -> dict:
    seeds = jax.random.split(jax.random.key(seed), 8)
    own_keys = jax.random.split(jax.random.fold_in(seeds[7], part), 8)
    return {
        "hidden": normal_values(own_keys[0], (ROWS, STEPS, D), 1.0, 6.0, ((0, 8), (2, 2))),
        "base_weight": normal_values(seeds[1], (D, 2, KVH, HD), D ** -0.5, 0.078125, ((0, 2),)),
        "factor_a": normal_values(own_keys[2], (D, R), D ** -0.5, 0.078125, ((0, 2), (1, 8))),
        "factor_b": normal_values(own_keys[3], (R, 2, KVH, HD), R ** -0.5, 0.75, ((0, 8),)),
        "queries": draw_queries(jax.random.fold_in(jax.random.fold_in(seeds[7], part), 71), part),
        "cache": draw_cache(jax.random.fold_in(jax.random.fold_in(seeds[7], part), 71), part),
        "lengths": draw_lengths(jax.random.fold_in(jax.random.fold_in(seeds[7], part), 71), part),
    }


def attend(queries, cache, fresh, lengths):
    rows, steps, heads, size = queries.shape
    kvh = cache.shape[3]
    slots = cache.shape[1]
    scale = size ** -0.5
    grouped = queries.reshape(rows, steps, kvh, heads // kvh, size).astype(jnp.float32)
    old_keys = cache[:, :, 0].astype(jnp.float32)
    old_vals = cache[:, :, 1].astype(jnp.float32)
    new_keys = fresh[:, :, 0].astype(jnp.float32)
    new_vals = fresh[:, :, 1].astype(jnp.float32)
    s_old = jnp.einsum('rtgqd,rjgd->rtgqj', grouped, old_keys) * scale
    s_new = jnp.einsum('rtgqd,rjgd->rtgqj', grouped, new_keys) * scale
    live_old = (jnp.arange(slots)[None, :] < lengths[:, None])[:, None, None, None, :]
    live_new = (jnp.arange(steps)[None, :] <= jnp.arange(steps)[:, None])[None, :, None, None, :]
    s_old = jnp.where(live_old, s_old, -1e30)
    s_new = jnp.where(live_new, s_new, -1e30)
    top = jnp.maximum(jnp.max(s_old, axis=-1), jnp.max(s_new, axis=-1))[..., None]
    e_old = jnp.where(live_old, jnp.exp(s_old - top), 0.0)
    e_new = jnp.where(live_new, jnp.exp(s_new - top), 0.0)
    total = jnp.sum(e_old, axis=-1) + jnp.sum(e_new, axis=-1)
    w_old = lax.optimization_barrier(e_old.astype(jnp.bfloat16)).astype(jnp.float32)
    w_new = lax.optimization_barrier(e_new.astype(jnp.bfloat16)).astype(jnp.float32)
    summed = jnp.einsum('rtgqj,rjgd->rtgqd', w_old, old_vals) + jnp.einsum('rtgqj,rjgd->rtgqd', w_new, new_vals)
    result = summed / total[..., None]
    return result.reshape(rows, steps, heads, size).astype(jnp.bfloat16)


def reference(hidden, base_weight, factor_a, factor_b, queries, cache, lengths):
    width = base_weight.shape[0]
    flat_base = base_weight.reshape(width, -1)
    low_rank = jnp.dot(factor_a, factor_b.reshape(factor_b.shape[0], -1), preferred_element_type=jnp.float32)
    merged = (flat_base.astype(jnp.float32) + low_rank).astype(jnp.bfloat16)
    rows, steps = hidden.shape[0], hidden.shape[1]
    projected = jnp.dot(hidden.reshape(rows * steps, width), merged, preferred_element_type=jnp.float32)
    fresh = projected.astype(jnp.bfloat16).reshape(rows, steps, 2, base_weight.shape[2], base_weight.shape[3])
    context = attend(queries, cache, fresh, lengths)
    return fresh, context
```

```python
import jax
import jax.numpy as jnp
from jax import lax
from jax.sharding import PartitionSpec as P


def gather_blocks(x, count):
    blocks = [x]
    for k in range(1, count):
        blocks.append(lax.ppermute(x, "dp", [(i, i ^ k) for i in range(count)]))
    return blocks


def attend_cached(queries, cache, lengths):
    rows, steps, heads, size = queries.shape
    slots, kvh = cache.shape[1], cache.shape[3]
    grouped = queries.reshape(rows, steps, kvh, heads // kvh, size)
    scores = (
        jnp.einsum("rtgqd,rjgd->rtgqj", grouped, cache[:, :, 0], preferred_element_type=jnp.float32)
        * size ** (-0.5)
    )
    live = (jnp.arange(slots)[None, :] < lengths[:, None])[:, None, None, None, :]
    scores = jnp.where(live, scores, -1e30)
    top = jnp.max(scores, axis=-1, keepdims=True)
    expo = jnp.where(live, jnp.exp(scores - top), 0.0)
    total = jnp.sum(expo, axis=-1, keepdims=True)
    summed = jnp.einsum(
        "rtgqj,rjgd->rtgqd", expo.astype(jnp.bfloat16), cache[:, :, 1], preferred_element_type=jnp.float32
    )
    return top, total, summed


def attend_new(queries, fresh, top_old, total_old, summed_old):
    rows, steps, heads, size = queries.shape
    kvh = fresh.shape[3]
    grouped = queries.reshape(rows, steps, kvh, heads // kvh, size)
    scores = (
        jnp.einsum("rtgqd,rjgd->rtgqj", grouped, fresh[:, :, 0], preferred_element_type=jnp.float32)
        * size ** (-0.5)
    )
    live = (jnp.arange(steps)[None, :] <= jnp.arange(steps)[:, None])[None, :, None, None, :]
    scores = jnp.where(live, scores, -1e30)
    top = jnp.maximum(top_old, jnp.max(scores, axis=-1, keepdims=True))
    expo = jnp.where(live, jnp.exp(scores - top), 0.0)
    back = jnp.exp(top_old - top)
    total = back * total_old + jnp.sum(expo, axis=-1, keepdims=True)
    summed = back * summed_old + jnp.einsum(
        "rtgqj,rjgd->rtgqd", expo.astype(jnp.bfloat16), fresh[:, :, 1], preferred_element_type=jnp.float32
    )
    return (summed / total).reshape(rows, steps, heads, size).astype(jnp.bfloat16)


def shards(dp, tp, hidden, base_weight, factor_a, factor_b, queries, cache, lengths):
    width, _, kvh_all, size = base_weight.shape
    columns = 2 * kvh_all * size
    own = cache.shape[3]
    rows, steps = hidden.shape[:2]
    if dp & (dp - 1) == 0 and dp <= 8:
        down = jnp.concatenate(gather_blocks(factor_a.T, dp), axis=0)
        up = jnp.concatenate(gather_blocks(factor_b, dp), axis=0)
    else:
        down = lax.all_gather(factor_a.T, "dp", axis=0, tiled=True)
        up = lax.all_gather(factor_b, "dp", axis=0, tiled=True)
    top, total, summed = attend_cached(queries, cache, lengths)
    low_rank = lax.dot_general(
        down, up.reshape(up.shape[0], columns), (((0,), (0,)), ((), ())), preferred_element_type=jnp.float32
    )
    merged = (base_weight.reshape(width, columns).astype(jnp.float32) + low_rank).astype(jnp.bfloat16)
    part = jnp.dot(hidden.reshape(rows * steps, width), merged, preferred_element_type=jnp.float32)
    part = part.reshape(rows, steps, 2, tp, own, size)
    me = lax.axis_index("tp")
    mine = lax.dynamic_index_in_dim(part, me, 3, keepdims=False)
    for k in range(1, tp):
        other = lax.dynamic_index_in_dim(part, me ^ k, 3, keepdims=False)
        mine = mine + lax.ppermute(other, "tp", [(i, i ^ k) for i in range(tp)])
    fresh = mine.astype(jnp.bfloat16)
    return fresh, attend_new(queries, fresh, top, total, summed)


def solution(mesh):
    dp, tp = mesh.shape["dp"], mesh.shape["tp"]

    def body(*args):
        return shards(dp, tp, *args)

    return jax.shard_map(
        body,
        mesh=mesh,
        in_specs=(
            P(("parts", "dp"), None, "tp"),
            P("tp", None, None, None),
            P(("parts", "tp"), "dp"),
            P(("parts", "dp"), None, None, None),
            P(("parts", "dp"), None, "tp", None),
            P(("parts", "dp"), None, None, "tp", None),
            P(("parts", "dp")),
        ),
        out_specs=(
            P(("parts", "dp"), None, None, "tp", None),
            P(("parts", "dp"), None, "tp", None),
        ),
        check_vma=False,
    )
```

```python
import jax
import jax.numpy as jnp
from jax import lax
from jax.sharding import PartitionSpec as P


def gather_rows(x, count):
    copies = jnp.broadcast_to(x[None], (count,) + x.shape)
    return lax.all_to_all(copies, "dp", 0, 0, tiled=True).reshape((count * x.shape[0],) + x.shape[1:])


def attend_cached(queries, cache, lengths):
    rows, steps, heads, size = queries.shape
    slots, kvh = cache.shape[1], cache.shape[3]
    grouped = queries.reshape(rows, steps, kvh, heads // kvh, size)
    scores = (
        jnp.einsum("rtgqd,rjgd->rtgqj", grouped, cache[:, :, 0], preferred_element_type=jnp.float32)
        * size ** (-0.5)
    )
    live = (jnp.arange(slots)[None, :] < lengths[:, None])[:, None, None, None, :]
    scores = jnp.where(live, scores, -1e30)
    top = jnp.max(scores, axis=-1, keepdims=True)
    expo = jnp.where(live, jnp.exp(scores - top), 0.0)
    total = jnp.sum(expo, axis=-1, keepdims=True)
    summed = jnp.einsum(
        "rtgqj,rjgd->rtgqd", expo.astype(jnp.bfloat16), cache[:, :, 1], preferred_element_type=jnp.float32
    )
    return top, total, summed


def attend_new(queries, fresh, top_old, total_old, summed_old):
    rows, steps, heads, size = queries.shape
    kvh = fresh.shape[3]
    grouped = queries.reshape(rows, steps, kvh, heads // kvh, size)
    scores = (
        jnp.einsum("rtgqd,rjgd->rtgqj", grouped, fresh[:, :, 0], preferred_element_type=jnp.float32)
        * size ** (-0.5)
    )
    live = (jnp.arange(steps)[None, :] <= jnp.arange(steps)[:, None])[None, :, None, None, :]
    scores = jnp.where(live, scores, -1e30)
    top = jnp.maximum(top_old, jnp.max(scores, axis=-1, keepdims=True))
    expo = jnp.where(live, jnp.exp(scores - top), 0.0)
    back = jnp.exp(top_old - top)
    total = back * total_old + jnp.sum(expo, axis=-1, keepdims=True)
    summed = back * summed_old + jnp.einsum(
        "rtgqj,rjgd->rtgqd", expo.astype(jnp.bfloat16), fresh[:, :, 1], preferred_element_type=jnp.float32
    )
    return (summed / total).reshape(rows, steps, heads, size).astype(jnp.bfloat16)


def shards(dp, tp, hidden, base_weight, factor_a, factor_b, queries, cache, lengths):
    width, _, kvh_all, size = base_weight.shape
    columns = 2 * kvh_all * size
    own = cache.shape[3]
    rows, steps = hidden.shape[:2]
    payload = jnp.concatenate([factor_a.T, factor_b.reshape(factor_b.shape[0], columns)], axis=1)
    gathered = gather_rows(payload, dp)
    down, up = gathered[:, :width], gathered[:, width:]
    top, total, summed = attend_cached(queries, cache, lengths)
    low_rank = lax.dot_general(
        down, up, (((0,), (0,)), ((), ())), preferred_element_type=jnp.float32
    )
    merged = (base_weight.reshape(width, columns).astype(jnp.float32) + low_rank).astype(jnp.bfloat16)
    part = jnp.dot(hidden.reshape(rows * steps, width), merged, preferred_element_type=jnp.float32)
    part = part.reshape(rows, steps, 2, tp, own, size)
    me = lax.axis_index("tp")
    mine = lax.dynamic_index_in_dim(part, me, 3, keepdims=False)
    for k in range(1, tp):
        other = lax.dynamic_index_in_dim(part, me ^ k, 3, keepdims=False)
        mine = mine + lax.ppermute(other, "tp", [(i, i ^ k) for i in range(tp)])
    fresh = mine.astype(jnp.bfloat16)
    return fresh, attend_new(queries, fresh, top, total, summed)


def solution(mesh):
    dp, tp = mesh.shape["dp"], mesh.shape["tp"]

    def body(*args):
        return shards(dp, tp, *args)

    return jax.shard_map(
        body,
        mesh=mesh,
        in_specs=(
            P(("parts", "dp"), None, "tp"),
            P("tp", None, None, None),
            P(("parts", "tp"), "dp"),
            P(("parts", "dp"), None, None, None),
            P(("parts", "dp"), None, "tp", None),
            P(("parts", "dp"), None, None, "tp", None),
            P(("parts", "dp")),
        ),
        out_specs=(
            P(("parts", "dp"), None, None, "tp", None),
            P(("parts", "dp"), None, "tp", None),
        ),
        check_vma=False,
    )
```

```python
import functools

import jax
import jax.numpy as jnp
from jax import lax
from jax.experimental import pallas as pl
from jax.experimental.pallas import tpu as pltpu
from jax.sharding import PartitionSpec as P

LOW = -1e30
NT = (((1,), (1,)), ((), ()))
VMEM = pl.BlockSpec(memory_space=pltpu.VMEM)


def params(mib):
    return pltpu.CompilerParams(vmem_limit_bytes=mib * 1024 * 1024)


def cost(flops, moved, exps=0):
    return pl.CostEstimate(flops=flops, bytes_accessed=moved, transcendentals=exps)


def payload_kernel(down_ref, up_ref, out_ref, wide):
    ranks, width = down_ref.shape
    groups = up_ref.shape[1] * up_ref.shape[2]
    size = up_ref.shape[3]
    wide[...] = up_ref.reshape(ranks * groups, size)[...].astype(jnp.float32)
    down = down_ref[...]
    ups = [wide[pl.ds(n, ranks, stride=groups), :].astype(jnp.bfloat16) for n in range(groups)]
    for i in range(out_ref.shape[0]):
        out_ref[i, :, :width] = down
        for n in range(groups):
            out_ref[i, :, width + n * size : width + (n + 1) * size] = ups[n]


def make_payload(down, up, count):
    ranks, width = down.shape
    columns = up.shape[1] * up.shape[2] * up.shape[3]
    return pl.pallas_call(
        payload_kernel,
        out_shape=jax.ShapeDtypeStruct((count, ranks, width + columns), jnp.bfloat16),
        in_specs=[VMEM, VMEM],
        out_specs=VMEM,
        scratch_shapes=[pltpu.VMEM((ranks * columns // up.shape[3], up.shape[3]), jnp.float32)],
        compiler_params=params(8),
        name="payload",
    )(down, up)


def arrange_kernel(own, base_ref, out_ref, wide):
    width, two, kvh, size = base_ref.shape
    groups = two * kvh
    wide[...] = base_ref.reshape(width * groups, size)[...].astype(jnp.float32)
    for n in range(groups):
        part, at = n // own, n % own
        out_ref[part, :, at * size : (at + 1) * size] = wide[pl.ds(n, width, stride=groups), :].astype(jnp.bfloat16)


def arrange_base(base, own, step=512):
    width, two, kvh, size = base.shape
    groups = two * kvh
    return pl.pallas_call(
        functools.partial(arrange_kernel, own),
        grid=(width // step,),
        out_shape=jax.ShapeDtypeStruct((groups // own, width, own * size), jnp.bfloat16),
        in_specs=[pl.BlockSpec((step, two, kvh, size), lambda i: (i, 0, 0, 0))],
        out_specs=pl.BlockSpec((groups // own, step, own * size), lambda i: (0, i, 0)),
        scratch_shapes=[pltpu.VMEM((step * groups, size), jnp.float32)],
        compiler_params=params(24),
        cost_estimate=cost(0, 4 * base.size),
        name="arrange_base",
    )(base)


def cached_kernel(heads, scale, lengths_ref, q_ref, k_ref, v_ref, sum_ref, total_ref, top_ref):
    rows, queries, size = q_ref.shape
    slots, own = k_ref.shape[1], k_ref.shape[2]
    keys = slots * own
    at = pl.program_id(0) * rows
    column = lax.broadcasted_iota(jnp.int32, (queries, keys), 1)
    head = lax.broadcasted_iota(jnp.int32, (queries, keys), 0) % heads
    column = jnp.where(column % own == head // (heads // own), column, own * slots)
    ones = jnp.ones((keys, size), jnp.bfloat16)
    k_all = k_ref.reshape(rows, keys, size)
    v_all = v_ref.reshape(rows, keys, size)
    for r in range(rows):
        scores = lax.dot_general(q_ref[r], k_all[r], NT, preferred_element_type=jnp.float32)
        scores = jnp.where(column < own * lengths_ref[at + r], scores, LOW)
        top = jnp.max(scores, axis=-1, keepdims=True)
        weights = jnp.exp((scores - top) * scale).astype(jnp.bfloat16)
        both = jnp.dot(
            weights, jnp.concatenate([v_all[r], ones], axis=1), preferred_element_type=jnp.float32
        )
        sum_ref[r] = both[:, :size]
        total_ref[r] = both[:, size:]
        top_ref[r] = jnp.broadcast_to(top, (queries, size))


def attend_cached(queries, cache, lengths, step=8):
    rows, steps, heads, size = queries.shape
    slots, own = cache.shape[1], cache.shape[3]
    many = steps * heads
    state = jax.ShapeDtypeStruct((rows, many, size), jnp.float32)
    block = pl.BlockSpec((step, many, size), lambda i, *_: (i, 0, 0))

    def half(c):
        return pl.BlockSpec((step, slots, None, own, size), lambda i, *_: (i, 0, c, 0, 0))

    return pl.pallas_call(
        functools.partial(cached_kernel, heads, size ** (-0.5)),
        out_shape=(state, state, state),
        grid_spec=pltpu.PrefetchScalarGridSpec(
            num_scalar_prefetch=1,
            grid=(rows // step,),
            in_specs=[block, half(0), half(1)],
            out_specs=(block, block, block),
        ),
        compiler_params=params(24),
        cost_estimate=cost(
            8 * rows * many * slots * size, 2 * (cache.size + queries.size) + 12 * rows * many * size, rows * many * slots
        ),
        name="attend_cached",
    )(lengths, queries.reshape(rows, many, size), cache, cache)


def project_kernel(down_at, which_ref, hidden_ref, gathered_ref, base_ref, out_ref, merged):
    width, columns = merged.shape
    part = which_ref[0]
    parts = base_ref.shape[0] // 2
    half = columns // 2
    up = jnp.concatenate(
        [
            gathered_ref[:, pl.ds(pl.multiple_of(down_at + (c * parts + part) * half, 128), half)]
            for c in range(2)
        ],
        axis=1,
    )
    step = 512
    for f in range(0, width, step):
        down = gathered_ref[:, f : f + step].T
        low_rank = jnp.dot(down, up, preferred_element_type=jnp.float32)
        for c in range(2):
            base = base_ref[c * parts + part, f : f + step, :].astype(jnp.float32)
            merged[f : f + step, c * half : (c + 1) * half] = (base + low_rank[:, c * half : (c + 1) * half]).astype(
                jnp.bfloat16
            )
    out_ref[...] = jnp.dot(hidden_ref[...], merged[...], preferred_element_type=jnp.float32)


def project(which, hidden, gathered, base):
    tokens, width = hidden.shape
    columns = 2 * base.shape[2]
    return pl.pallas_call(
        functools.partial(project_kernel, width),
        out_shape=jax.ShapeDtypeStruct((tokens, columns), jnp.float32),
        in_specs=[pl.BlockSpec(memory_space=pltpu.SMEM), VMEM, VMEM, VMEM],
        out_specs=VMEM,
        scratch_shapes=[pltpu.VMEM((width, columns), jnp.bfloat16)],
        compiler_params=params(24),
        cost_estimate=cost(
            2 * width * columns * (tokens + gathered.shape[0]), 2 * width * columns + 2 * width * tokens
        ),
        name="project",
    )(which, hidden, gathered, base)


def finish_kernel(steps, heads, scale, group, terms, *refs):
    parts, refs = refs[:terms], refs[terms:]
    q_ref, sum_ref, total_ref, top_ref, fresh_ref, context_ref, wide, bias = refs
    rows, queries, size = q_ref.shape
    own = fresh_ref.shape[3]
    fresh = parts[0][...]
    for part in parts[1:]:
        fresh = fresh + part[...]
    for n in range(2 * own):
        wide[pl.ds(n, rows * steps, stride=2 * own), :] = fresh[:, n * size : (n + 1) * size]
    fresh_ref.reshape(rows * steps * 2 * own, size)[...] = wide[...].astype(jnp.bfloat16)
    fresh = fresh.astype(jnp.bfloat16)
    many, keys = group * queries, own * group * steps
    query = lax.broadcasted_iota(jnp.int32, (many, keys), 0)
    key = lax.broadcasted_iota(jnp.int32, (many, keys), 1)
    same_head = (query % heads) // (heads // own) == key // (group * steps)
    same_row = query // queries == (key // steps) % group
    seen = (query % queries) // heads >= key % steps
    bias[...] = jnp.where(same_head & same_row & seen, 0.0, LOW)
    ones = jnp.ones((keys, size), jnp.bfloat16)
    for at in range(0, rows, group):
        tokens = slice(at * steps, (at + group) * steps)
        keys_new, values_new = [
            jnp.concatenate(
                [fresh[tokens, (c * own + g) * size : (c * own + g + 1) * size] for g in range(own)], axis=0
            )
            for c in range(2)
        ]
        values_new = jnp.concatenate([values_new, ones], axis=1)
        mine = slice(at, at + group)
        scores = lax.dot_general(
            q_ref[mine].reshape(many, size), keys_new, NT, preferred_element_type=jnp.float32
        )
        scores = scores + bias[...]
        top_old = top_ref[mine].reshape(many, size)
        top = jnp.maximum(top_old, jnp.max(scores, axis=-1, keepdims=True))
        weights = jnp.exp((scores - top) * scale).astype(jnp.bfloat16)
        back = jnp.exp((top_old - top) * scale)
        both = jnp.dot(weights, values_new, preferred_element_type=jnp.float32)
        total = back * total_ref[mine].reshape(many, size) + both[:, size:]
        summed = back * sum_ref[mine].reshape(many, size) + both[:, :size]
        context_ref[mine] = (summed / total).astype(jnp.bfloat16).reshape(group, queries, size)


def finish(parts, queries, state, own):
    rows, steps, heads, size = queries.shape
    group = size // (own * steps)
    many = steps * heads
    fresh, context = pl.pallas_call(
        functools.partial(finish_kernel, steps, heads, size ** (-0.5), group, len(parts)),
        out_shape=(
            jax.ShapeDtypeStruct((rows, steps, 2, own, size), jnp.bfloat16),
            jax.ShapeDtypeStruct((rows, many, size), jnp.bfloat16),
        ),
        in_specs=[VMEM] * (len(parts) + 1 + len(state)),
        out_specs=(VMEM, VMEM),
        scratch_shapes=[
            pltpu.VMEM((rows * steps * 2 * own, size), jnp.float32),
            pltpu.VMEM((group * many, own * group * steps), jnp.float32),
        ],
        compiler_params=params(24),
        cost_estimate=cost(rows * many * size * size * 6, 12 * rows * many * size, rows * many * size * 2),
        name="finish",
    )(*parts, queries.reshape(rows, many, size), *state)
    return fresh, context.reshape(rows, steps, heads, size)


def shards(dp, tp, hidden, base_weight, factor_a, factor_b, queries, cache, lengths):
    rows, steps, width = hidden.shape
    own = cache.shape[3]
    payload = make_payload(factor_a.T, factor_b, dp)
    gathered = lax.all_to_all(payload, "dp", 0, 0, tiled=True)
    gathered = gathered.reshape(-1, gathered.shape[-1])
    base = arrange_base(base_weight, own)
    state = attend_cached(queries, cache, lengths)
    tokens = hidden.reshape(rows * steps, width)
    me = lax.axis_index("tp")
    received = []
    for k in range(1, tp):
        other = project(jnp.full((1,), me ^ k, jnp.int32), tokens, gathered, base)
        received.append(lax.ppermute(other, "tp", [(i, i ^ k) for i in range(tp)]))
    mine = project(jnp.full((1,), me, jnp.int32), tokens, gathered, base)
    return finish([mine] + received, queries, state, own)


def solution(mesh):
    return jax.shard_map(
        functools.partial(shards, mesh.shape["dp"], mesh.shape["tp"]),
        mesh=mesh,
        in_specs=(
            P(("parts", "dp"), None, "tp"),
            P("tp", None, None, None),
            P(("parts", "tp"), "dp"),
            P(("parts", "dp"), None, None, None),
            P(("parts", "dp"), None, "tp", None),
            P(("parts", "dp"), None, None, "tp", None),
            P(("parts", "dp")),
        ),
        out_specs=(
            P(("parts", "dp"), None, None, "tp", None),
            P(("parts", "dp"), None, "tp", None),
        ),
        check_vma=False,
    )
```

```python
import functools

import jax
import jax.numpy as jnp
from jax import lax
from jax.experimental import pallas as pl
from jax.experimental.pallas import tpu as pltpu
from jax.sharding import PartitionSpec as P

LOW = -1e30
NT = (((1,), (1,)), ((), ()))
VMEM = pl.BlockSpec(memory_space=pltpu.VMEM)


def params(mib):
    return pltpu.CompilerParams(vmem_limit_bytes=mib * 1024 * 1024)


def cost(flops, moved, exps=0):
    return pl.CostEstimate(flops=flops, bytes_accessed=moved, transcendentals=exps)


def payload_kernel(down_hbm, up_hbm, out_hbm, held, ups, wide, sems):
    ranks, width = down_hbm.shape
    groups, size = ups.shape[1] * ups.shape[2], ups.shape[3]
    get_down = pltpu.make_async_copy(down_hbm, held.at[:, pl.ds(0, width)], sems.at[0])
    get_up = pltpu.make_async_copy(up_hbm, ups, sems.at[1])
    get_up.start()
    get_down.start()
    get_up.wait()
    wide[...] = ups.reshape(ranks * groups, size)[...].astype(jnp.float32)
    for n in range(groups):
        held[:, width + n * size : width + (n + 1) * size] = wide[pl.ds(n, ranks, stride=groups), :].astype(
            jnp.bfloat16
        )
    get_down.wait()
    puts = [pltpu.make_async_copy(held, out_hbm.at[i], sems.at[2 + i]) for i in range(out_hbm.shape[0])]
    for put in puts:
        put.start()
    for put in puts:
        put.wait()


def make_payload(down, up, count):
    ranks, width = down.shape
    groups, size = up.shape[1] * up.shape[2], up.shape[3]
    held = (ranks, width + groups * size)
    return pl.pallas_call(
        payload_kernel,
        out_shape=jax.ShapeDtypeStruct((count,) + held, jnp.bfloat16),
        in_specs=[pl.BlockSpec(memory_space=pltpu.HBM)] * 2,
        out_specs=pl.BlockSpec(memory_space=pltpu.HBM),
        scratch_shapes=[
            pltpu.VMEM(held, jnp.bfloat16),
            pltpu.VMEM(up.shape, jnp.bfloat16),
            pltpu.VMEM((ranks * groups, size), jnp.float32),
            pltpu.SemaphoreType.DMA((2 + count,)),
        ],
        compiler_params=params(8),
        name="payload",
    )(down, up)


def arrange_kernel(own, tile, base_ref, out_ref):
    width, two, kvh, size = base_ref.shape
    groups = two * kvh
    some = tile // groups
    row = lax.broadcasted_iota(jnp.int32, (tile, tile), 0)
    column = lax.broadcasted_iota(jnp.int32, (tile, tile), 1)
    order = (column == (row % some) * groups + row // some).astype(jnp.float32).astype(jnp.bfloat16)
    flat = base_ref.reshape(width * groups, size)
    for f in range(0, width, 2 * some):
        at = f * groups
        pair = jnp.concatenate([flat[at : at + tile, :], flat[at + tile : at + 2 * tile, :]], axis=1)
        moved = jnp.dot(order, pair, preferred_element_type=jnp.float32).astype(jnp.bfloat16)
        for n in range(groups):
            lanes = slice((n % own) * size, (n % own + 1) * size)
            for h in range(2):
                out_ref[n // own, f + h * some : f + (h + 1) * some, lanes] = moved[
                    n * some : (n + 1) * some, h * size : (h + 1) * size
                ]


def arrange_base(base, own, step=512):
    width, two, kvh, size = base.shape
    groups = two * kvh
    return pl.pallas_call(
        functools.partial(arrange_kernel, own, 256),
        grid=(width // step,),
        out_shape=jax.ShapeDtypeStruct((groups // own, width, own * size), jnp.bfloat16),
        in_specs=[pl.BlockSpec((step, two, kvh, size), lambda i: (i, 0, 0, 0))],
        out_specs=pl.BlockSpec((groups // own, step, own * size), lambda i: (0, i, 0)),
        compiler_params=params(48),
        cost_estimate=cost(512 * base.size, 4 * base.size),
        name="arrange_base",
    )(base)


def cached_kernel(heads, scale, lengths_ref, q_ref, k_ref, v_ref, sum_ref, total_ref, top_ref):
    rows, queries, size = q_ref.shape
    slots, own = k_ref.shape[1], k_ref.shape[2]
    keys = slots * own
    at = pl.program_id(0) * rows
    column = lax.broadcasted_iota(jnp.int32, (queries, keys), 1)
    head = lax.broadcasted_iota(jnp.int32, (queries, keys), 0) % heads
    column = jnp.where(column % own == head // (heads // own), column, own * slots)
    ones = jnp.ones((keys, size), jnp.bfloat16)
    k_all = k_ref.reshape(rows, keys, size)
    v_all = v_ref.reshape(rows, keys, size)
    some = 4
    for first in range(0, rows, some):
        group = range(first, first + some)
        scores = [lax.dot_general(q_ref[r], k_all[r], NT, preferred_element_type=jnp.float32) for r in group]
        scores = [jnp.where(column < own * lengths_ref[at + r], s, LOW) for r, s in zip(group, scores)]
        tops = [jnp.max(s, axis=-1, keepdims=True) for s in scores]
        weights = [jnp.exp((s - t) * scale).astype(jnp.bfloat16) for s, t in zip(scores, tops)]
        for r, w, top in zip(group, weights, tops):
            both = jnp.dot(w, jnp.concatenate([v_all[r], ones], axis=1), preferred_element_type=jnp.float32)
            sum_ref[r] = both[:, :size]
            total_ref[r] = both[:, size:]
            top_ref[r] = jnp.broadcast_to(top, (queries, size))


def attend_cached(queries, cache, lengths, step=8):
    rows, steps, heads, size = queries.shape
    slots, own = cache.shape[1], cache.shape[3]
    many = steps * heads
    state = jax.ShapeDtypeStruct((rows, many, size), jnp.float32)
    block = pl.BlockSpec((step, many, size), lambda i, *_: (i, 0, 0))

    def half(c):
        return pl.BlockSpec((step, slots, None, own, size), lambda i, *_: (i, 0, c, 0, 0))

    return pl.pallas_call(
        functools.partial(cached_kernel, heads, size ** (-0.5)),
        out_shape=(state, state, state),
        grid_spec=pltpu.PrefetchScalarGridSpec(
            num_scalar_prefetch=1,
            grid=(rows // step,),
            in_specs=[block, half(0), half(1)],
            out_specs=(block, block, block),
        ),
        compiler_params=params(48),
        cost_estimate=cost(
            8 * rows * many * slots * size, 2 * (cache.size + queries.size) + 12 * rows * many * size, rows * many * slots
        ),
        name="attend_cached",
    )(lengths, queries.reshape(rows, many, size), cache, cache)


def project_kernel(down_at, which_ref, hidden_ref, gathered_ref, base_ref, out_ref, merged):
    width, columns = merged.shape
    part = which_ref[0]
    parts = base_ref.shape[0] // 2
    half = columns // 2
    up = jnp.concatenate(
        [
            gathered_ref[:, pl.ds(pl.multiple_of(down_at + (c * parts + part) * half, 128), half)]
            for c in range(2)
        ],
        axis=1,
    )
    step = 512
    for f in range(0, width, step):
        down = gathered_ref[:, f : f + step].T
        low_rank = jnp.dot(down, up, preferred_element_type=jnp.float32)
        for c in range(2):
            base = base_ref[c * parts + part, f : f + step, :].astype(jnp.float32)
            merged[f : f + step, c * half : (c + 1) * half] = (base + low_rank[:, c * half : (c + 1) * half]).astype(
                jnp.bfloat16
            )
    out_ref[...] = jnp.dot(hidden_ref[...], merged[...], preferred_element_type=jnp.float32)


def project(which, hidden, gathered, base):
    tokens, width = hidden.shape
    columns = 2 * base.shape[2]
    return pl.pallas_call(
        functools.partial(project_kernel, width),
        out_shape=jax.ShapeDtypeStruct((tokens, columns), jnp.float32),
        in_specs=[pl.BlockSpec(memory_space=pltpu.SMEM), VMEM, VMEM, VMEM],
        out_specs=VMEM,
        scratch_shapes=[pltpu.VMEM((width, columns), jnp.bfloat16)],
        compiler_params=params(24),
        cost_estimate=cost(
            2 * width * columns * (tokens + gathered.shape[0]), 2 * width * columns + 2 * width * tokens
        ),
        name="project",
    )(which, hidden, gathered, base)


def finish_kernel(steps, heads, scale, group, terms, *refs):
    parts, refs = refs[:terms], refs[terms:]
    q_ref, sum_ref, total_ref, top_ref, fresh_ref, context_ref, wide, bias = refs
    rows, queries, size = q_ref.shape
    own = fresh_ref.shape[3]
    fresh = parts[0][...]
    for part in parts[1:]:
        fresh = fresh + part[...]
    for n in range(2 * own):
        wide[pl.ds(n, rows * steps, stride=2 * own), :] = fresh[:, n * size : (n + 1) * size]
    fresh_ref.reshape(rows * steps * 2 * own, size)[...] = wide[...].astype(jnp.bfloat16)
    fresh = fresh.astype(jnp.bfloat16)
    many, keys = group * queries, own * group * steps
    query = lax.broadcasted_iota(jnp.int32, (many, keys), 0)
    key = lax.broadcasted_iota(jnp.int32, (many, keys), 1)
    same_head = (query % heads) // (heads // own) == key // (group * steps)
    same_row = query // queries == (key // steps) % group
    seen = (query % queries) // heads >= key % steps
    bias[...] = jnp.where(same_head & same_row & seen, 0.0, LOW)
    ones = jnp.ones((keys, size), jnp.bfloat16)
    for at in range(0, rows, group):
        tokens = slice(at * steps, (at + group) * steps)
        keys_new, values_new = [
            jnp.concatenate(
                [fresh[tokens, (c * own + g) * size : (c * own + g + 1) * size] for g in range(own)], axis=0
            )
            for c in range(2)
        ]
        values_new = jnp.concatenate([values_new, ones], axis=1)
        mine = slice(at, at + group)
        scores = lax.dot_general(
            q_ref[mine].reshape(many, size), keys_new, NT, preferred_element_type=jnp.float32
        )
        scores = scores + bias[...]
        top_old = top_ref[mine].reshape(many, size)
        top = jnp.maximum(top_old, jnp.max(scores, axis=-1, keepdims=True))
        weights = jnp.exp((scores - top) * scale).astype(jnp.bfloat16)
        back = jnp.exp((top_old - top) * scale)
        both = jnp.dot(weights, values_new, preferred_element_type=jnp.float32)
        total = back * total_ref[mine].reshape(many, size) + both[:, size:]
        summed = back * sum_ref[mine].reshape(many, size) + both[:, :size]
        context_ref[mine] = (summed / total).astype(jnp.bfloat16).reshape(group, queries, size)


def finish(parts, queries, state, own):
    rows, steps, heads, size = queries.shape
    group = size // (own * steps)
    many = steps * heads
    fresh, context = pl.pallas_call(
        functools.partial(finish_kernel, steps, heads, size ** (-0.5), group, len(parts)),
        out_shape=(
            jax.ShapeDtypeStruct((rows, steps, 2, own, size), jnp.bfloat16),
            jax.ShapeDtypeStruct((rows, many, size), jnp.bfloat16),
        ),
        in_specs=[VMEM] * (len(parts) + 1 + len(state)),
        out_specs=(VMEM, VMEM),
        scratch_shapes=[
            pltpu.VMEM((rows * steps * 2 * own, size), jnp.float32),
            pltpu.VMEM((group * many, own * group * steps), jnp.float32),
        ],
        compiler_params=params(24),
        cost_estimate=cost(rows * many * size * size * 6, 12 * rows * many * size, rows * many * size * 2),
        name="finish",
    )(*parts, queries.reshape(rows, many, size), *state)
    return fresh, context.reshape(rows, steps, heads, size)


def shards(dp, tp, hidden, base_weight, factor_a, factor_b, queries, cache, lengths):
    rows, steps, width = hidden.shape
    own = cache.shape[3]
    payload = make_payload(factor_a.T, factor_b, dp)
    gathered = lax.all_to_all(payload, "dp", 0, 0, tiled=True)
    gathered = gathered.reshape(-1, gathered.shape[-1])
    state = attend_cached(queries, cache, lengths)
    base_weight, state = lax.optimization_barrier((base_weight, state))
    base = arrange_base(base_weight, own)
    tokens = hidden.reshape(rows * steps, width)
    me = lax.axis_index("tp")
    received = []
    for k in range(1, tp):
        other = project(jnp.full((1,), me ^ k, jnp.int32), tokens, gathered, base)
        received.append(lax.ppermute(other, "tp", [(i, i ^ k) for i in range(tp)]))
    mine = project(jnp.full((1,), me, jnp.int32), tokens, gathered, base)
    return finish([mine] + received, queries, state, own)


def solution(mesh):
    return jax.shard_map(
        functools.partial(shards, mesh.shape["dp"], mesh.shape["tp"]),
        mesh=mesh,
        in_specs=(
            P(("parts", "dp"), None, "tp"),
            P("tp", None, None, None),
            P(("parts", "tp"), "dp"),
            P(("parts", "dp"), None, None, None),
            P(("parts", "dp"), None, "tp", None),
            P(("parts", "dp"), None, None, "tp", None),
            P(("parts", "dp")),
        ),
        out_specs=(
            P(("parts", "dp"), None, None, "tp", None),
            P(("parts", "dp"), None, "tp", None),
        ),
        check_vma=False,
    )
```

```python
import functools

import jax
import jax.numpy as jnp
from jax import lax
from jax.experimental import pallas as pl
from jax.experimental.pallas import tpu as pltpu
from jax.sharding import PartitionSpec as P

LOW = -1e30
NT = (((1,), (1,)), ((), ()))
VMEM = pl.BlockSpec(memory_space=pltpu.VMEM)


def params(mib):
    return pltpu.CompilerParams(vmem_limit_bytes=mib * 1024 * 1024)


def cost(flops, moved, exps=0):
    return pl.CostEstimate(flops=flops, bytes_accessed=moved, transcendentals=exps)


def payload_kernel(down_hbm, up_hbm, out_hbm, held, ups, wide, sems):
    ranks, width = down_hbm.shape
    groups, size = ups.shape[1] * ups.shape[2], ups.shape[3]
    get_down = pltpu.make_async_copy(down_hbm, held.at[:, pl.ds(0, width)], sems.at[0])
    get_up = pltpu.make_async_copy(up_hbm, ups, sems.at[1])
    get_up.start()
    get_down.start()
    get_up.wait()
    wide[...] = ups.reshape(ranks * groups, size)[...].astype(jnp.float32)
    for n in range(groups):
        held[:, width + n * size : width + (n + 1) * size] = wide[pl.ds(n, ranks, stride=groups), :].astype(
            jnp.bfloat16
        )
    get_down.wait()
    puts = [pltpu.make_async_copy(held, out_hbm.at[i], sems.at[2 + i]) for i in range(out_hbm.shape[0])]
    for put in puts:
        put.start()
    for put in puts:
        put.wait()


def make_payload(down, up, count):
    ranks, width = down.shape
    groups, size = up.shape[1] * up.shape[2], up.shape[3]
    held = (ranks, width + groups * size)
    return pl.pallas_call(
        payload_kernel,
        out_shape=jax.ShapeDtypeStruct((count,) + held, jnp.bfloat16),
        in_specs=[pl.BlockSpec(memory_space=pltpu.HBM)] * 2,
        out_specs=pl.BlockSpec(memory_space=pltpu.HBM),
        scratch_shapes=[
            pltpu.VMEM(held, jnp.bfloat16),
            pltpu.VMEM(up.shape, jnp.bfloat16),
            pltpu.VMEM((ranks * groups, size), jnp.float32),
            pltpu.SemaphoreType.DMA((2 + count,)),
        ],
        compiler_params=params(60),
        name="payload",
    )(down, up)


def local_kernel(chunks, heads, scale, *refs):
    lengths_ref, hidden_hbm, base_hbm, queries_hbm, cache_hbm = refs[:5]
    tokens_ref, base_ref, sum_ref, total_ref, top_ref = refs[5:10]
    hidden, base, q_all, k_all, v_all, sems = refs[10:]
    rows, queries, size = q_all.shape
    slots, own = k_all.shape[1:3]
    keys = slots * own
    width, two, kvh, _ = base.shape
    groups = two * kvh
    some_rows, some_width = rows // chunks, width // chunks

    def copies(i):
        mine = pl.ds(i * some_rows, some_rows)
        features = pl.ds(i * some_width, some_width)
        pairs = (
            (queries_hbm.at[mine], q_all.at[mine]),
            (cache_hbm.at[mine, :, 0], k_all.at[mine]),
            (cache_hbm.at[mine, :, 1], v_all.at[mine]),
            (base_hbm.at[features], base.at[features]),
        )
        return [pltpu.make_async_copy(a, b, sems.at[i, n]) for n, (a, b) in enumerate(pairs)]

    get_hidden = pltpu.make_async_copy(hidden_hbm, hidden, sems.at[chunks, 0])
    for i in range(chunks):
        for copy in copies(i):
            copy.start()
    get_hidden.start()

    column = lax.broadcasted_iota(jnp.int32, (queries, keys), 1)
    head = lax.broadcasted_iota(jnp.int32, (queries, keys), 0) % heads
    column = jnp.where(column % own == head // (heads // own), column, own * slots)
    ones = jnp.ones((keys, size), jnp.bfloat16)
    tile = 256
    some = tile // groups
    row = lax.broadcasted_iota(jnp.int32, (tile, tile), 0)
    place = lax.broadcasted_iota(jnp.int32, (tile, tile), 1)
    order = (place == (row % some) * groups + row // some).astype(jnp.float32).astype(jnp.bfloat16)
    flat_base = base.reshape(width * groups, size)
    flat_k = k_all.reshape(rows, keys, size)
    flat_v = v_all.reshape(rows, keys, size)

    def attend(at, count):
        group = [at + r for r in range(count)]
        scores = [lax.dot_general(q_all[r], flat_k[r], NT, preferred_element_type=jnp.float32) for r in group]
        scores = [jnp.where(column < own * lengths_ref[r], s, LOW) for r, s in zip(group, scores)]
        tops = [jnp.max(s, axis=-1, keepdims=True) for s in scores]
        weights = [jnp.exp((s - t) * scale).astype(jnp.bfloat16) for s, t in zip(scores, tops)]
        for r, w, top in zip(group, weights, tops):
            both = jnp.dot(w, jnp.concatenate([flat_v[r], ones], axis=1), preferred_element_type=jnp.float32)
            sum_ref[r] = both[:, :size]
            total_ref[r] = both[:, size:]
            top_ref[r] = jnp.broadcast_to(top, (queries, size))

    def arrange(f):
        at = pl.multiple_of(f * groups, tile)
        pair = jnp.concatenate([flat_base[pl.ds(at + h * tile, tile), :] for h in range(2)], axis=1)
        moved = jnp.dot(order, pair, preferred_element_type=jnp.float32).astype(jnp.bfloat16)
        for n in range(groups):
            lanes = slice((n % own) * size, (n % own + 1) * size)
            for h in range(2):
                base_ref[n // own, pl.ds(pl.multiple_of(f + h * some, some), some), lanes] = moved[
                    n * some : (n + 1) * some, h * size : (h + 1) * size
                ]

    @pl.loop(0, chunks)
    def _(i):
        for copy in copies(i):
            copy.wait()
        for r in range(0, some_rows, 3):
            attend(i * some_rows + r, 3)
        for f in range(0, some_width, 2 * some):
            arrange(i * some_width + f)

    get_hidden.wait()
    tokens_ref[...] = hidden.reshape(tokens_ref.shape)[...]


def local(hidden, base, queries, cache, lengths):
    rows, steps, heads, size = queries.shape
    slots, own = cache.shape[1], cache.shape[3]
    width, two, kvh, _ = base.shape
    many = steps * heads
    chunks = 8
    state = jax.ShapeDtypeStruct((rows, many, size), jnp.float32)
    half = (rows, slots, own, size)
    outs = (
        jax.ShapeDtypeStruct((rows * steps, width), jnp.bfloat16),
        jax.ShapeDtypeStruct((two * kvh // own, width, own * size), jnp.bfloat16),
        state,
        state,
        state,
    )
    tokens, base, *state = pl.pallas_call(
        functools.partial(local_kernel, chunks, heads, size ** (-0.5)),
        out_shape=outs,
        in_specs=[pl.BlockSpec(memory_space=pltpu.SMEM)] + [pl.BlockSpec(memory_space=pltpu.HBM)] * 4,
        out_specs=(VMEM,) * len(outs),
        scratch_shapes=[
            pltpu.VMEM(hidden.shape, jnp.bfloat16),
            pltpu.VMEM(base.shape, jnp.bfloat16),
            pltpu.VMEM((rows, many, size), jnp.bfloat16),
            pltpu.VMEM(half, jnp.bfloat16),
            pltpu.VMEM(half, jnp.bfloat16),
            pltpu.SemaphoreType.DMA((chunks + 1, 4)),
        ],
        compiler_params=params(44),
        cost_estimate=cost(
            8 * rows * many * slots * size + 512 * base.size,
            2 * (cache.size + queries.size + base.size + hidden.size),
            rows * many * slots,
        ),
        name="local",
    )(lengths, hidden, base, queries.reshape(rows, many, size), cache)
    return tokens, base, state


def project_kernel(down_at, which_ref, hidden_ref, gathered_ref, base_ref, out_ref, merged):
    width, columns = merged.shape
    part = which_ref[0]
    parts = base_ref.shape[0] // 2
    half = columns // 2
    up = jnp.concatenate(
        [
            gathered_ref[:, pl.ds(pl.multiple_of(down_at + (c * parts + part) * half, 128), half)]
            for c in range(2)
        ],
        axis=1,
    )
    step = 512
    for f in range(0, width, step):
        down = gathered_ref[:, f : f + step].T
        low_rank = jnp.dot(down, up, preferred_element_type=jnp.float32)
        for c in range(2):
            base = base_ref[c * parts + part, f : f + step, :].astype(jnp.float32)
            merged[f : f + step, c * half : (c + 1) * half] = (base + low_rank[:, c * half : (c + 1) * half]).astype(
                jnp.bfloat16
            )
    out_ref[...] = jnp.dot(hidden_ref[...], merged[...], preferred_element_type=jnp.float32)


def project(which, hidden, gathered, base):
    tokens, width = hidden.shape
    columns = 2 * base.shape[2]
    return pl.pallas_call(
        functools.partial(project_kernel, width),
        out_shape=jax.ShapeDtypeStruct((tokens, columns), jnp.float32),
        in_specs=[pl.BlockSpec(memory_space=pltpu.SMEM), VMEM, VMEM, VMEM],
        out_specs=VMEM,
        scratch_shapes=[pltpu.VMEM((width, columns), jnp.bfloat16)],
        compiler_params=params(24),
        cost_estimate=cost(
            2 * width * columns * (tokens + gathered.shape[0]), 2 * width * columns + 2 * width * tokens
        ),
        name="project",
    )(which, hidden, gathered, base)


def finish_kernel(steps, heads, scale, group, terms, *refs):
    parts, refs = refs[:terms], refs[terms:]
    q_ref, sum_ref, total_ref, top_ref, fresh_ref, context_ref, wide, bias = refs
    rows, queries, size = q_ref.shape
    own = fresh_ref.shape[3]
    fresh = parts[0][...]
    for part in parts[1:]:
        fresh = fresh + part[...]
    for n in range(2 * own):
        wide[pl.ds(n, rows * steps, stride=2 * own), :] = fresh[:, n * size : (n + 1) * size]
    fresh_ref.reshape(rows * steps * 2 * own, size)[...] = wide[...].astype(jnp.bfloat16)
    fresh = fresh.astype(jnp.bfloat16)
    many, keys = group * queries, own * group * steps
    query = lax.broadcasted_iota(jnp.int32, (many, keys), 0)
    key = lax.broadcasted_iota(jnp.int32, (many, keys), 1)
    same_head = (query % heads) // (heads // own) == key // (group * steps)
    same_row = query // queries == (key // steps) % group
    seen = (query % queries) // heads >= key % steps
    bias[...] = jnp.where(same_head & same_row & seen, 0.0, LOW)
    ones = jnp.ones((keys, size), jnp.bfloat16)
    for at in range(0, rows, group):
        tokens = slice(at * steps, (at + group) * steps)
        keys_new, values_new = [
            jnp.concatenate(
                [fresh[tokens, (c * own + g) * size : (c * own + g + 1) * size] for g in range(own)], axis=0
            )
            for c in range(2)
        ]
        values_new = jnp.concatenate([values_new, ones], axis=1)
        mine = slice(at, at + group)
        scores = lax.dot_general(
            q_ref[mine].reshape(many, size), keys_new, NT, preferred_element_type=jnp.float32
        )
        scores = scores + bias[...]
        top_old = top_ref[mine].reshape(many, size)
        top = jnp.maximum(top_old, jnp.max(scores, axis=-1, keepdims=True))
        weights = jnp.exp((scores - top) * scale).astype(jnp.bfloat16)
        back = jnp.exp((top_old - top) * scale)
        both = jnp.dot(weights, values_new, preferred_element_type=jnp.float32)
        total = back * total_ref[mine].reshape(many, size) + both[:, size:]
        summed = back * sum_ref[mine].reshape(many, size) + both[:, :size]
        context_ref[mine] = (summed / total).astype(jnp.bfloat16).reshape(group, queries, size)


def finish(parts, queries, state, own):
    rows, steps, heads, size = queries.shape
    group = size // (own * steps)
    many = steps * heads
    fresh, context = pl.pallas_call(
        functools.partial(finish_kernel, steps, heads, size ** (-0.5), group, len(parts)),
        out_shape=(
            jax.ShapeDtypeStruct((rows, steps, 2, own, size), jnp.bfloat16),
            jax.ShapeDtypeStruct((rows, many, size), jnp.bfloat16),
        ),
        in_specs=[VMEM] * (len(parts) + 1 + len(state)),
        out_specs=(VMEM, VMEM),
        scratch_shapes=[
            pltpu.VMEM((rows * steps * 2 * own, size), jnp.float32),
            pltpu.VMEM((group * many, own * group * steps), jnp.float32),
        ],
        compiler_params=params(24),
        cost_estimate=cost(rows * many * size * size * 6, 12 * rows * many * size, rows * many * size * 2),
        name="finish",
    )(*parts, queries.reshape(rows, many, size), *state)
    return fresh, context.reshape(rows, steps, heads, size)


def shards(dp, tp, hidden, base_weight, factor_a, factor_b, queries, cache, lengths):
    own = cache.shape[3]
    payload = make_payload(factor_a.T, factor_b, dp)
    gathered = lax.all_to_all(payload, "dp", 0, 0, tiled=True)
    gathered = gathered.reshape(-1, gathered.shape[-1])
    tokens, base, state = local(hidden, base_weight, queries, cache, lengths)
    gathered, base = lax.optimization_barrier((gathered, base))
    me = lax.axis_index("tp")
    received = []
    for k in range(1, tp):
        other = project(jnp.full((1,), me ^ k, jnp.int32), tokens, gathered, base)
        received.append(lax.ppermute(other, "tp", [(i, i ^ k) for i in range(tp)]))
    mine = project(jnp.full((1,), me, jnp.int32), tokens, gathered, base)
    return finish([mine] + received, queries, state, own)


def solution(mesh):
    return jax.shard_map(
        functools.partial(shards, mesh.shape["dp"], mesh.shape["tp"]),
        mesh=mesh,
        in_specs=(
            P(("parts", "dp"), None, "tp"),
            P("tp", None, None, None),
            P(("parts", "tp"), "dp"),
            P(("parts", "dp"), None, None, None),
            P(("parts", "dp"), None, "tp", None),
            P(("parts", "dp"), None, None, "tp", None),
            P(("parts", "dp")),
        ),
        out_specs=(
            P(("parts", "dp"), None, None, "tp", None),
            P(("parts", "dp"), None, "tp", None),
        ),
        check_vma=False,
    )
```

```python
import functools

import jax
import jax.numpy as jnp
from jax import lax
from jax.experimental import pallas as pl
from jax.experimental.pallas import tpu as pltpu
from jax.sharding import PartitionSpec as P

LOW = -1e30
NT = (((1,), (1,)), ((), ()))
VMEM = pl.BlockSpec(memory_space=pltpu.VMEM)


def params(mib):
    return pltpu.CompilerParams(vmem_limit_bytes=mib * 1024 * 1024)


def in_hbm(x):
    return pltpu.with_memory_space_constraint(x, pltpu.HBM)


def cost(flops, moved, exps=0):
    return pl.CostEstimate(flops=flops, bytes_accessed=moved, transcendentals=exps)


def payload_kernel(down_hbm, up_hbm, out_hbm, held, ups, wide, sems):
    ranks, width = down_hbm.shape
    groups, size = ups.shape[1] * ups.shape[2], ups.shape[3]
    get_down = pltpu.make_async_copy(down_hbm, held.at[:, pl.ds(0, width)], sems.at[0])
    get_up = pltpu.make_async_copy(up_hbm, ups, sems.at[1])
    get_up.start()
    get_down.start()
    get_up.wait()
    wide[...] = ups.reshape(ranks * groups, size)[...].astype(jnp.float32)
    for n in range(groups):
        held[:, width + n * size : width + (n + 1) * size] = wide[pl.ds(n, ranks, stride=groups), :].astype(
            jnp.bfloat16
        )
    get_down.wait()
    puts = [pltpu.make_async_copy(held, out_hbm.at[i], sems.at[2 + i]) for i in range(out_hbm.shape[0])]
    for put in puts:
        put.start()
    for put in puts:
        put.wait()


def make_payload(down, up, count):
    ranks, width = down.shape
    groups, size = up.shape[1] * up.shape[2], up.shape[3]
    held = (ranks, width + groups * size)
    return pl.pallas_call(
        payload_kernel,
        out_shape=jax.ShapeDtypeStruct((count,) + held, jnp.bfloat16),
        in_specs=[pl.BlockSpec(memory_space=pltpu.HBM)] * 2,
        out_specs=pl.BlockSpec(memory_space=pltpu.HBM),
        scratch_shapes=[
            pltpu.VMEM(held, jnp.bfloat16),
            pltpu.VMEM(up.shape, jnp.bfloat16),
            pltpu.VMEM((ranks * groups, size), jnp.float32),
            pltpu.SemaphoreType.DMA((2 + count,)),
        ],
        compiler_params=params(60),
        name="payload",
    )(in_hbm(down), in_hbm(up))


def local_kernel(chunks, heads, scale, *refs):
    lengths_hbm, hidden_hbm, base_hbm, queries_hbm, cache_hbm = refs[:5]
    tokens_ref, base_ref, q_all, sum_ref, total_ref, top_ref = refs[5:11]
    lengths_ref, hidden, base, k_all, v_all, sems = refs[11:]
    rows, queries, size = q_all.shape
    slots, own = k_all.shape[1:3]
    keys = slots * own
    width, two, kvh, _ = base.shape
    groups = two * kvh
    some_rows, some_width = rows // chunks, width // chunks

    def copies(i):
        mine = pl.ds(i * some_rows, some_rows)
        features = pl.ds(i * some_width, some_width)
        pairs = (
            (queries_hbm.at[mine], q_all.at[mine]),
            (cache_hbm.at[mine, :, 0], k_all.at[mine]),
            (cache_hbm.at[mine, :, 1], v_all.at[mine]),
            (base_hbm.at[features], base.at[features]),
        )
        return [pltpu.make_async_copy(a, b, sems.at[i, n]) for n, (a, b) in enumerate(pairs)]

    get_hidden = pltpu.make_async_copy(hidden_hbm, hidden, sems.at[chunks, 0])
    get_lengths = pltpu.make_async_copy(lengths_hbm, lengths_ref, sems.at[chunks, 1])
    get_lengths.start()
    for i in range(chunks):
        for copy in copies(i):
            copy.start()
    get_hidden.start()

    column = lax.broadcasted_iota(jnp.int32, (queries, keys), 1)
    head = lax.broadcasted_iota(jnp.int32, (queries, keys), 0) % heads
    column = jnp.where(column % own == head // (heads // own), column, own * slots)
    ones = jnp.ones((keys, size), jnp.bfloat16)
    tile = 256
    some = tile // groups
    row = lax.broadcasted_iota(jnp.int32, (tile, tile), 0)
    place = lax.broadcasted_iota(jnp.int32, (tile, tile), 1)
    order = (place == (row % some) * groups + row // some).astype(jnp.float32).astype(jnp.bfloat16)
    flat_base = base.reshape(width * groups, size)
    flat_k = k_all.reshape(rows, keys, size)
    flat_v = v_all.reshape(rows, keys, size)

    def attend(at, count):
        group = [at + r for r in range(count)]
        scores = [lax.dot_general(q_all[r], flat_k[r], NT, preferred_element_type=jnp.float32) for r in group]
        scores = [jnp.where(column < own * lengths_ref[r], s, LOW) for r, s in zip(group, scores)]
        tops = [jnp.max(s, axis=-1, keepdims=True) for s in scores]
        weights = [jnp.exp((s - t) * scale).astype(jnp.bfloat16) for s, t in zip(scores, tops)]
        for r, w, top in zip(group, weights, tops):
            both = jnp.dot(w, jnp.concatenate([flat_v[r], ones], axis=1), preferred_element_type=jnp.float32)
            sum_ref[r] = both[:, :size]
            total_ref[r] = both[:, size:]
            top_ref[r] = jnp.broadcast_to(top, (queries, size))

    def arrange(f):
        at = pl.multiple_of(f * groups, tile)
        pair = jnp.concatenate([flat_base[pl.ds(at + h * tile, tile), :] for h in range(2)], axis=1)
        moved = jnp.dot(order, pair, preferred_element_type=jnp.float32).astype(jnp.bfloat16)
        for n in range(groups):
            lanes = slice((n % own) * size, (n % own + 1) * size)
            for h in range(2):
                base_ref[n // own, pl.ds(pl.multiple_of(f + h * some, some), some), lanes] = moved[
                    n * some : (n + 1) * some, h * size : (h + 1) * size
                ]

    get_lengths.wait()

    @pl.loop(0, chunks)
    def _(i):
        for copy in copies(i):
            copy.wait()
        for r in range(0, some_rows, 3):
            attend(i * some_rows + r, 3)
        for f in range(0, some_width, 2 * some):
            arrange(i * some_width + f)

    get_hidden.wait()
    tokens_ref[...] = hidden.reshape(tokens_ref.shape)[...]


def local(hidden, base, queries, cache, lengths):
    rows, steps, heads, size = queries.shape
    slots, own = cache.shape[1], cache.shape[3]
    width, two, kvh, _ = base.shape
    many = steps * heads
    chunks = 8
    state = pltpu.VMEM((rows, many, size), jnp.float32)
    half = (rows, slots, own, size)
    outs = (
        pltpu.VMEM((rows * steps, width), jnp.bfloat16),
        pltpu.VMEM((two * kvh // own, width, own * size), jnp.bfloat16),
        pltpu.VMEM((rows, many, size), jnp.bfloat16),
        state,
        state,
        state,
    )
    tokens, base, queries, *state = pl.pallas_call(
        functools.partial(local_kernel, chunks, heads, size ** (-0.5)),
        out_shape=outs,
        in_specs=[pl.BlockSpec(memory_space=pltpu.HBM)] * 5,
        out_specs=(VMEM,) * len(outs),
        scratch_shapes=[
            pltpu.SMEM(lengths.shape, jnp.int32),
            pltpu.VMEM(hidden.shape, jnp.bfloat16),
            pltpu.VMEM(base.shape, jnp.bfloat16),
            pltpu.VMEM(half, jnp.bfloat16),
            pltpu.VMEM(half, jnp.bfloat16),
            pltpu.SemaphoreType.DMA((chunks + 1, 4)),
        ],
        compiler_params=params(28),
        cost_estimate=cost(
            8 * rows * many * slots * size + 512 * base.size,
            2 * (cache.size + queries.size + base.size + hidden.size),
            rows * many * slots,
        ),
        name="local",
    )(*map(in_hbm, (lengths, hidden, base, queries.reshape(rows, many, size), cache)))
    return tokens, base, queries, state


def project_kernel(down_at, which_ref, hidden_ref, gathered_ref, base_ref, out_ref, merged):
    width, columns = merged.shape
    part = which_ref[0]
    parts = base_ref.shape[0] // 2
    half = columns // 2
    up = jnp.concatenate(
        [
            gathered_ref[:, pl.ds(pl.multiple_of(down_at + (c * parts + part) * half, 128), half)]
            for c in range(2)
        ],
        axis=1,
    )
    step = 512
    for f in range(0, width, step):
        down = gathered_ref[:, f : f + step].T
        low_rank = jnp.dot(down, up, preferred_element_type=jnp.float32)
        for c in range(2):
            base = base_ref[c * parts + part, f : f + step, :].astype(jnp.float32)
            merged[f : f + step, c * half : (c + 1) * half] = (base + low_rank[:, c * half : (c + 1) * half]).astype(
                jnp.bfloat16
            )
    out_ref[...] = jnp.dot(hidden_ref[...], merged[...], preferred_element_type=jnp.float32)


def project(which, hidden, gathered, base):
    tokens, width = hidden.shape
    columns = 2 * base.shape[2]
    return pl.pallas_call(
        functools.partial(project_kernel, width),
        out_shape=jax.ShapeDtypeStruct((tokens, columns), jnp.float32),
        in_specs=[pl.BlockSpec(memory_space=pltpu.SMEM), VMEM, VMEM, VMEM],
        out_specs=VMEM,
        scratch_shapes=[pltpu.VMEM((width, columns), jnp.bfloat16)],
        compiler_params=params(24),
        cost_estimate=cost(
            2 * width * columns * (tokens + gathered.shape[0]), 2 * width * columns + 2 * width * tokens
        ),
        name="project",
    )(which, hidden, gathered, base)


def finish_kernel(steps, heads, scale, group, terms, *refs):
    parts, refs = refs[:terms], refs[terms:]
    q_ref, sum_ref, total_ref, top_ref, fresh_ref, context_ref, wide, bias = refs
    rows, queries, size = q_ref.shape
    own = fresh_ref.shape[3]
    fresh = parts[0][...]
    for part in parts[1:]:
        fresh = fresh + part[...]
    for n in range(2 * own):
        wide[pl.ds(n, rows * steps, stride=2 * own), :] = fresh[:, n * size : (n + 1) * size]
    fresh_ref.reshape(rows * steps * 2 * own, size)[...] = wide[...].astype(jnp.bfloat16)
    fresh = fresh.astype(jnp.bfloat16)
    many, keys = group * queries, own * group * steps
    query = lax.broadcasted_iota(jnp.int32, (many, keys), 0)
    key = lax.broadcasted_iota(jnp.int32, (many, keys), 1)
    same_head = (query % heads) // (heads // own) == key // (group * steps)
    same_row = query // queries == (key // steps) % group
    seen = (query % queries) // heads >= key % steps
    bias[...] = jnp.where(same_head & same_row & seen, 0.0, LOW)
    ones = jnp.ones((keys, size), jnp.bfloat16)
    for at in range(0, rows, group):
        tokens = slice(at * steps, (at + group) * steps)
        keys_new, values_new = [
            jnp.concatenate(
                [fresh[tokens, (c * own + g) * size : (c * own + g + 1) * size] for g in range(own)], axis=0
            )
            for c in range(2)
        ]
        values_new = jnp.concatenate([values_new, ones], axis=1)
        mine = slice(at, at + group)
        scores = lax.dot_general(
            q_ref[mine].reshape(many, size), keys_new, NT, preferred_element_type=jnp.float32
        )
        scores = scores + bias[...]
        top_old = top_ref[mine].reshape(many, size)
        top = jnp.maximum(top_old, jnp.max(scores, axis=-1, keepdims=True))
        weights = jnp.exp((scores - top) * scale).astype(jnp.bfloat16)
        back = jnp.exp((top_old - top) * scale)
        both = jnp.dot(weights, values_new, preferred_element_type=jnp.float32)
        total = back * total_ref[mine].reshape(many, size) + both[:, size:]
        summed = back * sum_ref[mine].reshape(many, size) + both[:, :size]
        context_ref[mine] = (summed / total).astype(jnp.bfloat16).reshape(group, queries, size)


def finish(parts, queries, state, steps, own):
    rows, many, size = queries.shape
    heads = many // steps
    group = size // (own * steps)
    fresh, context = pl.pallas_call(
        functools.partial(finish_kernel, steps, heads, size ** (-0.5), group, len(parts)),
        out_shape=(
            jax.ShapeDtypeStruct((rows, steps, 2, own, size), jnp.bfloat16),
            jax.ShapeDtypeStruct((rows, many, size), jnp.bfloat16),
        ),
        in_specs=[VMEM] * (len(parts) + 1 + len(state)),
        out_specs=(VMEM, VMEM),
        scratch_shapes=[
            pltpu.VMEM((rows * steps * 2 * own, size), jnp.float32),
            pltpu.VMEM((group * many, own * group * steps), jnp.float32),
        ],
        compiler_params=params(24),
        cost_estimate=cost(rows * many * size * size * 6, 12 * rows * many * size, rows * many * size * 2),
        name="finish",
    )(*parts, queries, *state)
    return fresh, context.reshape(rows, steps, heads, size)


def shards(dp, tp, hidden, base_weight, factor_a, factor_b, queries, cache, lengths):
    steps, own = queries.shape[1], cache.shape[3]
    payload = make_payload(factor_a.T, factor_b, dp)
    gathered = lax.all_to_all(payload, "dp", 0, 0, tiled=True)
    gathered = gathered.reshape(-1, gathered.shape[-1])
    tokens, base, queries, state = local(hidden, base_weight, queries, cache, lengths)
    gathered, base = lax.optimization_barrier((gathered, base))
    me = lax.axis_index("tp")
    received = []
    for k in range(1, tp):
        other = project(jnp.full((1,), me ^ k, jnp.int32), tokens, gathered, base)
        received.append(lax.ppermute(other, "tp", [(i, i ^ k) for i in range(tp)]))
    mine = project(jnp.full((1,), me, jnp.int32), tokens, gathered, base)
    return finish([mine] + received, queries, state, steps, own)


def solution(mesh):
    return jax.shard_map(
        functools.partial(shards, mesh.shape["dp"], mesh.shape["tp"]),
        mesh=mesh,
        in_specs=(
            P(("parts", "dp"), None, "tp"),
            P("tp", None, None, None),
            P(("parts", "tp"), "dp"),
            P(("parts", "dp"), None, None, None),
            P(("parts", "dp"), None, "tp", None),
            P(("parts", "dp"), None, None, "tp", None),
            P(("parts", "dp")),
        ),
        out_specs=(
            P(("parts", "dp"), None, None, "tp", None),
            P(("parts", "dp"), None, "tp", None),
        ),
        check_vma=False,
    )
```

```python
import functools

import jax
import jax.numpy as jnp
from jax import lax
from jax.experimental import pallas as pl
from jax.experimental.pallas import tpu as pltpu
from jax.sharding import PartitionSpec as P

LOW = -1e30
NT = (((1,), (1,)), ((), ()))
VMEM = pl.BlockSpec(memory_space=pltpu.VMEM)


def params(mib):
    return pltpu.CompilerParams(vmem_limit_bytes=mib * 1024 * 1024)


def in_hbm(x):
    return pltpu.with_memory_space_constraint(x, pltpu.HBM)


def cost(flops, moved, exps=0):
    return pl.CostEstimate(flops=flops, bytes_accessed=moved, transcendentals=exps)


def payload_kernel(down_hbm, up_hbm, out_hbm, held, ups, wide, sems):
    ranks, width = down_hbm.shape
    groups, size = ups.shape[1] * ups.shape[2], ups.shape[3]
    get_down = pltpu.make_async_copy(down_hbm, held.at[:, pl.ds(0, width)], sems.at[0])
    get_up = pltpu.make_async_copy(up_hbm, ups, sems.at[1])
    get_up.start()
    get_down.start()
    get_up.wait()
    wide[...] = ups.reshape(ranks * groups, size)[...].astype(jnp.float32)
    for n in range(groups):
        held[:, width + n * size : width + (n + 1) * size] = wide[pl.ds(n, ranks, stride=groups), :].astype(
            jnp.bfloat16
        )
    get_down.wait()
    puts = [pltpu.make_async_copy(held, out_hbm.at[i], sems.at[2 + i]) for i in range(out_hbm.shape[0])]
    for put in puts:
        put.start()
    for put in puts:
        put.wait()


def make_payload(down, up, count):
    ranks, width = down.shape
    groups, size = up.shape[1] * up.shape[2], up.shape[3]
    held = (ranks, width + groups * size)
    return pl.pallas_call(
        payload_kernel,
        out_shape=jax.ShapeDtypeStruct((count,) + held, jnp.bfloat16),
        in_specs=[pl.BlockSpec(memory_space=pltpu.HBM)] * 2,
        out_specs=pl.BlockSpec(memory_space=pltpu.HBM),
        scratch_shapes=[
            pltpu.VMEM(held, jnp.bfloat16),
            pltpu.VMEM(up.shape, jnp.bfloat16),
            pltpu.VMEM((ranks * groups, size), jnp.float32),
            pltpu.SemaphoreType.DMA((2 + count,)),
        ],
        compiler_params=params(60),
        name="payload",
    )(in_hbm(down), in_hbm(up))


def cached_kernel(chunks, heads, scale, *refs):
    lengths_hbm, queries_hbm, cache_hbm = refs[:3]
    outs_hbm = refs[3:6]
    lengths_ref, q_all, k_all, v_all, sum_ref, total_ref, top_ref, sems, out_sems, length_sem = refs[6:]
    rows, queries, size = q_all.shape
    slots, own = k_all.shape[1:3]
    keys = slots * own
    some = rows // chunks

    def copies(i):
        mine = pl.ds(i * some, some)
        pairs = (
            (queries_hbm.at[mine], q_all.at[mine]),
            (cache_hbm.at[mine, :, 0], k_all.at[mine]),
            (cache_hbm.at[mine, :, 1], v_all.at[mine]),
        )
        return [pltpu.make_async_copy(a, b, sems.at[i, n]) for n, (a, b) in enumerate(pairs)]

    def puts(i):
        mine = pl.ds(i * some, some)
        return [
            pltpu.make_async_copy(a.at[mine], b.at[mine], out_sems.at[i, n])
            for n, (a, b) in enumerate(zip((sum_ref, total_ref, top_ref), outs_hbm))
        ]

    get_lengths = pltpu.make_async_copy(lengths_hbm, lengths_ref, length_sem)
    get_lengths.start()
    for i in range(chunks):
        for copy in copies(i):
            copy.start()

    column = lax.broadcasted_iota(jnp.int32, (queries, keys), 1)
    head = lax.broadcasted_iota(jnp.int32, (queries, keys), 0) % heads
    column = jnp.where(column % own == head // (heads // own), column, own * slots)
    ones = jnp.ones((keys, size), jnp.bfloat16)
    flat_k = k_all.reshape(rows, keys, size)
    flat_v = v_all.reshape(rows, keys, size)

    def attend(at, count):
        group = [at + r for r in range(count)]
        scores = [lax.dot_general(q_all[r], flat_k[r], NT, preferred_element_type=jnp.float32) for r in group]
        scores = [jnp.where(column < own * lengths_ref[r], s, LOW) for r, s in zip(group, scores)]
        tops = [jnp.max(s, axis=-1, keepdims=True) for s in scores]
        weights = [jnp.exp((s - t) * scale).astype(jnp.bfloat16) for s, t in zip(scores, tops)]
        for r, w, top in zip(group, weights, tops):
            both = jnp.dot(w, jnp.concatenate([flat_v[r], ones], axis=1), preferred_element_type=jnp.float32)
            sum_ref[r] = both[:, :size]
            total_ref[r] = both[:, size:]
            top_ref[r] = jnp.broadcast_to(top, (queries, size))

    get_lengths.wait()

    @pl.loop(0, chunks)
    def _(i):
        for copy in copies(i):
            copy.wait()
        for r in range(0, some, 3):
            attend(i * some + r, 3)
        for put in puts(i):
            put.start()

    for i in range(chunks):
        for put in puts(i):
            put.wait()


def attend_cached(queries, cache, lengths):
    rows, steps, heads, size = queries.shape
    slots, own = cache.shape[1], cache.shape[3]
    many = steps * heads
    chunks = 8
    state = (rows, many, size)
    half = (rows, slots, own, size)
    return pl.pallas_call(
        functools.partial(cached_kernel, chunks, heads, size ** (-0.5)),
        out_shape=(pltpu.HBM(state, jnp.float32),) * 3,
        in_specs=[pl.BlockSpec(memory_space=pltpu.HBM)] * 3,
        out_specs=(pl.BlockSpec(memory_space=pltpu.HBM),) * 3,
        scratch_shapes=[
            pltpu.SMEM(lengths.shape, jnp.int32),
            pltpu.VMEM((rows, many, size), jnp.bfloat16),
            pltpu.VMEM(half, jnp.bfloat16),
            pltpu.VMEM(half, jnp.bfloat16),
            pltpu.VMEM(state, jnp.float32),
            pltpu.VMEM(state, jnp.float32),
            pltpu.VMEM(state, jnp.float32),
            pltpu.SemaphoreType.DMA((chunks, 3)),
            pltpu.SemaphoreType.DMA((chunks, 3)),
            pltpu.SemaphoreType.DMA,
        ],
        compiler_params=params(28),
        cost_estimate=cost(
            8 * rows * many * slots * size, 2 * (cache.size + queries.size) + 12 * rows * many * size, rows * many * slots
        ),
        name="attend_cached",
    )(*map(in_hbm, (lengths, queries.reshape(rows, many, size), cache)))


def arrange_kernel(chunks, own, hidden_hbm, base_hbm, tokens_ref, base_ref, hidden, base, sems):
    width, two, kvh, size = base.shape
    groups = two * kvh
    some_width = width // chunks

    def copy(i):
        features = pl.ds(i * some_width, some_width)
        return pltpu.make_async_copy(base_hbm.at[features], base.at[features], sems.at[i])

    get_hidden = pltpu.make_async_copy(hidden_hbm, hidden, sems.at[chunks])
    for i in range(chunks):
        copy(i).start()
    get_hidden.start()

    tile = 256
    some = tile // groups
    row = lax.broadcasted_iota(jnp.int32, (tile, tile), 0)
    place = lax.broadcasted_iota(jnp.int32, (tile, tile), 1)
    order = (place == (row % some) * groups + row // some).astype(jnp.float32).astype(jnp.bfloat16)
    flat_base = base.reshape(width * groups, size)

    def arrange(f):
        at = pl.multiple_of(f * groups, tile)
        pair = jnp.concatenate([flat_base[pl.ds(at + h * tile, tile), :] for h in range(2)], axis=1)
        moved = jnp.dot(order, pair, preferred_element_type=jnp.float32).astype(jnp.bfloat16)
        for n in range(groups):
            lanes = slice((n % own) * size, (n % own + 1) * size)
            for h in range(2):
                base_ref[n // own, pl.ds(pl.multiple_of(f + h * some, some), some), lanes] = moved[
                    n * some : (n + 1) * some, h * size : (h + 1) * size
                ]

    @pl.loop(0, chunks)
    def _(i):
        copy(i).wait()
        for f in range(0, some_width, 2 * some):
            arrange(i * some_width + f)

    get_hidden.wait()
    tokens_ref[...] = hidden.reshape(tokens_ref.shape)[...]


def arrange(hidden, base, own):
    rows, steps, _ = hidden.shape
    width, two, kvh, size = base.shape
    chunks = 8
    return pl.pallas_call(
        functools.partial(arrange_kernel, chunks, own),
        out_shape=(
            pltpu.VMEM((rows * steps, width), jnp.bfloat16),
            pltpu.VMEM((two * kvh // own, width, own * size), jnp.bfloat16),
        ),
        in_specs=[pl.BlockSpec(memory_space=pltpu.HBM)] * 2,
        out_specs=(VMEM, VMEM),
        scratch_shapes=[
            pltpu.VMEM(hidden.shape, jnp.bfloat16),
            pltpu.VMEM(base.shape, jnp.bfloat16),
            pltpu.SemaphoreType.DMA((chunks + 1,)),
        ],
        compiler_params=params(20),
        cost_estimate=cost(512 * base.size, 4 * (base.size + hidden.size)),
        name="arrange",
    )(in_hbm(hidden), in_hbm(base))


def project_kernel(which_ref, hidden_ref, base_ref, *refs):
    gathered, (out_ref, merged) = refs[:-2], refs[-2:]
    width, columns = merged.shape
    part = which_ref[0]
    parts = base_ref.shape[0] // 2
    half = columns // 2
    up = jnp.concatenate(
        [
            jnp.concatenate(
                [ref[:, pl.ds(pl.multiple_of(width + (c * parts + part) * half, 128), half)] for ref in gathered], axis=0
            )
            for c in range(2)
        ],
        axis=1,
    )
    step = 512
    for f in range(0, width, step):
        down = jnp.concatenate([ref[:, f : f + step] for ref in gathered], axis=0).T
        low_rank = jnp.dot(down, up, preferred_element_type=jnp.float32)
        for c in range(2):
            base = base_ref[c * parts + part, f : f + step, :].astype(jnp.float32)
            merged[f : f + step, c * half : (c + 1) * half] = (base + low_rank[:, c * half : (c + 1) * half]).astype(
                jnp.bfloat16
            )
    out_ref[...] = jnp.dot(hidden_ref[...], merged[...], preferred_element_type=jnp.float32)


def project(which, hidden, base, gathered):
    tokens, width = hidden.shape
    columns = 2 * base.shape[2]
    ranks = sum(g.shape[0] for g in gathered)
    return pl.pallas_call(
        project_kernel,
        out_shape=pltpu.VMEM((tokens, columns), jnp.float32),
        in_specs=[pl.BlockSpec(memory_space=pltpu.SMEM)] + [VMEM] * (2 + len(gathered)),
        out_specs=VMEM,
        scratch_shapes=[pltpu.VMEM((width, columns), jnp.bfloat16)],
        compiler_params=params(24),
        cost_estimate=cost(2 * width * columns * (tokens + ranks), 2 * width * columns + 2 * width * tokens),
        name="project",
    )(which, hidden, base, *gathered)


def finish_kernel(steps, heads, scale, group, terms, *refs):
    parts, refs = refs[:terms], refs[terms:]
    q_ref, sum_ref, total_ref, top_ref, fresh_ref, context_ref, wide, bias = refs
    rows, queries, size = q_ref.shape
    own = fresh_ref.shape[3]
    fresh = parts[0][...]
    for part in parts[1:]:
        fresh = fresh + part[...]
    for n in range(2 * own):
        wide[pl.ds(n, rows * steps, stride=2 * own), :] = fresh[:, n * size : (n + 1) * size]
    fresh_ref.reshape(rows * steps * 2 * own, size)[...] = wide[...].astype(jnp.bfloat16)
    fresh = fresh.astype(jnp.bfloat16)
    many, keys = group * queries, own * group * steps
    query = lax.broadcasted_iota(jnp.int32, (many, keys), 0)
    key = lax.broadcasted_iota(jnp.int32, (many, keys), 1)
    same_head = (query % heads) // (heads // own) == key // (group * steps)
    same_row = query // queries == (key // steps) % group
    seen = (query % queries) // heads >= key % steps
    bias[...] = jnp.where(same_head & same_row & seen, 0.0, LOW)
    ones = jnp.ones((keys, size), jnp.bfloat16)
    for at in range(0, rows, group):
        tokens = slice(at * steps, (at + group) * steps)
        keys_new, values_new = [
            jnp.concatenate(
                [fresh[tokens, (c * own + g) * size : (c * own + g + 1) * size] for g in range(own)], axis=0
            )
            for c in range(2)
        ]
        values_new = jnp.concatenate([values_new, ones], axis=1)
        mine = slice(at, at + group)
        scores = lax.dot_general(
            q_ref[mine].reshape(many, size), keys_new, NT, preferred_element_type=jnp.float32
        )
        scores = scores + bias[...]
        top_old = top_ref[mine].reshape(many, size)
        top = jnp.maximum(top_old, jnp.max(scores, axis=-1, keepdims=True))
        weights = jnp.exp((scores - top) * scale).astype(jnp.bfloat16)
        back = jnp.exp((top_old - top) * scale)
        both = jnp.dot(weights, values_new, preferred_element_type=jnp.float32)
        total = back * total_ref[mine].reshape(many, size) + both[:, size:]
        summed = back * sum_ref[mine].reshape(many, size) + both[:, :size]
        context_ref[mine] = (summed / total).astype(jnp.bfloat16).reshape(group, queries, size)


def finish(parts, queries, state, steps, own):
    rows, many, size = queries.shape
    heads = many // steps
    group = size // (own * steps)
    fresh, context = pl.pallas_call(
        functools.partial(finish_kernel, steps, heads, size ** (-0.5), group, len(parts)),
        out_shape=(
            jax.ShapeDtypeStruct((rows, steps, 2, own, size), jnp.bfloat16),
            jax.ShapeDtypeStruct((rows, many, size), jnp.bfloat16),
        ),
        in_specs=[VMEM] * (len(parts) + 1 + len(state)),
        out_specs=(VMEM, VMEM),
        scratch_shapes=[
            pltpu.VMEM((rows * steps * 2 * own, size), jnp.float32),
            pltpu.VMEM((group * many, own * group * steps), jnp.float32),
        ],
        compiler_params=params(24),
        cost_estimate=cost(rows * many * size * size * 6, 12 * rows * many * size, rows * many * size * 2),
        name="finish",
    )(*parts, queries, *state)
    return fresh, context.reshape(rows, steps, heads, size)


def gather(payload, dp):
    ranks, columns = payload.shape[1:]
    if dp % 2:
        return [lax.all_to_all(payload, "dp", 0, 0, tiled=True).reshape(dp * ranks, columns)], lambda x: []
    groups = [[i for i in range(dp) if i % 2 == n] for n in range(2)]
    mine = lax.all_to_all(payload, "dp", 0, 0, axis_index_groups=groups, tiled=True)
    return [mine.reshape(dp // 2 * ranks, columns)], lambda x: [lax.ppermute(x, "dp", [(i, i ^ 1) for i in range(dp)])]


def shards(dp, tp, hidden, base_weight, factor_a, factor_b, queries, cache, lengths):
    rows, steps, heads, size = queries.shape
    own = cache.shape[3]
    payload = make_payload(factor_a.T, factor_b, dp // 2 if dp % 2 == 0 else dp)
    gathered, rest = gather(payload, dp)
    state = attend_cached(queries, cache, lengths)
    gathered, state, hidden, base_weight = lax.optimization_barrier((gathered, state, hidden, base_weight))
    gathered = gathered + rest(gathered[0])
    tokens, base = arrange(hidden, base_weight, own)
    me = lax.axis_index("tp")
    received = []
    for k in range(1, tp):
        other = project(jnp.full((1,), me ^ k, jnp.int32), tokens, base, gathered)
        received.append(lax.ppermute(other, "tp", [(i, i ^ k) for i in range(tp)]))
    mine = project(jnp.full((1,), me, jnp.int32), tokens, base, gathered)
    return finish([mine] + received, queries.reshape(rows, steps * heads, size), state, steps, own)


def solution(mesh):
    return jax.shard_map(
        functools.partial(shards, mesh.shape["dp"], mesh.shape["tp"]),
        mesh=mesh,
        in_specs=(
            P(("parts", "dp"), None, "tp"),
            P("tp", None, None, None),
            P(("parts", "tp"), "dp"),
            P(("parts", "dp"), None, None, None),
            P(("parts", "dp"), None, "tp", None),
            P(("parts", "dp"), None, None, "tp", None),
            P(("parts", "dp")),
        ),
        out_specs=(
            P(("parts", "dp"), None, None, "tp", None),
            P(("parts", "dp"), None, "tp", None),
        ),
        check_vma=False,
    )
```

```python
import functools

import jax
import jax.numpy as jnp
from jax import lax
from jax.experimental import pallas as pl
from jax.experimental.pallas import tpu as pltpu
from jax.sharding import PartitionSpec as P

LOW = -1e30
NT = (((1,), (1,)), ((), ()))
VMEM = pl.BlockSpec(memory_space=pltpu.VMEM)


def params(mib):
    return pltpu.CompilerParams(vmem_limit_bytes=mib * 1024 * 1024)


def in_hbm(x):
    return pltpu.with_memory_space_constraint(x, pltpu.HBM)


def cost(flops, moved, exps=0):
    return pl.CostEstimate(flops=flops, bytes_accessed=moved, transcendentals=exps)


def payload_kernel(down_hbm, up_hbm, out_hbm, held, ups, wide, sems):
    ranks, width = down_hbm.shape
    groups, size = ups.shape[1] * ups.shape[2], ups.shape[3]
    get_down = pltpu.make_async_copy(down_hbm, held.at[:, pl.ds(0, width)], sems.at[0])
    get_up = pltpu.make_async_copy(up_hbm, ups, sems.at[1])
    get_up.start()
    get_down.start()
    get_up.wait()
    wide[...] = ups.reshape(ranks * groups, size)[...].astype(jnp.float32)
    for n in range(groups):
        held[:, width + n * size : width + (n + 1) * size] = wide[pl.ds(n, ranks, stride=groups), :].astype(
            jnp.bfloat16
        )
    get_down.wait()
    puts = [pltpu.make_async_copy(held, out_hbm.at[i], sems.at[2 + i]) for i in range(out_hbm.shape[0])]
    for put in puts:
        put.start()
    for put in puts:
        put.wait()


def make_payload(down, up, count):
    ranks, width = down.shape
    groups, size = up.shape[1] * up.shape[2], up.shape[3]
    held = (ranks, width + groups * size)
    return pl.pallas_call(
        payload_kernel,
        out_shape=jax.ShapeDtypeStruct((count,) + held, jnp.bfloat16),
        in_specs=[pl.BlockSpec(memory_space=pltpu.HBM)] * 2,
        out_specs=pl.BlockSpec(memory_space=pltpu.HBM),
        scratch_shapes=[
            pltpu.VMEM(held, jnp.bfloat16),
            pltpu.VMEM(up.shape, jnp.bfloat16),
            pltpu.VMEM((ranks * groups, size), jnp.float32),
            pltpu.SemaphoreType.DMA((2 + count,)),
        ],
        compiler_params=params(60),
        name="payload",
    )(in_hbm(down), in_hbm(up))


def cached_kernel(chunks, heads, scale, *refs):
    lengths_hbm, queries_hbm, cache_hbm, out_hbm, log_hbm = refs[:5]
    lengths_ref, q_all, k_all, v_all, out_ref, log_ref = refs[5:11]
    scores_refs, weights_refs, total_refs = refs[11:13], refs[13:15], refs[15:17]
    sems, out_sems, length_sem = refs[17:]
    rows, queries, size = q_all.shape
    slots, own = k_all.shape[1:3]
    keys = slots * own
    some = rows // chunks

    def copies(i):
        mine = pl.ds(i * some, some)
        pairs = (
            (queries_hbm.at[mine], q_all.at[mine]),
            (cache_hbm.at[mine, :, 0], k_all.at[mine]),
            (cache_hbm.at[mine, :, 1], v_all.at[mine]),
        )
        return [pltpu.make_async_copy(a, b, sems.at[i, n]) for n, (a, b) in enumerate(pairs)]

    def puts(i):
        mine = pl.ds(i * some, some)
        pairs = ((out_ref.at[mine], out_hbm.at[mine]), (log_ref.at[mine], log_hbm.at[mine]))
        return [pltpu.make_async_copy(a, b, out_sems.at[i, n]) for n, (a, b) in enumerate(pairs)]

    get_lengths = pltpu.make_async_copy(lengths_hbm, lengths_ref, length_sem)
    get_lengths.start()
    for i in range(chunks):
        for copy in copies(i):
            copy.start()

    column = lax.broadcasted_iota(jnp.int32, (queries, keys), 1)
    head = lax.broadcasted_iota(jnp.int32, (queries, keys), 0) % heads
    column = jnp.where(column % own == head // (heads // own), column, own * slots)
    nothing = jnp.zeros((queries, size), jnp.bfloat16)
    flat_k = k_all.reshape(rows, keys, size)
    flat_v = v_all.reshape(rows, keys, size)

    def await_chunk(i):
        for copy in copies(i):
            copy.wait()

    def score(i, slot):
        for p in range(some // 2):
            r = i * some + 2 * p
            both = jnp.concatenate(
                [
                    jnp.concatenate([q_all[r], nothing], axis=1),
                    jnp.concatenate([nothing, q_all[r + 1]], axis=1),
                ],
                axis=0,
            )
            both_k = jnp.concatenate([flat_k[r], flat_k[r + 1]], axis=1)
            scores_refs[slot][p] = lax.dot_general(both, both_k, NT, preferred_element_type=jnp.float32)

    def soften(i, slot):
        for p in range(some // 2):
            for h in range(2):
                r = i * some + 2 * p + h
                mine = slice(h * queries, (h + 1) * queries)
                scores = jnp.where(column < own * lengths_ref[r], scores_refs[slot][p, mine], LOW)
                top = jnp.max(scores, axis=-1, keepdims=True)
                expo = jnp.exp((scores - top) * scale)
                total = jnp.sum(expo, axis=-1, keepdims=True)
                weights_refs[slot][p, mine] = expo.astype(jnp.bfloat16)
                total_refs[slot][p, mine] = jnp.broadcast_to(1.0 / total, (queries, size))
                log_ref[r] = jnp.broadcast_to(top * scale + jnp.log(total), (queries, size))

    def collect(i, slot):
        for p in range(some // 2):
            r = i * some + 2 * p
            both_v = jnp.concatenate([flat_v[r], flat_v[r + 1]], axis=1)
            both = jnp.dot(weights_refs[slot][p], both_v, preferred_element_type=jnp.float32)
            for h in range(2):
                mine = slice(h * queries, (h + 1) * queries)
                out_ref[r + h] = both[mine, h * size : (h + 1) * size] * total_refs[slot][p, mine]
        for put in puts(i):
            put.start()

    get_lengths.wait()
    await_chunk(0)
    score(0, 0)
    await_chunk(1)
    score(1, 1)
    soften(0, 0)

    @pl.loop(1, chunks // 2)
    def _(t):
        for slot in range(2):
            i = 2 * t + slot
            await_chunk(i)
            score(i, slot)
            soften(i - 1, 1 - slot)
            collect(i - 2, slot)

    soften(chunks - 1, 1)
    collect(chunks - 2, 0)
    collect(chunks - 1, 1)
    for i in range(chunks):
        for put in puts(i):
            put.wait()


def attend_cached(queries, cache, lengths):
    rows, steps, heads, size = queries.shape
    slots, own = cache.shape[1], cache.shape[3]
    many = steps * heads
    chunks = 8
    pairs = rows // chunks // 2
    state = (rows, many, size)
    half = (rows, slots, own, size)
    return pl.pallas_call(
        functools.partial(cached_kernel, chunks, heads, size ** (-0.5)),
        out_shape=(pltpu.HBM(state, jnp.float32),) * 2,
        in_specs=[pl.BlockSpec(memory_space=pltpu.HBM)] * 3,
        out_specs=(pl.BlockSpec(memory_space=pltpu.HBM),) * 2,
        scratch_shapes=[
            pltpu.SMEM(lengths.shape, jnp.int32),
            pltpu.VMEM((rows, many, size), jnp.bfloat16),
            pltpu.VMEM(half, jnp.bfloat16),
            pltpu.VMEM(half, jnp.bfloat16),
            pltpu.VMEM(state, jnp.float32),
            pltpu.VMEM(state, jnp.float32),
            pltpu.VMEM((pairs, 2 * many, slots * own), jnp.float32),
            pltpu.VMEM((pairs, 2 * many, slots * own), jnp.float32),
            pltpu.VMEM((pairs, 2 * many, slots * own), jnp.bfloat16),
            pltpu.VMEM((pairs, 2 * many, slots * own), jnp.bfloat16),
            pltpu.VMEM((pairs, 2 * many, size), jnp.float32),
            pltpu.VMEM((pairs, 2 * many, size), jnp.float32),
            pltpu.SemaphoreType.DMA((chunks, 3)),
            pltpu.SemaphoreType.DMA((chunks, 2)),
            pltpu.SemaphoreType.DMA,
        ],
        compiler_params=params(28),
        cost_estimate=cost(
            8 * rows * many * slots * size, 2 * (cache.size + queries.size) + 8 * rows * many * size, rows * many * slots
        ),
        name="attend_cached",
    )(*map(in_hbm, (lengths, queries.reshape(rows, many, size), cache)))


def arrange_kernel(chunks, own, hidden_hbm, base_hbm, tokens_ref, base_ref, hidden, base, sems):
    width, two, kvh, size = base.shape
    groups = two * kvh
    some_width = width // chunks

    def copy(i):
        features = pl.ds(i * some_width, some_width)
        return pltpu.make_async_copy(base_hbm.at[features], base.at[features], sems.at[i])

    get_hidden = pltpu.make_async_copy(hidden_hbm, hidden, sems.at[chunks])
    get_hidden.start()
    for i in range(chunks):
        copy(i).start()

    tile = 256
    some = tile // groups
    row = lax.broadcasted_iota(jnp.int32, (tile, tile), 0)
    place = lax.broadcasted_iota(jnp.int32, (tile, tile), 1)
    order = (place == (row % some) * groups + row // some).astype(jnp.float32).astype(jnp.bfloat16)
    flat_base = base.reshape(width * groups, size)

    def arrange(f):
        at = pl.multiple_of(f * groups, tile)
        pair = jnp.concatenate([flat_base[pl.ds(at + h * tile, tile), :] for h in range(2)], axis=1)
        moved = jnp.dot(order, pair, preferred_element_type=jnp.float32).astype(jnp.bfloat16)
        for n in range(groups):
            lanes = slice((n % own) * size, (n % own + 1) * size)
            for h in range(2):
                base_ref[n // own, pl.ds(pl.multiple_of(f + h * some, some), some), lanes] = moved[
                    n * some : (n + 1) * some, h * size : (h + 1) * size
                ]

    get_hidden.wait()
    tokens_ref[...] = hidden.reshape(tokens_ref.shape)[...]

    @pl.loop(0, chunks)
    def _(i):
        copy(i).wait()
        for f in range(0, some_width, 2 * some):
            arrange(i * some_width + f)


def arrange(hidden, base, own):
    rows, steps, _ = hidden.shape
    width, two, kvh, size = base.shape
    chunks = 8
    return pl.pallas_call(
        functools.partial(arrange_kernel, chunks, own),
        out_shape=(
            pltpu.VMEM((rows * steps, width), jnp.bfloat16),
            pltpu.VMEM((two * kvh // own, width, own * size), jnp.bfloat16),
        ),
        in_specs=[pl.BlockSpec(memory_space=pltpu.HBM)] * 2,
        out_specs=(VMEM, VMEM),
        scratch_shapes=[
            pltpu.VMEM(hidden.shape, jnp.bfloat16),
            pltpu.VMEM(base.shape, jnp.bfloat16),
            pltpu.SemaphoreType.DMA((chunks + 1,)),
        ],
        compiler_params=params(20),
        cost_estimate=cost(512 * base.size, 4 * (base.size + hidden.size)),
        name="arrange",
    )(in_hbm(hidden), in_hbm(base))


def project_kernel(k, hidden_ref, base_ref, *refs):
    gathered, (out_ref, merged) = refs[:-2], refs[-2:]
    width, columns = merged.shape
    part = lax.axis_index("tp") ^ k
    parts = base_ref.shape[0] // 2
    half = columns // 2
    up = jnp.concatenate(
        [
            jnp.concatenate(
                [ref[:, pl.ds(pl.multiple_of(width + (c * parts + part) * half, 128), half)] for ref in gathered], axis=0
            )
            for c in range(2)
        ],
        axis=1,
    )
    step = 512
    for f in range(0, width, step):
        down = jnp.concatenate([ref[:, f : f + step] for ref in gathered], axis=0).T
        low_rank = jnp.dot(down, up, preferred_element_type=jnp.float32)
        for c in range(2):
            base = base_ref[c * parts + part, f : f + step, :].astype(jnp.float32)
            merged[f : f + step, c * half : (c + 1) * half] = (base + low_rank[:, c * half : (c + 1) * half]).astype(
                jnp.bfloat16
            )
    out_ref[...] = jnp.dot(hidden_ref[...], merged[...], preferred_element_type=jnp.float32)


def project(k, hidden, base, gathered):
    tokens, width = hidden.shape
    columns = 2 * base.shape[2]
    ranks = sum(g.shape[0] for g in gathered)
    return pl.pallas_call(
        functools.partial(project_kernel, k),
        out_shape=pltpu.VMEM((tokens, columns), jnp.float32),
        in_specs=[VMEM] * (2 + len(gathered)),
        out_specs=VMEM,
        scratch_shapes=[pltpu.VMEM((width, columns), jnp.bfloat16)],
        compiler_params=params(24),
        cost_estimate=cost(2 * width * columns * (tokens + ranks), 2 * width * columns + 2 * width * tokens),
        name="project",
    )(hidden, base, *gathered)


def finish_kernel(steps, heads, scale, group, terms, *refs):
    parts, refs = refs[:terms], refs[terms:]
    q_ref, old_ref, log_ref, fresh_ref, context_ref, wide, bias = refs
    rows, queries, size = q_ref.shape
    own = fresh_ref.shape[3]
    fresh = parts[0][...]
    for part in parts[1:]:
        fresh = fresh + part[...]
    for n in range(2 * own):
        wide[pl.ds(n, rows * steps, stride=2 * own), :] = fresh[:, n * size : (n + 1) * size]
    fresh_ref.reshape(rows * steps * 2 * own, size)[...] = wide[...].astype(jnp.bfloat16)
    fresh = fresh.astype(jnp.bfloat16)
    many, keys = group * queries, own * group * steps
    query = lax.broadcasted_iota(jnp.int32, (many, keys), 0)
    key = lax.broadcasted_iota(jnp.int32, (many, keys), 1)
    same_head = (query % heads) // (heads // own) == key // (group * steps)
    same_row = query // queries == (key // steps) % group
    seen = (query % queries) // heads >= key % steps
    bias[...] = jnp.where(same_head & same_row & seen, 0.0, LOW)
    ones = jnp.ones((keys, size), jnp.bfloat16)
    for at in range(0, rows, group):
        tokens = slice(at * steps, (at + group) * steps)
        keys_new, values_new = [
            jnp.concatenate(
                [fresh[tokens, (c * own + g) * size : (c * own + g + 1) * size] for g in range(own)], axis=0
            )
            for c in range(2)
        ]
        values_new = jnp.concatenate([values_new, ones], axis=1)
        mine = slice(at, at + group)
        scores = lax.dot_general(
            q_ref[mine].reshape(many, size), keys_new, NT, preferred_element_type=jnp.float32
        )
        scores = scores * scale + bias[...]
        log_old = log_ref[mine].reshape(many, size)
        top = jnp.maximum(log_old, jnp.max(scores, axis=-1, keepdims=True))
        weights = jnp.exp(scores - top).astype(jnp.bfloat16)
        back = jnp.exp(log_old - top)
        both = jnp.dot(weights, values_new, preferred_element_type=jnp.float32)
        total = back + both[:, size:]
        summed = back * old_ref[mine].reshape(many, size) + both[:, :size]
        context_ref[mine] = (summed / total).astype(jnp.bfloat16).reshape(group, queries, size)


def finish(parts, queries, state, steps, own):
    rows, many, size = queries.shape
    heads = many // steps
    group = size // (own * steps)
    fresh, context = pl.pallas_call(
        functools.partial(finish_kernel, steps, heads, size ** (-0.5), group, len(parts)),
        out_shape=(
            jax.ShapeDtypeStruct((rows, steps, 2, own, size), jnp.bfloat16),
            jax.ShapeDtypeStruct((rows, many, size), jnp.bfloat16),
        ),
        in_specs=[VMEM] * (len(parts) + 1 + len(state)),
        out_specs=(VMEM, VMEM),
        scratch_shapes=[
            pltpu.VMEM((rows * steps * 2 * own, size), jnp.float32),
            pltpu.VMEM((group * many, own * group * steps), jnp.float32),
        ],
        compiler_params=params(24),
        cost_estimate=cost(rows * many * size * size * 6, 12 * rows * many * size, rows * many * size * 2),
        name="finish",
    )(*parts, queries, *state)
    return fresh, context.reshape(rows, steps, heads, size)


def gather(payload, dp):
    ranks, columns = payload.shape[1:]
    if dp % 2:
        return [lax.all_to_all(payload, "dp", 0, 0, tiled=True).reshape(dp * ranks, columns)], lambda x: []
    groups = [[i for i in range(dp) if i % 2 == n] for n in range(2)]
    mine = lax.all_to_all(payload, "dp", 0, 0, axis_index_groups=groups, tiled=True)
    return [mine.reshape(dp // 2 * ranks, columns)], lambda x: [lax.ppermute(x, "dp", [(i, i ^ 1) for i in range(dp)])]


def shards(dp, tp, hidden, base_weight, factor_a, factor_b, queries, cache, lengths):
    rows, steps, heads, size = queries.shape
    own = cache.shape[3]
    payload = make_payload(factor_a.T, factor_b, dp // 2 if dp % 2 == 0 else dp)
    gathered, rest = gather(payload, dp)
    state = attend_cached(queries, cache, lengths)
    gathered, state, hidden, base_weight = lax.optimization_barrier((gathered, state, hidden, base_weight))
    gathered = gathered + rest(gathered[0])
    tokens, base = arrange(hidden, base_weight, own)
    received = []
    for k in range(1, tp):
        other = project(k, tokens, base, gathered)
        received.append(lax.ppermute(other, "tp", [(i, i ^ k) for i in range(tp)]))
    mine = project(0, tokens, base, gathered)
    return finish([mine] + received, queries.reshape(rows, steps * heads, size), state, steps, own)


def solution(mesh):
    return jax.shard_map(
        functools.partial(shards, mesh.shape["dp"], mesh.shape["tp"]),
        mesh=mesh,
        in_specs=(
            P(("parts", "dp"), None, "tp"),
            P("tp", None, None, None),
            P(("parts", "tp"), "dp"),
            P(("parts", "dp"), None, None, None),
            P(("parts", "dp"), None, "tp", None),
            P(("parts", "dp"), None, None, "tp", None),
            P(("parts", "dp")),
        ),
        out_specs=(
            P(("parts", "dp"), None, None, "tp", None),
            P(("parts", "dp"), None, "tp", None),
        ),
        check_vma=False,
    )
```

```python
import functools

import jax
import jax.numpy as jnp
from jax import lax
from jax.experimental import pallas as pl
from jax.experimental.pallas import tpu as pltpu
from jax.sharding import PartitionSpec as P

LOW = -1e30
NT = (((1,), (1,)), ((), ()))
VMEM = pl.BlockSpec(memory_space=pltpu.VMEM)


def params(mib):
    return pltpu.CompilerParams(vmem_limit_bytes=mib * 1024 * 1024)


def in_hbm(x):
    return pltpu.with_memory_space_constraint(x, pltpu.HBM)


def cost(flops, moved, exps=0):
    return pl.CostEstimate(flops=flops, bytes_accessed=moved, transcendentals=exps)


def payload_kernel(down_hbm, up_hbm, out_ref, ups, wide, sems):
    ranks, width = down_hbm.shape
    groups, size = ups.shape[1] * ups.shape[2], ups.shape[3]
    get_down = pltpu.make_async_copy(down_hbm, out_ref.at[:, pl.ds(0, width)], sems.at[0])
    get_up = pltpu.make_async_copy(up_hbm, ups, sems.at[1])
    get_up.start()
    get_down.start()
    get_up.wait()
    wide[...] = ups.reshape(ranks * groups, size)[...].astype(jnp.float32)
    for n in range(groups):
        out_ref[:, width + n * size : width + (n + 1) * size] = wide[pl.ds(n, ranks, stride=groups), :].astype(
            jnp.bfloat16
        )
    get_down.wait()


def make_payload(down, up):
    ranks, width = down.shape
    groups, size = up.shape[1] * up.shape[2], up.shape[3]
    return pl.pallas_call(
        payload_kernel,
        out_shape=pltpu.VMEM((ranks, width + groups * size), jnp.bfloat16),
        in_specs=[pl.BlockSpec(memory_space=pltpu.HBM)] * 2,
        out_specs=VMEM,
        scratch_shapes=[
            pltpu.VMEM(up.shape, jnp.bfloat16),
            pltpu.VMEM((ranks * groups, size), jnp.float32),
            pltpu.SemaphoreType.DMA((2,)),
        ],
        compiler_params=params(8),
        name="payload",
    )(in_hbm(down), in_hbm(up))


def cached_kernel(chunks, heads, scale, *refs):
    lengths_hbm, queries_hbm, cache_hbm, q_all, out_ref, log_ref = refs[:6]
    lengths_ref, k_all, v_all = refs[6:9]
    scores_refs, weights_refs, total_refs = refs[9:11], refs[11:13], refs[13:15]
    sems, length_sem = refs[15:]
    rows, queries, size = q_all.shape
    slots, own = k_all.shape[1:3]
    keys = slots * own
    some = rows // chunks

    def copies(i):
        mine = pl.ds(i * some, some)
        pairs = (
            (queries_hbm.at[mine], q_all.at[mine]),
            (cache_hbm.at[mine, :, 0], k_all.at[mine]),
            (cache_hbm.at[mine, :, 1], v_all.at[mine]),
        )
        return [pltpu.make_async_copy(a, b, sems.at[i, n]) for n, (a, b) in enumerate(pairs)]

    get_lengths = pltpu.make_async_copy(lengths_hbm, lengths_ref, length_sem)
    get_lengths.start()
    for i in range(chunks):
        for copy in copies(i):
            copy.start()

    column = lax.broadcasted_iota(jnp.int32, (queries, keys), 1)
    head = lax.broadcasted_iota(jnp.int32, (queries, keys), 0) % heads
    column = jnp.where(column % own == head // (heads // own), column, own * slots)
    nothing = jnp.zeros((queries, size), jnp.bfloat16)
    flat_k = k_all.reshape(rows, keys, size)
    flat_v = v_all.reshape(rows, keys, size)

    def await_chunk(i):
        for copy in copies(i):
            copy.wait()

    def score(i, slot):
        for p in range(some // 2):
            r = i * some + 2 * p
            both = jnp.concatenate(
                [
                    jnp.concatenate([q_all[r], nothing], axis=1),
                    jnp.concatenate([nothing, q_all[r + 1]], axis=1),
                ],
                axis=0,
            )
            both_k = jnp.concatenate([flat_k[r], flat_k[r + 1]], axis=1)
            scores_refs[slot][p] = lax.dot_general(both, both_k, NT, preferred_element_type=jnp.float32)

    def soften(i, slot):
        for p in range(some // 2):
            for h in range(2):
                r = i * some + 2 * p + h
                mine = slice(h * queries, (h + 1) * queries)
                scores = jnp.where(column < own * lengths_ref[r], scores_refs[slot][p, mine], LOW)
                top = jnp.max(scores, axis=-1, keepdims=True)
                expo = jnp.exp((scores - top) * scale)
                total = jnp.sum(expo, axis=-1, keepdims=True)
                weights_refs[slot][p, mine] = expo.astype(jnp.bfloat16)
                total_refs[slot][p, mine] = jnp.broadcast_to(1.0 / total, (queries, size))
                log_ref[r] = jnp.broadcast_to(top * scale + jnp.log(total), (queries, size))

    def collect(i, slot):
        for p in range(some // 2):
            r = i * some + 2 * p
            both_v = jnp.concatenate([flat_v[r], flat_v[r + 1]], axis=1)
            both = jnp.dot(weights_refs[slot][p], both_v, preferred_element_type=jnp.float32)
            for h in range(2):
                mine = slice(h * queries, (h + 1) * queries)
                out_ref[r + h] = both[mine, h * size : (h + 1) * size] * total_refs[slot][p, mine]

    get_lengths.wait()
    await_chunk(0)
    score(0, 0)
    await_chunk(1)
    score(1, 1)
    soften(0, 0)

    @pl.loop(1, chunks // 2)
    def _(t):
        for slot in range(2):
            i = 2 * t + slot
            await_chunk(i)
            score(i, slot)
            soften(i - 1, 1 - slot)
            collect(i - 2, slot)

    soften(chunks - 1, 1)
    collect(chunks - 2, 0)
    collect(chunks - 1, 1)


def attend_cached(queries, cache, lengths):
    rows, steps, heads, size = queries.shape
    slots, own = cache.shape[1], cache.shape[3]
    many = steps * heads
    chunks = 8
    pairs = rows // chunks // 2
    state = (rows, many, size)
    half = (rows, slots, own, size)
    return pl.pallas_call(
        functools.partial(cached_kernel, chunks, heads, size ** (-0.5)),
        out_shape=(
            pltpu.VMEM(state, jnp.bfloat16),
            pltpu.VMEM(state, jnp.float32),
            pltpu.VMEM(state, jnp.float32),
        ),
        in_specs=[pl.BlockSpec(memory_space=pltpu.HBM)] * 3,
        out_specs=(VMEM,) * 3,
        scratch_shapes=[
            pltpu.SMEM(lengths.shape, jnp.int32),
            pltpu.VMEM(half, jnp.bfloat16),
            pltpu.VMEM(half, jnp.bfloat16),
            pltpu.VMEM((pairs, 2 * many, slots * own), jnp.float32),
            pltpu.VMEM((pairs, 2 * many, slots * own), jnp.float32),
            pltpu.VMEM((pairs, 2 * many, slots * own), jnp.bfloat16),
            pltpu.VMEM((pairs, 2 * many, slots * own), jnp.bfloat16),
            pltpu.VMEM((pairs, 2 * many, size), jnp.float32),
            pltpu.VMEM((pairs, 2 * many, size), jnp.float32),
            pltpu.SemaphoreType.DMA((chunks, 3)),
            pltpu.SemaphoreType.DMA,
        ],
        compiler_params=params(28),
        cost_estimate=cost(
            8 * rows * many * slots * size, 2 * (cache.size + queries.size) + 8 * rows * many * size, rows * many * slots
        ),
        name="attend_cached",
    )(*map(in_hbm, (lengths, queries.reshape(rows, many, size), cache)))


def arrange_kernel(chunks, own, hidden_hbm, base_hbm, tokens_ref, base_ref, hidden, base, sems):
    width, two, kvh, size = base.shape
    groups = two * kvh
    some_width = width // chunks

    def copy(i):
        features = pl.ds(i * some_width, some_width)
        return pltpu.make_async_copy(base_hbm.at[features], base.at[features], sems.at[i])

    get_hidden = pltpu.make_async_copy(hidden_hbm, hidden, sems.at[chunks])
    get_hidden.start()
    for i in range(chunks):
        copy(i).start()

    tile = 256
    some = tile // groups
    row = lax.broadcasted_iota(jnp.int32, (tile, tile), 0)
    place = lax.broadcasted_iota(jnp.int32, (tile, tile), 1)
    order = (place == (row % some) * groups + row // some).astype(jnp.float32).astype(jnp.bfloat16)
    flat_base = base.reshape(width * groups, size)

    def arrange(f):
        at = pl.multiple_of(f * groups, tile)
        pair = jnp.concatenate([flat_base[pl.ds(at + h * tile, tile), :] for h in range(2)], axis=1)
        moved = jnp.dot(order, pair, preferred_element_type=jnp.float32).astype(jnp.bfloat16)
        for n in range(groups):
            lanes = slice((n % own) * size, (n % own + 1) * size)
            for h in range(2):
                base_ref[n // own, pl.ds(pl.multiple_of(f + h * some, some), some), lanes] = moved[
                    n * some : (n + 1) * some, h * size : (h + 1) * size
                ]

    get_hidden.wait()
    tokens_ref[...] = hidden.reshape(tokens_ref.shape)[...]

    @pl.loop(0, chunks)
    def _(i):
        copy(i).wait()
        for f in range(0, some_width, 2 * some):
            arrange(i * some_width + f)


def arrange(hidden, base, own):
    rows, steps, _ = hidden.shape
    width, two, kvh, size = base.shape
    chunks = 8
    return pl.pallas_call(
        functools.partial(arrange_kernel, chunks, own),
        out_shape=(
            pltpu.VMEM((rows * steps, width), jnp.bfloat16),
            pltpu.VMEM((two * kvh // own, width, own * size), jnp.bfloat16),
        ),
        in_specs=[pl.BlockSpec(memory_space=pltpu.HBM)] * 2,
        out_specs=(VMEM, VMEM),
        scratch_shapes=[
            pltpu.VMEM(hidden.shape, jnp.bfloat16),
            pltpu.VMEM(base.shape, jnp.bfloat16),
            pltpu.SemaphoreType.DMA((chunks + 1,)),
        ],
        compiler_params=params(20),
        cost_estimate=cost(512 * base.size, 4 * (base.size + hidden.size)),
        name="arrange",
    )(in_hbm(hidden), in_hbm(base))


def project_kernel(k, hidden_ref, base_ref, *refs):
    gathered, (out_ref, merged) = refs[:-2], refs[-2:]
    width, columns = merged.shape
    part = lax.axis_index("tp") ^ k
    parts = base_ref.shape[0] // 2
    half = columns // 2
    up = jnp.concatenate(
        [
            jnp.concatenate(
                [ref[:, pl.ds(pl.multiple_of(width + (c * parts + part) * half, 128), half)] for ref in gathered], axis=0
            )
            for c in range(2)
        ],
        axis=1,
    )
    step = 512
    for f in range(0, width, step):
        down = jnp.concatenate([ref[:, f : f + step] for ref in gathered], axis=0).T
        low_rank = jnp.dot(down, up, preferred_element_type=jnp.float32)
        for c in range(2):
            base = base_ref[c * parts + part, f : f + step, :].astype(jnp.float32)
            merged[f : f + step, c * half : (c + 1) * half] = (base + low_rank[:, c * half : (c + 1) * half]).astype(
                jnp.bfloat16
            )
    out_ref[...] = jnp.dot(hidden_ref[...], merged[...], preferred_element_type=jnp.float32)


def project(k, hidden, base, gathered):
    tokens, width = hidden.shape
    columns = 2 * base.shape[2]
    ranks = sum(g.shape[0] for g in gathered)
    return pl.pallas_call(
        functools.partial(project_kernel, k),
        out_shape=pltpu.VMEM((tokens, columns), jnp.float32),
        in_specs=[VMEM] * (2 + len(gathered)),
        out_specs=VMEM,
        scratch_shapes=[pltpu.VMEM((width, columns), jnp.bfloat16)],
        compiler_params=params(24),
        cost_estimate=cost(2 * width * columns * (tokens + ranks), 2 * width * columns + 2 * width * tokens),
        name="project",
    )(hidden, base, *gathered)


def finish_kernel(steps, heads, scale, group, terms, *refs):
    parts, refs = refs[:terms], refs[terms:]
    q_ref, old_ref, log_ref, fresh_ref, context_ref, wide, bias = refs
    rows, queries, size = q_ref.shape
    own = fresh_ref.shape[3]
    fresh = parts[0][...]
    for part in parts[1:]:
        fresh = fresh + part[...]
    for n in range(2 * own):
        wide[pl.ds(n, rows * steps, stride=2 * own), :] = fresh[:, n * size : (n + 1) * size]
    fresh_ref.reshape(rows * steps * 2 * own, size)[...] = wide[...].astype(jnp.bfloat16)
    fresh = fresh.astype(jnp.bfloat16)
    many, keys = group * queries, own * group * steps
    query = lax.broadcasted_iota(jnp.int32, (many, keys), 0)
    key = lax.broadcasted_iota(jnp.int32, (many, keys), 1)
    same_head = (query % heads) // (heads // own) == key // (group * steps)
    same_row = query // queries == (key // steps) % group
    seen = (query % queries) // heads >= key % steps
    bias[...] = jnp.where(same_head & same_row & seen, 0.0, LOW)
    ones = jnp.ones((keys, size), jnp.bfloat16)
    for at in range(0, rows, group):
        tokens = slice(at * steps, (at + group) * steps)
        keys_new, values_new = [
            jnp.concatenate(
                [fresh[tokens, (c * own + g) * size : (c * own + g + 1) * size] for g in range(own)], axis=0
            )
            for c in range(2)
        ]
        values_new = jnp.concatenate([values_new, ones], axis=1)
        mine = slice(at, at + group)
        scores = lax.dot_general(
            q_ref[mine].reshape(many, size), keys_new, NT, preferred_element_type=jnp.float32
        )
        scores = scores * scale + bias[...]
        log_old = log_ref[mine].reshape(many, size)
        top = jnp.maximum(log_old, jnp.max(scores, axis=-1, keepdims=True))
        weights = jnp.exp(scores - top).astype(jnp.bfloat16)
        back = jnp.exp(log_old - top)
        both = jnp.dot(weights, values_new, preferred_element_type=jnp.float32)
        total = back + both[:, size:]
        summed = back * old_ref[mine].reshape(many, size) + both[:, :size]
        context_ref[mine] = (summed / total).astype(jnp.bfloat16).reshape(group, queries, size)


def finish(parts, queries, state, steps, own):
    rows, many, size = queries.shape
    heads = many // steps
    group = size // (own * steps)
    fresh, context = pl.pallas_call(
        functools.partial(finish_kernel, steps, heads, size ** (-0.5), group, len(parts)),
        out_shape=(
            jax.ShapeDtypeStruct((rows, steps, 2, own, size), jnp.bfloat16),
            jax.ShapeDtypeStruct((rows, many, size), jnp.bfloat16),
        ),
        in_specs=[VMEM] * (len(parts) + 1 + len(state)),
        out_specs=(VMEM, VMEM),
        scratch_shapes=[
            pltpu.VMEM((rows * steps * 2 * own, size), jnp.float32),
            pltpu.VMEM((group * many, own * group * steps), jnp.float32),
        ],
        compiler_params=params(24),
        cost_estimate=cost(rows * many * size * size * 6, 12 * rows * many * size, rows * many * size * 2),
        name="finish",
    )(*parts, queries, *state)
    return fresh, context.reshape(rows, steps, heads, size)


def join_kernel(*refs):
    blocks, out_ref = refs[:-1], refs[-1]
    at = 0
    for block in blocks:
        out_ref[at : at + block.shape[0], :] = block[...]
        at += block.shape[0]


def join(blocks):
    rows = sum(b.shape[0] for b in blocks)
    return pl.pallas_call(
        join_kernel,
        out_shape=pltpu.VMEM((rows, blocks[0].shape[1]), jnp.bfloat16),
        in_specs=[VMEM] * len(blocks),
        out_specs=VMEM,
        compiler_params=params(8),
        name="join",
    )(*blocks)


def gather_second(factor_a, factor_b, dp):
    count = dp // 2
    ranks = factor_b.shape[0]
    if ranks % 8 == 0 and count in (1, 2, 4):
        payload = make_payload(factor_a.T, factor_b)
        return [payload] + [lax.ppermute(payload, "dp", [(i, i ^ (2 * k)) for i in range(dp)]) for k in range(1, count)]
    payload = jnp.concatenate([factor_a.T, factor_b.reshape(ranks, -1)], axis=1)
    groups = [[i for i in range(dp) if i % 2 == n] for n in range(2)]
    copies = jnp.broadcast_to(payload[None], (count,) + payload.shape)
    blocks = lax.all_to_all(copies, "dp", 0, 0, axis_index_groups=groups, tiled=True)
    return [blocks.reshape(count * ranks, payload.shape[1])]


def shards(dp, tp, hidden, base_weight, factor_a, factor_b, queries, cache, lengths):
    steps, own = queries.shape[1], cache.shape[3]
    assert dp % 2 == 0
    blocks = gather_second(factor_a, factor_b, dp)
    queries, *state = attend_cached(queries, cache, lengths)
    blocks, state, queries, hidden, base_weight = lax.optimization_barrier(
        (blocks, state, queries, hidden, base_weight)
    )
    gathered = join(blocks) if len(blocks) > 1 else blocks[0]
    gathered = [gathered, lax.ppermute(gathered, "dp", [(i, i ^ 1) for i in range(dp)])]
    tokens, base = arrange(hidden, base_weight, own)
    received = []
    for k in range(1, tp):
        other = project(k, tokens, base, gathered)
        received.append(lax.ppermute(other, "tp", [(i, i ^ k) for i in range(tp)]))
    mine = project(0, tokens, base, gathered)
    return finish([mine] + received, queries, state, steps, own)


def solution(mesh):
    return jax.shard_map(
        functools.partial(shards, mesh.shape["dp"], mesh.shape["tp"]),
        mesh=mesh,
        in_specs=(
            P(("parts", "dp"), None, "tp"),
            P("tp", None, None, None),
            P(("parts", "tp"), "dp"),
            P(("parts", "dp"), None, None, None),
            P(("parts", "dp"), None, "tp", None),
            P(("parts", "dp"), None, None, "tp", None),
            P(("parts", "dp")),
        ),
        out_specs=(
            P(("parts", "dp"), None, None, "tp", None),
            P(("parts", "dp"), None, "tp", None),
        ),
        check_vma=False,
    )
```

```python
import functools

import jax
import jax.numpy as jnp
from jax import lax
from jax.experimental import pallas as pl
from jax.experimental.pallas import tpu as pltpu
from jax.sharding import PartitionSpec as P

LOW = -1e30
NT = (((1,), (1,)), ((), ()))
VMEM = pl.BlockSpec(memory_space=pltpu.VMEM)


def params(mib):
    return pltpu.CompilerParams(vmem_limit_bytes=mib * 1024 * 1024)


def in_hbm(x):
    return pltpu.with_memory_space_constraint(x, pltpu.HBM)


def cost(flops, moved, exps=0):
    return pl.CostEstimate(flops=flops, bytes_accessed=moved, transcendentals=exps)


def payload_kernel(down_hbm, up_hbm, out_ref, ups, wide, sems):
    ranks, width = down_hbm.shape
    groups, size = ups.shape[1] * ups.shape[2], ups.shape[3]
    get_down = pltpu.make_async_copy(down_hbm, out_ref.at[:, pl.ds(0, width)], sems.at[0])
    get_up = pltpu.make_async_copy(up_hbm, ups, sems.at[1])
    get_up.start()
    get_down.start()
    get_up.wait()
    wide[...] = ups.reshape(ranks * groups, size)[...].astype(jnp.float32)
    for n in range(groups):
        out_ref[:, width + n * size : width + (n + 1) * size] = wide[pl.ds(n, ranks, stride=groups), :].astype(
            jnp.bfloat16
        )
    get_down.wait()


def make_payload(down, up):
    ranks, width = down.shape
    groups, size = up.shape[1] * up.shape[2], up.shape[3]
    return pl.pallas_call(
        payload_kernel,
        out_shape=pltpu.VMEM((ranks, width + groups * size), jnp.bfloat16),
        in_specs=[pl.BlockSpec(memory_space=pltpu.HBM)] * 2,
        out_specs=VMEM,
        scratch_shapes=[
            pltpu.VMEM(up.shape, jnp.bfloat16),
            pltpu.VMEM((ranks * groups, size), jnp.float32),
            pltpu.SemaphoreType.DMA((2,)),
        ],
        compiler_params=params(8),
        name="payload",
    )(in_hbm(down), in_hbm(up))


def cached_kernel(chunks, heads, scale, *refs):
    lengths_hbm, queries_hbm, cache_hbm, q_all, out_ref, log_ref = refs[:6]
    lengths_ref, cached = refs[6:8]
    scores_refs, weights_refs, total_refs = refs[8:10], refs[10:12], refs[12:14]
    sems, length_sem = refs[14:]
    rows, queries, size = q_all.shape
    slots, own = cached.shape[1], cached.shape[3]
    lines = slots * 2 * own
    some = rows // chunks

    def copies(i):
        mine = pl.ds(i * some, some)
        pairs = (
            (queries_hbm.at[mine], q_all.at[mine]),
            (cache_hbm.at[mine], cached.at[pl.ds(1 + i * some, some)]),
        )
        return [pltpu.make_async_copy(a, b, sems.at[i, n]) for n, (a, b) in enumerate(pairs)]

    get_lengths = pltpu.make_async_copy(lengths_hbm, lengths_ref, length_sem)
    get_lengths.start()
    for i in range(chunks):
        for copy in copies(i):
            copy.start()

    each = (own, heads // own, lines)
    line = lax.broadcasted_iota(jnp.int32, each, 2)
    fits = ((line // own) % 2 == 1) & (line % own == lax.broadcasted_iota(jnp.int32, each, 0))
    line = jnp.where(fits, line, lines)
    nothing = jnp.zeros((queries, size), jnp.bfloat16)
    flat = cached.reshape((rows + 1) * lines, size)

    def keys(r):
        return flat[pl.ds(pl.multiple_of((r + 1) * lines - own, own), lines), :]

    def values(r):
        return flat[pl.ds(pl.multiple_of((r + 1) * lines, own), lines), :]

    def await_chunk(i):
        for copy in copies(i):
            copy.wait()

    def score(i, slot):
        for p in range(some // 2):
            r = i * some + 2 * p
            both = jnp.concatenate(
                [
                    jnp.concatenate([q_all[r], nothing], axis=1),
                    jnp.concatenate([nothing, q_all[r + 1]], axis=1),
                ],
                axis=0,
            )
            both_k = jnp.concatenate([keys(r), keys(r + 1)], axis=1)
            scores_refs[slot][p] = lax.dot_general(both, both_k, NT, preferred_element_type=jnp.float32)

    def soften(i, slot):
        for p in range(some // 2):
            for h in range(2):
                r = i * some + 2 * p + h
                mine = slice(h * queries, (h + 1) * queries)
                live = line < 2 * own * lengths_ref[r]
                scores = scores_refs[slot][p, mine].reshape((queries // heads,) + each)
                scores = jnp.where(live[None], scores, LOW).reshape(queries, lines)
                top = jnp.max(scores, axis=-1, keepdims=True)
                expo = jnp.exp((scores - top) * scale)
                total = jnp.sum(expo, axis=-1, keepdims=True)
                weights_refs[slot][p, mine] = expo.astype(jnp.bfloat16)
                total_refs[slot][p, mine] = jnp.broadcast_to(1.0 / total, (queries, size))
                log_ref[r] = jnp.broadcast_to(top * scale + jnp.log(total), (queries, size))

    def collect(i, slot):
        for p in range(some // 2):
            r = i * some + 2 * p
            both_v = jnp.concatenate([values(r), values(r + 1)], axis=1)
            both = jnp.dot(weights_refs[slot][p], both_v, preferred_element_type=jnp.float32)
            for h in range(2):
                mine = slice(h * queries, (h + 1) * queries)
                out_ref[r + h] = both[mine, h * size : (h + 1) * size] * total_refs[slot][p, mine]

    get_lengths.wait()
    await_chunk(0)
    score(0, 0)
    await_chunk(1)
    score(1, 1)
    soften(0, 0)

    @pl.loop(1, chunks // 2)
    def _(t):
        for slot in range(2):
            i = 2 * t + slot
            await_chunk(i)
            score(i, slot)
            soften(i - 1, 1 - slot)
            collect(i - 2, slot)

    soften(chunks - 1, 1)
    collect(chunks - 2, 0)
    collect(chunks - 1, 1)


def attend_cached(queries, cache, lengths):
    rows, steps, heads, size = queries.shape
    slots, own = cache.shape[1], cache.shape[3]
    many = steps * heads
    chunks = 8
    pairs = rows // chunks // 2
    lines = slots * 2 * own
    state = (rows, many, size)
    return pl.pallas_call(
        functools.partial(cached_kernel, chunks, heads, size ** (-0.5)),
        out_shape=(
            pltpu.VMEM(state, jnp.bfloat16),
            pltpu.VMEM(state, jnp.float32),
            pltpu.VMEM(state, jnp.float32),
        ),
        in_specs=[pl.BlockSpec(memory_space=pltpu.HBM)] * 3,
        out_specs=(VMEM,) * 3,
        scratch_shapes=[
            pltpu.SMEM(lengths.shape, jnp.int32),
            pltpu.VMEM((rows + 1,) + cache.shape[1:], jnp.bfloat16),
            pltpu.VMEM((pairs, 2 * many, lines), jnp.float32),
            pltpu.VMEM((pairs, 2 * many, lines), jnp.float32),
            pltpu.VMEM((pairs, 2 * many, lines), jnp.bfloat16),
            pltpu.VMEM((pairs, 2 * many, lines), jnp.bfloat16),
            pltpu.VMEM((pairs, 2 * many, size), jnp.float32),
            pltpu.VMEM((pairs, 2 * many, size), jnp.float32),
            pltpu.SemaphoreType.DMA((chunks, 2)),
            pltpu.SemaphoreType.DMA,
        ],
        compiler_params=params(28),
        cost_estimate=cost(
            16 * rows * many * slots * size, 2 * (cache.size + queries.size) + 8 * rows * many * size, rows * many * lines
        ),
        name="attend_cached",
    )(*map(in_hbm, (lengths, queries.reshape(rows, many, size), cache)))


def arrange_kernel(chunks, own, hidden_hbm, base_hbm, tokens_ref, base_ref, hidden, base, sems):
    width, two, kvh, size = base.shape
    groups = two * kvh
    some_width = width // chunks

    def copy(i):
        features = pl.ds(i * some_width, some_width)
        return pltpu.make_async_copy(base_hbm.at[features], base.at[features], sems.at[i])

    get_hidden = pltpu.make_async_copy(hidden_hbm, hidden, sems.at[chunks])
    for i in range(chunks):
        copy(i).start()
    get_hidden.start()

    tile = 256
    some = tile // groups
    row = lax.broadcasted_iota(jnp.int32, (tile, tile), 0)
    place = lax.broadcasted_iota(jnp.int32, (tile, tile), 1)
    order = (place == (row % some) * groups + row // some).astype(jnp.float32).astype(jnp.bfloat16)
    flat_base = base.reshape(width * groups, size)

    def arrange(f):
        at = pl.multiple_of(f * groups, tile)
        pair = jnp.concatenate([flat_base[pl.ds(at + h * tile, tile), :] for h in range(2)], axis=1)
        moved = jnp.dot(order, pair, preferred_element_type=jnp.float32).astype(jnp.bfloat16)
        for n in range(groups):
            lanes = slice((n % own) * size, (n % own + 1) * size)
            for h in range(2):
                base_ref[n // own, pl.ds(pl.multiple_of(f + h * some, some), some), lanes] = moved[
                    n * some : (n + 1) * some, h * size : (h + 1) * size
                ]

    @pl.loop(0, chunks)
    def _(i):
        copy(i).wait()
        for f in range(0, some_width, 2 * some):
            arrange(i * some_width + f)

    get_hidden.wait()
    tokens_ref[...] = hidden.reshape(tokens_ref.shape)[...]


def arrange(hidden, base, own):
    rows, steps, _ = hidden.shape
    width, two, kvh, size = base.shape
    chunks = 4
    return pl.pallas_call(
        functools.partial(arrange_kernel, chunks, own),
        out_shape=(
            pltpu.VMEM((rows * steps, width), jnp.bfloat16),
            pltpu.VMEM((two * kvh // own, width, own * size), jnp.bfloat16),
        ),
        in_specs=[pl.BlockSpec(memory_space=pltpu.HBM)] * 2,
        out_specs=(VMEM, VMEM),
        scratch_shapes=[
            pltpu.VMEM(hidden.shape, jnp.bfloat16),
            pltpu.VMEM(base.shape, jnp.bfloat16),
            pltpu.SemaphoreType.DMA((chunks + 1,)),
        ],
        compiler_params=params(20),
        cost_estimate=cost(512 * base.size, 4 * (base.size + hidden.size)),
        name="arrange",
    )(in_hbm(hidden), in_hbm(base))


def project_kernel(k, hidden_ref, base_ref, *refs):
    gathered, (out_ref, merged) = refs[:-2], refs[-2:]
    width, columns = merged.shape
    part = lax.axis_index("tp") ^ k
    parts = base_ref.shape[0] // 2
    half = columns // 2
    up = jnp.concatenate(
        [
            jnp.concatenate(
                [ref[:, pl.ds(pl.multiple_of(width + (c * parts + part) * half, 128), half)] for ref in gathered], axis=0
            )
            for c in range(2)
        ],
        axis=1,
    )
    step = 512
    for f in range(0, width, step):
        down = jnp.concatenate([ref[:, f : f + step] for ref in gathered], axis=0).T
        low_rank = jnp.dot(down, up, preferred_element_type=jnp.float32)
        for c in range(2):
            base = base_ref[c * parts + part, f : f + step, :].astype(jnp.float32)
            merged[f : f + step, c * half : (c + 1) * half] = (base + low_rank[:, c * half : (c + 1) * half]).astype(
                jnp.bfloat16
            )
    out_ref[...] = jnp.dot(hidden_ref[...], merged[...], preferred_element_type=jnp.float32)


def project(k, hidden, base, gathered):
    tokens, width = hidden.shape
    columns = 2 * base.shape[2]
    ranks = sum(g.shape[0] for g in gathered)
    return pl.pallas_call(
        functools.partial(project_kernel, k),
        out_shape=pltpu.VMEM((tokens, columns), jnp.float32),
        in_specs=[VMEM] * (2 + len(gathered)),
        out_specs=VMEM,
        scratch_shapes=[pltpu.VMEM((width, columns), jnp.bfloat16)],
        compiler_params=params(24),
        cost_estimate=cost(2 * width * columns * (tokens + ranks), 2 * width * columns + 2 * width * tokens),
        name="project",
    )(hidden, base, *gathered)


def finish_kernel(steps, heads, scale, group, terms, *refs):
    parts, refs = refs[:terms], refs[terms:]
    q_ref, old_ref, log_ref, fresh_ref, context_ref, wide, bias = refs
    rows, queries, size = q_ref.shape
    own = fresh_ref.shape[3]
    fresh = parts[0][...]
    for part in parts[1:]:
        fresh = fresh + part[...]
    for n in range(2 * own):
        wide[pl.ds(n, rows * steps, stride=2 * own), :] = fresh[:, n * size : (n + 1) * size]
    fresh_ref.reshape(rows * steps * 2 * own, size)[...] = wide[...].astype(jnp.bfloat16)
    fresh = fresh.astype(jnp.bfloat16)
    many, keys = group * queries, own * group * steps
    query = lax.broadcasted_iota(jnp.int32, (many, keys), 0)
    key = lax.broadcasted_iota(jnp.int32, (many, keys), 1)
    same_head = (query % heads) // (heads // own) == key // (group * steps)
    same_row = query // queries == (key // steps) % group
    seen = (query % queries) // heads >= key % steps
    bias[...] = jnp.where(same_head & same_row & seen, 0.0, LOW)
    ones = jnp.ones((keys, size), jnp.bfloat16)
    for at in range(0, rows, group):
        tokens = slice(at * steps, (at + group) * steps)
        keys_new, values_new = [
            jnp.concatenate(
                [fresh[tokens, (c * own + g) * size : (c * own + g + 1) * size] for g in range(own)], axis=0
            )
            for c in range(2)
        ]
        values_new = jnp.concatenate([values_new, ones], axis=1)
        mine = slice(at, at + group)
        scores = lax.dot_general(
            q_ref[mine].reshape(many, size), keys_new, NT, preferred_element_type=jnp.float32
        )
        scores = scores * scale + bias[...]
        log_old = log_ref[mine].reshape(many, size)
        top = jnp.maximum(log_old, jnp.max(scores, axis=-1, keepdims=True))
        weights = jnp.exp(scores - top).astype(jnp.bfloat16)
        back = jnp.exp(log_old - top)
        both = jnp.dot(weights, values_new, preferred_element_type=jnp.float32)
        total = back + both[:, size:]
        summed = back * old_ref[mine].reshape(many, size) + both[:, :size]
        context_ref[mine] = (summed / total).astype(jnp.bfloat16).reshape(group, queries, size)


def finish(parts, queries, state, steps, own):
    rows, many, size = queries.shape
    heads = many // steps
    group = size // (own * steps)
    fresh, context = pl.pallas_call(
        functools.partial(finish_kernel, steps, heads, size ** (-0.5), group, len(parts)),
        out_shape=(
            jax.ShapeDtypeStruct((rows, steps, 2, own, size), jnp.bfloat16),
            jax.ShapeDtypeStruct((rows, many, size), jnp.bfloat16),
        ),
        in_specs=[VMEM] * (len(parts) + 1 + len(state)),
        out_specs=(VMEM, VMEM),
        scratch_shapes=[
            pltpu.VMEM((rows * steps * 2 * own, size), jnp.float32),
            pltpu.VMEM((group * many, own * group * steps), jnp.float32),
        ],
        compiler_params=params(24),
        cost_estimate=cost(rows * many * size * size * 6, 12 * rows * many * size, rows * many * size * 2),
        name="finish",
    )(*parts, queries, *state)
    return fresh, context.reshape(rows, steps, heads, size)


def join_kernel(*refs):
    blocks, out_ref = refs[:-1], refs[-1]
    at = 0
    for block in blocks:
        out_ref[at : at + block.shape[0], :] = block[...]
        at += block.shape[0]


def join(blocks):
    rows = sum(b.shape[0] for b in blocks)
    return pl.pallas_call(
        join_kernel,
        out_shape=pltpu.VMEM((rows, blocks[0].shape[1]), jnp.bfloat16),
        in_specs=[VMEM] * len(blocks),
        out_specs=VMEM,
        compiler_params=params(8),
        name="join",
    )(*blocks)


def gather_second(factor_a, factor_b, dp):
    count = dp // 2
    ranks = factor_b.shape[0]
    if ranks % 8 == 0 and count in (1, 2, 4):
        payload = make_payload(factor_a.T, factor_b)
        return [payload] + [lax.ppermute(payload, "dp", [(i, i ^ (2 * k)) for i in range(dp)]) for k in range(1, count)]
    payload = jnp.concatenate([factor_a.T, factor_b.reshape(ranks, -1)], axis=1)
    groups = [[i for i in range(dp) if i % 2 == n] for n in range(2)]
    copies = jnp.broadcast_to(payload[None], (count,) + payload.shape)
    blocks = lax.all_to_all(copies, "dp", 0, 0, axis_index_groups=groups, tiled=True)
    return [blocks.reshape(count * ranks, payload.shape[1])]


def shards(dp, tp, hidden, base_weight, factor_a, factor_b, queries, cache, lengths):
    steps, own = queries.shape[1], cache.shape[3]
    assert dp % 2 == 0
    blocks = gather_second(factor_a, factor_b, dp)
    queries, *state = attend_cached(queries, cache, lengths)
    blocks, state, queries, hidden, base_weight = lax.optimization_barrier(
        (blocks, state, queries, hidden, base_weight)
    )
    gathered = join(blocks) if len(blocks) > 1 else blocks[0]
    gathered = [gathered, lax.ppermute(gathered, "dp", [(i, i ^ 1) for i in range(dp)])]
    tokens, base = arrange(hidden, base_weight, own)
    received = []
    for k in range(1, tp):
        other = project(k, tokens, base, gathered)
        received.append(lax.ppermute(other, "tp", [(i, i ^ k) for i in range(tp)]))
    mine = project(0, tokens, base, gathered)
    return finish([mine] + received, queries, state, steps, own)


def solution(mesh):
    return jax.shard_map(
        functools.partial(shards, mesh.shape["dp"], mesh.shape["tp"]),
        mesh=mesh,
        in_specs=(
            P(("parts", "dp"), None, "tp"),
            P("tp", None, None, None),
            P(("parts", "tp"), "dp"),
            P(("parts", "dp"), None, None, None),
            P(("parts", "dp"), None, "tp", None),
            P(("parts", "dp"), None, None, "tp", None),
            P(("parts", "dp")),
        ),
        out_specs=(
            P(("parts", "dp"), None, None, "tp", None),
            P(("parts", "dp"), None, "tp", None),
        ),
        check_vma=False,
    )
```

```python
import functools

import jax
import jax.numpy as jnp
from jax import lax
from jax.experimental import pallas as pl
from jax.experimental.pallas import tpu as pltpu
from jax.sharding import PartitionSpec as P

LOW = -1e30
NT = (((1,), (1,)), ((), ()))
TN = (((0,), (0,)), ((), ()))
VMEM = pl.BlockSpec(memory_space=pltpu.VMEM)


def params(mib):
    return pltpu.CompilerParams(vmem_limit_bytes=mib * 1024 * 1024)


def in_hbm(x):
    return pltpu.with_memory_space_constraint(x, pltpu.HBM)


def cost(flops, moved, exps=0):
    return pl.CostEstimate(flops=flops, bytes_accessed=moved, transcendentals=exps)


def payload_kernel(down_hbm, up_hbm, out_ref, ups, wide, sems):
    ranks, width = down_hbm.shape
    groups, size = ups.shape[1] * ups.shape[2], ups.shape[3]
    get_down = pltpu.make_async_copy(down_hbm, out_ref.at[:, pl.ds(0, width)], sems.at[0])
    get_up = pltpu.make_async_copy(up_hbm, ups, sems.at[1])
    get_up.start()
    get_down.start()
    get_up.wait()
    wide[...] = ups.reshape(ranks * groups, size)[...].astype(jnp.float32)
    for n in range(groups):
        out_ref[:, width + n * size : width + (n + 1) * size] = wide[pl.ds(n, ranks, stride=groups), :].astype(
            jnp.bfloat16
        )
    get_down.wait()


def make_payload(down, up):
    ranks, width = down.shape
    groups, size = up.shape[1] * up.shape[2], up.shape[3]
    return pl.pallas_call(
        payload_kernel,
        out_shape=pltpu.VMEM((ranks, width + groups * size), jnp.bfloat16),
        in_specs=[pl.BlockSpec(memory_space=pltpu.HBM)] * 2,
        out_specs=VMEM,
        scratch_shapes=[
            pltpu.VMEM(up.shape, jnp.bfloat16),
            pltpu.VMEM((ranks * groups, size), jnp.float32),
            pltpu.SemaphoreType.DMA((2,)),
        ],
        compiler_params=params(8),
        name="payload",
    )(in_hbm(down), in_hbm(up))


def cached_kernel(chunks, heads, scale, *refs):
    lengths_hbm, queries_hbm, cache_hbm, q_all, sum_ref, top_ref, total_ref = refs[:7]
    lengths_ref, k_all, v_all = refs[7:10]
    scores_refs, weights_refs = refs[10:12], refs[12:14]
    sems, length_sem = refs[14:]
    rows, queries, size = q_all.shape
    slots, own = k_all.shape[1:3]
    keys = slots * own
    some = rows // chunks

    def copies(i):
        mine = pl.ds(i * some, some)
        pairs = (
            (queries_hbm.at[mine], q_all.at[mine]),
            (cache_hbm.at[mine, :, 0], k_all.at[mine]),
            (cache_hbm.at[mine, :, 1], v_all.at[mine]),
        )
        return [pltpu.make_async_copy(a, b, sems.at[i, n]) for n, (a, b) in enumerate(pairs)]

    get_lengths = pltpu.make_async_copy(lengths_hbm, lengths_ref, length_sem)
    get_lengths.start()
    for i in range(chunks):
        for copy in copies(i):
            copy.start()

    line = lax.broadcasted_iota(jnp.int32, (keys, 2 * queries), 0)
    query = lax.broadcasted_iota(jnp.int32, (keys, 2 * queries), 1)
    line = jnp.where(line % own == (query % heads) // (heads // own), line, keys)
    first = lax.broadcasted_iota(jnp.int32, (1, 2 * queries), 1) < queries
    nothing = jnp.zeros((queries, size), jnp.bfloat16)
    flat_k = k_all.reshape(rows, keys, size)
    flat_v = v_all.reshape(rows, keys, size)

    def await_chunk(i):
        for copy in copies(i):
            copy.wait()

    def score(i, slot):
        for p in range(some // 2):
            r = i * some + 2 * p
            both_q = jnp.concatenate(
                [
                    jnp.concatenate([q_all[r], nothing], axis=1),
                    jnp.concatenate([nothing, q_all[r + 1]], axis=1),
                ],
                axis=0,
            )
            both_k = jnp.concatenate([flat_k[r], flat_k[r + 1]], axis=1)
            scores_refs[slot][p] = lax.dot_general(both_k, both_q, NT, preferred_element_type=jnp.float32)

    def soften(i, slot):
        for p in range(some // 2):
            r = i * some + 2 * p
            limit = jnp.where(first, own * lengths_ref[r], own * lengths_ref[r + 1])
            scores = jnp.where(line < limit, scores_refs[slot][p], LOW)
            top = jnp.max(scores, axis=0, keepdims=True)
            expo = jnp.exp((scores - top) * scale)
            weights_refs[slot][p] = expo.astype(jnp.bfloat16)
            pair = pl.ds(i * (some // 2) + p, 1)
            top_ref[pair, :] = top
            total_ref[pair, :] = jnp.sum(expo, axis=0, keepdims=True)

    def collect(i, slot):
        for p in range(some // 2):
            r = i * some + 2 * p
            both_v = jnp.concatenate([flat_v[r], flat_v[r + 1]], axis=1)
            both = lax.dot_general(weights_refs[slot][p], both_v, TN, preferred_element_type=jnp.float32)
            for h in range(2):
                sum_ref[r + h] = both[h * queries : (h + 1) * queries, h * size : (h + 1) * size]

    get_lengths.wait()
    await_chunk(0)
    score(0, 0)
    await_chunk(1)
    score(1, 1)
    soften(0, 0)

    @pl.loop(1, chunks // 2)
    def _(t):
        for slot in range(2):
            i = 2 * t + slot
            await_chunk(i)
            score(i, slot)
            soften(i - 1, 1 - slot)
            collect(i - 2, slot)

    soften(chunks - 1, 1)
    collect(chunks - 2, 0)
    collect(chunks - 1, 1)


def attend_cached(queries, cache, lengths):
    rows, steps, heads, size = queries.shape
    slots, own = cache.shape[1], cache.shape[3]
    many = steps * heads
    chunks = 8
    pairs = rows // chunks // 2
    keys = slots * own
    state = (rows, many, size)
    half = (rows, slots, own, size)
    return pl.pallas_call(
        functools.partial(cached_kernel, chunks, heads, size ** (-0.5)),
        out_shape=(
            pltpu.VMEM(state, jnp.bfloat16),
            pltpu.VMEM(state, jnp.float32),
            pltpu.VMEM((rows // 2, 2 * many), jnp.float32),
            pltpu.VMEM((rows // 2, 2 * many), jnp.float32),
        ),
        in_specs=[pl.BlockSpec(memory_space=pltpu.HBM)] * 3,
        out_specs=(VMEM,) * 4,
        scratch_shapes=[
            pltpu.SMEM(lengths.shape, jnp.int32),
            pltpu.VMEM(half, jnp.bfloat16),
            pltpu.VMEM(half, jnp.bfloat16),
            pltpu.VMEM((pairs, keys, 2 * many), jnp.float32),
            pltpu.VMEM((pairs, keys, 2 * many), jnp.float32),
            pltpu.VMEM((pairs, keys, 2 * many), jnp.bfloat16),
            pltpu.VMEM((pairs, keys, 2 * many), jnp.bfloat16),
            pltpu.SemaphoreType.DMA((chunks, 3)),
            pltpu.SemaphoreType.DMA,
        ],
        compiler_params=params(28),
        cost_estimate=cost(
            8 * rows * many * slots * size, 2 * (cache.size + queries.size) + 4 * rows * many * size, rows * many * keys
        ),
        name="attend_cached",
    )(*map(in_hbm, (lengths, queries.reshape(rows, many, size), cache)))


def arrange_kernel(chunks, own, hidden_hbm, base_hbm, tokens_ref, base_ref, hidden, base, sems):
    width, two, kvh, size = base.shape
    groups = two * kvh
    some_width = width // chunks

    def copy(i):
        features = pl.ds(i * some_width, some_width)
        return pltpu.make_async_copy(base_hbm.at[features], base.at[features], sems.at[i])

    get_hidden = pltpu.make_async_copy(hidden_hbm, hidden, sems.at[chunks])
    for i in range(chunks):
        copy(i).start()
    get_hidden.start()

    tile = 256
    some = tile // groups
    row = lax.broadcasted_iota(jnp.int32, (tile, tile), 0)
    place = lax.broadcasted_iota(jnp.int32, (tile, tile), 1)
    order = (place == (row % some) * groups + row // some).astype(jnp.float32).astype(jnp.bfloat16)
    flat_base = base.reshape(width * groups, size)

    def arrange(f):
        at = pl.multiple_of(f * groups, tile)
        pair = jnp.concatenate([flat_base[pl.ds(at + h * tile, tile), :] for h in range(2)], axis=1)
        moved = jnp.dot(order, pair, preferred_element_type=jnp.float32).astype(jnp.bfloat16)
        for n in range(groups):
            lanes = slice((n % own) * size, (n % own + 1) * size)
            for h in range(2):
                base_ref[n // own, pl.ds(pl.multiple_of(f + h * some, some), some), lanes] = moved[
                    n * some : (n + 1) * some, h * size : (h + 1) * size
                ]

    @pl.loop(0, chunks)
    def _(i):
        copy(i).wait()
        for f in range(0, some_width, 2 * some):
            arrange(i * some_width + f)

    get_hidden.wait()
    tokens_ref[...] = hidden.reshape(tokens_ref.shape)[...]


def arrange(hidden, base, own):
    rows, steps, _ = hidden.shape
    width, two, kvh, size = base.shape
    chunks = 4
    return pl.pallas_call(
        functools.partial(arrange_kernel, chunks, own),
        out_shape=(
            pltpu.VMEM((rows * steps, width), jnp.bfloat16),
            pltpu.VMEM((two * kvh // own, width, own * size), jnp.bfloat16),
        ),
        in_specs=[pl.BlockSpec(memory_space=pltpu.HBM)] * 2,
        out_specs=(VMEM, VMEM),
        scratch_shapes=[
            pltpu.VMEM(hidden.shape, jnp.bfloat16),
            pltpu.VMEM(base.shape, jnp.bfloat16),
            pltpu.SemaphoreType.DMA((chunks + 1,)),
        ],
        compiler_params=params(20),
        cost_estimate=cost(512 * base.size, 4 * (base.size + hidden.size)),
        name="arrange",
    )(in_hbm(hidden), in_hbm(base))


def project_kernel(k, hidden_ref, base_ref, *refs):
    gathered, (out_ref, merged) = refs[:-2], refs[-2:]
    width, columns = merged.shape
    part = lax.axis_index("tp") ^ k
    parts = base_ref.shape[0] // 2
    half = columns // 2
    up = jnp.concatenate(
        [
            jnp.concatenate(
                [ref[:, pl.ds(pl.multiple_of(width + (c * parts + part) * half, 128), half)] for ref in gathered], axis=0
            )
            for c in range(2)
        ],
        axis=1,
    )
    step = 512
    for f in range(0, width, step):
        down = jnp.concatenate([ref[:, f : f + step] for ref in gathered], axis=0).T
        low_rank = jnp.dot(down, up, preferred_element_type=jnp.float32)
        for c in range(2):
            base = base_ref[c * parts + part, f : f + step, :].astype(jnp.float32)
            merged[f : f + step, c * half : (c + 1) * half] = (base + low_rank[:, c * half : (c + 1) * half]).astype(
                jnp.bfloat16
            )
    out_ref[...] = jnp.dot(hidden_ref[...], merged[...], preferred_element_type=jnp.float32)


def project(k, hidden, base, gathered):
    tokens, width = hidden.shape
    columns = 2 * base.shape[2]
    ranks = sum(g.shape[0] for g in gathered)
    return pl.pallas_call(
        functools.partial(project_kernel, k),
        out_shape=pltpu.VMEM((tokens, columns), jnp.float32),
        in_specs=[VMEM] * (2 + len(gathered)),
        out_specs=VMEM,
        scratch_shapes=[pltpu.VMEM((width, columns), jnp.bfloat16)],
        compiler_params=params(24),
        cost_estimate=cost(2 * width * columns * (tokens + ranks), 2 * width * columns + 2 * width * tokens),
        name="project",
    )(hidden, base, *gathered)


def finish_kernel(steps, heads, scale, group, terms, *refs):
    parts, refs = refs[:terms], refs[terms:]
    q_ref, old_ref, top_ref, total_ref, fresh_hbm, context_hbm, wide, fresh_ref, context_ref, sems = refs
    rows, queries, size = q_ref.shape
    own = fresh_ref.shape[3]
    fresh = parts[0][...]
    for part in parts[1:]:
        fresh = fresh + part[...]
    for n in range(2 * own):
        wide[pl.ds(n, rows * steps, stride=2 * own), :] = fresh[:, n * size : (n + 1) * size]
    fresh_ref.reshape(rows * steps * 2 * own, size)[...] = wide[...].astype(jnp.bfloat16)
    puts = [pltpu.make_async_copy(fresh_ref, fresh_hbm, sems.at[0])]
    puts[0].start()
    keys, many = 2 * own * steps, 2 * queries
    key = lax.broadcasted_iota(jnp.int32, (keys, many), 0)
    query = lax.broadcasted_iota(jnp.int32, (keys, many), 1)
    same_head = (query % heads) // (heads // own) == key // (2 * steps)
    same_row = query // queries == (key // steps) % 2
    live = same_head & same_row & ((query % queries) // heads >= key % steps)
    nothing = jnp.zeros((keys, size), jnp.bfloat16)

    def new_lines(c, pair):
        tokens = slice(pair * 2 * steps, (pair + 1) * 2 * steps)
        lines = [fresh[tokens, (c * own + g) * size : (c * own + g + 1) * size] for g in range(own)]
        return jnp.concatenate(lines, axis=0).astype(jnp.bfloat16)

    for at in range(0, rows // 2, group):
        pairs = range(at, at + group)
        scores = [
            lax.dot_general(
                new_lines(0, p), q_ref[2 * p : 2 * p + 2].reshape(many, size), NT, preferred_element_type=jnp.float32
            )
            for p in pairs
        ]
        scores = jnp.stack([jnp.where(live, s, LOW) for s in scores])
        old_top = top_ref[at : at + group, :]
        top = jnp.maximum(old_top, jnp.max(scores, axis=1))
        expo = jnp.exp((scores - top[:, None, :]) * scale)
        back = jnp.exp((old_top - top) * scale)
        inverse = 1.0 / (back * total_ref[at : at + group, :] + jnp.sum(expo, axis=1))
        weights = (expo * inverse[:, None, :]).astype(jnp.bfloat16).reshape(group * keys, many)
        back = (back * inverse).T
        values = jnp.concatenate(
            [
                jnp.concatenate([new_lines(1, p) if n == p else nothing for n in pairs], axis=1)
                for p in pairs
            ],
            axis=0,
        )
        new = lax.dot_general(weights, values, TN, preferred_element_type=jnp.float32)
        for n, p in enumerate(pairs):
            old = old_ref[2 * p : 2 * p + 2].reshape(many, size)
            both = new[:, n * size : (n + 1) * size] + back[:, n : n + 1] * old
            context_ref[2 * p : 2 * p + 2] = both.astype(jnp.bfloat16).reshape(2, queries, size)
        mine = pl.ds(2 * at, 2 * group)
        puts.append(pltpu.make_async_copy(context_ref.at[mine], context_hbm.at[mine], sems.at[1 + at // group]))
        puts[-1].start()
    for put in puts:
        put.wait()


def finish(parts, queries, state, steps, own):
    rows, many, size = queries.shape
    heads = many // steps
    group = size // (2 * own * steps)
    fresh = (rows, steps, 2, own, size)
    fresh, context = pl.pallas_call(
        functools.partial(finish_kernel, steps, heads, size ** (-0.5), group, len(parts)),
        out_shape=(
            jax.ShapeDtypeStruct(fresh, jnp.bfloat16),
            jax.ShapeDtypeStruct((rows, many, size), jnp.bfloat16),
        ),
        in_specs=[VMEM] * (len(parts) + 1 + len(state)),
        out_specs=(pl.BlockSpec(memory_space=pltpu.HBM),) * 2,
        scratch_shapes=[
            pltpu.VMEM((rows * steps * 2 * own, size), jnp.float32),
            pltpu.VMEM(fresh, jnp.bfloat16),
            pltpu.VMEM((rows, many, size), jnp.bfloat16),
            pltpu.SemaphoreType.DMA((1 + rows // 2 // group,)),
        ],
        compiler_params=params(24),
        cost_estimate=cost(rows * many * size * size * 6, 8 * rows * many * size, rows * many * size * 2),
        name="finish",
    )(*parts, queries, *state)
    return fresh, context.reshape(rows, steps, heads, size)


def join_kernel(*refs):
    blocks, out_ref = refs[:-1], refs[-1]
    at = 0
    for block in blocks:
        out_ref[at : at + block.shape[0], :] = block[...]
        at += block.shape[0]


def join(blocks):
    rows = sum(b.shape[0] for b in blocks)
    return pl.pallas_call(
        join_kernel,
        out_shape=pltpu.VMEM((rows, blocks[0].shape[1]), jnp.bfloat16),
        in_specs=[VMEM] * len(blocks),
        out_specs=VMEM,
        compiler_params=params(8),
        name="join",
    )(*blocks)


def gather_second(factor_a, factor_b, dp):
    count = dp // 2
    ranks = factor_b.shape[0]
    if ranks % 8 == 0 and count in (1, 2, 4):
        payload = make_payload(factor_a.T, factor_b)
        return [payload] + [lax.ppermute(payload, "dp", [(i, i ^ (2 * k)) for i in range(dp)]) for k in range(1, count)]
    payload = jnp.concatenate([factor_a.T, factor_b.reshape(ranks, -1)], axis=1)
    groups = [[i for i in range(dp) if i % 2 == n] for n in range(2)]
    copies = jnp.broadcast_to(payload[None], (count,) + payload.shape)
    blocks = lax.all_to_all(copies, "dp", 0, 0, axis_index_groups=groups, tiled=True)
    return [blocks.reshape(count * ranks, payload.shape[1])]


def shards(dp, tp, hidden, base_weight, factor_a, factor_b, queries, cache, lengths):
    steps, own = queries.shape[1], cache.shape[3]
    assert dp % 2 == 0
    blocks = gather_second(factor_a, factor_b, dp)
    queries, *state = attend_cached(queries, cache, lengths)
    blocks, state, queries, hidden, base_weight = lax.optimization_barrier(
        (blocks, state, queries, hidden, base_weight)
    )
    gathered = join(blocks) if len(blocks) > 1 else blocks[0]
    gathered = [gathered, lax.ppermute(gathered, "dp", [(i, i ^ 1) for i in range(dp)])]
    tokens, base = arrange(hidden, base_weight, own)
    received = []
    for k in range(1, tp):
        other = project(k, tokens, base, gathered)
        received.append(lax.ppermute(other, "tp", [(i, i ^ k) for i in range(tp)]))
    mine = project(0, tokens, base, gathered)
    return finish([mine] + received, queries, state, steps, own)


def solution(mesh):
    return jax.shard_map(
        functools.partial(shards, mesh.shape["dp"], mesh.shape["tp"]),
        mesh=mesh,
        in_specs=(
            P(("parts", "dp"), None, "tp"),
            P("tp", None, None, None),
            P(("parts", "tp"), "dp"),
            P(("parts", "dp"), None, None, None),
            P(("parts", "dp"), None, "tp", None),
            P(("parts", "dp"), None, None, "tp", None),
            P(("parts", "dp")),
        ),
        out_specs=(
            P(("parts", "dp"), None, None, "tp", None),
            P(("parts", "dp"), None, "tp", None),
        ),
        check_vma=False,
    )
```

```python
import functools

import jax
import jax.numpy as jnp
from jax import lax
from jax.experimental import pallas as pl
from jax.experimental.pallas import tpu as pltpu
from jax.sharding import PartitionSpec as P

LOW = -1e30
NT = (((1,), (1,)), ((), ()))
TN = (((0,), (0,)), ((), ()))
VMEM = pl.BlockSpec(memory_space=pltpu.VMEM)


def params(mib):
    return pltpu.CompilerParams(vmem_limit_bytes=mib * 1024 * 1024)


def in_hbm(x):
    return pltpu.with_memory_space_constraint(x, pltpu.HBM)


def cost(flops, moved, exps=0):
    return pl.CostEstimate(flops=flops, bytes_accessed=moved, transcendentals=exps)


def payload_kernel(down_hbm, up_hbm, out_ref, ups, wide, sems):
    ranks, width = down_hbm.shape
    groups, size = ups.shape[1] * ups.shape[2], ups.shape[3]
    get_down = pltpu.make_async_copy(down_hbm, out_ref.at[:, pl.ds(0, width)], sems.at[0])
    get_up = pltpu.make_async_copy(up_hbm, ups, sems.at[1])
    get_up.start()
    get_down.start()
    get_up.wait()
    wide[...] = ups.reshape(ranks * groups, size)[...].astype(jnp.float32)
    for n in range(groups):
        out_ref[:, width + n * size : width + (n + 1) * size] = wide[pl.ds(n, ranks, stride=groups), :].astype(
            jnp.bfloat16
        )
    get_down.wait()


def make_payload(down, up):
    ranks, width = down.shape
    groups, size = up.shape[1] * up.shape[2], up.shape[3]
    return pl.pallas_call(
        payload_kernel,
        out_shape=pltpu.VMEM((ranks, width + groups * size), jnp.bfloat16),
        in_specs=[pl.BlockSpec(memory_space=pltpu.HBM)] * 2,
        out_specs=VMEM,
        scratch_shapes=[
            pltpu.VMEM(up.shape, jnp.bfloat16),
            pltpu.VMEM((ranks * groups, size), jnp.float32),
            pltpu.SemaphoreType.DMA((2,)),
        ],
        compiler_params=params(8),
        name="payload",
    )(in_hbm(down), in_hbm(up))


def cached_kernel(chunks, heads, scale, *refs):
    lengths_hbm, queries_hbm, cache_hbm, q_all, sum_ref, top_ref, total_ref = refs[:7]
    lengths_ref, raw, k_all, v_all = refs[7:11]
    scores_refs, weights_refs = refs[11:13], refs[13:15]
    sems, length_sem = refs[15:]
    rows, queries, size = q_all.shape
    slots, own = k_all.shape[1:3]
    keys = slots * own
    some = rows // chunks

    def copies(i):
        mine = pl.ds(i * some, some)
        pairs = ((cache_hbm.at[mine], raw.at[mine]), (queries_hbm.at[mine], q_all.at[mine]))
        return [pltpu.make_async_copy(a, b, sems.at[i, n]) for n, (a, b) in enumerate(pairs)]

    def splits(i):
        mine = pl.ds(i * some, some)
        pairs = ((raw.at[mine, :, 0], k_all.at[mine]), (raw.at[mine, :, 1], v_all.at[mine]))
        return [pltpu.make_async_copy(a, b, sems.at[i, 2 + n]) for n, (a, b) in enumerate(pairs)]

    get_lengths = pltpu.make_async_copy(lengths_hbm, lengths_ref, length_sem)
    get_lengths.start()
    for i in range(chunks):
        for copy in copies(i):
            copy.start()

    line = lax.broadcasted_iota(jnp.int32, (keys, 2 * queries), 0)
    query = lax.broadcasted_iota(jnp.int32, (keys, 2 * queries), 1)
    line = jnp.where(line % own == (query % heads) // (heads // own), line, keys)
    first = lax.broadcasted_iota(jnp.int32, (1, 2 * queries), 1) < queries
    nothing = jnp.zeros((queries, size), jnp.bfloat16)
    flat_k = k_all.reshape(rows, keys, size)
    flat_v = v_all.reshape(rows, keys, size)

    def part_chunk(i):
        for copy in copies(i):
            copy.wait()
        for split in splits(i):
            split.start()

    def await_chunk(i):
        for split in splits(i):
            split.wait()

    def score(i, slot):
        for p in range(some // 2):
            r = i * some + 2 * p
            both_q = jnp.concatenate(
                [
                    jnp.concatenate([q_all[r], nothing], axis=1),
                    jnp.concatenate([nothing, q_all[r + 1]], axis=1),
                ],
                axis=0,
            )
            both_k = jnp.concatenate([flat_k[r], flat_k[r + 1]], axis=1)
            scores_refs[slot][p] = lax.dot_general(both_k, both_q, NT, preferred_element_type=jnp.float32)

    def soften(i, slot):
        for p in range(some // 2):
            r = i * some + 2 * p
            limit = jnp.where(first, own * lengths_ref[r], own * lengths_ref[r + 1])
            scores = jnp.where(line < limit, scores_refs[slot][p], LOW)
            top = jnp.max(scores, axis=0, keepdims=True)
            expo = jnp.exp((scores - top) * scale)
            weights_refs[slot][p] = expo.astype(jnp.bfloat16)
            pair = pl.ds(i * (some // 2) + p, 1)
            top_ref[pair, :] = top
            total_ref[pair, :] = jnp.sum(expo, axis=0, keepdims=True)

    def collect(i, slot):
        for p in range(some // 2):
            r = i * some + 2 * p
            both_v = jnp.concatenate([flat_v[r], flat_v[r + 1]], axis=1)
            both = lax.dot_general(weights_refs[slot][p], both_v, TN, preferred_element_type=jnp.float32)
            for h in range(2):
                sum_ref[r + h] = both[h * queries : (h + 1) * queries, h * size : (h + 1) * size]

    get_lengths.wait()
    part_chunk(0)
    part_chunk(1)
    await_chunk(0)
    score(0, 0)
    part_chunk(2)
    await_chunk(1)
    score(1, 1)
    soften(0, 0)

    @pl.loop(1, chunks // 2)
    def _(t):
        for slot in range(2):
            i = 2 * t + slot

            @pl.when(i + 1 < chunks)
            def _():
                part_chunk(i + 1)

            await_chunk(i)
            score(i, slot)
            soften(i - 1, 1 - slot)
            collect(i - 2, slot)

    soften(chunks - 1, 1)
    collect(chunks - 2, 0)
    collect(chunks - 1, 1)


def attend_cached(queries, cache, lengths):
    rows, steps, heads, size = queries.shape
    slots, own = cache.shape[1], cache.shape[3]
    many = steps * heads
    chunks = 8
    pairs = rows // chunks // 2
    keys = slots * own
    state = (rows, many, size)
    half = (rows, slots, own, size)
    return pl.pallas_call(
        functools.partial(cached_kernel, chunks, heads, size ** (-0.5)),
        out_shape=(
            pltpu.VMEM(state, jnp.bfloat16),
            pltpu.VMEM(state, jnp.float32),
            pltpu.VMEM((rows // 2, 2 * many), jnp.float32),
            pltpu.VMEM((rows // 2, 2 * many), jnp.float32),
        ),
        in_specs=[pl.BlockSpec(memory_space=pltpu.HBM)] * 3,
        out_specs=(VMEM,) * 4,
        scratch_shapes=[
            pltpu.SMEM(lengths.shape, jnp.int32),
            pltpu.VMEM(cache.shape, jnp.bfloat16),
            pltpu.VMEM(half, jnp.bfloat16),
            pltpu.VMEM(half, jnp.bfloat16),
            pltpu.VMEM((pairs, keys, 2 * many), jnp.float32),
            pltpu.VMEM((pairs, keys, 2 * many), jnp.float32),
            pltpu.VMEM((pairs, keys, 2 * many), jnp.bfloat16),
            pltpu.VMEM((pairs, keys, 2 * many), jnp.bfloat16),
            pltpu.SemaphoreType.DMA((chunks, 4)),
            pltpu.SemaphoreType.DMA,
        ],
        compiler_params=params(28),
        cost_estimate=cost(
            8 * rows * many * slots * size, 2 * (cache.size + queries.size) + 4 * rows * many * size, rows * many * keys
        ),
        name="attend_cached",
    )(*map(in_hbm, (lengths, queries.reshape(rows, many, size), cache)))


def arrange_kernel(chunks, own, hidden_hbm, base_hbm, tokens_ref, base_ref, hidden, base, sems):
    width, two, kvh, size = base.shape
    groups = two * kvh
    some_width = width // chunks

    def copy(i):
        features = pl.ds(i * some_width, some_width)
        return pltpu.make_async_copy(base_hbm.at[features], base.at[features], sems.at[i])

    get_hidden = pltpu.make_async_copy(hidden_hbm, hidden, sems.at[chunks])
    for i in range(chunks):
        copy(i).start()
    get_hidden.start()

    tile = 256
    some = tile // groups
    row = lax.broadcasted_iota(jnp.int32, (tile, tile), 0)
    place = lax.broadcasted_iota(jnp.int32, (tile, tile), 1)
    order = (place == (row % some) * groups + row // some).astype(jnp.float32).astype(jnp.bfloat16)
    flat_base = base.reshape(width * groups, size)

    def arrange(f):
        at = pl.multiple_of(f * groups, tile)
        pair = jnp.concatenate([flat_base[pl.ds(at + h * tile, tile), :] for h in range(2)], axis=1)
        moved = jnp.dot(order, pair, preferred_element_type=jnp.float32).astype(jnp.bfloat16)
        for n in range(groups):
            lanes = slice((n % own) * size, (n % own + 1) * size)
            for h in range(2):
                base_ref[n // own, pl.ds(pl.multiple_of(f + h * some, some), some), lanes] = moved[
                    n * some : (n + 1) * some, h * size : (h + 1) * size
                ]

    @pl.loop(0, chunks)
    def _(i):
        copy(i).wait()
        for f in range(0, some_width, 2 * some):
            arrange(i * some_width + f)

    get_hidden.wait()
    tokens_ref[...] = hidden.reshape(tokens_ref.shape)[...]


def arrange(hidden, base, own):
    rows, steps, _ = hidden.shape
    width, two, kvh, size = base.shape
    chunks = 4
    return pl.pallas_call(
        functools.partial(arrange_kernel, chunks, own),
        out_shape=(
            pltpu.VMEM((rows * steps, width), jnp.bfloat16),
            pltpu.VMEM((two * kvh // own, width, own * size), jnp.bfloat16),
        ),
        in_specs=[pl.BlockSpec(memory_space=pltpu.HBM)] * 2,
        out_specs=(VMEM, VMEM),
        scratch_shapes=[
            pltpu.VMEM(hidden.shape, jnp.bfloat16),
            pltpu.VMEM(base.shape, jnp.bfloat16),
            pltpu.SemaphoreType.DMA((chunks + 1,)),
        ],
        compiler_params=params(20),
        cost_estimate=cost(512 * base.size, 4 * (base.size + hidden.size)),
        name="arrange",
    )(in_hbm(hidden), in_hbm(base))


def project_kernel(k, hidden_ref, base_ref, *refs):
    gathered, (out_ref, merged) = refs[:-2], refs[-2:]
    width, columns = merged.shape
    part = lax.axis_index("tp") ^ k
    parts = base_ref.shape[0] // 2
    half = columns // 2
    up = jnp.concatenate(
        [
            jnp.concatenate(
                [ref[:, pl.ds(pl.multiple_of(width + (c * parts + part) * half, 128), half)] for ref in gathered], axis=0
            )
            for c in range(2)
        ],
        axis=1,
    )
    step = 512
    for f in range(0, width, step):
        down = jnp.concatenate([ref[:, f : f + step] for ref in gathered], axis=0).T
        low_rank = jnp.dot(down, up, preferred_element_type=jnp.float32)
        for c in range(2):
            base = base_ref[c * parts + part, f : f + step, :].astype(jnp.float32)
            merged[f : f + step, c * half : (c + 1) * half] = (base + low_rank[:, c * half : (c + 1) * half]).astype(
                jnp.bfloat16
            )
    out_ref[...] = jnp.dot(hidden_ref[...], merged[...], preferred_element_type=jnp.float32)


def project(k, hidden, base, gathered):
    tokens, width = hidden.shape
    columns = 2 * base.shape[2]
    ranks = sum(g.shape[0] for g in gathered)
    return pl.pallas_call(
        functools.partial(project_kernel, k),
        out_shape=pltpu.VMEM((tokens, columns), jnp.float32),
        in_specs=[VMEM] * (2 + len(gathered)),
        out_specs=VMEM,
        scratch_shapes=[pltpu.VMEM((width, columns), jnp.bfloat16)],
        compiler_params=params(24),
        cost_estimate=cost(2 * width * columns * (tokens + ranks), 2 * width * columns + 2 * width * tokens),
        name="project",
    )(hidden, base, *gathered)


def finish_kernel(steps, heads, scale, group, terms, *refs):
    parts, refs = refs[:terms], refs[terms:]
    q_ref, old_ref, top_ref, total_ref, fresh_hbm, context_hbm, wide, fresh_ref, context_ref, sems = refs
    rows, queries, size = q_ref.shape
    own = fresh_ref.shape[3]
    fresh = parts[0][...]
    for part in parts[1:]:
        fresh = fresh + part[...]
    for n in range(2 * own):
        wide[pl.ds(n, rows * steps, stride=2 * own), :] = fresh[:, n * size : (n + 1) * size]
    fresh_ref.reshape(rows * steps * 2 * own, size)[...] = wide[...].astype(jnp.bfloat16)
    puts = [pltpu.make_async_copy(fresh_ref, fresh_hbm, sems.at[0])]
    puts[0].start()
    keys, many = 2 * own * steps, 2 * queries
    key = lax.broadcasted_iota(jnp.int32, (keys, many), 0)
    query = lax.broadcasted_iota(jnp.int32, (keys, many), 1)
    same_head = (query % heads) // (heads // own) == key // (2 * steps)
    same_row = query // queries == (key // steps) % 2
    live = same_head & same_row & ((query % queries) // heads >= key % steps)
    nothing = jnp.zeros((keys, size), jnp.bfloat16)

    def new_lines(c, pair):
        tokens = slice(pair * 2 * steps, (pair + 1) * 2 * steps)
        lines = [fresh[tokens, (c * own + g) * size : (c * own + g + 1) * size] for g in range(own)]
        return jnp.concatenate(lines, axis=0).astype(jnp.bfloat16)

    for at in range(0, rows // 2, group):
        pairs = range(at, at + group)
        scores = [
            lax.dot_general(
                new_lines(0, p), q_ref[2 * p : 2 * p + 2].reshape(many, size), NT, preferred_element_type=jnp.float32
            )
            for p in pairs
        ]
        scores = jnp.stack([jnp.where(live, s, LOW) for s in scores])
        old_top = top_ref[at : at + group, :]
        top = jnp.maximum(old_top, jnp.max(scores, axis=1))
        expo = jnp.exp((scores - top[:, None, :]) * scale)
        back = jnp.exp((old_top - top) * scale)
        inverse = 1.0 / (back * total_ref[at : at + group, :] + jnp.sum(expo, axis=1))
        weights = (expo * inverse[:, None, :]).astype(jnp.bfloat16).reshape(group * keys, many)
        back = (back * inverse).T
        values = jnp.concatenate(
            [
                jnp.concatenate([new_lines(1, p) if n == p else nothing for n in pairs], axis=1)
                for p in pairs
            ],
            axis=0,
        )
        new = lax.dot_general(weights, values, TN, preferred_element_type=jnp.float32)
        for n, p in enumerate(pairs):
            old = old_ref[2 * p : 2 * p + 2].reshape(many, size)
            both = new[:, n * size : (n + 1) * size] + back[:, n : n + 1] * old
            context_ref[2 * p : 2 * p + 2] = both.astype(jnp.bfloat16).reshape(2, queries, size)
        mine = pl.ds(2 * at, 2 * group)
        puts.append(pltpu.make_async_copy(context_ref.at[mine], context_hbm.at[mine], sems.at[1 + at // group]))
        puts[-1].start()
    for put in puts:
        put.wait()


def finish(parts, queries, state, steps, own):
    rows, many, size = queries.shape
    heads = many // steps
    group = size // (2 * own * steps)
    fresh = (rows, steps, 2, own, size)
    fresh, context = pl.pallas_call(
        functools.partial(finish_kernel, steps, heads, size ** (-0.5), group, len(parts)),
        out_shape=(
            jax.ShapeDtypeStruct(fresh, jnp.bfloat16),
            jax.ShapeDtypeStruct((rows, many, size), jnp.bfloat16),
        ),
        in_specs=[VMEM] * (len(parts) + 1 + len(state)),
        out_specs=(pl.BlockSpec(memory_space=pltpu.HBM),) * 2,
        scratch_shapes=[
            pltpu.VMEM((rows * steps * 2 * own, size), jnp.float32),
            pltpu.VMEM(fresh, jnp.bfloat16),
            pltpu.VMEM((rows, many, size), jnp.bfloat16),
            pltpu.SemaphoreType.DMA((1 + rows // 2 // group,)),
        ],
        compiler_params=params(24),
        cost_estimate=cost(rows * many * size * size * 6, 8 * rows * many * size, rows * many * size * 2),
        name="finish",
    )(*parts, queries, *state)
    return fresh, context.reshape(rows, steps, heads, size)


def join_kernel(counts, *refs):
    blocks, outs = refs[: sum(counts)], refs[sum(counts) :]
    first = 0
    for count, out_ref in zip(counts, outs):
        at = 0
        for block in blocks[first : first + count]:
            out_ref[at : at + block.shape[0], :] = block[...]
            at += block.shape[0]
        first += count


def join(*lists):
    blocks = [block for blocks in lists for block in blocks]
    rows = [sum(b.shape[0] for b in blocks) for blocks in lists]
    return pl.pallas_call(
        functools.partial(join_kernel, [len(blocks) for blocks in lists]),
        out_shape=[pltpu.VMEM((n, blocks[0].shape[1]), jnp.bfloat16) for n in rows],
        in_specs=[VMEM] * len(blocks),
        out_specs=[VMEM] * len(lists),
        compiler_params=params(8),
        name="join",
    )(*blocks)


def shards(dp, tp, hidden, base_weight, factor_a, factor_b, queries, cache, lengths):
    steps, own = queries.shape[1], cache.shape[3]
    ranks = factor_b.shape[0]

    def swap(x, k):
        return lax.ppermute(x, "dp", [(i, i ^ k) for i in range(dp)])

    def local(operands):
        done, *state = attend_cached(queries, cache, lengths)
        return lax.optimization_barrier((operands, done, state, hidden, base_weight))

    if dp == 8 and ranks % 8 == 0:
        payload = make_payload(factor_a.T, factor_b)
        blocks = {k: swap(payload, k) for k in (6, 4, 2, 3, 1)}
        blocks, rotated, state, hidden, base_weight = local(blocks)
        rest, gathered = join([blocks[4], blocks[6]], [payload] + [blocks[k] for k in (1, 2, 3, 4, 6)])
        gathered = [gathered, swap(rest, 1)]
    else:
        payload = jnp.concatenate([factor_a.T, factor_b.reshape(ranks, -1)], axis=1)
        copies = jnp.broadcast_to(payload[None], (dp,) + payload.shape)
        blocks = lax.all_to_all(copies, "dp", 0, 0, tiled=True)
        gathered = [blocks.reshape(dp * ranks, payload.shape[1])]
        gathered, rotated, state, hidden, base_weight = local(gathered)
    tokens, base = arrange(hidden, base_weight, own)
    received = []
    for k in range(1, tp):
        other = project(k, tokens, base, gathered)
        received.append(lax.ppermute(other, "tp", [(i, i ^ k) for i in range(tp)]))
    mine = project(0, tokens, base, gathered)
    return finish([mine] + received, rotated, state, steps, own)


def solution(mesh):
    return jax.shard_map(
        functools.partial(shards, mesh.shape["dp"], mesh.shape["tp"]),
        mesh=mesh,
        in_specs=(
            P(("parts", "dp"), None, "tp"),
            P("tp", None, None, None),
            P(("parts", "tp"), "dp"),
            P(("parts", "dp"), None, None, None),
            P(("parts", "dp"), None, "tp", None),
            P(("parts", "dp"), None, None, "tp", None),
            P(("parts", "dp")),
        ),
        out_specs=(
            P(("parts", "dp"), None, None, "tp", None),
            P(("parts", "dp"), None, "tp", None),
        ),
        check_vma=False,
    )
```

```python
import functools

import jax
import jax.numpy as jnp
from jax import lax
from jax.experimental import pallas as pl
from jax.experimental.pallas import tpu as pltpu
from jax.sharding import PartitionSpec as P

LOW = -1e30
NT = (((1,), (1,)), ((), ()))
TN = (((0,), (0,)), ((), ()))
VMEM = pl.BlockSpec(memory_space=pltpu.VMEM)


def params(mib):
    return pltpu.CompilerParams(vmem_limit_bytes=mib * 1024 * 1024)


def in_hbm(x):
    return pltpu.with_memory_space_constraint(x, pltpu.HBM)


def cost(flops, moved, exps=0):
    return pl.CostEstimate(flops=flops, bytes_accessed=moved, transcendentals=exps)


def payload_kernel(down_hbm, up_hbm, out_ref, ups, wide, sems):
    ranks, width = down_hbm.shape
    groups, size = ups.shape[1] * ups.shape[2], ups.shape[3]
    get_down = pltpu.make_async_copy(down_hbm, out_ref.at[:, pl.ds(0, width)], sems.at[0])
    get_up = pltpu.make_async_copy(up_hbm, ups, sems.at[1])
    get_up.start()
    get_down.start()
    get_up.wait()
    wide[...] = ups.reshape(ranks * groups, size)[...].astype(jnp.float32)
    for n in range(groups):
        out_ref[:, width + n * size : width + (n + 1) * size] = wide[pl.ds(n, ranks, stride=groups), :].astype(
            jnp.bfloat16
        )
    get_down.wait()


def make_payload(down, up):
    ranks, width = down.shape
    groups, size = up.shape[1] * up.shape[2], up.shape[3]
    return pl.pallas_call(
        payload_kernel,
        out_shape=pltpu.VMEM((ranks, width + groups * size), jnp.bfloat16),
        in_specs=[pl.BlockSpec(memory_space=pltpu.HBM)] * 2,
        out_specs=VMEM,
        scratch_shapes=[
            pltpu.VMEM(up.shape, jnp.bfloat16),
            pltpu.VMEM((ranks * groups, size), jnp.float32),
            pltpu.SemaphoreType.DMA((2,)),
        ],
        compiler_params=params(8),
        name="payload",
    )(in_hbm(down), in_hbm(up))


class Cached:
    def __init__(self, first, chunk, heads, scale, inputs, outputs, scratch):
        self.first, self.chunk, self.heads, self.scale = first, chunk, heads, scale
        self.lengths_hbm, self.queries_hbm, self.cache_hbm = inputs
        self.q, self.sums, self.tops, self.totals = outputs
        self.lengths, self.k, self.v, *rest = scratch
        self.scores, self.weights = rest[0:2], rest[2:4]
        self.sems, self.length_sem = rest[4:]
        self.rows, self.queries, self.size = self.q.shape
        self.slots, self.own = self.k.shape[1:3]
        self.keys = self.slots * self.own
        own, queries = self.own, self.queries
        line = lax.broadcasted_iota(jnp.int32, (self.keys, 2 * queries), 0)
        query = lax.broadcasted_iota(jnp.int32, (self.keys, 2 * queries), 1)
        self.line = jnp.where(line % own == (query % heads) // (heads // own), line, self.keys)
        self.one = lax.broadcasted_iota(jnp.int32, (1, 2 * queries), 1) < queries
        self.nothing = jnp.zeros((queries, self.size), jnp.bfloat16)

    @staticmethod
    def outputs(rows, many, size):
        return (
            pltpu.VMEM((rows, many, size), jnp.bfloat16),
            pltpu.VMEM((rows, many, size), jnp.float32),
            pltpu.VMEM((rows // 2, 2 * many), jnp.float32),
            pltpu.VMEM((rows // 2, 2 * many), jnp.float32),
        )

    @staticmethod
    def scratch(rows, chunk, many, cache, lengths):
        slots, own, size = cache.shape[1], cache.shape[3], cache.shape[4]
        half = (rows, slots, own, size)
        scores = (chunk // 2, slots * own, 2 * many)
        return [
            pltpu.SMEM(lengths.shape, jnp.int32),
            pltpu.VMEM(half, jnp.bfloat16),
            pltpu.VMEM(half, jnp.bfloat16),
            pltpu.VMEM(scores, jnp.float32),
            pltpu.VMEM(scores, jnp.float32),
            pltpu.VMEM(scores, jnp.bfloat16),
            pltpu.VMEM(scores, jnp.bfloat16),
            pltpu.SemaphoreType.DMA((rows // chunk, 3)),
            pltpu.SemaphoreType.DMA,
        ]

    def copies(self, i):
        mine, theirs = pl.ds(i * self.chunk, self.chunk), pl.ds(self.first + i * self.chunk, self.chunk)
        pairs = (
            (self.queries_hbm.at[theirs], self.q.at[mine]),
            (self.cache_hbm.at[theirs, :, 0], self.k.at[mine]),
            (self.cache_hbm.at[theirs, :, 1], self.v.at[mine]),
        )
        return [pltpu.make_async_copy(a, b, self.sems.at[i, n]) for n, (a, b) in enumerate(pairs)]

    def lengths_copy(self):
        return pltpu.make_async_copy(self.lengths_hbm, self.lengths, self.length_sem)

    def start(self, i):
        for copy in self.copies(i):
            copy.start()

    def arrive(self, i):
        for copy in self.copies(i):
            copy.wait()

    def lines(self, ref, r):
        flat = ref.reshape(self.rows, self.keys, self.size)
        return jnp.concatenate([flat[r], flat[r + 1]], axis=1)

    def score(self, i, slot):
        for p in range(self.chunk // 2):
            r = i * self.chunk + 2 * p
            both_q = jnp.concatenate(
                [
                    jnp.concatenate([self.q[r], self.nothing], axis=1),
                    jnp.concatenate([self.nothing, self.q[r + 1]], axis=1),
                ],
                axis=0,
            )
            self.scores[slot][p] = lax.dot_general(
                self.lines(self.k, r), both_q, NT, preferred_element_type=jnp.float32
            )

    def soften(self, i, slot):
        for p in range(self.chunk // 2):
            r = self.first + i * self.chunk + 2 * p
            limit = jnp.where(self.one, self.own * self.lengths[r], self.own * self.lengths[r + 1])
            scores = jnp.where(self.line < limit, self.scores[slot][p], LOW)
            top = jnp.max(scores, axis=0, keepdims=True)
            expo = jnp.exp((scores - top) * self.scale)
            self.weights[slot][p] = expo.astype(jnp.bfloat16)
            pair = pl.ds(i * (self.chunk // 2) + p, 1)
            self.tops[pair, :] = top
            self.totals[pair, :] = jnp.sum(expo, axis=0, keepdims=True)

    def collect(self, i, slot):
        queries, size = self.queries, self.size
        for p in range(self.chunk // 2):
            r = i * self.chunk + 2 * p
            both = lax.dot_general(
                self.weights[slot][p], self.lines(self.v, r), TN, preferred_element_type=jnp.float32
            )
            for h in range(2):
                self.sums[r + h] = both[h * queries : (h + 1) * queries, h * size : (h + 1) * size]


def cached_kernel(chunk, heads, scale, *refs):
    cached = Cached(0, chunk, heads, scale, refs[:3], refs[3:7], refs[7:])
    chunks = cached.rows // chunk
    cached.lengths_copy().start()
    for i in range(chunks):
        cached.start(i)
    cached.lengths_copy().wait()
    cached.arrive(0)
    cached.score(0, 0)
    cached.arrive(1)
    cached.score(1, 1)
    cached.soften(0, 0)

    @pl.loop(1, chunks // 2)
    def _(t):
        for slot in range(2):
            i = 2 * t + slot
            cached.arrive(i)
            cached.score(i, slot)
            cached.soften(i - 1, 1 - slot)
            cached.collect(i - 2, slot)

    cached.soften(chunks - 1, 1)
    cached.collect(chunks - 2, 0)
    cached.collect(chunks - 1, 1)


def attend_cached(queries, cache, lengths, rows):
    _, steps, heads, size = queries.shape
    slots, own = cache.shape[1], cache.shape[3]
    many = steps * heads
    chunk = 4
    return pl.pallas_call(
        functools.partial(cached_kernel, chunk, heads, size ** (-0.5)),
        out_shape=Cached.outputs(rows, many, size),
        in_specs=[pl.BlockSpec(memory_space=pltpu.HBM)] * 3,
        out_specs=(VMEM,) * 4,
        scratch_shapes=Cached.scratch(rows, chunk, many, cache, lengths),
        compiler_params=params(28),
        cost_estimate=cost(
            8 * rows * many * slots * size, 4 * rows * slots * own * size, rows * many * slots * own
        ),
        name="attend_cached",
    )(*map(in_hbm, (lengths, queries.reshape(-1, many, size), cache)))


def arrange_kernel(first, chunk, chunks, own, heads, scale, *refs):
    hidden_hbm, base_hbm = refs[:2]
    tokens_ref, base_ref = refs[5:7]
    hidden, base, sems = refs[11:14]
    cached = Cached(first, chunk, heads, scale, refs[2:5], refs[7:11], refs[14:])
    width, two, kvh, size = base.shape
    groups = two * kvh
    some_width = width // chunks

    def copy(i):
        features = pl.ds(i * some_width, some_width)
        return pltpu.make_async_copy(base_hbm.at[features], base.at[features], sems.at[i])

    get_hidden = pltpu.make_async_copy(hidden_hbm, hidden, sems.at[chunks])
    cached.lengths_copy().start()
    copy(0).start()
    cached.start(0)
    copy(1).start()
    cached.start(1)
    for i in range(2, chunks):
        copy(i).start()
    get_hidden.start()

    tile = 256
    some = tile // groups
    row = lax.broadcasted_iota(jnp.int32, (tile, tile), 0)
    place = lax.broadcasted_iota(jnp.int32, (tile, tile), 1)
    order = (place == (row % some) * groups + row // some).astype(jnp.float32).astype(jnp.bfloat16)
    flat_base = base.reshape(width * groups, size)

    def arrange(f):
        at = f * groups
        pair = jnp.concatenate([flat_base[at + h * tile : at + (h + 1) * tile, :] for h in range(2)], axis=1)
        moved = jnp.dot(order, pair, preferred_element_type=jnp.float32).astype(jnp.bfloat16)
        for n in range(groups):
            lanes = slice((n % own) * size, (n % own + 1) * size)
            for h in range(2):
                base_ref[n // own, f + h * some : f + (h + 1) * some, lanes] = moved[
                    n * some : (n + 1) * some, h * size : (h + 1) * size
                ]

    cached.lengths_copy().wait()
    for i in range(chunks):
        copy(i).wait()
        if i < 2:
            cached.arrive(i)
            cached.score(i, i)
        if 1 <= i < 3:
            cached.soften(i - 1, i - 1)
        if 2 <= i < 4:
            cached.collect(i - 2, i - 2)
        for f in range(i * some_width, (i + 1) * some_width, 2 * some):
            arrange(f)
    get_hidden.wait()
    tokens_ref[...] = hidden.reshape(tokens_ref.shape)[...]


def arrange(hidden, base, queries, cache, lengths, rows):
    _, steps, heads, size = queries.shape
    slots, own = cache.shape[1], cache.shape[3]
    many = steps * heads
    width, two, kvh, size = base.shape
    chunks = 4
    rest = hidden.shape[0] - rows
    chunk = rest // 2
    outs = (
        pltpu.VMEM((hidden.shape[0] * steps, width), jnp.bfloat16),
        pltpu.VMEM((two * kvh // own, width, own * size), jnp.bfloat16),
    ) + Cached.outputs(rest, many, size)
    tokens, base, *state = pl.pallas_call(
        functools.partial(arrange_kernel, rows, chunk, chunks, own, heads, size ** (-0.5)),
        out_shape=outs,
        in_specs=[pl.BlockSpec(memory_space=pltpu.HBM)] * 5,
        out_specs=(VMEM,) * len(outs),
        scratch_shapes=[
            pltpu.VMEM(hidden.shape, jnp.bfloat16),
            pltpu.VMEM(base.shape, jnp.bfloat16),
            pltpu.SemaphoreType.DMA((chunks + 1,)),
        ]
        + Cached.scratch(rest, chunk, many, cache, lengths),
        compiler_params=params(28),
        cost_estimate=cost(
            512 * base.size + 8 * rest * many * slots * size,
            4 * (base.size + hidden.size + rest * slots * own * size),
            rest * many * slots * own,
        ),
        name="arrange",
    )(*map(in_hbm, (hidden, base, lengths, queries.reshape(-1, many, size), cache)))
    return tokens, base, state


def project_kernel(k, hidden_ref, base_ref, *refs):
    gathered, (out_ref, merged) = refs[:-2], refs[-2:]
    width, columns = merged.shape
    part = lax.axis_index("tp") ^ k
    parts = base_ref.shape[0] // 2
    half = columns // 2
    up = jnp.concatenate(
        [
            jnp.concatenate(
                [ref[:, pl.ds(pl.multiple_of(width + (c * parts + part) * half, 128), half)] for ref in gathered], axis=0
            )
            for c in range(2)
        ],
        axis=1,
    )
    step = 512
    for f in range(0, width, step):
        down = jnp.concatenate([ref[:, f : f + step] for ref in gathered], axis=0).T
        low_rank = jnp.dot(down, up, preferred_element_type=jnp.float32)
        for c in range(2):
            base = base_ref[c * parts + part, f : f + step, :].astype(jnp.float32)
            merged[f : f + step, c * half : (c + 1) * half] = (base + low_rank[:, c * half : (c + 1) * half]).astype(
                jnp.bfloat16
            )
    out_ref[...] = jnp.dot(hidden_ref[...], merged[...], preferred_element_type=jnp.float32)


def project(k, hidden, base, gathered):
    tokens, width = hidden.shape
    columns = 2 * base.shape[2]
    ranks = sum(g.shape[0] for g in gathered)
    return pl.pallas_call(
        functools.partial(project_kernel, k),
        out_shape=pltpu.VMEM((tokens, columns), jnp.float32),
        in_specs=[VMEM] * (2 + len(gathered)),
        out_specs=VMEM,
        scratch_shapes=[pltpu.VMEM((width, columns), jnp.bfloat16)],
        compiler_params=params(24),
        cost_estimate=cost(2 * width * columns * (tokens + ranks), 2 * width * columns + 2 * width * tokens),
        name="project",
    )(hidden, base, *gathered)


def finish_kernel(steps, heads, scale, terms, *refs):
    parts, refs = refs[:terms], refs[terms:]
    states, refs = (refs[:4], refs[4:8]), refs[8:]
    fresh_hbm, context_hbm, wide, fresh_ref, context_ref, sems = refs
    rows, queries, size = context_ref.shape
    own = fresh_ref.shape[3]
    fresh = parts[0][...]
    for part in parts[1:]:
        fresh = fresh + part[...]
    keys, many = 2 * own * steps, 2 * queries
    group = size // keys
    key = lax.broadcasted_iota(jnp.int32, (keys, many), 0)
    query = lax.broadcasted_iota(jnp.int32, (keys, many), 1)
    same_head = (query % heads) // (heads // own) == key // (2 * steps)
    same_row = query // queries == (key // steps) % 2
    live = same_head & same_row & ((query % queries) // heads >= key % steps)
    nothing = jnp.zeros((keys, size), jnp.bfloat16)

    def new_lines(c, pair):
        tokens = slice(pair * 2 * steps, (pair + 1) * 2 * steps)
        lines = [fresh[tokens, (c * own + g) * size : (c * own + g + 1) * size] for g in range(own)]
        return jnp.concatenate(lines, axis=0).astype(jnp.bfloat16)

    def old(n, pair):
        count = states[0][0].shape[0] // 2
        return (states[0][n], pair) if pair < count else (states[1][n], pair - count)

    def rows_of(n, pair):
        ref, at = old(n, pair)
        return ref[2 * at : 2 * at + 2].reshape(many, size)

    scores = [
        lax.dot_general(new_lines(0, p), rows_of(0, p), NT, preferred_element_type=jnp.float32)
        for p in range(rows // 2)
    ]
    scores = jnp.stack([jnp.where(live, s, LOW) for s in scores])
    old_top, old_total = [jnp.concatenate([states[0][n][...], states[1][n][...]], axis=0) for n in (2, 3)]
    top = jnp.maximum(old_top, jnp.max(scores, axis=1))
    expo = jnp.exp((scores - top[:, None, :]) * scale)
    back = jnp.exp((old_top - top) * scale)
    inverse = 1.0 / (back * old_total + jnp.sum(expo, axis=1))
    weights = (expo * inverse[:, None, :]).astype(jnp.bfloat16)
    back = back * inverse

    for n in range(2 * own):
        wide[pl.ds(n, rows * steps, stride=2 * own), :] = fresh[:, n * size : (n + 1) * size]
    fresh_ref.reshape(rows * steps * 2 * own, size)[...] = wide[...].astype(jnp.bfloat16)
    puts = [pltpu.make_async_copy(fresh_ref, fresh_hbm, sems.at[0])]
    puts[0].start()

    for at in range(0, rows // 2, group):
        pairs = range(at, at + group)
        values = jnp.concatenate(
            [
                jnp.concatenate([new_lines(1, p) if n == p else nothing for n in pairs], axis=1)
                for p in pairs
            ],
            axis=0,
        )
        new = lax.dot_general(
            weights[at : at + group].reshape(group * keys, many), values, TN, preferred_element_type=jnp.float32
        )
        factors = back[at : at + group].T
        for n, p in enumerate(pairs):
            both = new[:, n * size : (n + 1) * size] + factors[:, n : n + 1] * rows_of(1, p)
            context_ref[2 * p : 2 * p + 2] = both.astype(jnp.bfloat16).reshape(2, queries, size)
        mine = pl.ds(2 * at, 2 * group)
        puts.append(pltpu.make_async_copy(context_ref.at[mine], context_hbm.at[mine], sems.at[1 + at // group]))
        puts[-1].start()
    for put in puts:
        put.wait()


def finish(parts, states, steps, own):
    _, many, size = states[0][0].shape
    rows = sum(state[0].shape[0] for state in states)
    heads = many // steps
    groups = rows * own * steps // size
    fresh = (rows, steps, 2, own, size)
    fresh, context = pl.pallas_call(
        functools.partial(finish_kernel, steps, heads, size ** (-0.5), len(parts)),
        out_shape=(
            jax.ShapeDtypeStruct(fresh, jnp.bfloat16),
            jax.ShapeDtypeStruct((rows, many, size), jnp.bfloat16),
        ),
        in_specs=[VMEM] * (len(parts) + 8),
        out_specs=(pl.BlockSpec(memory_space=pltpu.HBM),) * 2,
        scratch_shapes=[
            pltpu.VMEM((rows * steps * 2 * own, size), jnp.float32),
            pltpu.VMEM(fresh, jnp.bfloat16),
            pltpu.VMEM((rows, many, size), jnp.bfloat16),
            pltpu.SemaphoreType.DMA((1 + groups,)),
        ],
        compiler_params=params(24),
        cost_estimate=cost(rows * many * size * size * 6, 8 * rows * many * size, rows * many * size * 2),
        name="finish",
    )(*parts, *states[0], *states[1])
    return fresh, context.reshape(rows, steps, heads, size)


def join_kernel(*refs):
    blocks, out_ref = refs[:-1], refs[-1]
    at = 0
    for block in blocks:
        out_ref[at : at + block.shape[0], :] = block[...]
        at += block.shape[0]


def join(blocks):
    rows = sum(b.shape[0] for b in blocks)
    return pl.pallas_call(
        join_kernel,
        out_shape=pltpu.VMEM((rows, blocks[0].shape[1]), jnp.bfloat16),
        in_specs=[VMEM] * len(blocks),
        out_specs=VMEM,
        compiler_params=params(8),
        name="join",
    )(*blocks)


def gather_second(factor_a, factor_b, dp):
    count = dp // 2
    ranks = factor_b.shape[0]
    if ranks % 8 == 0 and count in (1, 2, 4):
        payload = make_payload(factor_a.T, factor_b)
        return [payload] + [lax.ppermute(payload, "dp", [(i, i ^ (2 * k)) for i in range(dp)]) for k in range(1, count)]
    payload = jnp.concatenate([factor_a.T, factor_b.reshape(ranks, -1)], axis=1)
    groups = [[i for i in range(dp) if i % 2 == n] for n in range(2)]
    copies = jnp.broadcast_to(payload[None], (count,) + payload.shape)
    blocks = lax.all_to_all(copies, "dp", 0, 0, axis_index_groups=groups, tiled=True)
    return [blocks.reshape(count * ranks, payload.shape[1])]


def shards(dp, tp, hidden, base_weight, factor_a, factor_b, queries, cache, lengths):
    steps, own = queries.shape[1], cache.shape[3]
    assert dp % 2 == 0
    early = queries.shape[0] * 2 // 3
    blocks = gather_second(factor_a, factor_b, dp)
    state = attend_cached(queries, cache, lengths, early)
    blocks, state, hidden, base_weight = lax.optimization_barrier((blocks, state, hidden, base_weight))
    gathered = join(blocks) if len(blocks) > 1 else blocks[0]
    gathered = [gathered, lax.ppermute(gathered, "dp", [(i, i ^ 1) for i in range(dp)])]
    tokens, base, late = arrange(hidden, base_weight, queries, cache, lengths, early)
    received = []
    for k in range(1, tp):
        other = project(k, tokens, base, gathered)
        received.append(lax.ppermute(other, "tp", [(i, i ^ k) for i in range(tp)]))
    mine = project(0, tokens, base, gathered)
    return finish([mine] + received, [state, late], steps, own)


def solution(mesh):
    return jax.shard_map(
        functools.partial(shards, mesh.shape["dp"], mesh.shape["tp"]),
        mesh=mesh,
        in_specs=(
            P(("parts", "dp"), None, "tp"),
            P("tp", None, None, None),
            P(("parts", "tp"), "dp"),
            P(("parts", "dp"), None, None, None),
            P(("parts", "dp"), None, "tp", None),
            P(("parts", "dp"), None, None, "tp", None),
            P(("parts", "dp")),
        ),
        out_specs=(
            P(("parts", "dp"), None, None, "tp", None),
            P(("parts", "dp"), None, "tp", None),
        ),
        check_vma=False,
    )
```

```python
import functools

import jax
import jax.numpy as jnp
from jax import lax
from jax.experimental import pallas as pl
from jax.experimental.pallas import tpu as pltpu
from jax.sharding import PartitionSpec as P

LOW = -1e30
NT = (((1,), (1,)), ((), ()))
TN = (((0,), (0,)), ((), ()))
VMEM = pl.BlockSpec(memory_space=pltpu.VMEM)


def params(mib):
    return pltpu.CompilerParams(vmem_limit_bytes=mib * 1024 * 1024)


def in_hbm(x):
    return pltpu.with_memory_space_constraint(x, pltpu.HBM)


def cost(flops, moved, exps=0):
    return pl.CostEstimate(flops=flops, bytes_accessed=moved, transcendentals=exps)


def payload_kernel(down_hbm, up_hbm, out_ref, ups, wide, sems):
    ranks, width = down_hbm.shape
    groups, size = ups.shape[1] * ups.shape[2], ups.shape[3]
    get_down = pltpu.make_async_copy(down_hbm, out_ref.at[:, pl.ds(0, width)], sems.at[0])
    get_up = pltpu.make_async_copy(up_hbm, ups, sems.at[1])
    get_up.start()
    get_down.start()
    get_up.wait()
    wide[...] = ups.reshape(ranks * groups, size)[...].astype(jnp.float32)
    for n in range(groups):
        out_ref[:, width + n * size : width + (n + 1) * size] = wide[pl.ds(n, ranks, stride=groups), :].astype(
            jnp.bfloat16
        )
    get_down.wait()


def make_payload(down, up):
    ranks, width = down.shape
    groups, size = up.shape[1] * up.shape[2], up.shape[3]
    return pl.pallas_call(
        payload_kernel,
        out_shape=pltpu.VMEM((ranks, width + groups * size), jnp.bfloat16),
        in_specs=[pl.BlockSpec(memory_space=pltpu.HBM)] * 2,
        out_specs=VMEM,
        scratch_shapes=[
            pltpu.VMEM(up.shape, jnp.bfloat16),
            pltpu.VMEM((ranks * groups, size), jnp.float32),
            pltpu.SemaphoreType.DMA((2,)),
        ],
        compiler_params=params(8),
        name="payload",
    )(in_hbm(down), in_hbm(up))


class Cached:
    def __init__(self, first, chunk, heads, scale, inputs, outputs, scratch):
        self.first, self.chunk, self.heads, self.scale = first, chunk, heads, scale
        self.lengths_hbm, self.queries_hbm, self.cache_hbm = inputs
        self.q, self.sums, self.tops, self.totals = outputs
        self.lengths, self.k, self.v, *rest = scratch
        self.scores, self.weights = rest[0:2], rest[2:4]
        self.sems, self.length_sem = rest[4:]
        self.rows, self.queries, self.size = self.q.shape
        self.slots, self.own = self.k.shape[1:3]
        self.keys = self.slots * self.own
        own, queries = self.own, self.queries
        line = lax.broadcasted_iota(jnp.int32, (self.keys, 2 * queries), 0)
        query = lax.broadcasted_iota(jnp.int32, (self.keys, 2 * queries), 1)
        self.line = jnp.where(line % own == (query % heads) // (heads // own), line, self.keys)
        self.one = lax.broadcasted_iota(jnp.int32, (1, 2 * queries), 1) < queries
        self.nothing = jnp.zeros((queries, self.size), jnp.bfloat16)

    @staticmethod
    def outputs(rows, many, size):
        return (
            pltpu.VMEM((rows, many, size), jnp.bfloat16),
            pltpu.VMEM((rows, many, size), jnp.float32),
            pltpu.VMEM((rows // 2, 2 * many), jnp.float32),
            pltpu.VMEM((rows // 2, 2 * many), jnp.float32),
        )

    @staticmethod
    def scratch(rows, chunk, many, cache, lengths):
        slots, own, size = cache.shape[1], cache.shape[3], cache.shape[4]
        half = (rows, slots, own, size)
        scores = (chunk // 2, slots * own, 2 * many)
        return [
            pltpu.SMEM(lengths.shape, jnp.int32),
            pltpu.VMEM(half, jnp.bfloat16),
            pltpu.VMEM(half, jnp.bfloat16),
            pltpu.VMEM(scores, jnp.float32),
            pltpu.VMEM(scores, jnp.float32),
            pltpu.VMEM(scores, jnp.bfloat16),
            pltpu.VMEM(scores, jnp.bfloat16),
            pltpu.SemaphoreType.DMA((rows // chunk, 3)),
            pltpu.SemaphoreType.DMA,
        ]

    def copies(self, i):
        mine, theirs = pl.ds(i * self.chunk, self.chunk), pl.ds(self.first + i * self.chunk, self.chunk)
        pairs = (
            (self.queries_hbm.at[theirs], self.q.at[mine]),
            (self.cache_hbm.at[theirs, :, 0], self.k.at[mine]),
            (self.cache_hbm.at[theirs, :, 1], self.v.at[mine]),
        )
        return [pltpu.make_async_copy(a, b, self.sems.at[i, n]) for n, (a, b) in enumerate(pairs)]

    def lengths_copy(self):
        return pltpu.make_async_copy(self.lengths_hbm, self.lengths, self.length_sem)

    def start(self, i):
        for copy in self.copies(i):
            copy.start()

    def arrive(self, i):
        for copy in self.copies(i):
            copy.wait()

    def lines(self, ref, r):
        flat = ref.reshape(self.rows, self.keys, self.size)
        return jnp.concatenate([flat[r], flat[r + 1]], axis=1)

    def score(self, i, slot):
        for p in range(self.chunk // 2):
            r = i * self.chunk + 2 * p
            both_q = jnp.concatenate(
                [
                    jnp.concatenate([self.q[r], self.nothing], axis=1),
                    jnp.concatenate([self.nothing, self.q[r + 1]], axis=1),
                ],
                axis=0,
            )
            self.scores[slot][p] = lax.dot_general(
                self.lines(self.k, r), both_q, NT, preferred_element_type=jnp.float32
            )

    def soften(self, i, slot):
        for p in range(self.chunk // 2):
            r = self.first + i * self.chunk + 2 * p
            limit = jnp.where(self.one, self.own * self.lengths[r], self.own * self.lengths[r + 1])
            scores = jnp.where(self.line < limit, self.scores[slot][p], LOW)
            top = jnp.max(scores, axis=0, keepdims=True)
            expo = jnp.exp((scores - top) * self.scale)
            self.weights[slot][p] = expo.astype(jnp.bfloat16)
            pair = pl.ds(i * (self.chunk // 2) + p, 1)
            self.tops[pair, :] = top
            self.totals[pair, :] = jnp.sum(expo, axis=0, keepdims=True)

    def collect(self, i, slot):
        queries, size = self.queries, self.size
        for p in range(self.chunk // 2):
            r = i * self.chunk + 2 * p
            both = lax.dot_general(
                self.weights[slot][p], self.lines(self.v, r), TN, preferred_element_type=jnp.float32
            )
            for h in range(2):
                self.sums[r + h] = both[h * queries : (h + 1) * queries, h * size : (h + 1) * size]


def cached_kernel(chunk, heads, scale, *refs):
    hidden_hbm, tokens_ref, hidden, hidden_sem = refs[3], refs[8], refs[9], refs[10]
    cached = Cached(0, chunk, heads, scale, refs[:3], refs[4:8], refs[11:])
    chunks = cached.rows // chunk
    get_hidden = pltpu.make_async_copy(hidden_hbm, hidden, hidden_sem)
    cached.lengths_copy().start()
    for i in range(chunks):
        cached.start(i)
    get_hidden.start()
    cached.lengths_copy().wait()
    cached.arrive(0)
    cached.score(0, 0)
    cached.arrive(1)
    cached.score(1, 1)
    cached.soften(0, 0)

    @pl.loop(1, chunks // 2)
    def _(t):
        for slot in range(2):
            i = 2 * t + slot
            cached.arrive(i)
            cached.score(i, slot)
            cached.soften(i - 1, 1 - slot)
            cached.collect(i - 2, slot)

    get_hidden.wait()
    cached.soften(chunks - 1, 1)
    cached.collect(chunks - 2, 0)
    tokens_ref[...] = hidden.reshape(tokens_ref.shape)[...]
    cached.collect(chunks - 1, 1)


def attend_cached(queries, cache, lengths, hidden):
    rows, steps, heads, size = queries.shape
    slots, own = cache.shape[1], cache.shape[3]
    many = steps * heads
    chunk = 6
    outs = Cached.outputs(rows, many, size) + (pltpu.VMEM((rows * steps, hidden.shape[2]), jnp.bfloat16),)
    *state, tokens = pl.pallas_call(
        functools.partial(cached_kernel, chunk, heads, size ** (-0.5)),
        out_shape=outs,
        in_specs=[pl.BlockSpec(memory_space=pltpu.HBM)] * 4,
        out_specs=(VMEM,) * 5,
        scratch_shapes=[pltpu.VMEM(hidden.shape, jnp.bfloat16), pltpu.SemaphoreType.DMA]
        + Cached.scratch(rows, chunk, many, cache, lengths),
        compiler_params=params(28),
        cost_estimate=cost(
            8 * rows * many * slots * size, 4 * rows * slots * own * size, rows * many * slots * own
        ),
        name="attend_cached",
    )(*map(in_hbm, (lengths, queries.reshape(-1, many, size), cache, hidden)))
    return state, tokens


def arrange_kernel(first, chunks, own, base_hbm, base_ref, base, sems):
    width, two, kvh, size = base.shape
    groups = two * kvh
    some_width = width // chunks

    def copy(i):
        theirs, mine = pl.ds(first + i * some_width, some_width), pl.ds(i * some_width, some_width)
        return pltpu.make_async_copy(base_hbm.at[theirs], base.at[mine], sems.at[i])

    for i in range(chunks):
        copy(i).start()

    tile = 256
    some = tile // groups
    row = lax.broadcasted_iota(jnp.int32, (tile, tile), 0)
    place = lax.broadcasted_iota(jnp.int32, (tile, tile), 1)
    order = (place == (row % some) * groups + row // some).astype(jnp.float32).astype(jnp.bfloat16)
    flat_base = base.reshape(width * groups, size)

    def arrange(f):
        at = f * groups
        pair = jnp.concatenate([flat_base[at + h * tile : at + (h + 1) * tile, :] for h in range(2)], axis=1)
        moved = jnp.dot(order, pair, preferred_element_type=jnp.float32).astype(jnp.bfloat16)
        for n in range(groups):
            lanes = slice((n % own) * size, (n % own + 1) * size)
            for h in range(2):
                base_ref[n // own, f + h * some : f + (h + 1) * some, lanes] = moved[
                    n * some : (n + 1) * some, h * size : (h + 1) * size
                ]

    for i in range(chunks):
        copy(i).wait()
        for f in range(i * some_width, (i + 1) * some_width, 2 * some):
            arrange(f)


def arrange(base, own, first, count):
    width, two, kvh, size = base.shape
    chunks = 2
    return pl.pallas_call(
        functools.partial(arrange_kernel, first, chunks, own),
        out_shape=pltpu.VMEM((two * kvh // own, count, own * size), jnp.bfloat16),
        in_specs=[pl.BlockSpec(memory_space=pltpu.HBM)],
        out_specs=VMEM,
        scratch_shapes=[
            pltpu.VMEM((count, two, kvh, size), jnp.bfloat16),
            pltpu.SemaphoreType.DMA((chunks,)),
        ],
        compiler_params=params(20),
        cost_estimate=cost(512 * two * kvh * size * count, 4 * two * kvh * size * count),
        name="arrange",
    )(in_hbm(base))


def project_kernel(k, bases, hidden_ref, *refs):
    bases, gathered, (out_ref, merged) = refs[:bases], refs[bases:-2], refs[-2:]
    width, columns = merged.shape
    some_width = bases[0].shape[1]
    part = lax.axis_index("tp") ^ k
    parts = bases[0].shape[0] // 2
    half = columns // 2
    up = jnp.concatenate(
        [
            jnp.concatenate(
                [ref[:, pl.ds(pl.multiple_of(width + (c * parts + part) * half, 128), half)] for ref in gathered], axis=0
            )
            for c in range(2)
        ],
        axis=1,
    )
    step = 256
    for f in range(0, width, step):
        down = jnp.concatenate([ref[:, f : f + step] for ref in gathered], axis=0).T
        low_rank = jnp.dot(down, up, preferred_element_type=jnp.float32)
        for c in range(2):
            base_ref, at = bases[f // some_width], f % some_width
            base = base_ref[c * parts + part, at : at + step, :].astype(jnp.float32)
            merged[f : f + step, c * half : (c + 1) * half] = (base + low_rank[:, c * half : (c + 1) * half]).astype(
                jnp.bfloat16
            )
    out_ref[...] = jnp.dot(hidden_ref[...], merged[...], preferred_element_type=jnp.float32)


def project(k, hidden, bases, gathered):
    tokens, width = hidden.shape
    columns = 2 * bases[0].shape[2]
    ranks = sum(g.shape[0] for g in gathered)
    return pl.pallas_call(
        functools.partial(project_kernel, k, len(bases)),
        out_shape=pltpu.VMEM((tokens, columns), jnp.float32),
        in_specs=[VMEM] * (1 + len(bases) + len(gathered)),
        out_specs=VMEM,
        scratch_shapes=[pltpu.VMEM((width, columns), jnp.bfloat16)],
        compiler_params=params(24),
        cost_estimate=cost(2 * width * columns * (tokens + ranks), 2 * width * columns + 2 * width * tokens),
        name="project",
    )(hidden, *bases, *gathered)


def finish_kernel(steps, heads, scale, terms, *refs):
    parts, refs = refs[:terms], refs[terms:]
    q_ref, old_ref, top_ref, total_ref = refs[:4]
    refs = refs[4:]
    fresh_hbm, context_hbm, wide, fresh_ref, context_ref, sems = refs
    rows, queries, size = context_ref.shape
    own = fresh_ref.shape[3]
    fresh = parts[0][...]
    for part in parts[1:]:
        fresh = fresh + part[...]
    keys, many = 2 * own * steps, 2 * queries
    group = size // keys
    key = lax.broadcasted_iota(jnp.int32, (keys, many), 0)
    query = lax.broadcasted_iota(jnp.int32, (keys, many), 1)
    same_head = (query % heads) // (heads // own) == key // (2 * steps)
    same_row = query // queries == (key // steps) % 2
    live = same_head & same_row & ((query % queries) // heads >= key % steps)
    nothing = jnp.zeros((keys, size), jnp.bfloat16)

    def new_lines(c, pair):
        tokens = slice(pair * 2 * steps, (pair + 1) * 2 * steps)
        lines = [fresh[tokens, (c * own + g) * size : (c * own + g + 1) * size] for g in range(own)]
        return jnp.concatenate(lines, axis=0).astype(jnp.bfloat16)

    def rows_of(ref, pair):
        return ref[2 * pair : 2 * pair + 2].reshape(many, size)

    scores = [
        lax.dot_general(new_lines(0, p), rows_of(q_ref, p), NT, preferred_element_type=jnp.float32)
        for p in range(rows // 2)
    ]
    scores = jnp.stack([jnp.where(live, s, LOW) for s in scores])
    old_top = top_ref[...]
    top = jnp.maximum(old_top, jnp.max(scores, axis=1))
    expo = jnp.exp((scores - top[:, None, :]) * scale)
    back = jnp.exp((old_top - top) * scale)
    inverse = 1.0 / (back * total_ref[...] + jnp.sum(expo, axis=1))
    weights = (expo * inverse[:, None, :]).astype(jnp.bfloat16)
    back = back * inverse

    for n in range(2 * own):
        wide[pl.ds(n, rows * steps, stride=2 * own), :] = fresh[:, n * size : (n + 1) * size]
    fresh_ref.reshape(rows * steps * 2 * own, size)[...] = wide[...].astype(jnp.bfloat16)
    puts = [pltpu.make_async_copy(fresh_ref, fresh_hbm, sems.at[0])]
    puts[0].start()

    for at in range(0, rows // 2, group):
        pairs = range(at, at + group)
        values = jnp.concatenate(
            [
                jnp.concatenate([new_lines(1, p) if n == p else nothing for n in pairs], axis=1)
                for p in pairs
            ],
            axis=0,
        )
        new = lax.dot_general(
            weights[at : at + group].reshape(group * keys, many), values, TN, preferred_element_type=jnp.float32
        )
        factors = back[at : at + group].T
        for n, p in enumerate(pairs):
            both = new[:, n * size : (n + 1) * size] + factors[:, n : n + 1] * rows_of(old_ref, p)
            context_ref[2 * p : 2 * p + 2] = both.astype(jnp.bfloat16).reshape(2, queries, size)
        mine = pl.ds(2 * at, 2 * group)
        puts.append(pltpu.make_async_copy(context_ref.at[mine], context_hbm.at[mine], sems.at[1 + at // group]))
        puts[-1].start()
    for put in puts:
        put.wait()


def finish(parts, state, steps, own):
    rows, many, size = state[0].shape
    heads = many // steps
    groups = rows * own * steps // size
    fresh = (rows, steps, 2, own, size)
    fresh, context = pl.pallas_call(
        functools.partial(finish_kernel, steps, heads, size ** (-0.5), len(parts)),
        out_shape=(
            jax.ShapeDtypeStruct(fresh, jnp.bfloat16),
            jax.ShapeDtypeStruct((rows, many, size), jnp.bfloat16),
        ),
        in_specs=[VMEM] * (len(parts) + 4),
        out_specs=(pl.BlockSpec(memory_space=pltpu.HBM),) * 2,
        scratch_shapes=[
            pltpu.VMEM((rows * steps * 2 * own, size), jnp.float32),
            pltpu.VMEM(fresh, jnp.bfloat16),
            pltpu.VMEM((rows, many, size), jnp.bfloat16),
            pltpu.SemaphoreType.DMA((1 + groups,)),
        ],
        compiler_params=params(24),
        cost_estimate=cost(rows * many * size * size * 6, 8 * rows * many * size, rows * many * size * 2),
        name="finish",
    )(*parts, *state)
    return fresh, context.reshape(rows, steps, heads, size)


def join_kernel(*refs):
    blocks, out_ref = refs[:-1], refs[-1]
    at = 0
    for block in blocks:
        out_ref[at : at + block.shape[0], :] = block[...]
        at += block.shape[0]


def join(blocks):
    rows = sum(b.shape[0] for b in blocks)
    return pl.pallas_call(
        join_kernel,
        out_shape=pltpu.VMEM((rows, blocks[0].shape[1]), jnp.bfloat16),
        in_specs=[VMEM] * len(blocks),
        out_specs=VMEM,
        compiler_params=params(8),
        name="join",
    )(*blocks)


def shards(dp, tp, hidden, base_weight, factor_a, factor_b, queries, cache, lengths):
    steps, own = queries.shape[1], cache.shape[3]
    ranks = factor_b.shape[0]
    half = base_weight.shape[0] // 2

    def swap(x, k):
        return lax.ppermute(x, "dp", [(i, i ^ k) for i in range(dp)])

    if dp == 8 and ranks % 8 == 0:
        block = make_payload(factor_a.T, factor_b)
        other = swap(block, 4)
        base = arrange(base_weight, own, 0, half)
        block, other, base, base_weight = lax.optimization_barrier((block, other, base, base_weight))
        block = join([block, other])
        other = swap(block, 2)
        bases = [base, arrange(base_weight, own, half, half)]
        block, other, bases, cache = lax.optimization_barrier((block, other, bases, cache))
        block = join([block, other])
        gathered = [block, swap(block, 1)]
    else:
        payload = jnp.concatenate([factor_a.T, factor_b.reshape(ranks, -1)], axis=1)
        copies = jnp.broadcast_to(payload[None], (dp,) + payload.shape)
        blocks = lax.all_to_all(copies, "dp", 0, 0, tiled=True)
        gathered = [blocks.reshape(dp * ranks, payload.shape[1])]
        bases = [arrange(base_weight, own, n * half, half) for n in range(2)]
    state, tokens = attend_cached(queries, cache, lengths, hidden)
    received = []
    for k in range(1, tp):
        other = project(k, tokens, bases, gathered)
        received.append(lax.ppermute(other, "tp", [(i, i ^ k) for i in range(tp)]))
    mine = project(0, tokens, bases, gathered)
    return finish([mine] + received, state, steps, own)


def solution(mesh):
    return jax.shard_map(
        functools.partial(shards, mesh.shape["dp"], mesh.shape["tp"]),
        mesh=mesh,
        in_specs=(
            P(("parts", "dp"), None, "tp"),
            P("tp", None, None, None),
            P(("parts", "tp"), "dp"),
            P(("parts", "dp"), None, None, None),
            P(("parts", "dp"), None, "tp", None),
            P(("parts", "dp"), None, None, "tp", None),
            P(("parts", "dp")),
        ),
        out_specs=(
            P(("parts", "dp"), None, None, "tp", None),
            P(("parts", "dp"), None, "tp", None),
        ),
        check_vma=False,
    )
```

```python
import functools

import jax
import jax.numpy as jnp
from jax import lax
from jax.experimental import pallas as pl
from jax.experimental.pallas import tpu as pltpu
from jax.sharding import PartitionSpec as P

LOW = -1e30
NT = (((1,), (1,)), ((), ()))
TN = (((0,), (0,)), ((), ()))
VMEM = pl.BlockSpec(memory_space=pltpu.VMEM)


def params(mib):
    return pltpu.CompilerParams(vmem_limit_bytes=mib * 1024 * 1024)


def in_hbm(x):
    return pltpu.with_memory_space_constraint(x, pltpu.HBM)


def cost(flops, moved, exps=0):
    return pl.CostEstimate(flops=flops, bytes_accessed=moved, transcendentals=exps)


def payload_kernel(down_hbm, up_hbm, out_ref, ups, wide, sems):
    ranks, width = down_hbm.shape
    groups, size = ups.shape[1] * ups.shape[2], ups.shape[3]
    get_down = pltpu.make_async_copy(down_hbm, out_ref.at[:, pl.ds(0, width)], sems.at[0])
    get_up = pltpu.make_async_copy(up_hbm, ups, sems.at[1])
    get_up.start()
    get_down.start()
    get_up.wait()
    wide[...] = ups.reshape(ranks * groups, size)[...].astype(jnp.float32)
    for n in range(groups):
        out_ref[:, width + n * size : width + (n + 1) * size] = wide[pl.ds(n, ranks, stride=groups), :].astype(
            jnp.bfloat16
        )
    get_down.wait()


def make_payload(down, up):
    ranks, width = down.shape
    groups, size = up.shape[1] * up.shape[2], up.shape[3]
    return pl.pallas_call(
        payload_kernel,
        out_shape=pltpu.VMEM((ranks, width + groups * size), jnp.bfloat16),
        in_specs=[pl.BlockSpec(memory_space=pltpu.HBM)] * 2,
        out_specs=VMEM,
        scratch_shapes=[
            pltpu.VMEM(up.shape, jnp.bfloat16),
            pltpu.VMEM((ranks * groups, size), jnp.float32),
            pltpu.SemaphoreType.DMA((2,)),
        ],
        compiler_params=params(8),
        name="payload",
    )(in_hbm(down), in_hbm(up))


class Cached:
    def __init__(self, first, chunk, heads, scale, inputs, outputs, scratch):
        self.first, self.chunk, self.heads, self.scale = first, chunk, heads, scale
        self.lengths_hbm, self.queries_hbm, self.cache_hbm = inputs
        self.q, self.sums, self.tops, self.totals = outputs
        self.lengths, self.k, self.v, *rest = scratch
        self.scores, self.weights = rest[0:2], rest[2:4]
        self.sems, self.length_sem = rest[4:]
        self.rows, self.queries, self.size = self.q.shape
        self.slots, self.own = self.k.shape[1:3]
        self.keys = self.slots * self.own
        own, queries = self.own, self.queries
        line = lax.broadcasted_iota(jnp.int32, (self.keys, 2 * queries), 0)
        query = lax.broadcasted_iota(jnp.int32, (self.keys, 2 * queries), 1)
        self.line = jnp.where(line % own == (query % heads) // (heads // own), line, self.keys)
        self.one = lax.broadcasted_iota(jnp.int32, (1, 2 * queries), 1) < queries
        self.nothing = jnp.zeros((queries, self.size), jnp.bfloat16)

    @staticmethod
    def outputs(rows, many, size):
        return (
            pltpu.VMEM((rows, many, size), jnp.bfloat16),
            pltpu.VMEM((rows, many, size), jnp.float32),
            pltpu.VMEM((rows // 2, 2 * many), jnp.float32),
            pltpu.VMEM((rows // 2, 2 * many), jnp.float32),
        )

    @staticmethod
    def scratch(rows, chunk, many, cache, lengths):
        slots, own, size = cache.shape[1], cache.shape[3], cache.shape[4]
        half = (rows, slots, own, size)
        scores = (chunk // 2, slots * own, 2 * many)
        return [
            pltpu.SMEM(lengths.shape, jnp.int32),
            pltpu.VMEM(half, jnp.bfloat16),
            pltpu.VMEM(half, jnp.bfloat16),
            pltpu.VMEM(scores, jnp.float32),
            pltpu.VMEM(scores, jnp.float32),
            pltpu.VMEM(scores, jnp.bfloat16),
            pltpu.VMEM(scores, jnp.bfloat16),
            pltpu.SemaphoreType.DMA((rows // chunk, 3)),
            pltpu.SemaphoreType.DMA,
        ]

    def copies(self, i):
        mine, theirs = pl.ds(i * self.chunk, self.chunk), pl.ds(self.first + i * self.chunk, self.chunk)
        pairs = (
            (self.queries_hbm.at[theirs], self.q.at[mine]),
            (self.cache_hbm.at[theirs, :, 0], self.k.at[mine]),
            (self.cache_hbm.at[theirs, :, 1], self.v.at[mine]),
        )
        return [pltpu.make_async_copy(a, b, self.sems.at[i, n]) for n, (a, b) in enumerate(pairs)]

    def lengths_copy(self):
        return pltpu.make_async_copy(self.lengths_hbm, self.lengths, self.length_sem)

    def start(self, i):
        for n, copy in enumerate(self.copies(i)):
            copy.start(priority=n // 2)

    def arrive(self, i):
        for copy in self.copies(i):
            copy.wait()

    def lines(self, ref, r):
        flat = ref.reshape(self.rows, self.keys, self.size)
        return jnp.concatenate([flat[r], flat[r + 1]], axis=1)

    def score(self, i, slot):
        for p in range(self.chunk // 2):
            r = i * self.chunk + 2 * p
            both_q = jnp.concatenate(
                [
                    jnp.concatenate([self.q[r], self.nothing], axis=1),
                    jnp.concatenate([self.nothing, self.q[r + 1]], axis=1),
                ],
                axis=0,
            )
            self.scores[slot][p] = lax.dot_general(
                self.lines(self.k, r), both_q, NT, preferred_element_type=jnp.float32
            )

    def soften(self, i, slot):
        for p in range(self.chunk // 2):
            r = self.first + i * self.chunk + 2 * p
            limit = jnp.where(self.one, self.own * self.lengths[r], self.own * self.lengths[r + 1])
            scores = jnp.where(self.line < limit, self.scores[slot][p], LOW)
            top = jnp.max(scores, axis=0, keepdims=True)
            expo = jnp.exp((scores - top) * self.scale)
            self.weights[slot][p] = expo.astype(jnp.bfloat16)
            pair = pl.ds(i * (self.chunk // 2) + p, 1)
            self.tops[pair, :] = top
            self.totals[pair, :] = jnp.sum(expo, axis=0, keepdims=True)

    def collect(self, i, slot):
        queries, size = self.queries, self.size
        for p in range(self.chunk // 2):
            r = i * self.chunk + 2 * p
            both = lax.dot_general(
                self.weights[slot][p], self.lines(self.v, r), TN, preferred_element_type=jnp.float32
            )
            for h in range(2):
                self.sums[r + h] = both[h * queries : (h + 1) * queries, h * size : (h + 1) * size]


def cached_kernel(chunk, heads, scale, *refs):
    cached = Cached(0, chunk, heads, scale, refs[:3], refs[3:7], refs[7:])
    chunks = cached.rows // chunk
    cached.lengths_copy().start()
    for i in range(chunks):
        cached.start(i)
    cached.lengths_copy().wait()
    cached.arrive(0)
    cached.score(0, 0)
    cached.arrive(1)
    cached.score(1, 1)
    cached.soften(0, 0)

    @pl.loop(1, chunks // 2)
    def _(t):
        for slot in range(2):
            i = 2 * t + slot
            cached.arrive(i)
            cached.score(i, slot)
            cached.soften(i - 1, 1 - slot)
            cached.collect(i - 2, slot)

    cached.soften(chunks - 1, 1)
    cached.collect(chunks - 2, 0)
    cached.collect(chunks - 1, 1)


def attend_cached(queries, cache, lengths, rows):
    _, steps, heads, size = queries.shape
    slots, own = cache.shape[1], cache.shape[3]
    many = steps * heads
    chunk = 4
    return pl.pallas_call(
        functools.partial(cached_kernel, chunk, heads, size ** (-0.5)),
        out_shape=Cached.outputs(rows, many, size),
        in_specs=[pl.BlockSpec(memory_space=pltpu.HBM)] * 3,
        out_specs=(VMEM,) * 4,
        scratch_shapes=Cached.scratch(rows, chunk, many, cache, lengths),
        compiler_params=params(28),
        cost_estimate=cost(
            8 * rows * many * slots * size, 4 * rows * slots * own * size, rows * many * slots * own
        ),
        name="attend_cached",
    )(*map(in_hbm, (lengths, queries.reshape(-1, many, size), cache)))


def arrange_kernel(first, chunk, chunks, own, heads, scale, *refs):
    hidden_hbm, base_hbm = refs[:2]
    tokens_ref, base_ref = refs[5:7]
    hidden, base, sems = refs[11:14]
    cached = Cached(first, chunk, heads, scale, refs[2:5], refs[7:11], refs[14:])
    width, two, kvh, size = base.shape
    groups = two * kvh
    some_width = width // chunks

    def copy(i):
        features = pl.ds(i * some_width, some_width)
        return pltpu.make_async_copy(base_hbm.at[features], base.at[features], sems.at[i])

    get_hidden = pltpu.make_async_copy(hidden_hbm, hidden, sems.at[chunks])
    cached.lengths_copy().start()
    copy(0).start()
    cached.start(0)
    copy(1).start()
    cached.start(1)
    for i in range(2, chunks):
        copy(i).start()
    get_hidden.start()

    tile = 256
    some = tile // groups
    row = lax.broadcasted_iota(jnp.int32, (tile, tile), 0)
    place = lax.broadcasted_iota(jnp.int32, (tile, tile), 1)
    order = (place == (row % some) * groups + row // some).astype(jnp.float32).astype(jnp.bfloat16)
    flat_base = base.reshape(width * groups, size)

    def arrange(f):
        at = f * groups
        pair = jnp.concatenate([flat_base[at + h * tile : at + (h + 1) * tile, :] for h in range(2)], axis=1)
        moved = jnp.dot(order, pair, preferred_element_type=jnp.float32).astype(jnp.bfloat16)
        for n in range(groups):
            lanes = slice((n % own) * size, (n % own + 1) * size)
            for h in range(2):
                base_ref[n // own, f + h * some : f + (h + 1) * some, lanes] = moved[
                    n * some : (n + 1) * some, h * size : (h + 1) * size
                ]

    cached.lengths_copy().wait()
    for i in range(chunks):
        copy(i).wait()
        if i < 2:
            cached.arrive(i)
            cached.score(i, i)
        if 1 <= i < 3:
            cached.soften(i - 1, i - 1)
        if 2 <= i < 4:
            cached.collect(i - 2, i - 2)
        for f in range(i * some_width, (i + 1) * some_width, 2 * some):
            arrange(f)
    get_hidden.wait()
    tokens_ref[...] = hidden.reshape(tokens_ref.shape)[...]


def arrange(hidden, base, queries, cache, lengths, rows):
    _, steps, heads, size = queries.shape
    slots, own = cache.shape[1], cache.shape[3]
    many = steps * heads
    width, two, kvh, size = base.shape
    chunks = 4
    rest = hidden.shape[0] - rows
    chunk = rest // 2
    outs = (
        pltpu.VMEM((hidden.shape[0] * steps, width), jnp.bfloat16),
        pltpu.VMEM((two * kvh // own, width, own * size), jnp.bfloat16),
    ) + Cached.outputs(rest, many, size)
    tokens, base, *state = pl.pallas_call(
        functools.partial(arrange_kernel, rows, chunk, chunks, own, heads, size ** (-0.5)),
        out_shape=outs,
        in_specs=[pl.BlockSpec(memory_space=pltpu.HBM)] * 5,
        out_specs=(VMEM,) * len(outs),
        scratch_shapes=[
            pltpu.VMEM(hidden.shape, jnp.bfloat16),
            pltpu.VMEM(base.shape, jnp.bfloat16),
            pltpu.SemaphoreType.DMA((chunks + 1,)),
        ]
        + Cached.scratch(rest, chunk, many, cache, lengths),
        compiler_params=params(28),
        cost_estimate=cost(
            512 * base.size + 8 * rest * many * slots * size,
            4 * (base.size + hidden.size + rest * slots * own * size),
            rest * many * slots * own,
        ),
        name="arrange",
    )(*map(in_hbm, (hidden, base, lengths, queries.reshape(-1, many, size), cache)))
    return tokens, base, state


def project_kernel(k, hidden_ref, base_ref, *refs):
    gathered, (out_ref, merged) = refs[:-2], refs[-2:]
    width, columns = merged.shape
    part = lax.axis_index("tp") ^ k
    parts = base_ref.shape[0] // 2
    half = columns // 2
    up = jnp.concatenate(
        [
            jnp.concatenate(
                [ref[:, pl.ds(pl.multiple_of(width + (c * parts + part) * half, 128), half)] for ref in gathered], axis=0
            )
            for c in range(2)
        ],
        axis=1,
    )
    step = 512
    for f in range(0, width, step):
        down = jnp.concatenate([ref[:, f : f + step] for ref in gathered], axis=0).T
        low_rank = jnp.dot(down, up, preferred_element_type=jnp.float32)
        for c in range(2):
            base = base_ref[c * parts + part, f : f + step, :].astype(jnp.float32)
            merged[f : f + step, c * half : (c + 1) * half] = (base + low_rank[:, c * half : (c + 1) * half]).astype(
                jnp.bfloat16
            )
    out_ref[...] = jnp.dot(hidden_ref[...], merged[...], preferred_element_type=jnp.float32)


def project(k, hidden, base, gathered):
    tokens, width = hidden.shape
    columns = 2 * base.shape[2]
    ranks = sum(g.shape[0] for g in gathered)
    return pl.pallas_call(
        functools.partial(project_kernel, k),
        out_shape=pltpu.VMEM((tokens, columns), jnp.float32),
        in_specs=[VMEM] * (2 + len(gathered)),
        out_specs=VMEM,
        scratch_shapes=[pltpu.VMEM((width, columns), jnp.bfloat16)],
        compiler_params=params(24),
        cost_estimate=cost(2 * width * columns * (tokens + ranks), 2 * width * columns + 2 * width * tokens),
        name="project",
    )(hidden, base, *gathered)


def finish_kernel(steps, heads, scale, terms, *refs):
    parts, refs = refs[:terms], refs[terms:]
    states, refs = (refs[:4], refs[4:8]), refs[8:]
    fresh_hbm, context_hbm, wide, fresh_ref, context_ref, sems = refs
    rows, queries, size = context_ref.shape
    own = fresh_ref.shape[3]
    fresh = parts[0][...]
    for part in parts[1:]:
        fresh = fresh + part[...]
    keys, many = 2 * own * steps, 2 * queries
    group = size // keys
    key = lax.broadcasted_iota(jnp.int32, (keys, many), 0)
    query = lax.broadcasted_iota(jnp.int32, (keys, many), 1)
    same_head = (query % heads) // (heads // own) == key // (2 * steps)
    same_row = query // queries == (key // steps) % 2
    live = same_head & same_row & ((query % queries) // heads >= key % steps)
    nothing = jnp.zeros((keys, size), jnp.bfloat16)

    def new_lines(c, pair):
        tokens = slice(pair * 2 * steps, (pair + 1) * 2 * steps)
        lines = [fresh[tokens, (c * own + g) * size : (c * own + g + 1) * size] for g in range(own)]
        return jnp.concatenate(lines, axis=0).astype(jnp.bfloat16)

    def old(n, pair):
        count = states[0][0].shape[0] // 2
        return (states[0][n], pair) if pair < count else (states[1][n], pair - count)

    def rows_of(n, pair):
        ref, at = old(n, pair)
        return ref[2 * at : 2 * at + 2].reshape(many, size)

    scores = [
        lax.dot_general(new_lines(0, p), rows_of(0, p), NT, preferred_element_type=jnp.float32)
        for p in range(rows // 2)
    ]
    scores = jnp.stack([jnp.where(live, s, LOW) for s in scores])
    old_top, old_total = [jnp.concatenate([states[0][n][...], states[1][n][...]], axis=0) for n in (2, 3)]
    top = jnp.maximum(old_top, jnp.max(scores, axis=1))
    expo = jnp.exp((scores - top[:, None, :]) * scale)
    back = jnp.exp((old_top - top) * scale)
    inverse = 1.0 / (back * old_total + jnp.sum(expo, axis=1))
    weights = (expo * inverse[:, None, :]).astype(jnp.bfloat16)
    back = back * inverse

    for n in range(2 * own):
        wide[pl.ds(n, rows * steps, stride=2 * own), :] = fresh[:, n * size : (n + 1) * size]
    fresh_ref.reshape(rows * steps * 2 * own, size)[...] = wide[...].astype(jnp.bfloat16)
    puts = [pltpu.make_async_copy(fresh_ref, fresh_hbm, sems.at[0])]
    puts[0].start()

    for at in range(0, rows // 2, group):
        pairs = range(at, at + group)
        values = jnp.concatenate(
            [
                jnp.concatenate([new_lines(1, p) if n == p else nothing for n in pairs], axis=1)
                for p in pairs
            ],
            axis=0,
        )
        new = lax.dot_general(
            weights[at : at + group].reshape(group * keys, many), values, TN, preferred_element_type=jnp.float32
        )
        factors = back[at : at + group].T
        for n, p in enumerate(pairs):
            both = new[:, n * size : (n + 1) * size] + factors[:, n : n + 1] * rows_of(1, p)
            context_ref[2 * p : 2 * p + 2] = both.astype(jnp.bfloat16).reshape(2, queries, size)
        mine = pl.ds(2 * at, 2 * group)
        puts.append(pltpu.make_async_copy(context_ref.at[mine], context_hbm.at[mine], sems.at[1 + at // group]))
        puts[-1].start()
    for put in puts:
        put.wait()


def finish(parts, states, steps, own):
    _, many, size = states[0][0].shape
    rows = sum(state[0].shape[0] for state in states)
    heads = many // steps
    groups = rows * own * steps // size
    fresh = (rows, steps, 2, own, size)
    fresh, context = pl.pallas_call(
        functools.partial(finish_kernel, steps, heads, size ** (-0.5), len(parts)),
        out_shape=(
            jax.ShapeDtypeStruct(fresh, jnp.bfloat16),
            jax.ShapeDtypeStruct((rows, many, size), jnp.bfloat16),
        ),
        in_specs=[VMEM] * (len(parts) + 8),
        out_specs=(pl.BlockSpec(memory_space=pltpu.HBM),) * 2,
        scratch_shapes=[
            pltpu.VMEM((rows * steps * 2 * own, size), jnp.float32),
            pltpu.VMEM(fresh, jnp.bfloat16),
            pltpu.VMEM((rows, many, size), jnp.bfloat16),
            pltpu.SemaphoreType.DMA((1 + groups,)),
        ],
        compiler_params=params(24),
        cost_estimate=cost(rows * many * size * size * 6, 8 * rows * many * size, rows * many * size * 2),
        name="finish",
    )(*parts, *states[0], *states[1])
    return fresh, context.reshape(rows, steps, heads, size)


def join_kernel(*refs):
    blocks, out_ref = refs[:-1], refs[-1]
    at = 0
    for block in blocks:
        out_ref[at : at + block.shape[0], :] = block[...]
        at += block.shape[0]


def join(blocks):
    rows = sum(b.shape[0] for b in blocks)
    return pl.pallas_call(
        join_kernel,
        out_shape=pltpu.VMEM((rows, blocks[0].shape[1]), jnp.bfloat16),
        in_specs=[VMEM] * len(blocks),
        out_specs=VMEM,
        compiler_params=params(8),
        name="join",
    )(*blocks)


def gather_second(factor_a, factor_b, dp):
    count = dp // 2
    ranks = factor_b.shape[0]
    if ranks % 8 == 0 and count in (1, 2, 4):
        payload = make_payload(factor_a.T, factor_b)
        return [payload] + [lax.ppermute(payload, "dp", [(i, i ^ (2 * k)) for i in range(dp)]) for k in range(1, count)]
    payload = jnp.concatenate([factor_a.T, factor_b.reshape(ranks, -1)], axis=1)
    groups = [[i for i in range(dp) if i % 2 == n] for n in range(2)]
    copies = jnp.broadcast_to(payload[None], (count,) + payload.shape)
    blocks = lax.all_to_all(copies, "dp", 0, 0, axis_index_groups=groups, tiled=True)
    return [blocks.reshape(count * ranks, payload.shape[1])]


def shards(dp, tp, hidden, base_weight, factor_a, factor_b, queries, cache, lengths):
    steps, own = queries.shape[1], cache.shape[3]
    assert dp % 2 == 0
    early = queries.shape[0] * 5 // 6
    blocks = gather_second(factor_a, factor_b, dp)
    state = attend_cached(queries, cache, lengths, early)
    blocks, state, hidden, base_weight = lax.optimization_barrier((blocks, state, hidden, base_weight))
    gathered = join(blocks) if len(blocks) > 1 else blocks[0]
    gathered = [gathered, lax.ppermute(gathered, "dp", [(i, i ^ 1) for i in range(dp)])]
    tokens, base, late = arrange(hidden, base_weight, queries, cache, lengths, early)
    received = []
    for k in range(1, tp):
        other = project(k, tokens, base, gathered)
        received.append(lax.ppermute(other, "tp", [(i, i ^ k) for i in range(tp)]))
    mine = project(0, tokens, base, gathered)
    return finish([mine] + received, [state, late], steps, own)


def solution(mesh):
    return jax.shard_map(
        functools.partial(shards, mesh.shape["dp"], mesh.shape["tp"]),
        mesh=mesh,
        in_specs=(
            P(("parts", "dp"), None, "tp"),
            P("tp", None, None, None),
            P(("parts", "tp"), "dp"),
            P(("parts", "dp"), None, None, None),
            P(("parts", "dp"), None, "tp", None),
            P(("parts", "dp"), None, None, "tp", None),
            P(("parts", "dp")),
        ),
        out_specs=(
            P(("parts", "dp"), None, None, "tp", None),
            P(("parts", "dp"), None, "tp", None),
        ),
        check_vma=False,
    )
```

```python
import functools

import jax
import jax.numpy as jnp
from jax import lax
from jax.experimental import pallas as pl
from jax.experimental.pallas import tpu as pltpu
from jax.sharding import PartitionSpec as P

LOW = -1e30
NT = (((1,), (1,)), ((), ()))
TN = (((0,), (0,)), ((), ()))
VMEM = pl.BlockSpec(memory_space=pltpu.VMEM)


def params(mib):
    return pltpu.CompilerParams(vmem_limit_bytes=mib * 1024 * 1024)


def in_hbm(x):
    return pltpu.with_memory_space_constraint(x, pltpu.HBM)


def cost(flops, moved, exps=0):
    return pl.CostEstimate(flops=flops, bytes_accessed=moved, transcendentals=exps)


def payload_kernel(down_hbm, up_hbm, out_ref, ups, wide, sems):
    ranks, width = down_hbm.shape
    groups, size = ups.shape[1] * ups.shape[2], ups.shape[3]
    get_down = pltpu.make_async_copy(down_hbm, out_ref.at[:, pl.ds(0, width)], sems.at[0])
    get_up = pltpu.make_async_copy(up_hbm, ups, sems.at[1])
    get_up.start()
    get_down.start()
    get_up.wait()
    wide[...] = ups.reshape(ranks * groups, size)[...].astype(jnp.float32)
    for n in range(groups):
        out_ref[:, width + n * size : width + (n + 1) * size] = wide[pl.ds(n, ranks, stride=groups), :].astype(
            jnp.bfloat16
        )
    get_down.wait()


def make_payload(down, up):
    ranks, width = down.shape
    groups, size = up.shape[1] * up.shape[2], up.shape[3]
    return pl.pallas_call(
        payload_kernel,
        out_shape=pltpu.VMEM((ranks, width + groups * size), jnp.bfloat16),
        in_specs=[pl.BlockSpec(memory_space=pltpu.HBM)] * 2,
        out_specs=VMEM,
        scratch_shapes=[
            pltpu.VMEM(up.shape, jnp.bfloat16),
            pltpu.VMEM((ranks * groups, size), jnp.float32),
            pltpu.SemaphoreType.DMA((2,)),
        ],
        compiler_params=params(8),
        name="payload",
    )(in_hbm(down), in_hbm(up))


class Cached:
    def __init__(self, first, chunk, heads, scale, inputs, outputs, scratch):
        self.first, self.chunk, self.heads, self.scale = first, chunk, heads, scale
        self.lengths_hbm, self.queries_hbm, self.cache_hbm = inputs
        self.q, self.sums, self.tops, self.totals = outputs
        self.lengths, self.k, self.v, *rest = scratch
        self.scores, self.weights, self.sems, self.length_sem = rest
        self.rows, self.queries, self.size = self.q.shape
        self.slots, self.own = self.k.shape[1:3]
        self.keys = self.slots * self.own
        own, queries = self.own, self.queries
        line = lax.broadcasted_iota(jnp.int32, (self.keys, 2 * queries), 0)
        query = lax.broadcasted_iota(jnp.int32, (self.keys, 2 * queries), 1)
        self.line = jnp.where(line % own == (query % heads) // (heads // own), line, self.keys)
        self.one = lax.broadcasted_iota(jnp.int32, (1, 2 * queries), 1) < queries
        self.nothing = jnp.zeros((queries, self.size), jnp.bfloat16)

    @staticmethod
    def outputs(rows, many, size):
        return (
            pltpu.VMEM((rows, many, size), jnp.bfloat16),
            pltpu.VMEM((rows, many, size), jnp.float32),
            pltpu.VMEM((rows // 2, 2 * many), jnp.float32),
            pltpu.VMEM((rows // 2, 2 * many), jnp.float32),
        )

    @staticmethod
    def scratch(rows, chunk, many, cache, lengths):
        slots, own, size = cache.shape[1], cache.shape[3], cache.shape[4]
        half = (rows, slots, own, size)
        scores = (2, chunk // 2, slots * own, 2 * many)
        return [
            pltpu.SMEM(lengths.shape, jnp.int32),
            pltpu.VMEM(half, jnp.bfloat16),
            pltpu.VMEM(half, jnp.bfloat16),
            pltpu.VMEM(scores, jnp.float32),
            pltpu.VMEM(scores, jnp.bfloat16),
            pltpu.SemaphoreType.DMA((rows // chunk, 3)),
            pltpu.SemaphoreType.DMA,
        ]

    def copies(self, i):
        mine, theirs = pl.ds(i * self.chunk, self.chunk), pl.ds(self.first + i * self.chunk, self.chunk)
        pairs = (
            (self.queries_hbm.at[theirs], self.q.at[mine]),
            (self.cache_hbm.at[theirs, :, 0], self.k.at[mine]),
            (self.cache_hbm.at[theirs, :, 1], self.v.at[mine]),
        )
        return [pltpu.make_async_copy(a, b, self.sems.at[i, n]) for n, (a, b) in enumerate(pairs)]

    def lengths_copy(self):
        return pltpu.make_async_copy(self.lengths_hbm, self.lengths, self.length_sem)

    def start(self, i):
        for copy in self.copies(i):
            copy.start()

    def arrive(self, i):
        for copy in self.copies(i):
            copy.wait()

    def lines(self, ref, r):
        flat = ref.reshape(self.rows, self.keys, self.size)
        return jnp.concatenate([flat[r], flat[r + 1]], axis=1)

    def score(self, i, slot):
        for p in range(self.chunk // 2):
            r = i * self.chunk + 2 * p
            both_q = jnp.concatenate(
                [
                    jnp.concatenate([self.q[r], self.nothing], axis=1),
                    jnp.concatenate([self.nothing, self.q[r + 1]], axis=1),
                ],
                axis=0,
            )
            self.scores[slot, p] = lax.dot_general(
                self.lines(self.k, r), both_q, NT, preferred_element_type=jnp.float32
            )

    def soften(self, i, slot):
        for p in range(self.chunk // 2):
            r = self.first + i * self.chunk + 2 * p
            limit = jnp.where(self.one, self.own * self.lengths[r], self.own * self.lengths[r + 1])
            scores = jnp.where(self.line < limit, self.scores[slot, p], LOW)
            top = jnp.max(scores, axis=0, keepdims=True)
            expo = jnp.exp((scores - top) * self.scale)
            self.weights[slot, p] = expo.astype(jnp.bfloat16)
            pair = pl.ds(i * (self.chunk // 2) + p, 1)
            self.tops[pair, :] = top
            self.totals[pair, :] = jnp.sum(expo, axis=0, keepdims=True)

    def collect(self, i, slot):
        queries, size = self.queries, self.size
        for p in range(self.chunk // 2):
            r = i * self.chunk + 2 * p
            both = lax.dot_general(
                self.weights[slot, p], self.lines(self.v, r), TN, preferred_element_type=jnp.float32
            )
            for h in range(2):
                self.sums[r + h] = both[h * queries : (h + 1) * queries, h * size : (h + 1) * size]


def cached_kernel(chunk, heads, scale, *refs):
    cached = Cached(0, chunk, heads, scale, refs[:3], refs[3:7], refs[7:])
    chunks = cached.rows // chunk
    cached.lengths_copy().start()
    for i in range(chunks):
        cached.start(i)
    cached.lengths_copy().wait()

    @pl.loop(0, chunks + 2)
    def _(i):
        @pl.when(i < chunks)
        def _():
            cached.arrive(i)

        slot = i % 2
        cached.collect(jnp.clip(i - 2, 0, chunks - 1), slot)
        cached.soften(jnp.clip(i - 1, 0, chunks - 1), 1 - slot)
        cached.score(jnp.minimum(i, chunks - 1), slot)


def attend_cached(queries, cache, lengths):
    rows, steps, heads, size = queries.shape
    slots, own = cache.shape[1], cache.shape[3]
    many = steps * heads
    chunk = 6
    return pl.pallas_call(
        functools.partial(cached_kernel, chunk, heads, size ** (-0.5)),
        out_shape=Cached.outputs(rows, many, size),
        in_specs=[pl.BlockSpec(memory_space=pltpu.HBM)] * 3,
        out_specs=(VMEM,) * 4,
        scratch_shapes=Cached.scratch(rows, chunk, many, cache, lengths),
        compiler_params=params(28),
        cost_estimate=cost(
            8 * rows * many * slots * size, 4 * rows * slots * own * size, rows * many * slots * own
        ),
        name="attend_cached",
    )(*map(in_hbm, (lengths, queries.reshape(-1, many, size), cache)))


def arrange_kernel(chunks, own, hidden_hbm, base_hbm, tokens_ref, base_ref, hidden, base, sems):
    width, two, kvh, size = base.shape
    groups = two * kvh
    some_width = width // chunks

    def copy(i):
        features = pl.ds(i * some_width, some_width)
        return pltpu.make_async_copy(base_hbm.at[features], base.at[features], sems.at[i])

    get_hidden = pltpu.make_async_copy(hidden_hbm, hidden, sems.at[chunks])
    for i in range(chunks):
        copy(i).start()
    get_hidden.start()

    tile = 256
    some = tile // groups
    row = lax.broadcasted_iota(jnp.int32, (tile, tile), 0)
    place = lax.broadcasted_iota(jnp.int32, (tile, tile), 1)
    order = (place == (row % some) * groups + row // some).astype(jnp.float32).astype(jnp.bfloat16)
    flat_base = base.reshape(width * groups, size)

    def arrange(f):
        at = pl.multiple_of(f * groups, tile)
        pair = jnp.concatenate([flat_base[pl.ds(at + h * tile, tile), :] for h in range(2)], axis=1)
        moved = jnp.dot(order, pair, preferred_element_type=jnp.float32).astype(jnp.bfloat16)
        for n in range(groups):
            lanes = slice((n % own) * size, (n % own + 1) * size)
            for h in range(2):
                base_ref[n // own, pl.ds(pl.multiple_of(f + h * some, some), some), lanes] = moved[
                    n * some : (n + 1) * some, h * size : (h + 1) * size
                ]

    @pl.loop(0, chunks)
    def _(i):
        copy(i).wait()
        for f in range(0, some_width, 2 * some):
            arrange(i * some_width + f)

    get_hidden.wait()
    tokens_ref[...] = hidden.reshape(tokens_ref.shape)[...]


def arrange(hidden, base, own):
    rows, steps, _ = hidden.shape
    width, two, kvh, size = base.shape
    chunks = 4
    return pl.pallas_call(
        functools.partial(arrange_kernel, chunks, own),
        out_shape=(
            pltpu.VMEM((rows * steps, width), jnp.bfloat16),
            pltpu.VMEM((two * kvh // own, width, own * size), jnp.bfloat16),
        ),
        in_specs=[pl.BlockSpec(memory_space=pltpu.HBM)] * 2,
        out_specs=(VMEM, VMEM),
        scratch_shapes=[
            pltpu.VMEM(hidden.shape, jnp.bfloat16),
            pltpu.VMEM(base.shape, jnp.bfloat16),
            pltpu.SemaphoreType.DMA((chunks + 1,)),
        ],
        compiler_params=params(20),
        cost_estimate=cost(512 * base.size, 4 * (base.size + hidden.size)),
        name="arrange",
    )(in_hbm(hidden), in_hbm(base))


def project_kernel(k, hidden_ref, base_ref, *refs):
    gathered, (out_ref, merged) = refs[:-2], refs[-2:]
    width, columns = merged.shape
    part = lax.axis_index("tp") ^ k
    parts = base_ref.shape[0] // 2
    half = columns // 2
    up = jnp.concatenate(
        [
            jnp.concatenate(
                [ref[:, pl.ds(pl.multiple_of(width + (c * parts + part) * half, 128), half)] for ref in gathered], axis=0
            )
            for c in range(2)
        ],
        axis=1,
    )
    step = 512
    for f in range(0, width, step):
        down = jnp.concatenate([ref[:, f : f + step] for ref in gathered], axis=0).T
        low_rank = jnp.dot(down, up, preferred_element_type=jnp.float32)
        for c in range(2):
            base = base_ref[c * parts + part, f : f + step, :].astype(jnp.float32)
            merged[f : f + step, c * half : (c + 1) * half] = (base + low_rank[:, c * half : (c + 1) * half]).astype(
                jnp.bfloat16
            )
    out_ref[...] = jnp.dot(hidden_ref[...], merged[...], preferred_element_type=jnp.float32)


def project(k, hidden, base, gathered):
    tokens, width = hidden.shape
    columns = 2 * base.shape[2]
    ranks = sum(g.shape[0] for g in gathered)
    return pl.pallas_call(
        functools.partial(project_kernel, k),
        out_shape=pltpu.VMEM((tokens, columns), jnp.float32),
        in_specs=[VMEM] * (2 + len(gathered)),
        out_specs=VMEM,
        scratch_shapes=[pltpu.VMEM((width, columns), jnp.bfloat16)],
        compiler_params=params(24),
        cost_estimate=cost(2 * width * columns * (tokens + ranks), 2 * width * columns + 2 * width * tokens),
        name="project",
    )(hidden, base, *gathered)


def finish_kernel(steps, heads, scale, terms, *refs):
    parts, refs = refs[:terms], refs[terms:]
    q_ref, old_ref, top_ref, total_ref = refs[:4]
    refs = refs[4:]
    fresh_hbm, context_hbm, wide, fresh_ref, context_ref, sems = refs
    rows, queries, size = context_ref.shape
    own = fresh_ref.shape[3]
    fresh = parts[0][...]
    for part in parts[1:]:
        fresh = fresh + part[...]
    keys, many = 2 * own * steps, 2 * queries
    group = size // keys
    key = lax.broadcasted_iota(jnp.int32, (keys, many), 0)
    query = lax.broadcasted_iota(jnp.int32, (keys, many), 1)
    same_head = (query % heads) // (heads // own) == key // (2 * steps)
    same_row = query // queries == (key // steps) % 2
    live = same_head & same_row & ((query % queries) // heads >= key % steps)
    nothing = jnp.zeros((keys, size), jnp.bfloat16)

    def new_lines(c, pair):
        tokens = slice(pair * 2 * steps, (pair + 1) * 2 * steps)
        lines = [fresh[tokens, (c * own + g) * size : (c * own + g + 1) * size] for g in range(own)]
        return jnp.concatenate(lines, axis=0).astype(jnp.bfloat16)

    def rows_of(ref, pair):
        return ref[2 * pair : 2 * pair + 2].reshape(many, size)

    scores = [
        lax.dot_general(new_lines(0, p), rows_of(q_ref, p), NT, preferred_element_type=jnp.float32)
        for p in range(rows // 2)
    ]
    scores = jnp.stack([jnp.where(live, s, LOW) for s in scores])
    old_top = top_ref[...]
    top = jnp.maximum(old_top, jnp.max(scores, axis=1))
    expo = jnp.exp((scores - top[:, None, :]) * scale)
    back = jnp.exp((old_top - top) * scale)
    inverse = 1.0 / (back * total_ref[...] + jnp.sum(expo, axis=1))
    weights = (expo * inverse[:, None, :]).astype(jnp.bfloat16)
    back = back * inverse

    for n in range(2 * own):
        wide[pl.ds(n, rows * steps, stride=2 * own), :] = fresh[:, n * size : (n + 1) * size]
    fresh_ref.reshape(rows * steps * 2 * own, size)[...] = wide[...].astype(jnp.bfloat16)
    puts = [pltpu.make_async_copy(fresh_ref, fresh_hbm, sems.at[0])]
    puts[0].start()

    for at in range(0, rows // 2, group):
        pairs = range(at, at + group)
        values = jnp.concatenate(
            [
                jnp.concatenate([new_lines(1, p) if n == p else nothing for n in pairs], axis=1)
                for p in pairs
            ],
            axis=0,
        )
        new = lax.dot_general(
            weights[at : at + group].reshape(group * keys, many), values, TN, preferred_element_type=jnp.float32
        )
        factors = back[at : at + group].T
        for n, p in enumerate(pairs):
            both = new[:, n * size : (n + 1) * size] + factors[:, n : n + 1] * rows_of(old_ref, p)
            context_ref[2 * p : 2 * p + 2] = both.astype(jnp.bfloat16).reshape(2, queries, size)
        mine = pl.ds(2 * at, 2 * group)
        puts.append(pltpu.make_async_copy(context_ref.at[mine], context_hbm.at[mine], sems.at[1 + at // group]))
        puts[-1].start()
    for put in puts:
        put.wait()


def finish(parts, state, steps, own):
    rows, many, size = state[0].shape
    heads = many // steps
    groups = rows * own * steps // size
    fresh = (rows, steps, 2, own, size)
    fresh, context = pl.pallas_call(
        functools.partial(finish_kernel, steps, heads, size ** (-0.5), len(parts)),
        out_shape=(
            jax.ShapeDtypeStruct(fresh, jnp.bfloat16),
            jax.ShapeDtypeStruct((rows, many, size), jnp.bfloat16),
        ),
        in_specs=[VMEM] * (len(parts) + 4),
        out_specs=(pl.BlockSpec(memory_space=pltpu.HBM),) * 2,
        scratch_shapes=[
            pltpu.VMEM((rows * steps * 2 * own, size), jnp.float32),
            pltpu.VMEM(fresh, jnp.bfloat16),
            pltpu.VMEM((rows, many, size), jnp.bfloat16),
            pltpu.SemaphoreType.DMA((1 + groups,)),
        ],
        compiler_params=params(24),
        cost_estimate=cost(rows * many * size * size * 6, 8 * rows * many * size, rows * many * size * 2),
        name="finish",
    )(*parts, *state)
    return fresh, context.reshape(rows, steps, heads, size)


def join_kernel(*refs):
    blocks, out_ref = refs[:-1], refs[-1]
    at = 0
    for block in blocks:
        out_ref[at : at + block.shape[0], :] = block[...]
        at += block.shape[0]


def join(blocks):
    rows = sum(b.shape[0] for b in blocks)
    return pl.pallas_call(
        join_kernel,
        out_shape=pltpu.VMEM((rows, blocks[0].shape[1]), jnp.bfloat16),
        in_specs=[VMEM] * len(blocks),
        out_specs=VMEM,
        compiler_params=params(8),
        name="join",
    )(*blocks)


def gather_second(factor_a, factor_b, dp):
    count = dp // 2
    ranks = factor_b.shape[0]
    if ranks % 8 == 0 and count in (1, 2, 4):
        payload = make_payload(factor_a.T, factor_b)
        return [payload] + [lax.ppermute(payload, "dp", [(i, i ^ (2 * k)) for i in range(dp)]) for k in range(1, count)]
    payload = jnp.concatenate([factor_a.T, factor_b.reshape(ranks, -1)], axis=1)
    groups = [[i for i in range(dp) if i % 2 == n] for n in range(2)]
    copies = jnp.broadcast_to(payload[None], (count,) + payload.shape)
    blocks = lax.all_to_all(copies, "dp", 0, 0, axis_index_groups=groups, tiled=True)
    return [blocks.reshape(count * ranks, payload.shape[1])]


def shards(dp, tp, hidden, base_weight, factor_a, factor_b, queries, cache, lengths):
    steps, own = queries.shape[1], cache.shape[3]
    assert dp % 2 == 0
    blocks = gather_second(factor_a, factor_b, dp)
    state = attend_cached(queries, cache, lengths)
    blocks, state, hidden, base_weight = lax.optimization_barrier((blocks, state, hidden, base_weight))
    gathered = join(blocks) if len(blocks) > 1 else blocks[0]
    gathered = [gathered, lax.ppermute(gathered, "dp", [(i, i ^ 1) for i in range(dp)])]
    tokens, base = arrange(hidden, base_weight, own)
    received = []
    for k in range(1, tp):
        other = project(k, tokens, base, gathered)
        received.append(lax.ppermute(other, "tp", [(i, i ^ k) for i in range(tp)]))
    mine = project(0, tokens, base, gathered)
    return finish([mine] + received, state, steps, own)


def solution(mesh):
    return jax.shard_map(
        functools.partial(shards, mesh.shape["dp"], mesh.shape["tp"]),
        mesh=mesh,
        in_specs=(
            P(("parts", "dp"), None, "tp"),
            P("tp", None, None, None),
            P(("parts", "tp"), "dp"),
            P(("parts", "dp"), None, None, None),
            P(("parts", "dp"), None, "tp", None),
            P(("parts", "dp"), None, None, "tp", None),
            P(("parts", "dp")),
        ),
        out_specs=(
            P(("parts", "dp"), None, None, "tp", None),
            P(("parts", "dp"), None, "tp", None),
        ),
        check_vma=False,
    )
```

```python
import functools

import jax
import jax.numpy as jnp
from jax import lax
from jax.experimental import pallas as pl
from jax.experimental.pallas import tpu as pltpu
from jax.sharding import PartitionSpec as P

LOW = -1e30
NT = (((1,), (1,)), ((), ()))
TN = (((0,), (0,)), ((), ()))
VMEM = pl.BlockSpec(memory_space=pltpu.VMEM)


def params(mib):
    return pltpu.CompilerParams(vmem_limit_bytes=mib * 1024 * 1024)


def in_hbm(x):
    return pltpu.with_memory_space_constraint(x, pltpu.HBM)


def cost(flops, moved, exps=0):
    return pl.CostEstimate(flops=flops, bytes_accessed=moved, transcendentals=exps)


def payload_kernel(down_hbm, up_hbm, out_ref, ups, wide, sems):
    ranks, width = down_hbm.shape
    groups, size = ups.shape[1] * ups.shape[2], ups.shape[3]
    get_down = pltpu.make_async_copy(down_hbm, out_ref.at[:, pl.ds(0, width)], sems.at[0])
    get_up = pltpu.make_async_copy(up_hbm, ups, sems.at[1])
    get_up.start()
    get_down.start()
    get_up.wait()
    wide[...] = ups.reshape(ranks * groups, size)[...].astype(jnp.float32)
    for n in range(groups):
        out_ref[:, width + n * size : width + (n + 1) * size] = wide[pl.ds(n, ranks, stride=groups), :].astype(
            jnp.bfloat16
        )
    get_down.wait()


def make_payload(down, up):
    ranks, width = down.shape
    groups, size = up.shape[1] * up.shape[2], up.shape[3]
    return pl.pallas_call(
        payload_kernel,
        out_shape=pltpu.VMEM((ranks, width + groups * size), jnp.bfloat16),
        in_specs=[pl.BlockSpec(memory_space=pltpu.HBM)] * 2,
        out_specs=VMEM,
        scratch_shapes=[
            pltpu.VMEM(up.shape, jnp.bfloat16),
            pltpu.VMEM((ranks * groups, size), jnp.float32),
            pltpu.SemaphoreType.DMA((2,)),
        ],
        compiler_params=params(8),
        name="payload",
    )(in_hbm(down), in_hbm(up))


class Cached:
    def __init__(self, first, chunk, heads, scale, inputs, outputs, scratch):
        self.first, self.chunk, self.heads, self.scale = first, chunk, heads, scale
        self.lengths_hbm, self.queries_hbm, self.cache_hbm = inputs
        self.q, self.sums, self.tops, self.totals = outputs
        self.lengths, self.k, self.v, *rest = scratch
        self.scores, self.weights = rest[0:2], rest[2:4]
        self.sems, self.length_sem = rest[4:]
        self.rows, self.queries, self.size = self.q.shape
        self.slots, self.own = self.k.shape[1:3]
        self.keys = self.slots * self.own
        own, queries = self.own, self.queries
        line = lax.broadcasted_iota(jnp.int32, (self.keys, 2 * queries), 0)
        query = lax.broadcasted_iota(jnp.int32, (self.keys, 2 * queries), 1)
        self.line = jnp.where(line % own == (query % heads) // (heads // own), line, self.keys)
        self.one = lax.broadcasted_iota(jnp.int32, (1, 2 * queries), 1) < queries
        self.nothing = jnp.zeros((queries, self.size), jnp.bfloat16)

    @staticmethod
    def outputs(rows, many, size):
        return (
            pltpu.VMEM((rows, many, size), jnp.bfloat16),
            pltpu.VMEM((rows, many, size), jnp.float32),
            pltpu.VMEM((rows // 2, 2 * many), jnp.float32),
            pltpu.VMEM((rows // 2, 2 * many), jnp.float32),
        )

    @staticmethod
    def scratch(rows, chunk, many, cache, lengths):
        slots, own, size = cache.shape[1], cache.shape[3], cache.shape[4]
        half = (rows, slots, own, size)
        scores = (chunk // 2, slots * own, 2 * many)
        return [
            pltpu.SMEM(lengths.shape, jnp.int32),
            pltpu.VMEM(half, jnp.bfloat16),
            pltpu.VMEM(half, jnp.bfloat16),
            pltpu.VMEM(scores, jnp.float32),
            pltpu.VMEM(scores, jnp.float32),
            pltpu.VMEM(scores, jnp.bfloat16),
            pltpu.VMEM(scores, jnp.bfloat16),
            pltpu.SemaphoreType.DMA((rows // chunk, 3)),
            pltpu.SemaphoreType.DMA,
        ]

    def copies(self, i):
        mine, theirs = pl.ds(i * self.chunk, self.chunk), pl.ds(self.first + i * self.chunk, self.chunk)
        pairs = (
            (self.queries_hbm.at[theirs], self.q.at[mine]),
            (self.cache_hbm.at[theirs, :, 0], self.k.at[mine]),
            (self.cache_hbm.at[theirs, :, 1], self.v.at[mine]),
        )
        return [pltpu.make_async_copy(a, b, self.sems.at[i, n]) for n, (a, b) in enumerate(pairs)]

    def lengths_copy(self):
        return pltpu.make_async_copy(self.lengths_hbm, self.lengths, self.length_sem)

    def start(self, i):
        for copy in self.copies(i):
            copy.start()

    def arrive(self, i):
        for copy in self.copies(i):
            copy.wait()

    def lines(self, ref, r):
        flat = ref.reshape(self.rows, self.keys, self.size)
        return jnp.concatenate([flat[r], flat[r + 1]], axis=1)

    def score(self, i, slot):
        for p in range(self.chunk // 2):
            r = i * self.chunk + 2 * p
            both_q = jnp.concatenate(
                [
                    jnp.concatenate([self.q[r], self.nothing], axis=1),
                    jnp.concatenate([self.nothing, self.q[r + 1]], axis=1),
                ],
                axis=0,
            )
            self.scores[slot][p] = lax.dot_general(
                self.lines(self.k, r), both_q, NT, preferred_element_type=jnp.float32
            )

    def soften(self, i, slot):
        for p in range(self.chunk // 2):
            r = self.first + i * self.chunk + 2 * p
            limit = jnp.where(self.one, self.own * self.lengths[r], self.own * self.lengths[r + 1])
            scores = jnp.where(self.line < limit, self.scores[slot][p], LOW)
            top = jnp.max(scores, axis=0, keepdims=True)
            expo = jnp.exp((scores - top) * self.scale)
            self.weights[slot][p] = expo.astype(jnp.bfloat16)
            pair = pl.ds(i * (self.chunk // 2) + p, 1)
            self.tops[pair, :] = top
            self.totals[pair, :] = jnp.sum(expo, axis=0, keepdims=True)

    def collect(self, i, slot):
        queries, size = self.queries, self.size
        for p in range(self.chunk // 2):
            r = i * self.chunk + 2 * p
            both = lax.dot_general(
                self.weights[slot][p], self.lines(self.v, r), TN, preferred_element_type=jnp.float32
            )
            for h in range(2):
                self.sums[r + h] = both[h * queries : (h + 1) * queries, h * size : (h + 1) * size]


def cached_kernel(chunk, heads, scale, *refs):
    cached = Cached(0, chunk, heads, scale, refs[:3], refs[3:7], refs[7:])
    chunks = cached.rows // chunk
    cached.lengths_copy().start()
    for i in range(chunks):
        cached.start(i)
    cached.lengths_copy().wait()
    cached.arrive(0)
    cached.score(0, 0)
    cached.arrive(1)
    cached.score(1, 1)
    cached.soften(0, 0)

    @pl.loop(1, chunks // 2)
    def _(t):
        for slot in range(2):
            i = 2 * t + slot
            cached.arrive(i)
            cached.score(i, slot)
            cached.soften(i - 1, 1 - slot)
            cached.collect(i - 2, slot)

    cached.soften(chunks - 1, 1)
    cached.collect(chunks - 2, 0)
    cached.collect(chunks - 1, 1)


def attend_cached(queries, cache, lengths):
    rows, steps, heads, size = queries.shape
    slots, own = cache.shape[1], cache.shape[3]
    many = steps * heads
    chunk = 6
    return pl.pallas_call(
        functools.partial(cached_kernel, chunk, heads, size ** (-0.5)),
        out_shape=Cached.outputs(rows, many, size),
        in_specs=[pl.BlockSpec(memory_space=pltpu.HBM)] * 3,
        out_specs=(VMEM,) * 4,
        scratch_shapes=Cached.scratch(rows, chunk, many, cache, lengths),
        compiler_params=params(28),
        cost_estimate=cost(
            8 * rows * many * slots * size, 4 * rows * slots * own * size, rows * many * slots * own
        ),
        name="attend_cached",
    )(*map(in_hbm, (lengths, queries.reshape(-1, many, size), cache)))


def arrange_kernel(chunks, own, hidden_hbm, base_hbm, tokens_ref, base_ref, hidden, base, sems):
    width, two, kvh, size = base.shape
    groups = two * kvh
    some_width = width // chunks

    def copy(i):
        features = pl.ds(i * some_width, some_width)
        return pltpu.make_async_copy(base_hbm.at[features], base.at[features], sems.at[i])

    get_hidden = pltpu.make_async_copy(hidden_hbm, hidden, sems.at[chunks])
    for i in range(chunks):
        copy(i).start()
    get_hidden.start()

    tile = 256
    some = tile // groups
    row = lax.broadcasted_iota(jnp.int32, (tile, tile), 0)
    place = lax.broadcasted_iota(jnp.int32, (tile, tile), 1)
    order = (place == (row % some) * groups + row // some).astype(jnp.float32).astype(jnp.bfloat16)
    flat_base = base.reshape(width * groups, size)

    def arrange(f):
        at = pl.multiple_of(f * groups, tile)
        pair = jnp.concatenate([flat_base[pl.ds(at + h * tile, tile), :] for h in range(2)], axis=1)
        moved = jnp.dot(order, pair, preferred_element_type=jnp.float32).astype(jnp.bfloat16)
        for n in range(groups):
            lanes = slice((n % own) * size, (n % own + 1) * size)
            for h in range(2):
                base_ref[n // own, pl.ds(pl.multiple_of(f + h * some, some), some), lanes] = moved[
                    n * some : (n + 1) * some, h * size : (h + 1) * size
                ]

    @pl.loop(0, chunks)
    def _(i):
        copy(i).wait()
        for f in range(0, some_width, 2 * some):
            arrange(i * some_width + f)

    get_hidden.wait()
    tokens_ref[...] = hidden.reshape(tokens_ref.shape)[...]


def arrange(hidden, base, own):
    rows, steps, _ = hidden.shape
    width, two, kvh, size = base.shape
    chunks = 4
    return pl.pallas_call(
        functools.partial(arrange_kernel, chunks, own),
        out_shape=(
            pltpu.VMEM((rows * steps, width), jnp.bfloat16),
            pltpu.VMEM((two * kvh // own, width, own * size), jnp.bfloat16),
        ),
        in_specs=[pl.BlockSpec(memory_space=pltpu.HBM)] * 2,
        out_specs=(VMEM, VMEM),
        scratch_shapes=[
            pltpu.VMEM(hidden.shape, jnp.bfloat16),
            pltpu.VMEM(base.shape, jnp.bfloat16),
            pltpu.SemaphoreType.DMA((chunks + 1,)),
        ],
        compiler_params=params(20),
        cost_estimate=cost(512 * base.size, 4 * (base.size + hidden.size)),
        name="arrange",
    )(in_hbm(hidden), in_hbm(base))


def project_kernel(k, hidden_ref, base_ref, *refs):
    gathered, (out_ref, merged) = refs[:-2], refs[-2:]
    width, columns = merged.shape
    part = lax.axis_index("tp") ^ k
    parts = base_ref.shape[0] // 2
    half = columns // 2
    up = jnp.concatenate(
        [
            jnp.concatenate(
                [ref[:, pl.ds(pl.multiple_of(width + (c * parts + part) * half, 128), half)] for ref in gathered], axis=0
            )
            for c in range(2)
        ],
        axis=1,
    )
    step = 512
    for f in range(0, width, step):
        down = jnp.concatenate([ref[:, f : f + step] for ref in gathered], axis=0).T
        low_rank = jnp.dot(down, up, preferred_element_type=jnp.float32)
        for c in range(2):
            base = base_ref[c * parts + part, f : f + step, :].astype(jnp.float32)
            merged[f : f + step, c * half : (c + 1) * half] = (base + low_rank[:, c * half : (c + 1) * half]).astype(
                jnp.bfloat16
            )
    out_ref[...] = jnp.dot(hidden_ref[...], merged[...], preferred_element_type=jnp.float32)


def project(k, hidden, base, gathered):
    tokens, width = hidden.shape
    columns = 2 * base.shape[2]
    ranks = sum(g.shape[0] for g in gathered)
    return pl.pallas_call(
        functools.partial(project_kernel, k),
        out_shape=pltpu.VMEM((tokens, columns), jnp.float32),
        in_specs=[VMEM] * (2 + len(gathered)),
        out_specs=VMEM,
        scratch_shapes=[pltpu.VMEM((width, columns), jnp.bfloat16)],
        compiler_params=params(24),
        cost_estimate=cost(2 * width * columns * (tokens + ranks), 2 * width * columns + 2 * width * tokens),
        name="project",
    )(hidden, base, *gathered)


def finish_kernel(steps, heads, scale, terms, *refs):
    parts, refs = refs[:terms], refs[terms:]
    q_ref, old_ref, top_ref, total_ref = refs[:4]
    refs = refs[4:]
    fresh_hbm, context_hbm, wide, fresh_ref, context_ref, sems = refs
    rows, queries, size = context_ref.shape
    own = fresh_ref.shape[3]
    fresh = parts[0][...]
    for part in parts[1:]:
        fresh = fresh + part[...]
    keys, many = 2 * own * steps, 2 * queries
    group = size // keys
    key = lax.broadcasted_iota(jnp.int32, (keys, many), 0)
    query = lax.broadcasted_iota(jnp.int32, (keys, many), 1)
    same_head = (query % heads) // (heads // own) == key // (2 * steps)
    same_row = query // queries == (key // steps) % 2
    live = same_head & same_row & ((query % queries) // heads >= key % steps)
    nothing = jnp.zeros((keys, size), jnp.bfloat16)

    def new_lines(c, pair):
        tokens = slice(pair * 2 * steps, (pair + 1) * 2 * steps)
        lines = [fresh[tokens, (c * own + g) * size : (c * own + g + 1) * size] for g in range(own)]
        return jnp.concatenate(lines, axis=0).astype(jnp.bfloat16)

    def rows_of(ref, pair):
        return ref[2 * pair : 2 * pair + 2].reshape(many, size)

    scores = [
        lax.dot_general(new_lines(0, p), rows_of(q_ref, p), NT, preferred_element_type=jnp.float32)
        for p in range(rows // 2)
    ]
    scores = jnp.stack([jnp.where(live, s, LOW) for s in scores])
    old_top = top_ref[...]
    top = jnp.maximum(old_top, jnp.max(scores, axis=1))
    expo = jnp.exp((scores - top[:, None, :]) * scale)
    back = jnp.exp((old_top - top) * scale)
    inverse = 1.0 / (back * total_ref[...] + jnp.sum(expo, axis=1))
    weights = (expo * inverse[:, None, :]).astype(jnp.bfloat16)
    back = back * inverse

    for n in range(2 * own):
        wide[pl.ds(n, rows * steps, stride=2 * own), :] = fresh[:, n * size : (n + 1) * size]
    fresh_ref.reshape(rows * steps * 2 * own, size)[...] = wide[...].astype(jnp.bfloat16)
    puts = [pltpu.make_async_copy(fresh_ref, fresh_hbm, sems.at[0])]
    puts[0].start()

    for at in range(0, rows // 2, group):
        pairs = range(at, at + group)
        values = jnp.concatenate(
            [
                jnp.concatenate([new_lines(1, p) if n == p else nothing for n in pairs], axis=1)
                for p in pairs
            ],
            axis=0,
        )
        new = lax.dot_general(
            weights[at : at + group].reshape(group * keys, many), values, TN, preferred_element_type=jnp.float32
        )
        factors = back[at : at + group].T
        for n, p in enumerate(pairs):
            both = new[:, n * size : (n + 1) * size] + factors[:, n : n + 1] * rows_of(old_ref, p)
            context_ref[2 * p : 2 * p + 2] = both.astype(jnp.bfloat16).reshape(2, queries, size)
        mine = pl.ds(2 * at, 2 * group)
        puts.append(pltpu.make_async_copy(context_ref.at[mine], context_hbm.at[mine], sems.at[1 + at // group]))
        puts[-1].start()
    for put in puts:
        put.wait()


def finish(parts, state, steps, own):
    rows, many, size = state[0].shape
    heads = many // steps
    groups = rows * own * steps // size
    fresh = (rows, steps, 2, own, size)
    fresh, context = pl.pallas_call(
        functools.partial(finish_kernel, steps, heads, size ** (-0.5), len(parts)),
        out_shape=(
            jax.ShapeDtypeStruct(fresh, jnp.bfloat16),
            jax.ShapeDtypeStruct((rows, many, size), jnp.bfloat16),
        ),
        in_specs=[VMEM] * (len(parts) + 4),
        out_specs=(pl.BlockSpec(memory_space=pltpu.HBM),) * 2,
        scratch_shapes=[
            pltpu.VMEM((rows * steps * 2 * own, size), jnp.float32),
            pltpu.VMEM(fresh, jnp.bfloat16),
            pltpu.VMEM((rows, many, size), jnp.bfloat16),
            pltpu.SemaphoreType.DMA((1 + groups,)),
        ],
        compiler_params=params(24),
        cost_estimate=cost(rows * many * size * size * 6, 8 * rows * many * size, rows * many * size * 2),
        name="finish",
    )(*parts, *state)
    return fresh, context.reshape(rows, steps, heads, size)


def join_kernel(*refs):
    blocks, out_ref = refs[:-1], refs[-1]
    at = 0
    for block in blocks:
        out_ref[at : at + block.shape[0], :] = block[...]
        at += block.shape[0]


def join(blocks):
    rows = sum(b.shape[0] for b in blocks)
    return pl.pallas_call(
        join_kernel,
        out_shape=pltpu.VMEM((rows, blocks[0].shape[1]), jnp.bfloat16),
        in_specs=[VMEM] * len(blocks),
        out_specs=VMEM,
        compiler_params=params(8),
        name="join",
    )(*blocks)


def gather_second(factor_a, factor_b, dp):
    count = dp // 2
    ranks = factor_b.shape[0]
    if ranks % 8 == 0 and count in (1, 2, 4):
        payload = make_payload(factor_a.T, factor_b)
        return [payload] + [lax.ppermute(payload, "dp", [(i, i ^ (2 * k)) for i in range(dp)]) for k in range(1, count)]
    payload = jnp.concatenate([factor_a.T, factor_b.reshape(ranks, -1)], axis=1)
    groups = [[i for i in range(dp) if i % 2 == n] for n in range(2)]
    copies = jnp.broadcast_to(payload[None], (count,) + payload.shape)
    blocks = lax.all_to_all(copies, "dp", 0, 0, axis_index_groups=groups, tiled=True)
    return [blocks.reshape(count * ranks, payload.shape[1])]


def shards(dp, tp, hidden, base_weight, factor_a, factor_b, queries, cache, lengths):
    steps, own = queries.shape[1], cache.shape[3]
    assert dp % 2 == 0
    blocks = gather_second(factor_a, factor_b, dp)
    tokens, base = arrange(hidden, base_weight, own)
    blocks, tokens, base, cache = lax.optimization_barrier((blocks, tokens, base, cache))
    gathered = join(blocks) if len(blocks) > 1 else blocks[0]
    gathered = [gathered, lax.ppermute(gathered, "dp", [(i, i ^ 1) for i in range(dp)])]
    state = attend_cached(queries, cache, lengths)
    received = []
    for k in range(1, tp):
        other = project(k, tokens, base, gathered)
        received.append(lax.ppermute(other, "tp", [(i, i ^ k) for i in range(tp)]))
    mine = project(0, tokens, base, gathered)
    return finish([mine] + received, state, steps, own)


def solution(mesh):
    return jax.shard_map(
        functools.partial(shards, mesh.shape["dp"], mesh.shape["tp"]),
        mesh=mesh,
        in_specs=(
            P(("parts", "dp"), None, "tp"),
            P("tp", None, None, None),
            P(("parts", "tp"), "dp"),
            P(("parts", "dp"), None, None, None),
            P(("parts", "dp"), None, "tp", None),
            P(("parts", "dp"), None, None, "tp", None),
            P(("parts", "dp")),
        ),
        out_specs=(
            P(("parts", "dp"), None, None, "tp", None),
            P(("parts", "dp"), None, "tp", None),
        ),
        check_vma=False,
    )
```

```python
import functools

import jax
import jax.numpy as jnp
from jax import lax
from jax.experimental import pallas as pl
from jax.experimental.pallas import tpu as pltpu
from jax.sharding import PartitionSpec as P

LOW = -1e30
NT = (((1,), (1,)), ((), ()))
TN = (((0,), (0,)), ((), ()))
VMEM = pl.BlockSpec(memory_space=pltpu.VMEM)


def params(mib):
    return pltpu.CompilerParams(vmem_limit_bytes=mib * 1024 * 1024)


def in_hbm(x):
    return pltpu.with_memory_space_constraint(x, pltpu.HBM)


def in_vmem(x):
    return pltpu.with_memory_space_constraint(x, pltpu.VMEM)


def cost(flops, moved, exps=0):
    return pl.CostEstimate(flops=flops, bytes_accessed=moved, transcendentals=exps)


def payload_kernel(down_hbm, up_hbm, out_ref, ups, wide, sems):
    ranks, width = down_hbm.shape
    groups, size = ups.shape[1] * ups.shape[2], ups.shape[3]
    get_down = pltpu.make_async_copy(down_hbm, out_ref.at[:, pl.ds(0, width)], sems.at[0])
    get_up = pltpu.make_async_copy(up_hbm, ups, sems.at[1])
    get_up.start()
    get_down.start()
    get_up.wait()
    wide[...] = ups.reshape(ranks * groups, size)[...].astype(jnp.float32)
    for n in range(groups):
        out_ref[:, width + n * size : width + (n + 1) * size] = wide[pl.ds(n, ranks, stride=groups), :].astype(
            jnp.bfloat16
        )
    get_down.wait()


def make_payload(down, up):
    ranks, width = down.shape
    groups, size = up.shape[1] * up.shape[2], up.shape[3]
    return pl.pallas_call(
        payload_kernel,
        out_shape=pltpu.VMEM((ranks, width + groups * size), jnp.bfloat16),
        in_specs=[pl.BlockSpec(memory_space=pltpu.HBM)] * 2,
        out_specs=VMEM,
        scratch_shapes=[
            pltpu.VMEM(up.shape, jnp.bfloat16),
            pltpu.VMEM((ranks * groups, size), jnp.float32),
            pltpu.SemaphoreType.DMA((2,)),
        ],
        compiler_params=params(8),
        name="payload",
    )(in_hbm(down), in_hbm(up))


def cache_copies(cache_hbm, k, v, sems, i, chunk):
    mine = pl.ds(i * chunk, chunk)
    return [pltpu.make_async_copy(cache_hbm.at[mine, :, n], ref.at[mine], sems.at[i, n]) for n, ref in enumerate((k, v))]


class Cached:
    def __init__(self, chunk, heads, scale, inputs, outputs, scratch):
        self.chunk, self.heads, self.scale = chunk, heads, scale
        self.lengths_hbm, self.cache_hbm, self.q = inputs
        self.k, self.v, self.sums, self.tops, self.totals = outputs
        self.lengths, *rest = scratch
        self.scores, self.weights = rest[0:2], rest[2:4]
        self.sems, self.length_sem = rest[4:]
        self.rows, self.queries, self.size = self.q.shape
        self.slots, self.own = self.k.shape[1:3]
        self.keys = self.slots * self.own
        own, queries = self.own, self.queries
        line = lax.broadcasted_iota(jnp.int32, (self.keys, 2 * queries), 0)
        query = lax.broadcasted_iota(jnp.int32, (self.keys, 2 * queries), 1)
        self.line = jnp.where(line % own == (query % heads) // (heads // own), line, self.keys)
        self.one = lax.broadcasted_iota(jnp.int32, (1, 2 * queries), 1) < queries
        self.nothing = jnp.zeros((queries, self.size), jnp.bfloat16)

    def copies(self, i):
        return cache_copies(self.cache_hbm, self.k, self.v, self.sems, i, self.chunk)

    def lengths_copy(self):
        return pltpu.make_async_copy(self.lengths_hbm, self.lengths, self.length_sem)

    def start(self, i):
        for copy in self.copies(i):
            copy.start()

    def arrive(self, i):
        for copy in self.copies(i):
            copy.wait()

    def lines(self, ref, r):
        flat = ref.reshape(self.rows, self.keys, self.size)
        return jnp.concatenate([flat[r], flat[r + 1]], axis=1)

    def score(self, i, slot):
        for p in range(self.chunk // 2):
            r = i * self.chunk + 2 * p
            both_q = jnp.concatenate(
                [
                    jnp.concatenate([self.q[r], self.nothing], axis=1),
                    jnp.concatenate([self.nothing, self.q[r + 1]], axis=1),
                ],
                axis=0,
            )
            self.scores[slot][p] = lax.dot_general(
                self.lines(self.k, r), both_q, NT, preferred_element_type=jnp.float32
            )

    def soften(self, i, slot):
        for p in range(self.chunk // 2):
            r = i * self.chunk + 2 * p
            limit = jnp.where(self.one, self.own * self.lengths[r], self.own * self.lengths[r + 1])
            scores = jnp.where(self.line < limit, self.scores[slot][p], LOW)
            top = jnp.max(scores, axis=0, keepdims=True)
            expo = jnp.exp((scores - top) * self.scale)
            self.weights[slot][p] = expo.astype(jnp.bfloat16)
            pair = pl.ds(i * (self.chunk // 2) + p, 1)
            self.tops[pair, :] = top
            self.totals[pair, :] = jnp.sum(expo, axis=0, keepdims=True)

    def collect(self, i, slot):
        queries, size = self.queries, self.size
        for p in range(self.chunk // 2):
            r = i * self.chunk + 2 * p
            both = lax.dot_general(
                self.weights[slot][p], self.lines(self.v, r), TN, preferred_element_type=jnp.float32
            )
            for h in range(2):
                self.sums[r + h] = both[h * queries : (h + 1) * queries, h * size : (h + 1) * size]


def cached_kernel(chunk, early, heads, scale, *refs):
    cached = Cached(chunk, heads, scale, refs[:3], refs[5:10], refs[10:])
    chunks = cached.rows // chunk
    cached.lengths_copy().start()
    for i in range(early, chunks):
        cached.start(i)
    cached.lengths_copy().wait()
    cached.score(0, 0)
    cached.score(1, 1)
    cached.soften(0, 0)

    @pl.loop(1, chunks // 2)
    def _(t):
        for slot in range(2):
            i = 2 * t + slot

            @pl.when(i >= early)
            def _():
                cached.arrive(i)

            cached.score(i, slot)
            cached.soften(i - 1, 1 - slot)
            cached.collect(i - 2, slot)

    cached.soften(chunks - 1, 1)
    cached.collect(chunks - 2, 0)
    cached.collect(chunks - 1, 1)


def attend_cached(queries, cache, lengths, keys, values, steps, chunk, early):
    rows, many, size = queries.shape
    slots, own = cache.shape[1], cache.shape[3]
    heads = many // steps
    half = (rows, slots, own, size)
    scores = (chunk // 2, slots * own, 2 * many)
    line = (rows // 2, 2 * many)
    outs = (
        pltpu.VMEM(half, jnp.bfloat16),
        pltpu.VMEM(half, jnp.bfloat16),
        pltpu.VMEM((rows, many, size), jnp.float32),
        pltpu.VMEM(line, jnp.float32),
        pltpu.VMEM(line, jnp.float32),
    )
    _, _, *state = pl.pallas_call(
        functools.partial(cached_kernel, chunk, early, heads, size ** (-0.5)),
        out_shape=outs,
        in_specs=[pl.BlockSpec(memory_space=pltpu.HBM)] * 2 + [VMEM] * 3,
        out_specs=(VMEM,) * len(outs),
        scratch_shapes=[
            pltpu.SMEM(lengths.shape, jnp.int32),
            pltpu.VMEM(scores, jnp.float32),
            pltpu.VMEM(scores, jnp.float32),
            pltpu.VMEM(scores, jnp.bfloat16),
            pltpu.VMEM(scores, jnp.bfloat16),
            pltpu.SemaphoreType.DMA((rows // chunk, 2)),
            pltpu.SemaphoreType.DMA,
        ],
        input_output_aliases={3: 0, 4: 1},
        compiler_params=params(16),
        cost_estimate=cost(8 * rows * many * slots * size, 4 * rows * slots * own * size, rows * many * slots * own),
        name="attend_cached",
    )(in_hbm(lengths), in_hbm(cache), in_vmem(queries), keys, values)
    return [queries, *state]


def arrange_kernel(chunks, chunk, early, *refs):
    cache_hbm, hidden_hbm, base_hbm, tokens_ref, base_ref, k, v, hidden, base, base_sems, sems = refs
    width, two, kvh, size = base.shape
    own = k.shape[2]
    groups = two * kvh
    some_width = width // chunks
    copies = [copy for i in range(early) for copy in cache_copies(cache_hbm, k, v, sems, i, chunk)]
    get_hidden = pltpu.make_async_copy(hidden_hbm, hidden, base_sems.at[chunks])

    def get_base(i):
        features = pl.ds(i * some_width, some_width)
        return pltpu.make_async_copy(base_hbm.at[features], base.at[features], base_sems.at[i])

    for i in range(chunks):
        get_base(i).start()
    get_hidden.start()
    for copy in copies:
        copy.start()

    tile = 256
    some = tile // groups
    row = lax.broadcasted_iota(jnp.int32, (tile, tile), 0)
    place = lax.broadcasted_iota(jnp.int32, (tile, tile), 1)
    order = (place == (row % some) * groups + row // some).astype(jnp.float32).astype(jnp.bfloat16)
    flat_base = base.reshape(width * groups, size)

    def arrange(f):
        at = pl.multiple_of(f * groups, tile)
        pair = jnp.concatenate([flat_base[pl.ds(at + h * tile, tile), :] for h in range(2)], axis=1)
        moved = jnp.dot(order, pair, preferred_element_type=jnp.float32).astype(jnp.bfloat16)
        for n in range(groups):
            lanes = slice((n % own) * size, (n % own + 1) * size)
            for h in range(2):
                base_ref[n // own, pl.ds(pl.multiple_of(f + h * some, some), some), lanes] = moved[
                    n * some : (n + 1) * some, h * size : (h + 1) * size
                ]

    @pl.loop(0, chunks)
    def _(i):
        get_base(i).wait()
        for f in range(0, some_width, 2 * some):
            arrange(i * some_width + f)

    get_hidden.wait()
    tokens_ref[...] = hidden.reshape(tokens_ref.shape)[...]
    for copy in copies:
        copy.wait()


def arrange(hidden, base, cache, chunk, early):
    rows, steps, _ = hidden.shape
    slots, own = cache.shape[1], cache.shape[3]
    width, two, kvh, size = base.shape
    half = pltpu.VMEM((rows, slots, own, size), jnp.bfloat16)
    chunks = 4
    outs = (
        pltpu.VMEM((rows * steps, width), jnp.bfloat16),
        pltpu.VMEM((two * kvh // own, width, own * size), jnp.bfloat16),
        half,
        half,
    )
    return pl.pallas_call(
        functools.partial(arrange_kernel, chunks, chunk, early),
        out_shape=outs,
        in_specs=[pl.BlockSpec(memory_space=pltpu.HBM)] * 3,
        out_specs=(VMEM,) * len(outs),
        scratch_shapes=[
            pltpu.VMEM(hidden.shape, jnp.bfloat16),
            pltpu.VMEM(base.shape, jnp.bfloat16),
            pltpu.SemaphoreType.DMA((chunks + 1,)),
            pltpu.SemaphoreType.DMA((early, 2)),
        ],
        compiler_params=params(16),
        cost_estimate=cost(512 * base.size, 4 * (base.size + hidden.size)),
        name="arrange",
    )(in_hbm(cache), in_hbm(hidden), in_hbm(base))


def project_kernel(k, hidden_ref, base_ref, *refs):
    gathered, (out_ref, merged) = refs[:-2], refs[-2:]
    width, columns = merged.shape
    part = lax.axis_index("tp") ^ k
    parts = base_ref.shape[0] // 2
    half = columns // 2
    up = jnp.concatenate(
        [
            jnp.concatenate(
                [ref[:, pl.ds(pl.multiple_of(width + (c * parts + part) * half, 128), half)] for ref in gathered], axis=0
            )
            for c in range(2)
        ],
        axis=1,
    )
    step = 512
    for f in range(0, width, step):
        down = jnp.concatenate([ref[:, f : f + step] for ref in gathered], axis=0).T
        low_rank = jnp.dot(down, up, preferred_element_type=jnp.float32)
        for c in range(2):
            base = base_ref[c * parts + part, f : f + step, :].astype(jnp.float32)
            merged[f : f + step, c * half : (c + 1) * half] = (base + low_rank[:, c * half : (c + 1) * half]).astype(
                jnp.bfloat16
            )
    out_ref[...] = jnp.dot(hidden_ref[...], merged[...], preferred_element_type=jnp.float32)


def project(k, hidden, base, gathered):
    tokens, width = hidden.shape
    columns = 2 * base.shape[2]
    ranks = sum(g.shape[0] for g in gathered)
    return pl.pallas_call(
        functools.partial(project_kernel, k),
        out_shape=pltpu.VMEM((tokens, columns), jnp.float32),
        in_specs=[VMEM] * (2 + len(gathered)),
        out_specs=VMEM,
        scratch_shapes=[pltpu.VMEM((width, columns), jnp.bfloat16)],
        compiler_params=params(24),
        cost_estimate=cost(2 * width * columns * (tokens + ranks), 2 * width * columns + 2 * width * tokens),
        name="project",
    )(hidden, base, *gathered)


def finish_kernel(steps, heads, scale, terms, *refs):
    parts, refs = refs[:terms], refs[terms:]
    q_ref, old_ref, top_ref, total_ref = refs[:4]
    refs = refs[4:]
    fresh_hbm, context_hbm, wide, fresh_ref, context_ref, sems = refs
    rows, queries, size = context_ref.shape
    own = fresh_ref.shape[3]
    fresh = parts[0][...]
    for part in parts[1:]:
        fresh = fresh + part[...]
    keys, many = 2 * own * steps, 2 * queries
    group = size // keys
    key = lax.broadcasted_iota(jnp.int32, (keys, many), 0)
    query = lax.broadcasted_iota(jnp.int32, (keys, many), 1)
    same_head = (query % heads) // (heads // own) == key // (2 * steps)
    same_row = query // queries == (key // steps) % 2
    live = same_head & same_row & ((query % queries) // heads >= key % steps)
    nothing = jnp.zeros((keys, size), jnp.bfloat16)

    def new_lines(c, pair):
        tokens = slice(pair * 2 * steps, (pair + 1) * 2 * steps)
        lines = [fresh[tokens, (c * own + g) * size : (c * own + g + 1) * size] for g in range(own)]
        return jnp.concatenate(lines, axis=0).astype(jnp.bfloat16)

    def rows_of(ref, pair):
        return ref[2 * pair : 2 * pair + 2].reshape(many, size)

    scores = [
        lax.dot_general(new_lines(0, p), rows_of(q_ref, p), NT, preferred_element_type=jnp.float32)
        for p in range(rows // 2)
    ]
    scores = jnp.stack([jnp.where(live, s, LOW) for s in scores])
    old_top = top_ref[...]
    top = jnp.maximum(old_top, jnp.max(scores, axis=1))
    expo = jnp.exp((scores - top[:, None, :]) * scale)
    back = jnp.exp((old_top - top) * scale)
    inverse = 1.0 / (back * total_ref[...] + jnp.sum(expo, axis=1))
    weights = (expo * inverse[:, None, :]).astype(jnp.bfloat16)
    back = back * inverse

    for n in range(2 * own):
        wide[pl.ds(n, rows * steps, stride=2 * own), :] = fresh[:, n * size : (n + 1) * size]
    fresh_ref.reshape(rows * steps * 2 * own, size)[...] = wide[...].astype(jnp.bfloat16)
    puts = [pltpu.make_async_copy(fresh_ref, fresh_hbm, sems.at[0])]
    puts[0].start()

    for at in range(0, rows // 2, group):
        pairs = range(at, at + group)
        values = jnp.concatenate(
            [
                jnp.concatenate([new_lines(1, p) if n == p else nothing for n in pairs], axis=1)
                for p in pairs
            ],
            axis=0,
        )
        new = lax.dot_general(
            weights[at : at + group].reshape(group * keys, many), values, TN, preferred_element_type=jnp.float32
        )
        factors = back[at : at + group].T
        for n, p in enumerate(pairs):
            both = new[:, n * size : (n + 1) * size] + factors[:, n : n + 1] * rows_of(old_ref, p)
            context_ref[2 * p : 2 * p + 2] = both.astype(jnp.bfloat16).reshape(2, queries, size)
        mine = pl.ds(2 * at, 2 * group)
        puts.append(pltpu.make_async_copy(context_ref.at[mine], context_hbm.at[mine], sems.at[1 + at // group]))
        puts[-1].start()
    for put in puts:
        put.wait()


def finish(parts, state, steps, own):
    rows, many, size = state[0].shape
    heads = many // steps
    groups = rows * own * steps // size
    fresh = (rows, steps, 2, own, size)
    fresh, context = pl.pallas_call(
        functools.partial(finish_kernel, steps, heads, size ** (-0.5), len(parts)),
        out_shape=(
            jax.ShapeDtypeStruct(fresh, jnp.bfloat16),
            jax.ShapeDtypeStruct((rows, many, size), jnp.bfloat16),
        ),
        in_specs=[VMEM] * (len(parts) + 4),
        out_specs=(pl.BlockSpec(memory_space=pltpu.HBM),) * 2,
        scratch_shapes=[
            pltpu.VMEM((rows * steps * 2 * own, size), jnp.float32),
            pltpu.VMEM(fresh, jnp.bfloat16),
            pltpu.VMEM((rows, many, size), jnp.bfloat16),
            pltpu.SemaphoreType.DMA((1 + groups,)),
        ],
        compiler_params=params(24),
        cost_estimate=cost(rows * many * size * size * 6, 8 * rows * many * size, rows * many * size * 2),
        name="finish",
    )(*parts, *state)
    return fresh, context.reshape(rows, steps, heads, size)


def join_kernel(*refs):
    blocks, out_ref = refs[:-1], refs[-1]
    at = 0
    for block in blocks:
        out_ref[at : at + block.shape[0], :] = block[...]
        at += block.shape[0]


def join(blocks):
    rows = sum(b.shape[0] for b in blocks)
    return pl.pallas_call(
        join_kernel,
        out_shape=pltpu.VMEM((rows, blocks[0].shape[1]), jnp.bfloat16),
        in_specs=[VMEM] * len(blocks),
        out_specs=VMEM,
        compiler_params=params(8),
        name="join",
    )(*blocks)


def gather_second(factor_a, factor_b, dp):
    count = dp // 2
    ranks = factor_b.shape[0]
    if ranks % 8 == 0 and count in (1, 2, 4):
        payload = make_payload(factor_a.T, factor_b)
        return [payload] + [lax.ppermute(payload, "dp", [(i, i ^ (2 * k)) for i in range(dp)]) for k in range(1, count)]
    payload = jnp.concatenate([factor_a.T, factor_b.reshape(ranks, -1)], axis=1)
    groups = [[i for i in range(dp) if i % 2 == n] for n in range(2)]
    copies = jnp.broadcast_to(payload[None], (count,) + payload.shape)
    blocks = lax.all_to_all(copies, "dp", 0, 0, axis_index_groups=groups, tiled=True)
    return [blocks.reshape(count * ranks, payload.shape[1])]


def shards(dp, tp, hidden, base_weight, factor_a, factor_b, queries, cache, lengths):
    steps, own = queries.shape[1], cache.shape[3]
    assert dp % 2 == 0
    blocks = gather_second(factor_a, factor_b, dp)
    rows, steps, heads, size = queries.shape
    queries = queries.reshape(rows, steps * heads, size)
    chunk, early = 6, 2
    tokens, base, keys, values = arrange(hidden, base_weight, cache, chunk, early)
    blocks, tokens, base, keys, values = lax.optimization_barrier((blocks, tokens, base, keys, values))
    gathered = join(blocks) if len(blocks) > 1 else blocks[0]
    gathered = [gathered, lax.ppermute(gathered, "dp", [(i, i ^ 1) for i in range(dp)])]
    state = attend_cached(queries, cache, lengths, keys, values, steps, chunk, early)
    gathered, state, tokens, base = lax.optimization_barrier((gathered, state, tokens, base))
    received = []
    for k in range(1, tp):
        other = project(k, tokens, base, gathered)
        received.append(lax.ppermute(other, "tp", [(i, i ^ k) for i in range(tp)]))
    mine = project(0, tokens, base, gathered)
    return finish([mine] + received, state, steps, own)


def solution(mesh):
    return jax.shard_map(
        functools.partial(shards, mesh.shape["dp"], mesh.shape["tp"]),
        mesh=mesh,
        in_specs=(
            P(("parts", "dp"), None, "tp"),
            P("tp", None, None, None),
            P(("parts", "tp"), "dp"),
            P(("parts", "dp"), None, None, None),
            P(("parts", "dp"), None, "tp", None),
            P(("parts", "dp"), None, None, "tp", None),
            P(("parts", "dp")),
        ),
        out_specs=(
            P(("parts", "dp"), None, None, "tp", None),
            P(("parts", "dp"), None, "tp", None),
        ),
        check_vma=False,
    )
```

```python
import functools

import jax
import jax.numpy as jnp
from jax import lax
from jax.experimental import pallas as pl
from jax.experimental.pallas import tpu as pltpu
from jax.sharding import PartitionSpec as P

LOW = -1e30
NT = (((1,), (1,)), ((), ()))
TN = (((0,), (0,)), ((), ()))
VMEM = pl.BlockSpec(memory_space=pltpu.VMEM)


def params(mib):
    return pltpu.CompilerParams(vmem_limit_bytes=mib * 1024 * 1024)


def in_hbm(x):
    return pltpu.with_memory_space_constraint(x, pltpu.HBM)


def in_vmem(x):
    return pltpu.with_memory_space_constraint(x, pltpu.VMEM)


def cost(flops, moved, exps=0):
    return pl.CostEstimate(flops=flops, bytes_accessed=moved, transcendentals=exps)


def payload_kernel(down_hbm, up_hbm, out_ref, ups, wide, sems):
    ranks, width = down_hbm.shape
    groups, size = ups.shape[1] * ups.shape[2], ups.shape[3]
    get_down = pltpu.make_async_copy(down_hbm, out_ref.at[:, pl.ds(0, width)], sems.at[0])
    get_up = pltpu.make_async_copy(up_hbm, ups, sems.at[1])
    get_up.start()
    get_down.start()
    get_up.wait()
    wide[...] = ups.reshape(ranks * groups, size)[...].astype(jnp.float32)
    for n in range(groups):
        out_ref[:, width + n * size : width + (n + 1) * size] = wide[pl.ds(n, ranks, stride=groups), :].astype(
            jnp.bfloat16
        )
    get_down.wait()


def make_payload(down, up):
    ranks, width = down.shape
    groups, size = up.shape[1] * up.shape[2], up.shape[3]
    return pl.pallas_call(
        payload_kernel,
        out_shape=pltpu.VMEM((ranks, width + groups * size), jnp.bfloat16),
        in_specs=[pl.BlockSpec(memory_space=pltpu.HBM)] * 2,
        out_specs=VMEM,
        scratch_shapes=[
            pltpu.VMEM(up.shape, jnp.bfloat16),
            pltpu.VMEM((ranks * groups, size), jnp.float32),
            pltpu.SemaphoreType.DMA((2,)),
        ],
        compiler_params=params(8),
        name="payload",
    )(in_hbm(down), in_hbm(up))


def cache_copies(cache_hbm, k, v, sems, i, chunk):
    mine = pl.ds(i * chunk, chunk)
    return [pltpu.make_async_copy(cache_hbm.at[mine, :, n], ref.at[mine], sems.at[i, n]) for n, ref in enumerate((k, v))]


class Cached:
    def __init__(self, chunk, heads, scale, inputs, outputs, scratch):
        self.chunk, self.heads, self.scale = chunk, heads, scale
        self.lengths_hbm, self.cache_hbm, self.q = inputs
        self.k, self.v, self.sums, self.tops, self.totals = outputs
        self.lengths, *rest = scratch
        self.scores, self.weights = rest[0:2], rest[2:4]
        self.sems, self.length_sem = rest[4:]
        self.rows, self.queries, self.size = self.q.shape
        self.slots, self.own = self.k.shape[1:3]
        self.keys = self.slots * self.own
        own, queries = self.own, self.queries
        line = lax.broadcasted_iota(jnp.int32, (self.keys, 2 * queries), 0)
        query = lax.broadcasted_iota(jnp.int32, (self.keys, 2 * queries), 1)
        self.line = jnp.where(line % own == (query % heads) // (heads // own), line, self.keys)
        self.one = lax.broadcasted_iota(jnp.int32, (1, 2 * queries), 1) < queries
        self.nothing = jnp.zeros((queries, self.size), jnp.bfloat16)

    def copies(self, i):
        return cache_copies(self.cache_hbm, self.k, self.v, self.sems, i, self.chunk)

    def lengths_copy(self):
        return pltpu.make_async_copy(self.lengths_hbm, self.lengths, self.length_sem)

    def start(self, i):
        for copy in self.copies(i):
            copy.start()

    def arrive(self, i):
        for copy in self.copies(i):
            copy.wait()

    def lines(self, ref, r):
        flat = ref.reshape(self.rows, self.keys, self.size)
        return jnp.concatenate([flat[r], flat[r + 1]], axis=1)

    def score(self, i, slot):
        for p in range(self.chunk // 2):
            r = i * self.chunk + 2 * p
            both_q = jnp.concatenate(
                [
                    jnp.concatenate([self.q[r], self.nothing], axis=1),
                    jnp.concatenate([self.nothing, self.q[r + 1]], axis=1),
                ],
                axis=0,
            )
            self.scores[slot][p] = lax.dot_general(
                self.lines(self.k, r), both_q, NT, preferred_element_type=jnp.float32
            )

    def soften(self, i, slot):
        for p in range(self.chunk // 2):
            r = i * self.chunk + 2 * p
            limit = jnp.where(self.one, self.own * self.lengths[r], self.own * self.lengths[r + 1])
            scores = jnp.where(self.line < limit, self.scores[slot][p], LOW)
            top = jnp.max(scores, axis=0, keepdims=True)
            expo = jnp.exp((scores - top) * self.scale)
            self.weights[slot][p] = expo.astype(jnp.bfloat16)
            pair = pl.ds(i * (self.chunk // 2) + p, 1)
            self.tops[pair, :] = top
            self.totals[pair, :] = jnp.sum(expo, axis=0, keepdims=True)

    def collect(self, i, slot):
        queries, size = self.queries, self.size
        for p in range(self.chunk // 2):
            r = i * self.chunk + 2 * p
            both = lax.dot_general(
                self.weights[slot][p], self.lines(self.v, r), TN, preferred_element_type=jnp.float32
            )
            for h in range(2):
                self.sums[r + h] = both[h * queries : (h + 1) * queries, h * size : (h + 1) * size]


def cached_kernel(chunk, early, heads, scale, *refs):
    cached = Cached(chunk, heads, scale, refs[:3], refs[5:10], refs[10:])
    chunks = cached.rows // chunk
    cached.lengths_copy().start()
    for i in range(early, chunks):
        cached.start(i)
    cached.lengths_copy().wait()
    cached.score(0, 0)
    cached.score(1, 1)
    cached.soften(0, 0)

    @pl.loop(1, chunks // 2)
    def _(t):
        for slot in range(2):
            i = 2 * t + slot

            @pl.when(i >= early)
            def _():
                cached.arrive(i)

            cached.score(i, slot)
            cached.soften(i - 1, 1 - slot)
            cached.collect(i - 2, slot)

    cached.soften(chunks - 1, 1)
    cached.collect(chunks - 2, 0)
    cached.collect(chunks - 1, 1)


def attend_cached(queries, cache, lengths, keys, values, steps, chunk, early):
    rows, many, size = queries.shape
    slots, own = cache.shape[1], cache.shape[3]
    heads = many // steps
    half = (rows, slots, own, size)
    scores = (chunk // 2, slots * own, 2 * many)
    line = (rows // 2, 2 * many)
    outs = (
        pltpu.VMEM(half, jnp.bfloat16),
        pltpu.VMEM(half, jnp.bfloat16),
        pltpu.VMEM((rows, many, size), jnp.float32),
        pltpu.VMEM(line, jnp.float32),
        pltpu.VMEM(line, jnp.float32),
    )
    _, _, *state = pl.pallas_call(
        functools.partial(cached_kernel, chunk, early, heads, size ** (-0.5)),
        out_shape=outs,
        in_specs=[pl.BlockSpec(memory_space=pltpu.HBM)] * 2 + [VMEM] * 3,
        out_specs=(VMEM,) * len(outs),
        scratch_shapes=[
            pltpu.SMEM(lengths.shape, jnp.int32),
            pltpu.VMEM(scores, jnp.float32),
            pltpu.VMEM(scores, jnp.float32),
            pltpu.VMEM(scores, jnp.bfloat16),
            pltpu.VMEM(scores, jnp.bfloat16),
            pltpu.SemaphoreType.DMA((rows // chunk, 2)),
            pltpu.SemaphoreType.DMA,
        ],
        input_output_aliases={3: 0, 4: 1},
        compiler_params=params(16),
        cost_estimate=cost(8 * rows * many * slots * size, 4 * rows * slots * own * size, rows * many * slots * own),
        name="attend_cached",
    )(in_hbm(lengths), in_hbm(cache), in_vmem(queries), keys, values)
    return [queries, *state]


def arrange_kernel(chunks, chunk, early, *refs):
    cache_hbm, hidden_hbm, base_hbm, tokens_ref, base_ref, k, v, hidden, base, base_sems, sems = refs
    width, two, kvh, size = base.shape
    own = k.shape[2]
    groups = two * kvh
    some_width = width // chunks
    copies = [copy for i in range(early) for copy in cache_copies(cache_hbm, k, v, sems, i, chunk)]
    get_hidden = pltpu.make_async_copy(hidden_hbm, hidden, base_sems.at[chunks])

    def get_base(i):
        features = pl.ds(i * some_width, some_width)
        return pltpu.make_async_copy(base_hbm.at[features], base.at[features], base_sems.at[i])

    for i in range(chunks):
        get_base(i).start()
    get_hidden.start()
    for copy in copies:
        copy.start()

    tile = 256
    some = tile // groups
    row = lax.broadcasted_iota(jnp.int32, (tile, tile), 0)
    place = lax.broadcasted_iota(jnp.int32, (tile, tile), 1)
    order = (place == (row % some) * groups + row // some).astype(jnp.float32).astype(jnp.bfloat16)
    flat_base = base.reshape(width * groups, size)

    def arrange(f):
        at = pl.multiple_of(f * groups, tile)
        pair = jnp.concatenate([flat_base[pl.ds(at + h * tile, tile), :] for h in range(2)], axis=1)
        moved = jnp.dot(order, pair, preferred_element_type=jnp.float32).astype(jnp.bfloat16)
        for n in range(groups):
            lanes = slice((n % own) * size, (n % own + 1) * size)
            for h in range(2):
                base_ref[n // own, pl.ds(pl.multiple_of(f + h * some, some), some), lanes] = moved[
                    n * some : (n + 1) * some, h * size : (h + 1) * size
                ]

    @pl.loop(0, chunks)
    def _(i):
        get_base(i).wait()
        for f in range(0, some_width, 2 * some):
            arrange(i * some_width + f)

    get_hidden.wait()
    tokens_ref[...] = hidden.reshape(tokens_ref.shape)[...]
    for copy in copies:
        copy.wait()


def arrange(hidden, base, cache, chunk, early):
    rows, steps, _ = hidden.shape
    slots, own = cache.shape[1], cache.shape[3]
    width, two, kvh, size = base.shape
    half = pltpu.VMEM((rows, slots, own, size), jnp.bfloat16)
    chunks = 4
    outs = (
        pltpu.VMEM((rows * steps, width), jnp.bfloat16),
        pltpu.VMEM((two * kvh // own, width, own * size), jnp.bfloat16),
        half,
        half,
    )
    return pl.pallas_call(
        functools.partial(arrange_kernel, chunks, chunk, early),
        out_shape=outs,
        in_specs=[pl.BlockSpec(memory_space=pltpu.HBM)] * 3,
        out_specs=(VMEM,) * len(outs),
        scratch_shapes=[
            pltpu.VMEM(hidden.shape, jnp.bfloat16),
            pltpu.VMEM(base.shape, jnp.bfloat16),
            pltpu.SemaphoreType.DMA((chunks + 1,)),
            pltpu.SemaphoreType.DMA((early, 2)),
        ],
        compiler_params=params(16),
        cost_estimate=cost(512 * base.size, 4 * (base.size + hidden.size)),
        name="arrange",
    )(in_hbm(cache), in_hbm(hidden), in_hbm(base))


def project_kernel(k, hidden_ref, base_ref, *refs):
    gathered, (out_ref, merged) = refs[:-2], refs[-2:]
    width, columns = merged.shape
    part = lax.axis_index("tp") ^ k
    parts = base_ref.shape[0] // 2
    half = columns // 2
    up = jnp.concatenate(
        [
            jnp.concatenate(
                [ref[:, pl.ds(pl.multiple_of(width + (c * parts + part) * half, 128), half)] for ref in gathered], axis=0
            )
            for c in range(2)
        ],
        axis=1,
    )
    step = 512
    for f in range(0, width, step):
        down = jnp.concatenate([ref[:, f : f + step] for ref in gathered], axis=0).T
        low_rank = jnp.dot(down, up, preferred_element_type=jnp.float32)
        for c in range(2):
            base = base_ref[c * parts + part, f : f + step, :].astype(jnp.float32)
            merged[f : f + step, c * half : (c + 1) * half] = (base + low_rank[:, c * half : (c + 1) * half]).astype(
                jnp.bfloat16
            )
    out_ref[...] = jnp.dot(hidden_ref[...], merged[...], preferred_element_type=jnp.float32)


def project(k, hidden, base, gathered):
    tokens, width = hidden.shape
    columns = 2 * base.shape[2]
    ranks = sum(g.shape[0] for g in gathered)
    return pl.pallas_call(
        functools.partial(project_kernel, k),
        out_shape=pltpu.VMEM((tokens, columns), jnp.float32),
        in_specs=[VMEM] * (2 + len(gathered)),
        out_specs=VMEM,
        scratch_shapes=[pltpu.VMEM((width, columns), jnp.bfloat16)],
        compiler_params=params(24),
        cost_estimate=cost(2 * width * columns * (tokens + ranks), 2 * width * columns + 2 * width * tokens),
        name="project",
    )(hidden, base, *gathered)


def finish_kernel(steps, heads, scale, terms, *refs):
    parts, refs = refs[:terms], refs[terms:]
    q_ref, old_ref, top_ref, total_ref = refs[:4]
    refs = refs[4:]
    fresh_hbm, context_hbm, wide, fresh_ref, context_ref, sems = refs
    rows, queries, size = context_ref.shape
    own = fresh_ref.shape[3]
    fresh = parts[0][...]
    for part in parts[1:]:
        fresh = fresh + part[...]
    keys, many = 2 * own * steps, 2 * queries
    group = size // keys
    key = lax.broadcasted_iota(jnp.int32, (keys, many), 0)
    query = lax.broadcasted_iota(jnp.int32, (keys, many), 1)
    same_head = (query % heads) // (heads // own) == key // (2 * steps)
    same_row = query // queries == (key // steps) % 2
    live = same_head & same_row & ((query % queries) // heads >= key % steps)
    nothing = jnp.zeros((keys, size), jnp.bfloat16)

    def new_lines(c, pair):
        tokens = slice(pair * 2 * steps, (pair + 1) * 2 * steps)
        lines = [fresh[tokens, (c * own + g) * size : (c * own + g + 1) * size] for g in range(own)]
        return jnp.concatenate(lines, axis=0).astype(jnp.bfloat16)

    def rows_of(ref, pair):
        return ref[2 * pair : 2 * pair + 2].reshape(many, size)

    scores = [
        lax.dot_general(new_lines(0, p), rows_of(q_ref, p), NT, preferred_element_type=jnp.float32)
        for p in range(rows // 2)
    ]
    scores = jnp.stack([jnp.where(live, s, LOW) for s in scores])
    old_top = top_ref[...]
    top = jnp.maximum(old_top, jnp.max(scores, axis=1))
    expo = jnp.exp((scores - top[:, None, :]) * scale)
    back = jnp.exp((old_top - top) * scale)
    inverse = 1.0 / (back * total_ref[...] + jnp.sum(expo, axis=1))
    weights = (expo * inverse[:, None, :]).astype(jnp.bfloat16)
    back = back * inverse

    for n in range(2 * own):
        wide[pl.ds(n, rows * steps, stride=2 * own), :] = fresh[:, n * size : (n + 1) * size]
    fresh_ref.reshape(rows * steps * 2 * own, size)[...] = wide[...].astype(jnp.bfloat16)
    puts = [pltpu.make_async_copy(fresh_ref, fresh_hbm, sems.at[0])]
    puts[0].start()

    for at in range(0, rows // 2, group):
        pairs = range(at, at + group)
        values = jnp.concatenate(
            [
                jnp.concatenate([new_lines(1, p) if n == p else nothing for n in pairs], axis=1)
                for p in pairs
            ],
            axis=0,
        )
        new = lax.dot_general(
            weights[at : at + group].reshape(group * keys, many), values, TN, preferred_element_type=jnp.float32
        )
        factors = back[at : at + group].T
        for n, p in enumerate(pairs):
            both = new[:, n * size : (n + 1) * size] + factors[:, n : n + 1] * rows_of(old_ref, p)
            context_ref[2 * p : 2 * p + 2] = both.astype(jnp.bfloat16).reshape(2, queries, size)
        mine = pl.ds(2 * at, 2 * group)
        puts.append(pltpu.make_async_copy(context_ref.at[mine], context_hbm.at[mine], sems.at[1 + at // group]))
        puts[-1].start()
    for put in puts:
        put.wait()


def finish(parts, state, steps, own):
    rows, many, size = state[0].shape
    heads = many // steps
    groups = rows * own * steps // size
    fresh = (rows, steps, 2, own, size)
    fresh, context = pl.pallas_call(
        functools.partial(finish_kernel, steps, heads, size ** (-0.5), len(parts)),
        out_shape=(
            jax.ShapeDtypeStruct(fresh, jnp.bfloat16),
            jax.ShapeDtypeStruct((rows, many, size), jnp.bfloat16),
        ),
        in_specs=[VMEM] * (len(parts) + 4),
        out_specs=(pl.BlockSpec(memory_space=pltpu.HBM),) * 2,
        scratch_shapes=[
            pltpu.VMEM((rows * steps * 2 * own, size), jnp.float32),
            pltpu.VMEM(fresh, jnp.bfloat16),
            pltpu.VMEM((rows, many, size), jnp.bfloat16),
            pltpu.SemaphoreType.DMA((1 + groups,)),
        ],
        compiler_params=params(24),
        cost_estimate=cost(rows * many * size * size * 6, 8 * rows * many * size, rows * many * size * 2),
        name="finish",
    )(*parts, *state)
    return fresh, context.reshape(rows, steps, heads, size)


def join_kernel(*refs):
    blocks, out_ref = refs[:-1], refs[-1]
    at = 0
    for block in blocks:
        out_ref[at : at + block.shape[0], :] = block[...]
        at += block.shape[0]


def join(blocks):
    rows = sum(b.shape[0] for b in blocks)
    return pl.pallas_call(
        join_kernel,
        out_shape=pltpu.VMEM((rows, blocks[0].shape[1]), jnp.bfloat16),
        in_specs=[VMEM] * len(blocks),
        out_specs=VMEM,
        compiler_params=params(8),
        name="join",
    )(*blocks)


def gather_second(factor_a, factor_b, dp):
    count = dp // 2
    ranks = factor_b.shape[0]
    if ranks % 8 == 0 and count in (1, 2, 4):
        payload = make_payload(factor_a.T, factor_b)
        return [payload] + [lax.ppermute(payload, "dp", [(i, i ^ (2 * k)) for i in range(dp)]) for k in range(count - 1, 0, -1)]
    payload = jnp.concatenate([factor_a.T, factor_b.reshape(ranks, -1)], axis=1)
    groups = [[i for i in range(dp) if i % 2 == n] for n in range(2)]
    copies = jnp.broadcast_to(payload[None], (count,) + payload.shape)
    blocks = lax.all_to_all(copies, "dp", 0, 0, axis_index_groups=groups, tiled=True)
    return [blocks.reshape(count * ranks, payload.shape[1])]


def shards(dp, tp, hidden, base_weight, factor_a, factor_b, queries, cache, lengths):
    steps, own = queries.shape[1], cache.shape[3]
    assert dp % 2 == 0
    blocks = gather_second(factor_a, factor_b, dp)
    rows, steps, heads, size = queries.shape
    queries = queries.reshape(rows, steps * heads, size)
    chunk, early = 6, 3
    tokens, base, keys, values = arrange(hidden, base_weight, cache, chunk, early)
    blocks, tokens, base, keys, values = lax.optimization_barrier((blocks, tokens, base, keys, values))
    gathered = join(blocks) if len(blocks) > 1 else blocks[0]
    gathered = [gathered, lax.ppermute(gathered, "dp", [(i, i ^ 1) for i in range(dp)])]
    state = attend_cached(queries, cache, lengths, keys, values, steps, chunk, early)
    gathered, state, tokens, base = lax.optimization_barrier((gathered, state, tokens, base))
    received = []
    for k in range(1, tp):
        other = project(k, tokens, base, gathered)
        received.append(lax.ppermute(other, "tp", [(i, i ^ k) for i in range(tp)]))
    mine = project(0, tokens, base, gathered)
    return finish([mine] + received, state, steps, own)


def solution(mesh):
    return jax.shard_map(
        functools.partial(shards, mesh.shape["dp"], mesh.shape["tp"]),
        mesh=mesh,
        in_specs=(
            P(("parts", "dp"), None, "tp"),
            P("tp", None, None, None),
            P(("parts", "tp"), "dp"),
            P(("parts", "dp"), None, None, None),
            P(("parts", "dp"), None, "tp", None),
            P(("parts", "dp"), None, None, "tp", None),
            P(("parts", "dp")),
        ),
        out_specs=(
            P(("parts", "dp"), None, None, "tp", None),
            P(("parts", "dp"), None, "tp", None),
        ),
        check_vma=False,
    )
```

```python
import functools

import jax
import jax.numpy as jnp
from jax import lax
from jax.experimental import pallas as pl
from jax.experimental.pallas import tpu as pltpu
from jax.sharding import PartitionSpec as P

LOW = -1e30
NT = (((1,), (1,)), ((), ()))
TN = (((0,), (0,)), ((), ()))
VMEM = pl.BlockSpec(memory_space=pltpu.VMEM)


def params(mib):
    return pltpu.CompilerParams(vmem_limit_bytes=mib * 1024 * 1024)


def in_hbm(x):
    return pltpu.with_memory_space_constraint(x, pltpu.HBM)


def in_vmem(x):
    return pltpu.with_memory_space_constraint(x, pltpu.VMEM)


def cost(flops, moved, exps=0):
    return pl.CostEstimate(flops=flops, bytes_accessed=moved, transcendentals=exps)


def payload_kernel(down_hbm, up_hbm, out_ref, ups, wide, sems):
    ranks, width = down_hbm.shape
    groups, size = ups.shape[1] * ups.shape[2], ups.shape[3]
    get_down = pltpu.make_async_copy(down_hbm, out_ref.at[:, pl.ds(0, width)], sems.at[0])
    get_up = pltpu.make_async_copy(up_hbm, ups, sems.at[1])
    get_up.start()
    get_down.start()
    get_up.wait()
    wide[...] = ups.reshape(ranks * groups, size)[...].astype(jnp.float32)
    for n in range(groups):
        out_ref[:, width + n * size : width + (n + 1) * size] = wide[pl.ds(n, ranks, stride=groups), :].astype(
            jnp.bfloat16
        )
    get_down.wait()


def make_payload(down, up):
    ranks, width = down.shape
    groups, size = up.shape[1] * up.shape[2], up.shape[3]
    return pl.pallas_call(
        payload_kernel,
        out_shape=pltpu.VMEM((ranks, width + groups * size), jnp.bfloat16),
        in_specs=[pl.BlockSpec(memory_space=pltpu.HBM)] * 2,
        out_specs=VMEM,
        scratch_shapes=[
            pltpu.VMEM(up.shape, jnp.bfloat16),
            pltpu.VMEM((ranks * groups, size), jnp.float32),
            pltpu.SemaphoreType.DMA((2,)),
        ],
        compiler_params=params(8),
        name="payload",
    )(in_hbm(down), in_hbm(up))


def cache_copies(cache_hbm, k, v, sems, i, chunk):
    mine = pl.ds(i * chunk, chunk)
    return [pltpu.make_async_copy(cache_hbm.at[mine, :, n], ref.at[mine], sems.at[i, n]) for n, ref in enumerate((k, v))]


class Cached:
    def __init__(self, chunk, heads, scale, inputs, outputs, scratch):
        self.chunk, self.heads, self.scale = chunk, heads, scale
        self.lengths_hbm, self.cache_hbm, self.q = inputs
        self.k, self.v, self.sums, self.tops, self.totals = outputs
        self.lengths, *rest = scratch
        self.scores, self.weights = rest[0:2], rest[2:4]
        self.sems, self.length_sem = rest[4:]
        self.rows, self.queries, self.size = self.q.shape
        self.slots, self.own = self.k.shape[1:3]
        self.keys = self.slots * self.own
        own, queries = self.own, self.queries
        line = lax.broadcasted_iota(jnp.int32, (self.keys, 2 * queries), 0)
        query = lax.broadcasted_iota(jnp.int32, (self.keys, 2 * queries), 1)
        self.line = jnp.where(line % own == (query % heads) // (heads // own), line, self.keys)
        self.one = lax.broadcasted_iota(jnp.int32, (1, 2 * queries), 1) < queries
        self.nothing = jnp.zeros((queries, self.size), jnp.bfloat16)

    def copies(self, i):
        return cache_copies(self.cache_hbm, self.k, self.v, self.sems, i, self.chunk)

    def lengths_copy(self):
        return pltpu.make_async_copy(self.lengths_hbm, self.lengths, self.length_sem)

    def start(self, i):
        for copy in self.copies(i):
            copy.start()

    def arrive(self, i):
        for copy in self.copies(i):
            copy.wait()

    def lines(self, ref, r):
        flat = ref.reshape(self.rows, self.keys, self.size)
        return jnp.concatenate([flat[r], flat[r + 1]], axis=1)

    def score(self, i, slot):
        for p in range(self.chunk // 2):
            r = i * self.chunk + 2 * p
            both_q = jnp.concatenate(
                [
                    jnp.concatenate([self.q[r], self.nothing], axis=1),
                    jnp.concatenate([self.nothing, self.q[r + 1]], axis=1),
                ],
                axis=0,
            )
            self.scores[slot][p] = lax.dot_general(
                self.lines(self.k, r), both_q, NT, preferred_element_type=jnp.float32
            )

    def soften(self, i, slot):
        for p in range(self.chunk // 2):
            r = i * self.chunk + 2 * p
            limit = jnp.where(self.one, self.own * self.lengths[r], self.own * self.lengths[r + 1])
            scores = jnp.where(self.line < limit, self.scores[slot][p], LOW)
            top = jnp.max(scores, axis=0, keepdims=True)
            expo = jnp.exp((scores - top) * self.scale)
            self.weights[slot][p] = expo.astype(jnp.bfloat16)
            pair = pl.ds(i * (self.chunk // 2) + p, 1)
            self.tops[pair, :] = top
            self.totals[pair, :] = jnp.sum(expo, axis=0, keepdims=True)

    def collect(self, i, slot):
        queries, size = self.queries, self.size
        for p in range(self.chunk // 2):
            r = i * self.chunk + 2 * p
            both = lax.dot_general(
                self.weights[slot][p], self.lines(self.v, r), TN, preferred_element_type=jnp.float32
            )
            for h in range(2):
                self.sums[r + h] = both[h * queries : (h + 1) * queries, h * size : (h + 1) * size]


def cached_kernel(chunk, early, heads, scale, *refs):
    cached = Cached(chunk, heads, scale, refs[:3], refs[5:10], refs[10:])
    chunks = cached.rows // chunk
    cached.lengths_copy().start()
    for i in range(early, chunks):
        cached.start(i)
    cached.lengths_copy().wait()
    cached.score(0, 0)
    cached.score(1, 1)
    cached.soften(0, 0)

    @pl.loop(1, chunks // 2)
    def _(t):
        for slot in range(2):
            i = 2 * t + slot

            @pl.when(i >= early)
            def _():
                cached.arrive(i)

            cached.score(i, slot)
            cached.soften(i - 1, 1 - slot)
            cached.collect(i - 2, slot)

    cached.soften(chunks - 1, 1)
    cached.collect(chunks - 2, 0)
    cached.collect(chunks - 1, 1)


def attend_cached(queries, cache, lengths, keys, values, steps, chunk, early):
    rows, many, size = queries.shape
    slots, own = cache.shape[1], cache.shape[3]
    heads = many // steps
    half = (rows, slots, own, size)
    scores = (chunk // 2, slots * own, 2 * many)
    line = (rows // 2, 2 * many)
    outs = (
        pltpu.VMEM(half, jnp.bfloat16),
        pltpu.VMEM(half, jnp.bfloat16),
        pltpu.VMEM((rows, many, size), jnp.float32),
        pltpu.VMEM(line, jnp.float32),
        pltpu.VMEM(line, jnp.float32),
    )
    _, _, *state = pl.pallas_call(
        functools.partial(cached_kernel, chunk, early, heads, size ** (-0.5)),
        out_shape=outs,
        in_specs=[pl.BlockSpec(memory_space=pltpu.HBM)] * 2 + [VMEM] * 3,
        out_specs=(VMEM,) * len(outs),
        scratch_shapes=[
            pltpu.SMEM(lengths.shape, jnp.int32),
            pltpu.VMEM(scores, jnp.float32),
            pltpu.VMEM(scores, jnp.float32),
            pltpu.VMEM(scores, jnp.bfloat16),
            pltpu.VMEM(scores, jnp.bfloat16),
            pltpu.SemaphoreType.DMA((rows // chunk, 2)),
            pltpu.SemaphoreType.DMA,
        ],
        input_output_aliases={3: 0, 4: 1},
        compiler_params=params(16),
        cost_estimate=cost(8 * rows * many * slots * size, 4 * rows * slots * own * size, rows * many * slots * own),
        name="attend_cached",
    )(in_hbm(lengths), in_hbm(cache), in_vmem(queries), keys, values)
    return [queries, *state]


def arrange_kernel(chunks, chunk, early, *refs):
    cache_hbm, hidden_hbm, base_hbm, tokens_ref, base_ref, k, v, hidden, base, base_sems, sems = refs
    width, two, kvh, size = base.shape
    own = k.shape[2]
    groups = two * kvh
    some_width = width // chunks
    copies = [copy for i in range(early) for copy in cache_copies(cache_hbm, k, v, sems, i, chunk)]
    get_hidden = pltpu.make_async_copy(hidden_hbm, hidden, base_sems.at[chunks])

    def get_base(i):
        features = pl.ds(i * some_width, some_width)
        return pltpu.make_async_copy(base_hbm.at[features], base.at[features], base_sems.at[i])

    for i in range(chunks):
        get_base(i).start()
    get_hidden.start()
    for copy in copies:
        copy.start()

    tile = 256
    some = tile // groups
    row = lax.broadcasted_iota(jnp.int32, (tile, tile), 0)
    place = lax.broadcasted_iota(jnp.int32, (tile, tile), 1)
    order = (place == (row % some) * groups + row // some).astype(jnp.float32).astype(jnp.bfloat16)
    flat_base = base.reshape(width * groups, size)

    def arrange(f):
        at = pl.multiple_of(f * groups, tile)
        pair = jnp.concatenate([flat_base[pl.ds(at + h * tile, tile), :] for h in range(2)], axis=1)
        moved = jnp.dot(order, pair, preferred_element_type=jnp.float32).astype(jnp.bfloat16)
        for n in range(groups):
            lanes = slice((n % own) * size, (n % own + 1) * size)
            for h in range(2):
                base_ref[n // own, pl.ds(pl.multiple_of(f + h * some, some), some), lanes] = moved[
                    n * some : (n + 1) * some, h * size : (h + 1) * size
                ]

    @pl.loop(0, chunks)
    def _(i):
        get_base(i).wait()
        for f in range(0, some_width, 2 * some):
            arrange(i * some_width + f)

    get_hidden.wait()
    tokens_ref[...] = hidden.reshape(tokens_ref.shape)[...]
    for copy in copies:
        copy.wait()


def arrange(hidden, base, cache, chunk, early):
    rows, steps, _ = hidden.shape
    slots, own = cache.shape[1], cache.shape[3]
    width, two, kvh, size = base.shape
    half = pltpu.VMEM((rows, slots, own, size), jnp.bfloat16)
    chunks = 4
    outs = (
        pltpu.VMEM((rows * steps, width), jnp.bfloat16),
        pltpu.VMEM((two * kvh // own, width, own * size), jnp.bfloat16),
        half,
        half,
    )
    return pl.pallas_call(
        functools.partial(arrange_kernel, chunks, chunk, early),
        out_shape=outs,
        in_specs=[pl.BlockSpec(memory_space=pltpu.HBM)] * 3,
        out_specs=(VMEM,) * len(outs),
        scratch_shapes=[
            pltpu.VMEM(hidden.shape, jnp.bfloat16),
            pltpu.VMEM(base.shape, jnp.bfloat16),
            pltpu.SemaphoreType.DMA((chunks + 1,)),
            pltpu.SemaphoreType.DMA((early, 2)),
        ],
        compiler_params=params(16),
        cost_estimate=cost(512 * base.size, 4 * (base.size + hidden.size)),
        name="arrange",
    )(in_hbm(cache), in_hbm(hidden), in_hbm(base))


def project_kernel(k, hidden_ref, base_ref, *refs):
    gathered, (out_ref, merged) = refs[:-2], refs[-2:]
    width, columns = merged.shape
    part = lax.axis_index("tp") ^ k
    parts = base_ref.shape[0] // 2
    half = columns // 2
    up = jnp.concatenate(
        [
            jnp.concatenate(
                [ref[:, pl.ds(pl.multiple_of(width + (c * parts + part) * half, 128), half)] for ref in gathered], axis=0
            )
            for c in range(2)
        ],
        axis=1,
    )
    step = 512
    for f in range(0, width, step):
        down = jnp.concatenate([ref[:, f : f + step] for ref in gathered], axis=0).T
        low_rank = jnp.dot(down, up, preferred_element_type=jnp.float32)
        for c in range(2):
            base = base_ref[c * parts + part, f : f + step, :].astype(jnp.float32)
            merged[f : f + step, c * half : (c + 1) * half] = (base + low_rank[:, c * half : (c + 1) * half]).astype(
                jnp.bfloat16
            )
    out_ref[...] = jnp.dot(hidden_ref[...], merged[...], preferred_element_type=jnp.float32)


def project(k, hidden, base, gathered):
    tokens, width = hidden.shape
    columns = 2 * base.shape[2]
    ranks = sum(g.shape[0] for g in gathered)
    return pl.pallas_call(
        functools.partial(project_kernel, k),
        out_shape=pltpu.VMEM((tokens, columns), jnp.float32),
        in_specs=[VMEM] * (2 + len(gathered)),
        out_specs=VMEM,
        scratch_shapes=[pltpu.VMEM((width, columns), jnp.bfloat16)],
        compiler_params=params(24),
        cost_estimate=cost(2 * width * columns * (tokens + ranks), 2 * width * columns + 2 * width * tokens),
        name="project",
    )(hidden, base, *gathered)


def finish_kernel(steps, heads, scale, terms, *refs):
    parts, refs = refs[:terms], refs[terms:]
    q_ref, old_ref, top_ref, total_ref = refs[:4]
    refs = refs[4:]
    fresh_hbm, context_hbm, wide, fresh_ref, context_ref, sems = refs
    rows, queries, size = context_ref.shape
    own = fresh_ref.shape[3]
    fresh = parts[0][...]
    for part in parts[1:]:
        fresh = fresh + part[...]
    keys, many = 2 * own * steps, 2 * queries
    group = size // keys
    key = lax.broadcasted_iota(jnp.int32, (keys, many), 0)
    query = lax.broadcasted_iota(jnp.int32, (keys, many), 1)
    same_head = (query % heads) // (heads // own) == key // (2 * steps)
    same_row = query // queries == (key // steps) % 2
    live = same_head & same_row & ((query % queries) // heads >= key % steps)
    nothing = jnp.zeros((keys, size), jnp.bfloat16)

    def new_lines(c, pair):
        tokens = slice(pair * 2 * steps, (pair + 1) * 2 * steps)
        lines = [fresh[tokens, (c * own + g) * size : (c * own + g + 1) * size] for g in range(own)]
        return jnp.concatenate(lines, axis=0).astype(jnp.bfloat16)

    def rows_of(ref, pair):
        return ref[2 * pair : 2 * pair + 2].reshape(many, size)

    scores = [
        lax.dot_general(new_lines(0, p), rows_of(q_ref, p), NT, preferred_element_type=jnp.float32)
        for p in range(rows // 2)
    ]
    scores = jnp.stack([jnp.where(live, s, LOW) for s in scores])
    old_top = top_ref[...]
    top = jnp.maximum(old_top, jnp.max(scores, axis=1))
    expo = jnp.exp((scores - top[:, None, :]) * scale)
    back = jnp.exp((old_top - top) * scale)
    inverse = 1.0 / (back * total_ref[...] + jnp.sum(expo, axis=1))
    weights = (expo * inverse[:, None, :]).astype(jnp.bfloat16)
    back = back * inverse

    for n in range(2 * own):
        wide[pl.ds(n, rows * steps, stride=2 * own), :] = fresh[:, n * size : (n + 1) * size]
    fresh_ref.reshape(rows * steps * 2 * own, size)[...] = wide[...].astype(jnp.bfloat16)
    puts = [pltpu.make_async_copy(fresh_ref, fresh_hbm, sems.at[0])]
    puts[0].start()

    for at in range(0, rows // 2, group):
        pairs = range(at, at + group)
        values = jnp.concatenate(
            [
                jnp.concatenate([new_lines(1, p) if n == p else nothing for n in pairs], axis=1)
                for p in pairs
            ],
            axis=0,
        )
        new = lax.dot_general(
            weights[at : at + group].reshape(group * keys, many), values, TN, preferred_element_type=jnp.float32
        )
        factors = back[at : at + group].T
        for n, p in enumerate(pairs):
            both = new[:, n * size : (n + 1) * size] + factors[:, n : n + 1] * rows_of(old_ref, p)
            context_ref[2 * p : 2 * p + 2] = both.astype(jnp.bfloat16).reshape(2, queries, size)
        mine = pl.ds(2 * at, 2 * group)
        puts.append(pltpu.make_async_copy(context_ref.at[mine], context_hbm.at[mine], sems.at[1 + at // group]))
        puts[-1].start()
    for put in puts:
        put.wait()


def finish(parts, state, steps, own):
    rows, many, size = state[0].shape
    heads = many // steps
    groups = rows * own * steps // size
    fresh = (rows, steps, 2, own, size)
    fresh, context = pl.pallas_call(
        functools.partial(finish_kernel, steps, heads, size ** (-0.5), len(parts)),
        out_shape=(
            jax.ShapeDtypeStruct(fresh, jnp.bfloat16),
            jax.ShapeDtypeStruct((rows, many, size), jnp.bfloat16),
        ),
        in_specs=[VMEM] * (len(parts) + 4),
        out_specs=(pl.BlockSpec(memory_space=pltpu.HBM),) * 2,
        scratch_shapes=[
            pltpu.VMEM((rows * steps * 2 * own, size), jnp.float32),
            pltpu.VMEM(fresh, jnp.bfloat16),
            pltpu.VMEM((rows, many, size), jnp.bfloat16),
            pltpu.SemaphoreType.DMA((1 + groups,)),
        ],
        compiler_params=params(24),
        cost_estimate=cost(rows * many * size * size * 6, 8 * rows * many * size, rows * many * size * 2),
        name="finish",
    )(*parts, *state)
    return fresh, context.reshape(rows, steps, heads, size)


def join_kernel(*refs):
    blocks, out_ref = refs[:-1], refs[-1]
    at = 0
    for block in blocks:
        out_ref[at : at + block.shape[0], :] = block[...]
        at += block.shape[0]


def join(blocks):
    rows = sum(b.shape[0] for b in blocks)
    return pl.pallas_call(
        join_kernel,
        out_shape=pltpu.VMEM((rows, blocks[0].shape[1]), jnp.bfloat16),
        in_specs=[VMEM] * len(blocks),
        out_specs=VMEM,
        compiler_params=params(8),
        name="join",
    )(*blocks)


def gather_second(factor_a, factor_b, dp):
    count = dp // 2
    ranks = factor_b.shape[0]
    if ranks % 8 == 0 and count in (1, 2, 4):
        payload = make_payload(factor_a.T, factor_b)
        return [payload] + [lax.ppermute(payload, "dp", [(i, i ^ (2 * k)) for i in range(dp)]) for k in range(count - 1, 0, -1)]
    payload = jnp.concatenate([factor_a.T, factor_b.reshape(ranks, -1)], axis=1)
    groups = [[i for i in range(dp) if i % 2 == n] for n in range(2)]
    copies = jnp.broadcast_to(payload[None], (count,) + payload.shape)
    blocks = lax.all_to_all(copies, "dp", 0, 0, axis_index_groups=groups, tiled=True)
    return [blocks.reshape(count * ranks, payload.shape[1])]


def shards(dp, tp, hidden, base_weight, factor_a, factor_b, queries, cache, lengths):
    steps, own = queries.shape[1], cache.shape[3]
    assert dp % 2 == 0
    blocks = gather_second(factor_a, factor_b, dp)
    rows, steps, heads, size = queries.shape
    queries = queries.reshape(rows, steps * heads, size)
    chunk, early = 8, 3
    tokens, base, keys, values = arrange(hidden, base_weight, cache, chunk, early)
    blocks, tokens, base, keys, values = lax.optimization_barrier((blocks, tokens, base, keys, values))
    gathered = join(blocks) if len(blocks) > 1 else blocks[0]
    gathered = [gathered, lax.ppermute(gathered, "dp", [(i, i ^ 1) for i in range(dp)])]
    state = attend_cached(queries, cache, lengths, keys, values, steps, chunk, early)
    gathered, state, tokens, base = lax.optimization_barrier((gathered, state, tokens, base))
    received = []
    for k in range(1, tp):
        other = project(k, tokens, base, gathered)
        received.append(lax.ppermute(other, "tp", [(i, i ^ k) for i in range(tp)]))
    mine = project(0, tokens, base, gathered)
    return finish([mine] + received, state, steps, own)


def solution(mesh):
    return jax.shard_map(
        functools.partial(shards, mesh.shape["dp"], mesh.shape["tp"]),
        mesh=mesh,
        in_specs=(
            P(("parts", "dp"), None, "tp"),
            P("tp", None, None, None),
            P(("parts", "tp"), "dp"),
            P(("parts", "dp"), None, None, None),
            P(("parts", "dp"), None, "tp", None),
            P(("parts", "dp"), None, None, "tp", None),
            P(("parts", "dp")),
        ),
        out_specs=(
            P(("parts", "dp"), None, None, "tp", None),
            P(("parts", "dp"), None, "tp", None),
        ),
        check_vma=False,
    )
```

```python
import functools

import jax
import jax.numpy as jnp
from jax import lax
from jax.experimental import pallas as pl
from jax.experimental.pallas import tpu as pltpu
from jax.sharding import PartitionSpec as P

LOW = -1e30
NT = (((1,), (1,)), ((), ()))
TN = (((0,), (0,)), ((), ()))
VMEM = pl.BlockSpec(memory_space=pltpu.VMEM)


def params(mib):
    return pltpu.CompilerParams(vmem_limit_bytes=mib * 1024 * 1024)


def in_hbm(x):
    return pltpu.with_memory_space_constraint(x, pltpu.HBM)


def in_vmem(x):
    return pltpu.with_memory_space_constraint(x, pltpu.VMEM)


def cost(flops, moved, exps=0):
    return pl.CostEstimate(flops=flops, bytes_accessed=moved, transcendentals=exps)


def payload_kernel(down_hbm, up_hbm, out_ref, ups, wide, sems):
    ranks, width = down_hbm.shape
    groups, size = ups.shape[1] * ups.shape[2], ups.shape[3]
    get_down = pltpu.make_async_copy(down_hbm, out_ref.at[:, pl.ds(0, width)], sems.at[0])
    get_up = pltpu.make_async_copy(up_hbm, ups, sems.at[1])
    get_up.start()
    get_down.start()
    get_up.wait()
    wide[...] = ups.reshape(ranks * groups, size)[...].astype(jnp.float32)
    for n in range(groups):
        out_ref[:, width + n * size : width + (n + 1) * size] = wide[pl.ds(n, ranks, stride=groups), :].astype(
            jnp.bfloat16
        )
    get_down.wait()


def make_payload(down, up):
    ranks, width = down.shape
    groups, size = up.shape[1] * up.shape[2], up.shape[3]
    return pl.pallas_call(
        payload_kernel,
        out_shape=pltpu.VMEM((ranks, width + groups * size), jnp.bfloat16),
        in_specs=[pl.BlockSpec(memory_space=pltpu.HBM)] * 2,
        out_specs=VMEM,
        scratch_shapes=[
            pltpu.VMEM(up.shape, jnp.bfloat16),
            pltpu.VMEM((ranks * groups, size), jnp.float32),
            pltpu.SemaphoreType.DMA((2,)),
        ],
        compiler_params=params(8),
        name="payload",
    )(in_hbm(down), in_hbm(up))


def cache_copies(cache_hbm, k, v, sems, i, chunk):
    mine = pl.ds(i * chunk, chunk)
    return [pltpu.make_async_copy(cache_hbm.at[mine, :, n], ref.at[mine], sems.at[i, n]) for n, ref in enumerate((k, v))]


class Cached:
    def __init__(self, chunk, heads, scale, inputs, outputs, scratch):
        self.chunk, self.heads, self.scale = chunk, heads, scale
        self.lengths_hbm, self.cache_hbm, self.q = inputs
        self.k, self.v, self.sums, self.tops, self.totals = outputs
        self.lengths, *rest = scratch
        self.scores, self.weights = rest[0:2], rest[2:4]
        self.sems, self.length_sem = rest[4:]
        self.rows, self.queries, self.size = self.q.shape
        self.slots, self.own = self.k.shape[1:3]
        self.keys = self.slots * self.own
        own, queries = self.own, self.queries
        line = lax.broadcasted_iota(jnp.int32, (self.keys, 2 * queries), 0)
        query = lax.broadcasted_iota(jnp.int32, (self.keys, 2 * queries), 1)
        self.line = jnp.where(line % own == (query % heads) // (heads // own), line, self.keys)
        self.one = lax.broadcasted_iota(jnp.int32, (1, 2 * queries), 1) < queries
        self.nothing = jnp.zeros((queries, self.size), jnp.bfloat16)

    def copies(self, i):
        return cache_copies(self.cache_hbm, self.k, self.v, self.sems, i, self.chunk)

    def lengths_copy(self):
        return pltpu.make_async_copy(self.lengths_hbm, self.lengths, self.length_sem)

    def start(self, i):
        for copy in self.copies(i):
            copy.start()

    def arrive(self, i):
        for copy in self.copies(i):
            copy.wait()

    def lines(self, ref, r):
        flat = ref.reshape(self.rows, self.keys, self.size)
        return jnp.concatenate([flat[r], flat[r + 1]], axis=1)

    def score(self, i, slot):
        for p in range(self.chunk // 2):
            r = i * self.chunk + 2 * p
            both_q = jnp.concatenate(
                [
                    jnp.concatenate([self.q[r], self.nothing], axis=1),
                    jnp.concatenate([self.nothing, self.q[r + 1]], axis=1),
                ],
                axis=0,
            )
            self.scores[slot][p] = lax.dot_general(
                self.lines(self.k, r), both_q, NT, preferred_element_type=jnp.float32
            )

    def soften(self, i, slot):
        for p in range(self.chunk // 2):
            r = i * self.chunk + 2 * p
            limit = jnp.where(self.one, self.own * self.lengths[r], self.own * self.lengths[r + 1])
            scores = jnp.where(self.line < limit, self.scores[slot][p], LOW)
            top = jnp.max(scores, axis=0, keepdims=True)
            expo = jnp.exp((scores - top) * self.scale)
            self.weights[slot][p] = expo.astype(jnp.bfloat16)
            pair = pl.ds(i * (self.chunk // 2) + p, 1)
            self.tops[pair, :] = top
            self.totals[pair, :] = jnp.sum(expo, axis=0, keepdims=True)

    def collect(self, i, slot):
        queries, size = self.queries, self.size
        for p in range(self.chunk // 2):
            r = i * self.chunk + 2 * p
            both = lax.dot_general(
                self.weights[slot][p], self.lines(self.v, r), TN, preferred_element_type=jnp.float32
            )
            for h in range(2):
                self.sums[r + h] = both[h * queries : (h + 1) * queries, h * size : (h + 1) * size]


def cached_kernel(chunk, early, heads, scale, *refs):
    cached = Cached(chunk, heads, scale, refs[:3], refs[5:10], refs[10:])
    chunks = cached.rows // chunk
    cached.lengths_copy().start()
    for i in range(early, chunks):
        cached.start(i)
    cached.lengths_copy().wait()
    cached.score(0, 0)
    cached.score(1, 1)
    cached.soften(0, 0)

    @pl.loop(1, chunks // 2)
    def _(t):
        for slot in range(2):
            i = 2 * t + slot

            @pl.when(i >= early)
            def _():
                cached.arrive(i)

            cached.score(i, slot)
            cached.soften(i - 1, 1 - slot)
            cached.collect(i - 2, slot)

    cached.soften(chunks - 1, 1)
    cached.collect(chunks - 2, 0)
    cached.collect(chunks - 1, 1)


def attend_cached(queries, cache, lengths, keys, values, steps, chunk, early):
    rows, many, size = queries.shape
    slots, own = cache.shape[1], cache.shape[3]
    heads = many // steps
    half = (rows, slots, own, size)
    scores = (chunk // 2, slots * own, 2 * many)
    line = (rows // 2, 2 * many)
    outs = (
        pltpu.VMEM(half, jnp.bfloat16),
        pltpu.VMEM(half, jnp.bfloat16),
        pltpu.VMEM((rows, many, size), jnp.float32),
        pltpu.VMEM(line, jnp.float32),
        pltpu.VMEM(line, jnp.float32),
    )
    _, _, *state = pl.pallas_call(
        functools.partial(cached_kernel, chunk, early, heads, size ** (-0.5)),
        out_shape=outs,
        in_specs=[pl.BlockSpec(memory_space=pltpu.HBM)] * 2 + [VMEM] * 3,
        out_specs=(VMEM,) * len(outs),
        scratch_shapes=[
            pltpu.SMEM(lengths.shape, jnp.int32),
            pltpu.VMEM(scores, jnp.float32),
            pltpu.VMEM(scores, jnp.float32),
            pltpu.VMEM(scores, jnp.bfloat16),
            pltpu.VMEM(scores, jnp.bfloat16),
            pltpu.SemaphoreType.DMA((rows // chunk, 2)),
            pltpu.SemaphoreType.DMA,
        ],
        input_output_aliases={3: 0, 4: 1},
        compiler_params=params(16),
        cost_estimate=cost(8 * rows * many * slots * size, 4 * rows * slots * own * size, rows * many * slots * own),
        name="attend_cached",
    )(in_hbm(lengths), in_hbm(cache), in_vmem(queries), keys, values)
    return [queries, *state]


def arrange_kernel(chunks, chunk, early, *refs):
    cache_hbm, hidden_hbm, base_hbm, tokens_ref, base_ref, k, v, hidden, base, base_sems, sems = refs
    width, two, kvh, size = base.shape
    own = k.shape[2]
    groups = two * kvh
    some_width = width // chunks
    copies = [copy for i in range(early) for copy in cache_copies(cache_hbm, k, v, sems, i, chunk)]
    get_hidden = pltpu.make_async_copy(hidden_hbm, hidden, base_sems.at[chunks])

    def get_base(i):
        features = pl.ds(i * some_width, some_width)
        return pltpu.make_async_copy(base_hbm.at[features], base.at[features], base_sems.at[i])

    for i in range(chunks):
        get_base(i).start()
    get_hidden.start()
    for copy in copies:
        copy.start()

    tile = 256
    some = tile // groups
    row = lax.broadcasted_iota(jnp.int32, (tile, tile), 0)
    place = lax.broadcasted_iota(jnp.int32, (tile, tile), 1)
    order = (place == (row % some) * groups + row // some).astype(jnp.float32).astype(jnp.bfloat16)
    flat_base = base.reshape(width * groups, size)

    def arrange(f):
        at = pl.multiple_of(f * groups, tile)
        pair = jnp.concatenate([flat_base[pl.ds(at + h * tile, tile), :] for h in range(2)], axis=1)
        moved = jnp.dot(order, pair, preferred_element_type=jnp.float32).astype(jnp.bfloat16)
        for n in range(groups):
            lanes = slice((n % own) * size, (n % own + 1) * size)
            for h in range(2):
                base_ref[n // own, pl.ds(pl.multiple_of(f + h * some, some), some), lanes] = moved[
                    n * some : (n + 1) * some, h * size : (h + 1) * size
                ]

    @pl.loop(0, chunks)
    def _(i):
        get_base(i).wait()
        for f in range(0, some_width, 2 * some):
            arrange(i * some_width + f)

    get_hidden.wait()
    tokens_ref[...] = hidden.reshape(tokens_ref.shape)[...]
    for copy in copies:
        copy.wait()


def arrange(hidden, base, cache, chunk, early):
    rows, steps, _ = hidden.shape
    slots, own = cache.shape[1], cache.shape[3]
    width, two, kvh, size = base.shape
    half = pltpu.VMEM((rows, slots, own, size), jnp.bfloat16)
    chunks = 4
    outs = (
        pltpu.VMEM((rows * steps, width), jnp.bfloat16),
        pltpu.VMEM((two * kvh // own, width, own * size), jnp.bfloat16),
        half,
        half,
    )
    return pl.pallas_call(
        functools.partial(arrange_kernel, chunks, chunk, early),
        out_shape=outs,
        in_specs=[pl.BlockSpec(memory_space=pltpu.HBM)] * 3,
        out_specs=(VMEM,) * len(outs),
        scratch_shapes=[
            pltpu.VMEM(hidden.shape, jnp.bfloat16),
            pltpu.VMEM(base.shape, jnp.bfloat16),
            pltpu.SemaphoreType.DMA((chunks + 1,)),
            pltpu.SemaphoreType.DMA((early, 2)),
        ],
        compiler_params=params(16),
        cost_estimate=cost(512 * base.size, 4 * (base.size + hidden.size)),
        name="arrange",
    )(in_hbm(cache), in_hbm(hidden), in_hbm(base))


def project_kernel(k, hidden_ref, base_ref, *refs):
    gathered, (out_ref, merged) = refs[:-2], refs[-2:]
    width, columns = merged.shape
    part = lax.axis_index("tp") ^ k
    parts = base_ref.shape[0] // 2
    half = columns // 2
    up = jnp.concatenate(
        [
            jnp.concatenate(
                [ref[:, pl.ds(pl.multiple_of(width + (c * parts + part) * half, 128), half)] for ref in gathered], axis=0
            )
            for c in range(2)
        ],
        axis=1,
    )
    step = 256

    def merge(first, last):
        for f in range(first, last, step):
            down = jnp.concatenate([ref[:, f : f + step] for ref in gathered], axis=0).T
            low_rank = jnp.dot(down, up, preferred_element_type=jnp.float32)
            for c in range(2):
                base = base_ref[c * parts + part, f : f + step, :].astype(jnp.float32)
                merged[f : f + step, c * half : (c + 1) * half] = (
                    base + low_rank[:, c * half : (c + 1) * half]
                ).astype(jnp.bfloat16)

    cuts = [0, width // 2, width]
    total = None
    for first, last in zip(cuts, cuts[1:]):
        merge(first, last)
        product = jnp.dot(hidden_ref[:, first:last], merged[first:last, :], preferred_element_type=jnp.float32)
        total = product if total is None else total + product
    out_ref[...] = total


def project(k, hidden, base, gathered):
    tokens, width = hidden.shape
    columns = 2 * base.shape[2]
    ranks = sum(g.shape[0] for g in gathered)
    return pl.pallas_call(
        functools.partial(project_kernel, k),
        out_shape=pltpu.VMEM((tokens, columns), jnp.float32),
        in_specs=[VMEM] * (2 + len(gathered)),
        out_specs=VMEM,
        scratch_shapes=[pltpu.VMEM((width, columns), jnp.bfloat16)],
        compiler_params=params(24),
        cost_estimate=cost(2 * width * columns * (tokens + ranks), 2 * width * columns + 2 * width * tokens),
        name="project",
    )(hidden, base, *gathered)


def finish_kernel(steps, heads, scale, terms, *refs):
    parts, refs = refs[:terms], refs[terms:]
    q_ref, old_ref, top_ref, total_ref = refs[:4]
    refs = refs[4:]
    fresh_hbm, context_hbm, wide, fresh_ref, context_ref, sems = refs
    rows, queries, size = context_ref.shape
    own = fresh_ref.shape[3]
    fresh = parts[0][...]
    for part in parts[1:]:
        fresh = fresh + part[...]
    keys, many = 2 * own * steps, 2 * queries
    group = size // keys
    key = lax.broadcasted_iota(jnp.int32, (keys, many), 0)
    query = lax.broadcasted_iota(jnp.int32, (keys, many), 1)
    same_head = (query % heads) // (heads // own) == key // (2 * steps)
    same_row = query // queries == (key // steps) % 2
    live = same_head & same_row & ((query % queries) // heads >= key % steps)
    nothing = jnp.zeros((keys, size), jnp.bfloat16)

    def new_lines(c, pair):
        tokens = slice(pair * 2 * steps, (pair + 1) * 2 * steps)
        lines = [fresh[tokens, (c * own + g) * size : (c * own + g + 1) * size] for g in range(own)]
        return jnp.concatenate(lines, axis=0).astype(jnp.bfloat16)

    def rows_of(ref, pair):
        return ref[2 * pair : 2 * pair + 2].reshape(many, size)

    def two_scores(p):
        lines = jnp.concatenate(
            [
                jnp.concatenate([new_lines(0, p), nothing], axis=1),
                jnp.concatenate([nothing, new_lines(0, p + 1)], axis=1),
            ],
            axis=0,
        )
        both_q = jnp.concatenate([rows_of(q_ref, p), rows_of(q_ref, p + 1)], axis=1)
        return lax.dot_general(lines, both_q, NT, preferred_element_type=jnp.float32).reshape(2, keys, many)

    scores = jnp.concatenate([two_scores(p) for p in range(0, rows // 2, 2)], axis=0)
    scores = jnp.where(live[None], scores, LOW)
    old_top = top_ref[...]
    top = jnp.maximum(old_top, jnp.max(scores, axis=1))
    expo = jnp.exp((scores - top[:, None, :]) * scale)
    back = jnp.exp((old_top - top) * scale)
    inverse = 1.0 / (back * total_ref[...] + jnp.sum(expo, axis=1))
    weights = (expo * inverse[:, None, :]).astype(jnp.bfloat16)
    back = back * inverse

    for n in range(2 * own):
        wide[pl.ds(n, rows * steps, stride=2 * own), :] = fresh[:, n * size : (n + 1) * size]
    fresh_ref.reshape(rows * steps * 2 * own, size)[...] = wide[...].astype(jnp.bfloat16)
    puts = [pltpu.make_async_copy(fresh_ref, fresh_hbm, sems.at[0])]
    puts[0].start()

    for at in range(0, rows // 2, group):
        pairs = range(at, at + group)
        values = jnp.concatenate(
            [
                jnp.concatenate([new_lines(1, p) if n == p else nothing for n in pairs], axis=1)
                for p in pairs
            ],
            axis=0,
        )
        new = lax.dot_general(
            weights[at : at + group].reshape(group * keys, many), values, TN, preferred_element_type=jnp.float32
        )
        factors = back[at : at + group].T
        for n, p in enumerate(pairs):
            both = new[:, n * size : (n + 1) * size] + factors[:, n : n + 1] * rows_of(old_ref, p)
            context_ref[2 * p : 2 * p + 2] = both.astype(jnp.bfloat16).reshape(2, queries, size)
        mine = pl.ds(2 * at, 2 * group)
        puts.append(pltpu.make_async_copy(context_ref.at[mine], context_hbm.at[mine], sems.at[1 + at // group]))
        puts[-1].start()
    for put in puts:
        put.wait()


def finish(parts, state, steps, own):
    rows, many, size = state[0].shape
    heads = many // steps
    groups = rows * own * steps // size
    fresh = (rows, steps, 2, own, size)
    fresh, context = pl.pallas_call(
        functools.partial(finish_kernel, steps, heads, size ** (-0.5), len(parts)),
        out_shape=(
            jax.ShapeDtypeStruct(fresh, jnp.bfloat16),
            jax.ShapeDtypeStruct((rows, many, size), jnp.bfloat16),
        ),
        in_specs=[VMEM] * (len(parts) + 4),
        out_specs=(pl.BlockSpec(memory_space=pltpu.HBM),) * 2,
        scratch_shapes=[
            pltpu.VMEM((rows * steps * 2 * own, size), jnp.float32),
            pltpu.VMEM(fresh, jnp.bfloat16),
            pltpu.VMEM((rows, many, size), jnp.bfloat16),
            pltpu.SemaphoreType.DMA((1 + groups,)),
        ],
        compiler_params=params(24),
        cost_estimate=cost(rows * many * size * size * 6, 8 * rows * many * size, rows * many * size * 2),
        name="finish",
    )(*parts, *state)
    return fresh, context.reshape(rows, steps, heads, size)


def join_kernel(*refs):
    blocks, out_ref = refs[:-1], refs[-1]
    at = 0
    for block in blocks:
        out_ref[at : at + block.shape[0], :] = block[...]
        at += block.shape[0]


def join(blocks):
    rows = sum(b.shape[0] for b in blocks)
    return pl.pallas_call(
        join_kernel,
        out_shape=pltpu.VMEM((rows, blocks[0].shape[1]), jnp.bfloat16),
        in_specs=[VMEM] * len(blocks),
        out_specs=VMEM,
        compiler_params=params(8),
        name="join",
    )(*blocks)


def gather_second(factor_a, factor_b, dp):
    count = dp // 2
    ranks = factor_b.shape[0]
    if ranks % 8 == 0 and count in (1, 2, 4):
        payload = make_payload(factor_a.T, factor_b)
        return [payload] + [lax.ppermute(payload, "dp", [(i, i ^ (2 * k)) for i in range(dp)]) for k in range(count - 1, 0, -1)]
    payload = jnp.concatenate([factor_a.T, factor_b.reshape(ranks, -1)], axis=1)
    groups = [[i for i in range(dp) if i % 2 == n] for n in range(2)]
    copies = jnp.broadcast_to(payload[None], (count,) + payload.shape)
    blocks = lax.all_to_all(copies, "dp", 0, 0, axis_index_groups=groups, tiled=True)
    return [blocks.reshape(count * ranks, payload.shape[1])]


def shards(dp, tp, hidden, base_weight, factor_a, factor_b, queries, cache, lengths):
    steps, own = queries.shape[1], cache.shape[3]
    assert dp % 2 == 0
    blocks = gather_second(factor_a, factor_b, dp)
    rows, steps, heads, size = queries.shape
    queries = queries.reshape(rows, steps * heads, size)
    chunk, early = 12, 2
    tokens, base, keys, values = arrange(hidden, base_weight, cache, chunk, early)
    blocks, tokens, base, keys, values = lax.optimization_barrier((blocks, tokens, base, keys, values))
    gathered = join(blocks) if len(blocks) > 1 else blocks[0]
    gathered = [gathered, lax.ppermute(gathered, "dp", [(i, i ^ 1) for i in range(dp)])]
    state = attend_cached(queries, cache, lengths, keys, values, steps, chunk, early)
    gathered, state, tokens, base = lax.optimization_barrier((gathered, state, tokens, base))
    received = []
    for k in range(1, tp):
        other = project(k, tokens, base, gathered)
        received.append(lax.ppermute(other, "tp", [(i, i ^ k) for i in range(tp)]))
    mine = project(0, tokens, base, gathered)
    return finish([mine] + received, state, steps, own)


def solution(mesh):
    return jax.shard_map(
        functools.partial(shards, mesh.shape["dp"], mesh.shape["tp"]),
        mesh=mesh,
        in_specs=(
            P(("parts", "dp"), None, "tp"),
            P("tp", None, None, None),
            P(("parts", "tp"), "dp"),
            P(("parts", "dp"), None, None, None),
            P(("parts", "dp"), None, "tp", None),
            P(("parts", "dp"), None, None, "tp", None),
            P(("parts", "dp")),
        ),
        out_specs=(
            P(("parts", "dp"), None, None, "tp", None),
            P(("parts", "dp"), None, "tp", None),
        ),
        check_vma=False,
    )
```

```python
import functools

import jax
import jax.numpy as jnp
from jax import lax
from jax.experimental import pallas as pl
from jax.experimental.pallas import tpu as pltpu
from jax.sharding import PartitionSpec as P

LOW = -1e30
NT = (((1,), (1,)), ((), ()))
TN = (((0,), (0,)), ((), ()))
VMEM = pl.BlockSpec(memory_space=pltpu.VMEM)


def params(mib):
    return pltpu.CompilerParams(vmem_limit_bytes=mib * 1024 * 1024)


def in_hbm(x):
    return pltpu.with_memory_space_constraint(x, pltpu.HBM)


def in_vmem(x):
    return pltpu.with_memory_space_constraint(x, pltpu.VMEM)


def cost(flops, moved, exps=0):
    return pl.CostEstimate(flops=flops, bytes_accessed=moved, transcendentals=exps)


def payload_kernel(down_hbm, up_hbm, out_ref, ups, wide, sems):
    ranks, width = down_hbm.shape
    _, two, kvh, size = ups.shape
    groups, own = two * kvh, kvh // 2
    get_down = pltpu.make_async_copy(down_hbm, out_ref.at[:, pl.ds(0, width)], sems.at[0])
    get_up = pltpu.make_async_copy(up_hbm, ups, sems.at[1])
    get_up.start()
    get_down.start()
    get_up.wait()
    wide[...] = ups.reshape(ranks * groups, size)[...].astype(jnp.float32)
    other = 1 - lax.axis_index("tp")
    for n in range(groups // 2):
        head = n // own * kvh + other * own + n % own
        out_ref[:, width + n * size : width + (n + 1) * size] = wide[pl.ds(head, ranks, stride=groups), :].astype(
            jnp.bfloat16
        )
    get_down.wait()


def make_payload(down, up):
    ranks, width = down.shape
    groups, size = up.shape[1] * up.shape[2], up.shape[3]
    return pl.pallas_call(
        payload_kernel,
        out_shape=pltpu.VMEM((ranks, width + groups // 2 * size), jnp.bfloat16),
        in_specs=[pl.BlockSpec(memory_space=pltpu.HBM)] * 2,
        out_specs=VMEM,
        scratch_shapes=[
            pltpu.VMEM(up.shape, jnp.bfloat16),
            pltpu.VMEM((ranks * groups, size), jnp.float32),
            pltpu.SemaphoreType.DMA((2,)),
        ],
        compiler_params=params(8),
        name="payload",
    )(in_hbm(down), in_hbm(up))


def cache_copies(cache_hbm, k, v, sems, i, chunk):
    mine = pl.ds(i * chunk, chunk)
    return [pltpu.make_async_copy(cache_hbm.at[mine, :, n], ref.at[mine], sems.at[i, n]) for n, ref in enumerate((k, v))]


class Cached:
    def __init__(self, chunk, heads, scale, inputs, outputs, scratch):
        self.chunk, self.heads, self.scale = chunk, heads, scale
        self.lengths_hbm, self.cache_hbm, self.q = inputs
        self.k, self.v, self.sums, self.tops, self.totals = outputs
        self.lengths, *rest = scratch
        self.scores, self.weights = rest[0:2], rest[2:4]
        self.sems, self.length_sem = rest[4:]
        self.rows, self.queries, self.size = self.q.shape
        self.slots, self.own = self.k.shape[1:3]
        self.keys = self.slots * self.own
        own, queries = self.own, self.queries
        line = lax.broadcasted_iota(jnp.int32, (self.keys, 2 * queries), 0)
        query = lax.broadcasted_iota(jnp.int32, (self.keys, 2 * queries), 1)
        self.line = jnp.where(line % own == (query % heads) // (heads // own), line, self.keys)
        self.one = lax.broadcasted_iota(jnp.int32, (1, 2 * queries), 1) < queries
        self.nothing = jnp.zeros((queries, self.size), jnp.bfloat16)

    def copies(self, i):
        return cache_copies(self.cache_hbm, self.k, self.v, self.sems, i, self.chunk)

    def lengths_copy(self):
        return pltpu.make_async_copy(self.lengths_hbm, self.lengths, self.length_sem)

    def start(self, i):
        for copy in self.copies(i):
            copy.start()

    def arrive(self, i):
        for copy in self.copies(i):
            copy.wait()

    def lines(self, ref, r):
        flat = ref.reshape(self.rows, self.keys, self.size)
        return jnp.concatenate([flat[r], flat[r + 1]], axis=1)

    def score(self, i, slot):
        for p in range(self.chunk // 2):
            r = i * self.chunk + 2 * p
            both_q = jnp.concatenate(
                [
                    jnp.concatenate([self.q[r], self.nothing], axis=1),
                    jnp.concatenate([self.nothing, self.q[r + 1]], axis=1),
                ],
                axis=0,
            )
            self.scores[slot][p] = lax.dot_general(
                self.lines(self.k, r), both_q, NT, preferred_element_type=jnp.float32
            )

    def soften(self, i, slot):
        for p in range(self.chunk // 2):
            r = i * self.chunk + 2 * p
            limit = jnp.where(self.one, self.own * self.lengths[r], self.own * self.lengths[r + 1])
            scores = jnp.where(self.line < limit, self.scores[slot][p], LOW)
            top = jnp.max(scores, axis=0, keepdims=True)
            expo = jnp.exp((scores - top) * self.scale)
            self.weights[slot][p] = expo.astype(jnp.bfloat16)
            pair = pl.ds(i * (self.chunk // 2) + p, 1)
            self.tops[pair, :] = top
            self.totals[pair, :] = jnp.sum(expo, axis=0, keepdims=True)

    def collect(self, i, slot):
        queries, size = self.queries, self.size
        for p in range(self.chunk // 2):
            r = i * self.chunk + 2 * p
            both = lax.dot_general(
                self.weights[slot][p], self.lines(self.v, r), TN, preferred_element_type=jnp.float32
            )
            for h in range(2):
                self.sums[r + h] = both[h * queries : (h + 1) * queries, h * size : (h + 1) * size]


def cached_kernel(chunk, early, heads, scale, *refs):
    cached = Cached(chunk, heads, scale, refs[:3], refs[5:10], refs[10:])
    chunks = cached.rows // chunk
    cached.lengths_copy().start()
    for i in range(early, chunks):
        cached.start(i)
    cached.lengths_copy().wait()
    cached.score(0, 0)
    cached.score(1, 1)
    cached.soften(0, 0)

    @pl.loop(1, chunks // 2)
    def _(t):
        for slot in range(2):
            i = 2 * t + slot

            @pl.when(i >= early)
            def _():
                cached.arrive(i)

            cached.score(i, slot)
            cached.soften(i - 1, 1 - slot)
            cached.collect(i - 2, slot)

    cached.soften(chunks - 1, 1)
    cached.collect(chunks - 2, 0)
    cached.collect(chunks - 1, 1)


def attend_cached(queries, cache, lengths, keys, values, steps, chunk, early):
    rows, many, size = queries.shape
    slots, own = cache.shape[1], cache.shape[3]
    heads = many // steps
    half = (rows, slots, own, size)
    scores = (chunk // 2, slots * own, 2 * many)
    line = (rows // 2, 2 * many)
    outs = (
        pltpu.VMEM(half, jnp.bfloat16),
        pltpu.VMEM(half, jnp.bfloat16),
        pltpu.VMEM((rows, many, size), jnp.float32),
        pltpu.VMEM(line, jnp.float32),
        pltpu.VMEM(line, jnp.float32),
    )
    _, _, *state = pl.pallas_call(
        functools.partial(cached_kernel, chunk, early, heads, size ** (-0.5)),
        out_shape=outs,
        in_specs=[pl.BlockSpec(memory_space=pltpu.HBM)] * 2 + [VMEM] * 3,
        out_specs=(VMEM,) * len(outs),
        scratch_shapes=[
            pltpu.SMEM(lengths.shape, jnp.int32),
            pltpu.VMEM(scores, jnp.float32),
            pltpu.VMEM(scores, jnp.float32),
            pltpu.VMEM(scores, jnp.bfloat16),
            pltpu.VMEM(scores, jnp.bfloat16),
            pltpu.SemaphoreType.DMA((rows // chunk, 2)),
            pltpu.SemaphoreType.DMA,
        ],
        input_output_aliases={3: 0, 4: 1},
        compiler_params=params(16),
        cost_estimate=cost(8 * rows * many * slots * size, 4 * rows * slots * own * size, rows * many * slots * own),
        name="attend_cached",
    )(in_hbm(lengths), in_hbm(cache), in_vmem(queries), keys, values)
    return [queries, *state]


def arrange_kernel(chunks, chunk, early, *refs):
    cache_hbm, hidden_hbm, base_hbm, tokens_ref, base_ref, k, v, hidden, base, base_sems, sems = refs
    width, two, kvh, size = base.shape
    own = k.shape[2]
    groups = two * kvh
    some_width = width // chunks
    copies = [copy for i in range(early) for copy in cache_copies(cache_hbm, k, v, sems, i, chunk)]
    get_hidden = pltpu.make_async_copy(hidden_hbm, hidden, base_sems.at[chunks])

    def get_base(i):
        features = pl.ds(i * some_width, some_width)
        return pltpu.make_async_copy(base_hbm.at[features], base.at[features], base_sems.at[i])

    for i in range(chunks):
        get_base(i).start()
    get_hidden.start()
    for copy in copies:
        copy.start()

    tile = 256
    some = tile // groups
    row = lax.broadcasted_iota(jnp.int32, (tile, tile), 0)
    place = lax.broadcasted_iota(jnp.int32, (tile, tile), 1)
    order = (place == (row % some) * groups + row // some).astype(jnp.float32).astype(jnp.bfloat16)
    flat_base = base.reshape(width * groups, size)

    def arrange(f):
        at = pl.multiple_of(f * groups, tile)
        pair = jnp.concatenate([flat_base[pl.ds(at + h * tile, tile), :] for h in range(2)], axis=1)
        moved = jnp.dot(order, pair, preferred_element_type=jnp.float32).astype(jnp.bfloat16)
        for n in range(groups):
            lanes = slice((n % own) * size, (n % own + 1) * size)
            for h in range(2):
                base_ref[n // own, pl.ds(pl.multiple_of(f + h * some, some), some), lanes] = moved[
                    n * some : (n + 1) * some, h * size : (h + 1) * size
                ]

    @pl.loop(0, chunks)
    def _(i):
        get_base(i).wait()
        for f in range(0, some_width, 2 * some):
            arrange(i * some_width + f)

    get_hidden.wait()
    tokens_ref[...] = hidden.reshape(tokens_ref.shape)[...]
    for copy in copies:
        copy.wait()


def arrange(hidden, base, cache, chunk, early):
    rows, steps, _ = hidden.shape
    slots, own = cache.shape[1], cache.shape[3]
    width, two, kvh, size = base.shape
    half = pltpu.VMEM((rows, slots, own, size), jnp.bfloat16)
    chunks = 4
    outs = (
        pltpu.VMEM((rows * steps, width), jnp.bfloat16),
        pltpu.VMEM((two * kvh // own, width, own * size), jnp.bfloat16),
        half,
        half,
    )
    return pl.pallas_call(
        functools.partial(arrange_kernel, chunks, chunk, early),
        out_shape=outs,
        in_specs=[pl.BlockSpec(memory_space=pltpu.HBM)] * 3,
        out_specs=(VMEM,) * len(outs),
        scratch_shapes=[
            pltpu.VMEM(hidden.shape, jnp.bfloat16),
            pltpu.VMEM(base.shape, jnp.bfloat16),
            pltpu.SemaphoreType.DMA((chunks + 1,)),
            pltpu.SemaphoreType.DMA((early, 2)),
        ],
        compiler_params=params(16),
        cost_estimate=cost(512 * base.size, 4 * (base.size + hidden.size)),
        name="arrange",
    )(in_hbm(cache), in_hbm(hidden), in_hbm(base))


def project_kernel(k, at, count, hidden_ref, base_ref, *refs):
    downs, ups, (out_ref, merged) = refs[:count], refs[count:-2], refs[-2:]
    width, columns = merged.shape
    part = lax.axis_index("tp") ^ k
    parts = base_ref.shape[0] // 2
    half = columns // 2
    up = jnp.concatenate([ref[:, at : at + columns] for ref in ups], axis=0)
    step = 256

    def merge(first, last):
        for f in range(first, last, step):
            down = jnp.concatenate([ref[:, f : f + step] for ref in downs], axis=0).T
            low_rank = jnp.dot(down, up, preferred_element_type=jnp.float32)
            for c in range(2):
                base = base_ref[c * parts + part, f : f + step, :].astype(jnp.float32)
                merged[f : f + step, c * half : (c + 1) * half] = (
                    base + low_rank[:, c * half : (c + 1) * half]
                ).astype(jnp.bfloat16)

    cuts = [0, width // 2, width]
    total = None
    for first, last in zip(cuts, cuts[1:]):
        merge(first, last)
        product = jnp.dot(hidden_ref[:, first:last], merged[first:last, :], preferred_element_type=jnp.float32)
        total = product if total is None else total + product
    out_ref[...] = total


def project(k, hidden, base, downs, ups, at):
    tokens, width = hidden.shape
    columns = 2 * base.shape[2]
    ranks = sum(g.shape[0] for g in downs)
    return pl.pallas_call(
        functools.partial(project_kernel, k, at, len(downs)),
        out_shape=pltpu.VMEM((tokens, columns), jnp.float32),
        in_specs=[VMEM] * (2 + len(downs) + len(ups)),
        out_specs=VMEM,
        scratch_shapes=[pltpu.VMEM((width, columns), jnp.bfloat16)],
        compiler_params=params(24),
        cost_estimate=cost(2 * width * columns * (tokens + ranks), 2 * width * columns + 2 * width * tokens),
        name="project",
    )(hidden, base, *downs, *ups)


def finish_kernel(steps, heads, scale, terms, *refs):
    parts, refs = refs[:terms], refs[terms:]
    q_ref, old_ref, top_ref, total_ref = refs[:4]
    refs = refs[4:]
    fresh_hbm, context_hbm, wide, fresh_ref, context_ref, sems = refs
    rows, queries, size = context_ref.shape
    own = fresh_ref.shape[3]
    fresh = parts[0][...]
    for part in parts[1:]:
        fresh = fresh + part[...]
    keys, many = 2 * own * steps, 2 * queries
    group = size // keys
    key = lax.broadcasted_iota(jnp.int32, (keys, many), 0)
    query = lax.broadcasted_iota(jnp.int32, (keys, many), 1)
    same_head = (query % heads) // (heads // own) == key // (2 * steps)
    same_row = query // queries == (key // steps) % 2
    live = same_head & same_row & ((query % queries) // heads >= key % steps)
    nothing = jnp.zeros((keys, size), jnp.bfloat16)

    def new_lines(c, pair):
        tokens = slice(pair * 2 * steps, (pair + 1) * 2 * steps)
        lines = [fresh[tokens, (c * own + g) * size : (c * own + g + 1) * size] for g in range(own)]
        return jnp.concatenate(lines, axis=0).astype(jnp.bfloat16)

    def rows_of(ref, pair):
        return ref[2 * pair : 2 * pair + 2].reshape(many, size)

    scores = [
        lax.dot_general(new_lines(0, p), rows_of(q_ref, p), NT, preferred_element_type=jnp.float32)
        for p in range(rows // 2)
    ]
    scores = jnp.stack([jnp.where(live, s, LOW) for s in scores])
    old_top = top_ref[...]
    top = jnp.maximum(old_top, jnp.max(scores, axis=1))
    expo = jnp.exp((scores - top[:, None, :]) * scale)
    back = jnp.exp((old_top - top) * scale)
    inverse = 1.0 / (back * total_ref[...] + jnp.sum(expo, axis=1))
    weights = (expo * inverse[:, None, :]).astype(jnp.bfloat16)
    back = back * inverse

    for n in range(2 * own):
        wide[pl.ds(n, rows * steps, stride=2 * own), :] = fresh[:, n * size : (n + 1) * size]
    fresh_ref.reshape(rows * steps * 2 * own, size)[...] = wide[...].astype(jnp.bfloat16)
    puts = [pltpu.make_async_copy(fresh_ref, fresh_hbm, sems.at[0])]
    puts[0].start()

    for at in range(0, rows // 2, group):
        pairs = range(at, at + group)
        values = jnp.concatenate(
            [
                jnp.concatenate([new_lines(1, p) if n == p else nothing for n in pairs], axis=1)
                for p in pairs
            ],
            axis=0,
        )
        new = lax.dot_general(
            weights[at : at + group].reshape(group * keys, many), values, TN, preferred_element_type=jnp.float32
        )
        factors = back[at : at + group].T
        for n, p in enumerate(pairs):
            both = new[:, n * size : (n + 1) * size] + factors[:, n : n + 1] * rows_of(old_ref, p)
            context_ref[2 * p : 2 * p + 2] = both.astype(jnp.bfloat16).reshape(2, queries, size)
        mine = pl.ds(2 * at, 2 * group)
        puts.append(pltpu.make_async_copy(context_ref.at[mine], context_hbm.at[mine], sems.at[1 + at // group]))
        puts[-1].start()
    for put in puts:
        put.wait()


def finish(parts, state, steps, own):
    rows, many, size = state[0].shape
    heads = many // steps
    groups = rows * own * steps // size
    fresh = (rows, steps, 2, own, size)
    fresh, context = pl.pallas_call(
        functools.partial(finish_kernel, steps, heads, size ** (-0.5), len(parts)),
        out_shape=(
            jax.ShapeDtypeStruct(fresh, jnp.bfloat16),
            jax.ShapeDtypeStruct((rows, many, size), jnp.bfloat16),
        ),
        in_specs=[VMEM] * (len(parts) + 4),
        out_specs=(pl.BlockSpec(memory_space=pltpu.HBM),) * 2,
        scratch_shapes=[
            pltpu.VMEM((rows * steps * 2 * own, size), jnp.float32),
            pltpu.VMEM(fresh, jnp.bfloat16),
            pltpu.VMEM((rows, many, size), jnp.bfloat16),
            pltpu.SemaphoreType.DMA((1 + groups,)),
        ],
        compiler_params=params(24),
        cost_estimate=cost(rows * many * size * size * 6, 8 * rows * many * size, rows * many * size * 2),
        name="finish",
    )(*parts, *state)
    return fresh, context.reshape(rows, steps, heads, size)


def join_kernel(first, *refs):
    blocks, out_ref = refs[:-1], refs[-1]
    at = 0
    for block in blocks:
        out_ref[at : at + block.shape[0], :] = block[:, first:]
        at += block.shape[0]


def join(blocks, first=0):
    rows = sum(b.shape[0] for b in blocks)
    return pl.pallas_call(
        functools.partial(join_kernel, first),
        out_shape=pltpu.VMEM((rows, blocks[0].shape[1] - first), jnp.bfloat16),
        in_specs=[VMEM] * len(blocks),
        out_specs=VMEM,
        compiler_params=params(8),
        name="join",
    )(*blocks)


def shards(dp, tp, hidden, base_weight, factor_a, factor_b, queries, cache, lengths):
    rows, steps, heads, size = queries.shape
    own = cache.shape[3]
    ranks, width = factor_b.shape[0], factor_a.shape[0]
    queries = queries.reshape(rows, steps * heads, size)
    chunk, early = 12, 2

    def swap(x, axis, count, k):
        return lax.ppermute(x, axis, [(i, i ^ k) for i in range(count)])

    short = dp == 8 and tp == 2 and ranks % 8 == 0
    if short:
        payload = make_payload(factor_a.T, factor_b)
        blocks = [payload] + [swap(payload, "dp", dp, k) for k in (6, 4, 2)]
    else:
        payload = jnp.concatenate([factor_a.T, factor_b.reshape(ranks, -1)], axis=1)
        copies = jnp.broadcast_to(payload[None], (dp,) + payload.shape)
        blocks = [lax.all_to_all(copies, "dp", 0, 0, tiled=True).reshape(dp * ranks, payload.shape[1])]
    tokens, base, keys, values = arrange(hidden, base_weight, cache, chunk, early)
    blocks, tokens, base, keys, values = lax.optimization_barrier((blocks, tokens, base, keys, values))
    if short:
        block = join(blocks)
        blocks = [block, swap(block, "dp", dp, 1)]
    state = attend_cached(queries, cache, lengths, keys, values, steps, chunk, early)
    blocks, state, tokens, base = lax.optimization_barrier((blocks, state, tokens, base))
    if short:
        blocks, up = lax.optimization_barrier((blocks, join(blocks, width)))
        ups = {1: (blocks, width), 0: ([swap(up, "tp", tp, 1)], 0)}
    else:
        by_part = blocks[0][:, width:].reshape(-1, 2, tp, own * size)
        me = lax.axis_index("tp")
        pick = [lax.dynamic_index_in_dim(by_part, me ^ k, 2, keepdims=False) for k in range(tp)]
        ups = {k: ([pick[k].reshape(-1, 2 * own * size)], 0) for k in range(tp)}
    received = []
    for k in range(1, tp):
        other = project(k, tokens, base, blocks, *ups[k])
        received.append(swap(other, "tp", tp, k))
    mine = project(0, tokens, base, blocks, *ups[0])
    return finish([mine] + received, state, steps, own)


def solution(mesh):
    return jax.shard_map(
        functools.partial(shards, mesh.shape["dp"], mesh.shape["tp"]),
        mesh=mesh,
        in_specs=(
            P(("parts", "dp"), None, "tp"),
            P("tp", None, None, None),
            P(("parts", "tp"), "dp"),
            P(("parts", "dp"), None, None, None),
            P(("parts", "dp"), None, "tp", None),
            P(("parts", "dp"), None, None, "tp", None),
            P(("parts", "dp")),
        ),
        out_specs=(
            P(("parts", "dp"), None, None, "tp", None),
            P(("parts", "dp"), None, "tp", None),
        ),
        check_vma=False,
    )
```

```python
import functools

import jax
import jax.numpy as jnp
from jax import lax
from jax.experimental import pallas as pl
from jax.experimental.pallas import tpu as pltpu
from jax.sharding import PartitionSpec as P

LOW = -1e30
NT = (((1,), (1,)), ((), ()))
TN = (((0,), (0,)), ((), ()))
VMEM = pl.BlockSpec(memory_space=pltpu.VMEM)


def params(mib):
    return pltpu.CompilerParams(vmem_limit_bytes=mib * 1024 * 1024)


def in_hbm(x):
    return pltpu.with_memory_space_constraint(x, pltpu.HBM)


def in_vmem(x):
    return pltpu.with_memory_space_constraint(x, pltpu.VMEM)


def cost(flops, moved, exps=0):
    return pl.CostEstimate(flops=flops, bytes_accessed=moved, transcendentals=exps)


def payload_kernel(down_hbm, up_hbm, out_ref, ups, wide, sems):
    ranks, width = down_hbm.shape
    groups, size = ups.shape[1] * ups.shape[2], ups.shape[3]
    get_down = pltpu.make_async_copy(down_hbm, out_ref.at[:, pl.ds(0, width)], sems.at[0])
    get_up = pltpu.make_async_copy(up_hbm, ups, sems.at[1])
    get_up.start()
    get_down.start()
    get_up.wait()
    wide[...] = ups.reshape(ranks * groups, size)[...].astype(jnp.float32)
    for n in range(groups):
        out_ref[:, width + n * size : width + (n + 1) * size] = wide[pl.ds(n, ranks, stride=groups), :].astype(
            jnp.bfloat16
        )
    get_down.wait()


def make_payload(down, up):
    ranks, width = down.shape
    groups, size = up.shape[1] * up.shape[2], up.shape[3]
    return pl.pallas_call(
        payload_kernel,
        out_shape=pltpu.VMEM((ranks, width + groups * size), jnp.bfloat16),
        in_specs=[pl.BlockSpec(memory_space=pltpu.HBM)] * 2,
        out_specs=VMEM,
        scratch_shapes=[
            pltpu.VMEM(up.shape, jnp.bfloat16),
            pltpu.VMEM((ranks * groups, size), jnp.float32),
            pltpu.SemaphoreType.DMA((2,)),
        ],
        compiler_params=params(8),
        name="payload",
    )(in_hbm(down), in_hbm(up))


def cache_copies(cache_hbm, k, v, sems, i, chunk):
    mine = pl.ds(i * chunk, chunk)
    return [pltpu.make_async_copy(cache_hbm.at[mine, :, n], ref.at[mine], sems.at[i, n]) for n, ref in enumerate((k, v))]


class Cached:
    def __init__(self, chunk, heads, scale, inputs, outputs, scratch):
        self.chunk, self.heads, self.scale = chunk, heads, scale
        self.lengths_hbm, self.cache_hbm, self.q = inputs
        self.k, self.v, self.sums, self.tops, self.totals = outputs
        self.lengths, *rest = scratch
        self.scores, self.weights = rest[0:2], rest[2:4]
        self.sems, self.length_sem = rest[4:]
        self.rows, self.queries, self.size = self.q.shape
        self.slots, self.own = self.k.shape[1:3]
        self.keys = self.slots * self.own
        own, queries = self.own, self.queries
        line = lax.broadcasted_iota(jnp.int32, (self.keys, 2 * queries), 0)
        query = lax.broadcasted_iota(jnp.int32, (self.keys, 2 * queries), 1)
        self.line = jnp.where(line % own == (query % heads) // (heads // own), line, self.keys)
        self.one = lax.broadcasted_iota(jnp.int32, (1, 2 * queries), 1) < queries
        self.nothing = jnp.zeros((queries, self.size), jnp.bfloat16)

    def copies(self, i):
        return cache_copies(self.cache_hbm, self.k, self.v, self.sems, i, self.chunk)

    def lengths_copy(self):
        return pltpu.make_async_copy(self.lengths_hbm, self.lengths, self.length_sem)

    def start(self, i):
        for copy in self.copies(i):
            copy.start()

    def arrive(self, i):
        for copy in self.copies(i):
            copy.wait()

    def lines(self, ref, r):
        flat = ref.reshape(self.rows, self.keys, self.size)
        return jnp.concatenate([flat[r], flat[r + 1]], axis=1)

    def score(self, i, slot):
        for p in range(self.chunk // 2):
            r = i * self.chunk + 2 * p
            both_q = jnp.concatenate(
                [
                    jnp.concatenate([self.q[r], self.nothing], axis=1),
                    jnp.concatenate([self.nothing, self.q[r + 1]], axis=1),
                ],
                axis=0,
            )
            self.scores[slot][p] = lax.dot_general(
                self.lines(self.k, r), both_q, NT, preferred_element_type=jnp.float32
            )

    def soften(self, i, slot):
        for p in range(self.chunk // 2):
            r = i * self.chunk + 2 * p
            limit = jnp.where(self.one, self.own * self.lengths[r], self.own * self.lengths[r + 1])
            scores = jnp.where(self.line < limit, self.scores[slot][p], LOW)
            top = jnp.max(scores, axis=0, keepdims=True)
            expo = jnp.exp((scores - top) * self.scale)
            self.weights[slot][p] = expo.astype(jnp.bfloat16)
            pair = pl.ds(i * (self.chunk // 2) + p, 1)
            self.tops[pair, :] = top
            self.totals[pair, :] = jnp.sum(expo, axis=0, keepdims=True)

    def collect(self, i, slot):
        queries, size = self.queries, self.size
        for p in range(self.chunk // 2):
            r = i * self.chunk + 2 * p
            both = lax.dot_general(
                self.weights[slot][p], self.lines(self.v, r), TN, preferred_element_type=jnp.float32
            )
            for h in range(2):
                self.sums[r + h] = both[h * queries : (h + 1) * queries, h * size : (h + 1) * size]


def cached_kernel(chunk, early, heads, scale, *refs):
    cached = Cached(chunk, heads, scale, refs[:3], refs[5:10], refs[10:])
    chunks = cached.rows // chunk
    cached.lengths_copy().start()
    for i in range(early, chunks):
        cached.start(i)
    cached.lengths_copy().wait()
    cached.score(0, 0)
    cached.score(1, 1)
    cached.soften(0, 0)

    @pl.loop(1, chunks // 2)
    def _(t):
        for slot in range(2):
            i = 2 * t + slot

            @pl.when(i >= early)
            def _():
                cached.arrive(i)

            cached.score(i, slot)
            cached.soften(i - 1, 1 - slot)
            cached.collect(i - 2, slot)

    cached.soften(chunks - 1, 1)
    cached.collect(chunks - 2, 0)
    cached.collect(chunks - 1, 1)


def attend_cached(queries, cache, lengths, keys, values, steps, chunk, early):
    rows, many, size = queries.shape
    slots, own = cache.shape[1], cache.shape[3]
    heads = many // steps
    half = (rows, slots, own, size)
    scores = (chunk // 2, slots * own, 2 * many)
    line = (rows // 2, 2 * many)
    outs = (
        pltpu.VMEM(half, jnp.bfloat16),
        pltpu.VMEM(half, jnp.bfloat16),
        pltpu.VMEM((rows, many, size), jnp.float32),
        pltpu.VMEM(line, jnp.float32),
        pltpu.VMEM(line, jnp.float32),
    )
    _, _, *state = pl.pallas_call(
        functools.partial(cached_kernel, chunk, early, heads, size ** (-0.5)),
        out_shape=outs,
        in_specs=[pl.BlockSpec(memory_space=pltpu.HBM)] * 2 + [VMEM] * 3,
        out_specs=(VMEM,) * len(outs),
        scratch_shapes=[
            pltpu.SMEM(lengths.shape, jnp.int32),
            pltpu.VMEM(scores, jnp.float32),
            pltpu.VMEM(scores, jnp.float32),
            pltpu.VMEM(scores, jnp.bfloat16),
            pltpu.VMEM(scores, jnp.bfloat16),
            pltpu.SemaphoreType.DMA((rows // chunk, 2)),
            pltpu.SemaphoreType.DMA,
        ],
        input_output_aliases={3: 0, 4: 1},
        compiler_params=params(16),
        cost_estimate=cost(8 * rows * many * slots * size, 4 * rows * slots * own * size, rows * many * slots * own),
        name="attend_cached",
    )(in_hbm(lengths), in_hbm(cache), in_vmem(queries), keys, values)
    return [queries, *state]


def arrange_kernel(chunks, chunk, early, *refs):
    cache_hbm, hidden_hbm, base_hbm, tokens_ref, base_ref, k, v, hidden, base, base_sems, sems = refs
    width, two, kvh, size = base.shape
    own = k.shape[2]
    groups = two * kvh
    some_width = width // chunks
    copies = [copy for i in range(early) for copy in cache_copies(cache_hbm, k, v, sems, i, chunk)]
    get_hidden = pltpu.make_async_copy(hidden_hbm, hidden, base_sems.at[chunks])

    def get_base(i):
        features = pl.ds(i * some_width, some_width)
        return pltpu.make_async_copy(base_hbm.at[features], base.at[features], base_sems.at[i])

    for i in range(chunks):
        get_base(i).start()
    get_hidden.start()
    for copy in copies:
        copy.start()

    tile = 256
    some = tile // groups
    row = lax.broadcasted_iota(jnp.int32, (tile, tile), 0)
    place = lax.broadcasted_iota(jnp.int32, (tile, tile), 1)
    order = (place == (row % some) * groups + row // some).astype(jnp.float32).astype(jnp.bfloat16)
    flat_base = base.reshape(width * groups, size)

    def arrange(f):
        at = pl.multiple_of(f * groups, tile)
        pair = jnp.concatenate([flat_base[pl.ds(at + h * tile, tile), :] for h in range(2)], axis=1)
        moved = jnp.dot(order, pair, preferred_element_type=jnp.float32).astype(jnp.bfloat16)
        for n in range(groups):
            lanes = slice((n % own) * size, (n % own + 1) * size)
            for h in range(2):
                base_ref[n // own, pl.ds(pl.multiple_of(f + h * some, some), some), lanes] = moved[
                    n * some : (n + 1) * some, h * size : (h + 1) * size
                ]

    @pl.loop(0, chunks)
    def _(i):
        get_base(i).wait()
        for f in range(0, some_width, 2 * some):
            arrange(i * some_width + f)

    get_hidden.wait()
    tokens_ref[...] = hidden.reshape(tokens_ref.shape)[...]
    for copy in copies:
        copy.wait()


def arrange(hidden, base, cache, chunk, early):
    rows, steps, _ = hidden.shape
    slots, own = cache.shape[1], cache.shape[3]
    width, two, kvh, size = base.shape
    half = pltpu.VMEM((rows, slots, own, size), jnp.bfloat16)
    chunks = 4
    outs = (
        pltpu.VMEM((rows * steps, width), jnp.bfloat16),
        pltpu.VMEM((two * kvh // own, width, own * size), jnp.bfloat16),
        half,
        half,
    )
    return pl.pallas_call(
        functools.partial(arrange_kernel, chunks, chunk, early),
        out_shape=outs,
        in_specs=[pl.BlockSpec(memory_space=pltpu.HBM)] * 3,
        out_specs=(VMEM,) * len(outs),
        scratch_shapes=[
            pltpu.VMEM(hidden.shape, jnp.bfloat16),
            pltpu.VMEM(base.shape, jnp.bfloat16),
            pltpu.SemaphoreType.DMA((chunks + 1,)),
            pltpu.SemaphoreType.DMA((early, 2)),
        ],
        compiler_params=params(16),
        cost_estimate=cost(512 * base.size, 4 * (base.size + hidden.size)),
        name="arrange",
    )(in_hbm(cache), in_hbm(hidden), in_hbm(base))


def project_kernel(k, hidden_ref, base_ref, *refs):
    gathered, (out_ref, merged) = refs[:-2], refs[-2:]
    width, columns = merged.shape
    part = lax.axis_index("tp") ^ k
    parts = base_ref.shape[0] // 2
    half = columns // 2
    up = jnp.concatenate(
        [
            jnp.concatenate(
                [ref[:, pl.ds(pl.multiple_of(width + (c * parts + part) * half, 128), half)] for ref in gathered], axis=0
            )
            for c in range(2)
        ],
        axis=1,
    )
    step = 256

    def merge(first, last):
        for f in range(first, last, step):
            down = jnp.concatenate([ref[:, f : f + step] for ref in gathered], axis=0).T
            low_rank = jnp.dot(down, up, preferred_element_type=jnp.float32)
            for c in range(2):
                base = base_ref[c * parts + part, f : f + step, :].astype(jnp.float32)
                merged[f : f + step, c * half : (c + 1) * half] = (
                    base + low_rank[:, c * half : (c + 1) * half]
                ).astype(jnp.bfloat16)

    cuts = [0, width // 2, width]
    total = None
    for first, last in zip(cuts, cuts[1:]):
        merge(first, last)
        product = jnp.dot(hidden_ref[:, first:last], merged[first:last, :], preferred_element_type=jnp.float32)
        total = product if total is None else total + product
    out_ref[...] = total


def project(k, hidden, base, gathered):
    tokens, width = hidden.shape
    columns = 2 * base.shape[2]
    ranks = sum(g.shape[0] for g in gathered)
    return pl.pallas_call(
        functools.partial(project_kernel, k),
        out_shape=pltpu.VMEM((tokens, columns), jnp.float32),
        in_specs=[VMEM] * (2 + len(gathered)),
        out_specs=VMEM,
        scratch_shapes=[pltpu.VMEM((width, columns), jnp.bfloat16)],
        compiler_params=params(24),
        cost_estimate=cost(2 * width * columns * (tokens + ranks), 2 * width * columns + 2 * width * tokens),
        name="project",
    )(hidden, base, *gathered)


def finish_kernel(steps, heads, scale, terms, *refs):
    parts, refs = refs[:terms], refs[terms:]
    q_ref, old_ref, top_ref, total_ref = refs[:4]
    refs = refs[4:]
    fresh_hbm, context_hbm, wide, fresh_ref, context_ref, sems = refs
    rows, queries, size = context_ref.shape
    own = fresh_ref.shape[3]
    fresh = parts[0][...]
    for part in parts[1:]:
        fresh = fresh + part[...]
    keys, many = 2 * own * steps, 2 * queries
    group = size // keys
    key = lax.broadcasted_iota(jnp.int32, (keys, many), 0)
    query = lax.broadcasted_iota(jnp.int32, (keys, many), 1)
    same_head = (query % heads) // (heads // own) == key // (2 * steps)
    same_row = query // queries == (key // steps) % 2
    live = same_head & same_row & ((query % queries) // heads >= key % steps)
    nothing = jnp.zeros((keys, size), jnp.bfloat16)

    def new_lines(c, pair):
        tokens = slice(pair * 2 * steps, (pair + 1) * 2 * steps)
        lines = [fresh[tokens, (c * own + g) * size : (c * own + g + 1) * size] for g in range(own)]
        return jnp.concatenate(lines, axis=0).astype(jnp.bfloat16)

    def rows_of(ref, pair):
        return ref[2 * pair : 2 * pair + 2].reshape(many, size)

    scores = [
        lax.dot_general(new_lines(0, p), rows_of(q_ref, p), NT, preferred_element_type=jnp.float32)
        for p in range(rows // 2)
    ]
    scores = jnp.stack([jnp.where(live, s, LOW) for s in scores])
    old_top = top_ref[...]
    top = jnp.maximum(old_top, jnp.max(scores, axis=1))
    expo = jnp.exp((scores - top[:, None, :]) * scale)
    back = jnp.exp((old_top - top) * scale)
    inverse = 1.0 / (back * total_ref[...] + jnp.sum(expo, axis=1))
    weights = (expo * inverse[:, None, :]).astype(jnp.bfloat16)
    back = back * inverse

    for n in range(2 * own):
        wide[pl.ds(n, rows * steps, stride=2 * own), :] = fresh[:, n * size : (n + 1) * size]
    fresh_ref.reshape(rows * steps * 2 * own, size)[...] = wide[...].astype(jnp.bfloat16)
    puts = [pltpu.make_async_copy(fresh_ref, fresh_hbm, sems.at[0])]
    puts[0].start()

    for at in range(0, rows // 2, group):
        pairs = range(at, at + group)
        values = jnp.concatenate(
            [
                jnp.concatenate([new_lines(1, p) if n == p else nothing for n in pairs], axis=1)
                for p in pairs
            ],
            axis=0,
        )
        new = lax.dot_general(
            weights[at : at + group].reshape(group * keys, many), values, TN, preferred_element_type=jnp.float32
        )
        factors = back[at : at + group].T
        for n, p in enumerate(pairs):
            both = new[:, n * size : (n + 1) * size] + factors[:, n : n + 1] * rows_of(old_ref, p)
            context_ref[2 * p : 2 * p + 2] = both.astype(jnp.bfloat16).reshape(2, queries, size)
        mine = pl.ds(2 * at, 2 * group)
        puts.append(pltpu.make_async_copy(context_ref.at[mine], context_hbm.at[mine], sems.at[1 + at // group]))
        puts[-1].start()
    for put in puts:
        put.wait()


def finish(parts, state, steps, own):
    rows, many, size = state[0].shape
    heads = many // steps
    groups = rows * own * steps // size
    fresh = (rows, steps, 2, own, size)
    fresh, context = pl.pallas_call(
        functools.partial(finish_kernel, steps, heads, size ** (-0.5), len(parts)),
        out_shape=(
            jax.ShapeDtypeStruct(fresh, jnp.bfloat16),
            jax.ShapeDtypeStruct((rows, many, size), jnp.bfloat16),
        ),
        in_specs=[VMEM] * (len(parts) + 4),
        out_specs=(pl.BlockSpec(memory_space=pltpu.HBM),) * 2,
        scratch_shapes=[
            pltpu.VMEM((rows * steps * 2 * own, size), jnp.float32),
            pltpu.VMEM(fresh, jnp.bfloat16),
            pltpu.VMEM((rows, many, size), jnp.bfloat16),
            pltpu.SemaphoreType.DMA((1 + groups,)),
        ],
        compiler_params=params(24),
        cost_estimate=cost(rows * many * size * size * 6, 8 * rows * many * size, rows * many * size * 2),
        name="finish",
    )(*parts, *state)
    return fresh, context.reshape(rows, steps, heads, size)


def join_kernel(*refs):
    blocks, out_ref = refs[:-1], refs[-1]
    at = 0
    for block in blocks:
        out_ref[at : at + block.shape[0], :] = block[...]
        at += block.shape[0]


def join(blocks):
    rows = sum(b.shape[0] for b in blocks)
    return pl.pallas_call(
        join_kernel,
        out_shape=pltpu.VMEM((rows, blocks[0].shape[1]), jnp.bfloat16),
        in_specs=[VMEM] * len(blocks),
        out_specs=VMEM,
        compiler_params=params(8),
        name="join",
    )(*blocks)


def gather_second(factor_a, factor_b, dp):
    count = dp // 2
    ranks = factor_b.shape[0]
    if ranks % 8 == 0 and count in (1, 2, 4):
        order = {1: (), 2: (1,), 4: (2, 3, 1)}[count]
        payload = make_payload(factor_a.T, factor_b)
        return [payload] + [lax.ppermute(payload, "dp", [(i, i ^ (2 * k)) for i in range(dp)]) for k in order]
    payload = jnp.concatenate([factor_a.T, factor_b.reshape(ranks, -1)], axis=1)
    groups = [[i for i in range(dp) if i % 2 == n] for n in range(2)]
    copies = jnp.broadcast_to(payload[None], (count,) + payload.shape)
    blocks = lax.all_to_all(copies, "dp", 0, 0, axis_index_groups=groups, tiled=True)
    return [blocks.reshape(count * ranks, payload.shape[1])]


def shards(dp, tp, hidden, base_weight, factor_a, factor_b, queries, cache, lengths):
    steps, own = queries.shape[1], cache.shape[3]
    assert dp % 2 == 0
    blocks = gather_second(factor_a, factor_b, dp)
    rows, steps, heads, size = queries.shape
    queries = queries.reshape(rows, steps * heads, size)
    chunk, early = 12, 2
    tokens, base, keys, values = arrange(hidden, base_weight, cache, chunk, early)
    blocks, tokens, base, keys, values = lax.optimization_barrier((blocks, tokens, base, keys, values))
    gathered = join(blocks) if len(blocks) > 1 else blocks[0]
    gathered = [gathered, lax.ppermute(gathered, "dp", [(i, i ^ 1) for i in range(dp)])]
    state = attend_cached(queries, cache, lengths, keys, values, steps, chunk, early)
    gathered, state, tokens, base = lax.optimization_barrier((gathered, state, tokens, base))
    received = []
    for k in range(1, tp):
        other = project(k, tokens, base, gathered)
        received.append(lax.ppermute(other, "tp", [(i, i ^ k) for i in range(tp)]))
    mine = project(0, tokens, base, gathered)
    return finish([mine] + received, state, steps, own)


def solution(mesh):
    return jax.shard_map(
        functools.partial(shards, mesh.shape["dp"], mesh.shape["tp"]),
        mesh=mesh,
        in_specs=(
            P(("parts", "dp"), None, "tp"),
            P("tp", None, None, None),
            P(("parts", "tp"), "dp"),
            P(("parts", "dp"), None, None, None),
            P(("parts", "dp"), None, "tp", None),
            P(("parts", "dp"), None, None, "tp", None),
            P(("parts", "dp")),
        ),
        out_specs=(
            P(("parts", "dp"), None, None, "tp", None),
            P(("parts", "dp"), None, "tp", None),
        ),
        check_vma=False,
    )
```

```python
import functools

import jax
import jax.numpy as jnp
from jax import lax
from jax.experimental import pallas as pl
from jax.experimental.pallas import tpu as pltpu
from jax.sharding import PartitionSpec as P

LOW = -1e30
NT = (((1,), (1,)), ((), ()))
TN = (((0,), (0,)), ((), ()))
VMEM = pl.BlockSpec(memory_space=pltpu.VMEM)


def params(mib):
    return pltpu.CompilerParams(vmem_limit_bytes=mib * 1024 * 1024)


def in_hbm(x):
    return pltpu.with_memory_space_constraint(x, pltpu.HBM)


def in_vmem(x):
    return pltpu.with_memory_space_constraint(x, pltpu.VMEM)


def cost(flops, moved, exps=0):
    return pl.CostEstimate(flops=flops, bytes_accessed=moved, transcendentals=exps)


def payload_kernel(down_hbm, up_hbm, out_ref, ups, wide, sems):
    ranks, width = down_hbm.shape
    groups, size = ups.shape[1] * ups.shape[2], ups.shape[3]
    get_down = pltpu.make_async_copy(down_hbm, out_ref.at[:, pl.ds(0, width)], sems.at[0])
    get_up = pltpu.make_async_copy(up_hbm, ups, sems.at[1])
    get_up.start()
    get_down.start()
    get_up.wait()
    wide[...] = ups.reshape(ranks * groups, size)[...].astype(jnp.float32)
    for n in range(groups):
        out_ref[:, width + n * size : width + (n + 1) * size] = wide[pl.ds(n, ranks, stride=groups), :].astype(
            jnp.bfloat16
        )
    get_down.wait()


def make_payload(down, up):
    ranks, width = down.shape
    groups, size = up.shape[1] * up.shape[2], up.shape[3]
    return pl.pallas_call(
        payload_kernel,
        out_shape=pltpu.VMEM((ranks, width + groups * size), jnp.bfloat16),
        in_specs=[pl.BlockSpec(memory_space=pltpu.HBM)] * 2,
        out_specs=VMEM,
        scratch_shapes=[
            pltpu.VMEM(up.shape, jnp.bfloat16),
            pltpu.VMEM((ranks * groups, size), jnp.float32),
            pltpu.SemaphoreType.DMA((2,)),
        ],
        compiler_params=params(8),
        name="payload",
    )(in_hbm(down), in_hbm(up))


def cache_copies(cache_hbm, k, v, sems, i, chunk):
    mine = pl.ds(i * chunk, chunk)
    return [pltpu.make_async_copy(cache_hbm.at[mine, :, n], ref.at[mine], sems.at[i, n]) for n, ref in enumerate((k, v))]


def two_rows(ref, r):
    rows, slots, own, size = ref.shape
    flat = ref.reshape(rows, slots * own, size)
    return jnp.concatenate([flat[r], flat[r + 1]], axis=1)


def score_chunk(q_ref, k_ref, scores_ref, i, chunk):
    nothing = jnp.zeros(q_ref.shape[1:], jnp.bfloat16)
    for p in range(chunk // 2):
        r = i * chunk + 2 * p
        both_q = jnp.concatenate(
            [
                jnp.concatenate([q_ref[r], nothing], axis=1),
                jnp.concatenate([nothing, q_ref[r + 1]], axis=1),
            ],
            axis=0,
        )
        scores_ref[p] = lax.dot_general(two_rows(k_ref, r), both_q, NT, preferred_element_type=jnp.float32)


class Cached:
    def __init__(self, chunk, heads, scale, inputs, outputs, scratch):
        self.chunk, self.heads, self.scale = chunk, heads, scale
        self.lengths_hbm, self.cache_hbm, self.q = inputs
        self.k, self.v, first_scores, self.sums, self.tops, self.totals = outputs
        self.lengths, second_scores, *rest = scratch
        self.scores, self.weights = (first_scores, second_scores), rest[0:2]
        self.sems, self.length_sem = rest[2:]
        self.rows, self.queries, self.size = self.q.shape
        self.slots, self.own = self.k.shape[1:3]
        self.keys = self.slots * self.own
        own, queries = self.own, self.queries
        line = lax.broadcasted_iota(jnp.int32, (self.keys, 2 * queries), 0)
        query = lax.broadcasted_iota(jnp.int32, (self.keys, 2 * queries), 1)
        self.line = jnp.where(line % own == (query % heads) // (heads // own), line, self.keys)
        self.one = lax.broadcasted_iota(jnp.int32, (1, 2 * queries), 1) < queries

    def copies(self, i):
        return cache_copies(self.cache_hbm, self.k, self.v, self.sems, i, self.chunk)

    def lengths_copy(self):
        return pltpu.make_async_copy(self.lengths_hbm, self.lengths, self.length_sem)

    def start(self, i):
        for copy in self.copies(i):
            copy.start()

    def arrive(self, i):
        for copy in self.copies(i):
            copy.wait()

    def lines(self, ref, r):
        return two_rows(ref, r)

    def score(self, i, slot):
        score_chunk(self.q, self.k, self.scores[slot], i, self.chunk)

    def soften(self, i, slot):
        for p in range(self.chunk // 2):
            r = i * self.chunk + 2 * p
            limit = jnp.where(self.one, self.own * self.lengths[r], self.own * self.lengths[r + 1])
            scores = jnp.where(self.line < limit, self.scores[slot][p], LOW)
            top = jnp.max(scores, axis=0, keepdims=True)
            expo = jnp.exp((scores - top) * self.scale)
            self.weights[slot][p] = expo.astype(jnp.bfloat16)
            pair = pl.ds(i * (self.chunk // 2) + p, 1)
            self.tops[pair, :] = top
            self.totals[pair, :] = jnp.sum(expo, axis=0, keepdims=True)

    def collect(self, i, slot):
        queries, size = self.queries, self.size
        for p in range(self.chunk // 2):
            r = i * self.chunk + 2 * p
            both = lax.dot_general(
                self.weights[slot][p], self.lines(self.v, r), TN, preferred_element_type=jnp.float32
            )
            for h in range(2):
                self.sums[r + h] = both[h * queries : (h + 1) * queries, h * size : (h + 1) * size]


def cached_kernel(chunk, early, heads, scale, *refs):
    cached = Cached(chunk, heads, scale, refs[:3], refs[6:12], refs[12:])
    chunks = cached.rows // chunk
    cached.lengths_copy().start()
    for i in range(early, chunks):
        cached.start(i)
    cached.lengths_copy().wait()
    cached.score(1, 1)
    cached.soften(0, 0)

    @pl.loop(1, chunks // 2)
    def _(t):
        for slot in range(2):
            i = 2 * t + slot

            @pl.when(i >= early)
            def _():
                cached.arrive(i)

            cached.score(i, slot)
            cached.soften(i - 1, 1 - slot)
            cached.collect(i - 2, slot)

    cached.soften(chunks - 1, 1)
    cached.collect(chunks - 2, 0)
    cached.collect(chunks - 1, 1)


def attend_cached(queries, cache, lengths, keys, values, first_scores, steps, chunk, early):
    rows, many, size = queries.shape
    slots, own = cache.shape[1], cache.shape[3]
    heads = many // steps
    half = (rows, slots, own, size)
    scores = (chunk // 2, slots * own, 2 * many)
    line = (rows // 2, 2 * many)
    outs = (
        pltpu.VMEM(half, jnp.bfloat16),
        pltpu.VMEM(half, jnp.bfloat16),
        pltpu.VMEM(scores, jnp.float32),
        pltpu.VMEM((rows, many, size), jnp.float32),
        pltpu.VMEM(line, jnp.float32),
        pltpu.VMEM(line, jnp.float32),
    )
    _, _, _, *state = pl.pallas_call(
        functools.partial(cached_kernel, chunk, early, heads, size ** (-0.5)),
        out_shape=outs,
        in_specs=[pl.BlockSpec(memory_space=pltpu.HBM)] * 2 + [VMEM] * 4,
        out_specs=(VMEM,) * len(outs),
        scratch_shapes=[
            pltpu.SMEM(lengths.shape, jnp.int32),
            pltpu.VMEM(scores, jnp.float32),
            pltpu.VMEM(scores, jnp.bfloat16),
            pltpu.VMEM(scores, jnp.bfloat16),
            pltpu.SemaphoreType.DMA((rows // chunk, 2)),
            pltpu.SemaphoreType.DMA,
        ],
        input_output_aliases={3: 0, 4: 1, 5: 2},
        compiler_params=params(16),
        cost_estimate=cost(8 * rows * many * slots * size, 4 * rows * slots * own * size, rows * many * slots * own),
        name="attend_cached",
    )(in_hbm(lengths), in_hbm(cache), in_vmem(queries), keys, values, first_scores)
    return [queries, *state]


def arrange_kernel(chunks, chunk, early, *refs):
    cache_hbm, hidden_hbm, base_hbm, queries_hbm, tokens_ref, base_ref, k, v, scores_ref = refs[:9]
    hidden, base, q, base_sems, sems = refs[9:]
    width, two, kvh, size = base.shape
    own = k.shape[2]
    groups = two * kvh
    some_width = width // chunks
    copies = [copy for i in range(early) for copy in cache_copies(cache_hbm, k, v, sems, i, chunk)]
    get_hidden = pltpu.make_async_copy(hidden_hbm, hidden, base_sems.at[chunks])

    def get_base(i):
        features = pl.ds(i * some_width, some_width)
        return pltpu.make_async_copy(base_hbm.at[features], base.at[features], base_sems.at[i])

    for i in range(chunks):
        get_base(i).start()
    get_hidden.start()
    get_queries = pltpu.make_async_copy(queries_hbm.at[pl.ds(0, chunk)], q, base_sems.at[chunks + 1])
    get_queries.start()
    for copy in copies:
        copy.start()

    tile = 256
    some = tile // groups
    row = lax.broadcasted_iota(jnp.int32, (tile, tile), 0)
    place = lax.broadcasted_iota(jnp.int32, (tile, tile), 1)
    order = (place == (row % some) * groups + row // some).astype(jnp.float32).astype(jnp.bfloat16)
    flat_base = base.reshape(width * groups, size)

    def arrange(f):
        at = pl.multiple_of(f * groups, tile)
        pair = jnp.concatenate([flat_base[pl.ds(at + h * tile, tile), :] for h in range(2)], axis=1)
        moved = jnp.dot(order, pair, preferred_element_type=jnp.float32).astype(jnp.bfloat16)
        for n in range(groups):
            lanes = slice((n % own) * size, (n % own + 1) * size)
            for h in range(2):
                base_ref[n // own, pl.ds(pl.multiple_of(f + h * some, some), some), lanes] = moved[
                    n * some : (n + 1) * some, h * size : (h + 1) * size
                ]

    @pl.loop(0, chunks)
    def _(i):
        get_base(i).wait()
        for f in range(0, some_width, 2 * some):
            arrange(i * some_width + f)

    get_hidden.wait()
    tokens_ref[...] = hidden.reshape(tokens_ref.shape)[...]
    get_queries.wait()
    copies[0].wait()
    score_chunk(q, k, scores_ref, 0, chunk)
    for copy in copies[1:]:
        copy.wait()


def arrange(hidden, base, cache, queries, chunk, early):
    rows, steps, _ = hidden.shape
    slots, own = cache.shape[1], cache.shape[3]
    width, two, kvh, size = base.shape
    half = pltpu.VMEM((rows, slots, own, size), jnp.bfloat16)
    chunks = 4
    outs = (
        pltpu.VMEM((rows * steps, width), jnp.bfloat16),
        pltpu.VMEM((two * kvh // own, width, own * size), jnp.bfloat16),
        half,
        half,
        pltpu.VMEM((chunk // 2, slots * own, 2 * queries.shape[1]), jnp.float32),
    )
    return pl.pallas_call(
        functools.partial(arrange_kernel, chunks, chunk, early),
        out_shape=outs,
        in_specs=[pl.BlockSpec(memory_space=pltpu.HBM)] * 4,
        out_specs=(VMEM,) * len(outs),
        scratch_shapes=[
            pltpu.VMEM(hidden.shape, jnp.bfloat16),
            pltpu.VMEM(base.shape, jnp.bfloat16),
            pltpu.VMEM((chunk,) + queries.shape[1:], jnp.bfloat16),
            pltpu.SemaphoreType.DMA((chunks + 2,)),
            pltpu.SemaphoreType.DMA((early, 2)),
        ],
        compiler_params=params(16),
        cost_estimate=cost(512 * base.size, 4 * (base.size + hidden.size)),
        name="arrange",
    )(in_hbm(cache), in_hbm(hidden), in_hbm(base), in_hbm(queries))


def project_kernel(k, hidden_ref, base_ref, *refs):
    gathered, (out_ref, merged) = refs[:-2], refs[-2:]
    width, columns = merged.shape
    part = lax.axis_index("tp") ^ k
    parts = base_ref.shape[0] // 2
    half = columns // 2
    up = jnp.concatenate(
        [
            jnp.concatenate(
                [ref[:, pl.ds(pl.multiple_of(width + (c * parts + part) * half, 128), half)] for ref in gathered], axis=0
            )
            for c in range(2)
        ],
        axis=1,
    )
    step = 256

    def merge(first, last):
        for f in range(first, last, step):
            down = jnp.concatenate([ref[:, f : f + step] for ref in gathered], axis=0).T
            low_rank = jnp.dot(down, up, preferred_element_type=jnp.float32)
            for c in range(2):
                base = base_ref[c * parts + part, f : f + step, :].astype(jnp.float32)
                merged[f : f + step, c * half : (c + 1) * half] = (
                    base + low_rank[:, c * half : (c + 1) * half]
                ).astype(jnp.bfloat16)

    cuts = [0, width // 2, width]
    total = None
    for first, last in zip(cuts, cuts[1:]):
        merge(first, last)
        product = jnp.dot(hidden_ref[:, first:last], merged[first:last, :], preferred_element_type=jnp.float32)
        total = product if total is None else total + product
    out_ref[...] = total


def project(k, hidden, base, gathered):
    tokens, width = hidden.shape
    columns = 2 * base.shape[2]
    ranks = sum(g.shape[0] for g in gathered)
    return pl.pallas_call(
        functools.partial(project_kernel, k),
        out_shape=pltpu.VMEM((tokens, columns), jnp.float32),
        in_specs=[VMEM] * (2 + len(gathered)),
        out_specs=VMEM,
        scratch_shapes=[pltpu.VMEM((width, columns), jnp.bfloat16)],
        compiler_params=params(24),
        cost_estimate=cost(2 * width * columns * (tokens + ranks), 2 * width * columns + 2 * width * tokens),
        name="project",
    )(hidden, base, *gathered)


def finish_kernel(steps, heads, scale, terms, *refs):
    parts, refs = refs[:terms], refs[terms:]
    q_ref, old_ref, top_ref, total_ref = refs[:4]
    refs = refs[4:]
    fresh_hbm, context_hbm, wide, fresh_ref, context_ref, sems = refs
    rows, queries, size = context_ref.shape
    own = fresh_ref.shape[3]
    fresh = parts[0][...]
    for part in parts[1:]:
        fresh = fresh + part[...]
    keys, many = 2 * own * steps, 2 * queries
    group = size // keys
    key = lax.broadcasted_iota(jnp.int32, (keys, many), 0)
    query = lax.broadcasted_iota(jnp.int32, (keys, many), 1)
    same_head = (query % heads) // (heads // own) == key // (2 * steps)
    same_row = query // queries == (key // steps) % 2
    live = same_head & same_row & ((query % queries) // heads >= key % steps)
    nothing = jnp.zeros((keys, size), jnp.bfloat16)

    def new_lines(c, pair):
        tokens = slice(pair * 2 * steps, (pair + 1) * 2 * steps)
        lines = [fresh[tokens, (c * own + g) * size : (c * own + g + 1) * size] for g in range(own)]
        return jnp.concatenate(lines, axis=0).astype(jnp.bfloat16)

    def rows_of(ref, pair):
        return ref[2 * pair : 2 * pair + 2].reshape(many, size)

    scores = [
        lax.dot_general(new_lines(0, p), rows_of(q_ref, p), NT, preferred_element_type=jnp.float32)
        for p in range(rows // 2)
    ]
    scores = jnp.stack([jnp.where(live, s, LOW) for s in scores])
    old_top = top_ref[...]
    top = jnp.maximum(old_top, jnp.max(scores, axis=1))
    expo = jnp.exp((scores - top[:, None, :]) * scale)
    back = jnp.exp((old_top - top) * scale)
    inverse = 1.0 / (back * total_ref[...] + jnp.sum(expo, axis=1))
    weights = (expo * inverse[:, None, :]).astype(jnp.bfloat16)
    back = back * inverse

    for n in range(2 * own):
        wide[pl.ds(n, rows * steps, stride=2 * own), :] = fresh[:, n * size : (n + 1) * size]
    fresh_ref.reshape(rows * steps * 2 * own, size)[...] = wide[...].astype(jnp.bfloat16)
    puts = [pltpu.make_async_copy(fresh_ref, fresh_hbm, sems.at[0])]
    puts[0].start()

    for at in range(0, rows // 2, group):
        pairs = range(at, at + group)
        values = jnp.concatenate(
            [
                jnp.concatenate([new_lines(1, p) if n == p else nothing for n in pairs], axis=1)
                for p in pairs
            ],
            axis=0,
        )
        new = lax.dot_general(
            weights[at : at + group].reshape(group * keys, many), values, TN, preferred_element_type=jnp.float32
        )
        factors = back[at : at + group].T
        for n, p in enumerate(pairs):
            both = new[:, n * size : (n + 1) * size] + factors[:, n : n + 1] * rows_of(old_ref, p)
            context_ref[2 * p : 2 * p + 2] = both.astype(jnp.bfloat16).reshape(2, queries, size)
        mine = pl.ds(2 * at, 2 * group)
        puts.append(pltpu.make_async_copy(context_ref.at[mine], context_hbm.at[mine], sems.at[1 + at // group]))
        puts[-1].start()
    for put in puts:
        put.wait()


def finish(parts, state, steps, own):
    rows, many, size = state[0].shape
    heads = many // steps
    groups = rows * own * steps // size
    fresh = (rows, steps, 2, own, size)
    fresh, context = pl.pallas_call(
        functools.partial(finish_kernel, steps, heads, size ** (-0.5), len(parts)),
        out_shape=(
            jax.ShapeDtypeStruct(fresh, jnp.bfloat16),
            jax.ShapeDtypeStruct((rows, many, size), jnp.bfloat16),
        ),
        in_specs=[VMEM] * (len(parts) + 4),
        out_specs=(pl.BlockSpec(memory_space=pltpu.HBM),) * 2,
        scratch_shapes=[
            pltpu.VMEM((rows * steps * 2 * own, size), jnp.float32),
            pltpu.VMEM(fresh, jnp.bfloat16),
            pltpu.VMEM((rows, many, size), jnp.bfloat16),
            pltpu.SemaphoreType.DMA((1 + groups,)),
        ],
        compiler_params=params(24),
        cost_estimate=cost(rows * many * size * size * 6, 8 * rows * many * size, rows * many * size * 2),
        name="finish",
    )(*parts, *state)
    return fresh, context.reshape(rows, steps, heads, size)


def join_kernel(*refs):
    blocks, out_ref = refs[:-1], refs[-1]
    at = 0
    for block in blocks:
        out_ref[at : at + block.shape[0], :] = block[...]
        at += block.shape[0]


def join(blocks):
    rows = sum(b.shape[0] for b in blocks)
    return pl.pallas_call(
        join_kernel,
        out_shape=pltpu.VMEM((rows, blocks[0].shape[1]), jnp.bfloat16),
        in_specs=[VMEM] * len(blocks),
        out_specs=VMEM,
        compiler_params=params(8),
        name="join",
    )(*blocks)


def gather_second(factor_a, factor_b, dp):
    count = dp // 2
    ranks = factor_b.shape[0]
    if ranks % 8 == 0 and count in (1, 2, 4):
        order = {1: (), 2: (1,), 4: (2, 3, 1)}[count]
        payload = make_payload(factor_a.T, factor_b)
        return [payload] + [lax.ppermute(payload, "dp", [(i, i ^ (2 * k)) for i in range(dp)]) for k in order]
    payload = jnp.concatenate([factor_a.T, factor_b.reshape(ranks, -1)], axis=1)
    groups = [[i for i in range(dp) if i % 2 == n] for n in range(2)]
    copies = jnp.broadcast_to(payload[None], (count,) + payload.shape)
    blocks = lax.all_to_all(copies, "dp", 0, 0, axis_index_groups=groups, tiled=True)
    return [blocks.reshape(count * ranks, payload.shape[1])]


def shards(dp, tp, hidden, base_weight, factor_a, factor_b, queries, cache, lengths):
    steps, own = queries.shape[1], cache.shape[3]
    assert dp % 2 == 0
    blocks = gather_second(factor_a, factor_b, dp)
    rows, steps, heads, size = queries.shape
    queries = queries.reshape(rows, steps * heads, size)
    chunk, early = 12, 2
    tokens, base, keys, values, scores = arrange(hidden, base_weight, cache, queries, chunk, early)
    blocks, tokens, base, keys, values, scores = lax.optimization_barrier((blocks, tokens, base, keys, values, scores))
    gathered = join(blocks) if len(blocks) > 1 else blocks[0]
    gathered = [gathered, lax.ppermute(gathered, "dp", [(i, i ^ 1) for i in range(dp)])]
    state = attend_cached(queries, cache, lengths, keys, values, scores, steps, chunk, early)
    gathered, state, tokens, base = lax.optimization_barrier((gathered, state, tokens, base))
    received = []
    for k in range(1, tp):
        other = project(k, tokens, base, gathered)
        received.append(lax.ppermute(other, "tp", [(i, i ^ k) for i in range(tp)]))
    mine = project(0, tokens, base, gathered)
    return finish([mine] + received, state, steps, own)


def solution(mesh):
    return jax.shard_map(
        functools.partial(shards, mesh.shape["dp"], mesh.shape["tp"]),
        mesh=mesh,
        in_specs=(
            P(("parts", "dp"), None, "tp"),
            P("tp", None, None, None),
            P(("parts", "tp"), "dp"),
            P(("parts", "dp"), None, None, None),
            P(("parts", "dp"), None, "tp", None),
            P(("parts", "dp"), None, None, "tp", None),
            P(("parts", "dp")),
        ),
        out_specs=(
            P(("parts", "dp"), None, None, "tp", None),
            P(("parts", "dp"), None, "tp", None),
        ),
        check_vma=False,
    )
```

```python
import functools

import jax
import jax.numpy as jnp
from jax import lax
from jax.experimental import pallas as pl
from jax.experimental.pallas import tpu as pltpu
from jax.sharding import PartitionSpec as P

LOW = -1e30
NT = (((1,), (1,)), ((), ()))
TN = (((0,), (0,)), ((), ()))
VMEM = pl.BlockSpec(memory_space=pltpu.VMEM)


def params(mib):
    return pltpu.CompilerParams(vmem_limit_bytes=mib * 1024 * 1024)


def in_hbm(x):
    return pltpu.with_memory_space_constraint(x, pltpu.HBM)


def in_vmem(x):
    return pltpu.with_memory_space_constraint(x, pltpu.VMEM)


def cost(flops, moved, exps=0):
    return pl.CostEstimate(flops=flops, bytes_accessed=moved, transcendentals=exps)


def payload_kernel(down_hbm, up_hbm, out_ref, ups, wide, sems):
    ranks, width = down_hbm.shape
    groups, size = ups.shape[1] * ups.shape[2], ups.shape[3]
    get_down = pltpu.make_async_copy(down_hbm, out_ref.at[:, pl.ds(0, width)], sems.at[0])
    get_up = pltpu.make_async_copy(up_hbm, ups, sems.at[1])
    get_up.start()
    get_down.start()
    get_up.wait()
    wide[...] = ups.reshape(ranks * groups, size)[...].astype(jnp.float32)
    for n in range(groups):
        out_ref[:, width + n * size : width + (n + 1) * size] = wide[pl.ds(n, ranks, stride=groups), :].astype(
            jnp.bfloat16
        )
    get_down.wait()


def make_payload(down, up):
    ranks, width = down.shape
    groups, size = up.shape[1] * up.shape[2], up.shape[3]
    return pl.pallas_call(
        payload_kernel,
        out_shape=pltpu.VMEM((ranks, width + groups * size), jnp.bfloat16),
        in_specs=[pl.BlockSpec(memory_space=pltpu.HBM)] * 2,
        out_specs=VMEM,
        scratch_shapes=[
            pltpu.VMEM(up.shape, jnp.bfloat16),
            pltpu.VMEM((ranks * groups, size), jnp.float32),
            pltpu.SemaphoreType.DMA((2,)),
        ],
        compiler_params=params(8),
        name="payload",
    )(in_hbm(down), in_hbm(up))


def cache_copies(cache_hbm, k, v, sems, i, chunk):
    mine = pl.ds(i * chunk, chunk)
    return [pltpu.make_async_copy(cache_hbm.at[mine, :, n], ref.at[mine], sems.at[i, n]) for n, ref in enumerate((k, v))]


def two_rows(ref, r):
    rows, slots, own, size = ref.shape
    flat = ref.reshape(rows, slots * own, size)
    return jnp.concatenate([flat[r], flat[r + 1]], axis=1)


def score_chunk(q_ref, k_ref, scores_ref, i, chunk):
    nothing = jnp.zeros(q_ref.shape[1:], jnp.bfloat16)
    for p in range(chunk // 2):
        r = i * chunk + 2 * p
        both_q = jnp.concatenate(
            [
                jnp.concatenate([q_ref[r], nothing], axis=1),
                jnp.concatenate([nothing, q_ref[r + 1]], axis=1),
            ],
            axis=0,
        )
        scores_ref[p] = lax.dot_general(two_rows(k_ref, r), both_q, NT, preferred_element_type=jnp.float32)


class Cached:
    def __init__(self, chunk, heads, scale, inputs, outputs, scratch):
        self.chunk, self.heads, self.scale = chunk, heads, scale
        self.lengths_hbm, self.cache_hbm, self.q = inputs
        self.k, self.v, first_scores, self.sums, self.tops, self.totals = outputs
        self.lengths, second_scores, *rest = scratch
        self.scores, self.weights = (first_scores, second_scores), rest[0:2]
        self.sems, self.length_sem = rest[2:]
        self.rows, self.queries, self.size = self.q.shape
        self.slots, self.own = self.k.shape[1:3]
        self.keys = self.slots * self.own
        own, queries = self.own, self.queries
        line = lax.broadcasted_iota(jnp.int32, (self.keys, 2 * queries), 0)
        query = lax.broadcasted_iota(jnp.int32, (self.keys, 2 * queries), 1)
        self.line = jnp.where(line % own == (query % heads) // (heads // own), line, self.keys)
        self.one = lax.broadcasted_iota(jnp.int32, (1, 2 * queries), 1) < queries

    def copies(self, i):
        return cache_copies(self.cache_hbm, self.k, self.v, self.sems, i, self.chunk)

    def lengths_copy(self):
        return pltpu.make_async_copy(self.lengths_hbm, self.lengths, self.length_sem)

    def start(self, i):
        for copy in self.copies(i):
            copy.start()

    def arrive(self, i):
        for copy in self.copies(i):
            copy.wait()

    def lines(self, ref, r):
        return two_rows(ref, r)

    def score(self, i, slot):
        score_chunk(self.q, self.k, self.scores[slot], i, self.chunk)

    def soften(self, i, slot):
        for p in range(self.chunk // 2):
            r = i * self.chunk + 2 * p
            limit = jnp.where(self.one, self.own * self.lengths[r], self.own * self.lengths[r + 1])
            scores = jnp.where(self.line < limit, self.scores[slot][p], LOW)
            top = jnp.max(scores, axis=0, keepdims=True)
            expo = jnp.exp((scores - top) * self.scale)
            self.weights[slot][p] = expo.astype(jnp.bfloat16)
            pair = pl.ds(i * (self.chunk // 2) + p, 1)
            self.tops[pair, :] = top
            self.totals[pair, :] = jnp.sum(expo, axis=0, keepdims=True)

    def collect(self, i, slot):
        queries, size = self.queries, self.size
        for p in range(self.chunk // 2):
            r = i * self.chunk + 2 * p
            both = lax.dot_general(
                self.weights[slot][p], self.lines(self.v, r), TN, preferred_element_type=jnp.float32
            )
            for h in range(2):
                self.sums[r + h] = both[h * queries : (h + 1) * queries, h * size : (h + 1) * size]


def cached_kernel(chunk, early, heads, scale, *refs):
    cached = Cached(chunk, heads, scale, refs[:3], refs[6:12], refs[12:])
    chunks = cached.rows // chunk
    cached.lengths_copy().start()
    for i in range(early, chunks):
        cached.start(i)
    cached.lengths_copy().wait()
    cached.score(1, 1)
    cached.soften(0, 0)

    @pl.loop(1, chunks // 2)
    def _(t):
        for slot in range(2):
            i = 2 * t + slot

            @pl.when(i >= early)
            def _():
                cached.arrive(i)

            cached.score(i, slot)
            cached.soften(i - 1, 1 - slot)
            cached.collect(i - 2, slot)

    cached.soften(chunks - 1, 1)
    cached.collect(chunks - 2, 0)
    cached.collect(chunks - 1, 1)


def attend_cached(queries, cache, lengths, keys, values, first_scores, steps, chunk, early):
    rows, many, size = queries.shape
    slots, own = cache.shape[1], cache.shape[3]
    heads = many // steps
    half = (rows, slots, own, size)
    scores = (chunk // 2, slots * own, 2 * many)
    line = (rows // 2, 2 * many)
    outs = (
        pltpu.VMEM(half, jnp.bfloat16),
        pltpu.VMEM(half, jnp.bfloat16),
        pltpu.VMEM(scores, jnp.float32),
        pltpu.VMEM((rows, many, size), jnp.float32),
        pltpu.VMEM(line, jnp.float32),
        pltpu.VMEM(line, jnp.float32),
    )
    _, _, _, *state = pl.pallas_call(
        functools.partial(cached_kernel, chunk, early, heads, size ** (-0.5)),
        out_shape=outs,
        in_specs=[pl.BlockSpec(memory_space=pltpu.HBM)] * 2 + [VMEM] * 4,
        out_specs=(VMEM,) * len(outs),
        scratch_shapes=[
            pltpu.SMEM(lengths.shape, jnp.int32),
            pltpu.VMEM(scores, jnp.float32),
            pltpu.VMEM(scores, jnp.bfloat16),
            pltpu.VMEM(scores, jnp.bfloat16),
            pltpu.SemaphoreType.DMA((rows // chunk, 2)),
            pltpu.SemaphoreType.DMA,
        ],
        input_output_aliases={3: 0, 4: 1, 5: 2},
        compiler_params=params(16),
        cost_estimate=cost(8 * rows * many * slots * size, 4 * rows * slots * own * size, rows * many * slots * own),
        name="attend_cached",
    )(in_hbm(lengths), in_hbm(cache), in_vmem(queries), keys, values, first_scores)
    return [queries, *state]


def arrange_kernel(chunks, chunk, early, *refs):
    cache_hbm, hidden_hbm, base_hbm, queries_hbm, tokens_ref, base_ref, k, v, scores_ref = refs[:9]
    hidden, base, q, base_sems, sems = refs[9:]
    width, two, kvh, size = base.shape
    own = k.shape[2]
    groups = two * kvh
    some_width = width // chunks
    copies = [copy for i in range(early) for copy in cache_copies(cache_hbm, k, v, sems, i, chunk)]
    get_hidden = pltpu.make_async_copy(hidden_hbm, hidden, base_sems.at[chunks])

    def get_base(i):
        features = pl.ds(i * some_width, some_width)
        return pltpu.make_async_copy(base_hbm.at[features], base.at[features], base_sems.at[i])

    for i in range(chunks):
        get_base(i).start()
    get_hidden.start()
    get_queries = pltpu.make_async_copy(queries_hbm.at[pl.ds(0, chunk)], q, base_sems.at[chunks + 1])
    get_queries.start()
    for copy in copies:
        copy.start()

    tile = 256
    some = tile // groups
    row = lax.broadcasted_iota(jnp.int32, (tile, tile), 0)
    place = lax.broadcasted_iota(jnp.int32, (tile, tile), 1)
    order = (place == (row % some) * groups + row // some).astype(jnp.float32).astype(jnp.bfloat16)
    flat_base = base.reshape(width * groups, size)

    def arrange(f):
        at = pl.multiple_of(f * groups, tile)
        pair = jnp.concatenate([flat_base[pl.ds(at + h * tile, tile), :] for h in range(2)], axis=1)
        moved = jnp.dot(order, pair, preferred_element_type=jnp.float32).astype(jnp.bfloat16)
        for n in range(groups):
            lanes = slice((n % own) * size, (n % own + 1) * size)
            for h in range(2):
                base_ref[n // own, pl.ds(pl.multiple_of(f + h * some, some), some), lanes] = moved[
                    n * some : (n + 1) * some, h * size : (h + 1) * size
                ]

    @pl.loop(0, chunks)
    def _(i):
        get_base(i).wait()
        for f in range(0, some_width, 2 * some):
            arrange(i * some_width + f)

    get_hidden.wait()
    tokens_ref[...] = hidden.reshape(tokens_ref.shape)[...]
    get_queries.wait()
    copies[0].wait()
    score_chunk(q, k, scores_ref, 0, chunk)
    for copy in copies[1:]:
        copy.wait()


def arrange(hidden, base, cache, queries, chunk, early):
    rows, steps, _ = hidden.shape
    slots, own = cache.shape[1], cache.shape[3]
    width, two, kvh, size = base.shape
    half = pltpu.VMEM((rows, slots, own, size), jnp.bfloat16)
    chunks = 4
    outs = (
        pltpu.VMEM((rows * steps, width), jnp.bfloat16),
        pltpu.VMEM((two * kvh // own, width, own * size), jnp.bfloat16),
        half,
        half,
        pltpu.VMEM((chunk // 2, slots * own, 2 * queries.shape[1]), jnp.float32),
    )
    return pl.pallas_call(
        functools.partial(arrange_kernel, chunks, chunk, early),
        out_shape=outs,
        in_specs=[pl.BlockSpec(memory_space=pltpu.HBM)] * 4,
        out_specs=(VMEM,) * len(outs),
        scratch_shapes=[
            pltpu.VMEM(hidden.shape, jnp.bfloat16),
            pltpu.VMEM(base.shape, jnp.bfloat16),
            pltpu.VMEM((chunk,) + queries.shape[1:], jnp.bfloat16),
            pltpu.SemaphoreType.DMA((chunks + 2,)),
            pltpu.SemaphoreType.DMA((early, 2)),
        ],
        compiler_params=params(16),
        cost_estimate=cost(512 * base.size, 4 * (base.size + hidden.size)),
        name="arrange",
    )(in_hbm(cache), in_hbm(hidden), in_hbm(base), in_hbm(queries))


def project_kernel(k, hidden_ref, base_ref, *refs):
    gathered, (out_ref, merged) = refs[:-2], refs[-2:]
    width, columns = merged.shape
    part = lax.axis_index("tp") ^ k
    parts = base_ref.shape[0] // 2
    half = columns // 2
    up = jnp.concatenate(
        [
            jnp.concatenate(
                [ref[:, pl.ds(pl.multiple_of(width + (c * parts + part) * half, 128), half)] for ref in gathered], axis=0
            )
            for c in range(2)
        ],
        axis=1,
    )
    step = 256

    def merge(first, last):
        for f in range(first, last, step):
            down = jnp.concatenate([ref[:, f : f + step] for ref in gathered], axis=0).T
            low_rank = jnp.dot(down, up, preferred_element_type=jnp.float32)
            for c in range(2):
                base = base_ref[c * parts + part, f : f + step, :].astype(jnp.float32)
                merged[f : f + step, c * half : (c + 1) * half] = (
                    base + low_rank[:, c * half : (c + 1) * half]
                ).astype(jnp.bfloat16)

    cuts = [0, width // 2, width]
    total = None
    for first, last in zip(cuts, cuts[1:]):
        merge(first, last)
        product = jnp.dot(hidden_ref[:, first:last], merged[first:last, :], preferred_element_type=jnp.float32)
        total = product if total is None else total + product
    out_ref[...] = total


def project(k, hidden, base, gathered):
    tokens, width = hidden.shape
    columns = 2 * base.shape[2]
    ranks = sum(g.shape[0] for g in gathered)
    return pl.pallas_call(
        functools.partial(project_kernel, k),
        out_shape=pltpu.VMEM((tokens, columns), jnp.float32),
        in_specs=[VMEM] * (2 + len(gathered)),
        out_specs=VMEM,
        scratch_shapes=[pltpu.VMEM((width, columns), jnp.bfloat16)],
        compiler_params=params(24),
        cost_estimate=cost(2 * width * columns * (tokens + ranks), 2 * width * columns + 2 * width * tokens),
        name="project",
    )(hidden, base, *gathered)


def finish_kernel(steps, heads, scale, terms, *refs):
    parts, refs = refs[:terms], refs[terms:]
    q_ref, old_ref, top_ref, total_ref = refs[:4]
    refs = refs[4:]
    fresh_hbm, context_hbm, wide, fresh_ref, context_ref, sems = refs
    rows, queries, size = context_ref.shape
    own = fresh_ref.shape[3]
    fresh = parts[0][...]
    for part in parts[1:]:
        fresh = fresh + part[...]
    keys, many = 2 * own * steps, 2 * queries
    group = size // keys
    key = lax.broadcasted_iota(jnp.int32, (keys, many), 0)
    query = lax.broadcasted_iota(jnp.int32, (keys, many), 1)
    same_head = (query % heads) // (heads // own) == key // (2 * steps)
    same_row = query // queries == (key // steps) % 2
    live = same_head & same_row & ((query % queries) // heads >= key % steps)
    nothing = jnp.zeros((keys, size), jnp.bfloat16)

    def new_lines(c, pair):
        tokens = slice(pair * 2 * steps, (pair + 1) * 2 * steps)
        lines = [fresh[tokens, (c * own + g) * size : (c * own + g + 1) * size] for g in range(own)]
        return jnp.concatenate(lines, axis=0).astype(jnp.bfloat16)

    def rows_of(ref, pair):
        return ref[2 * pair : 2 * pair + 2].reshape(many, size)

    scores = [
        lax.dot_general(new_lines(0, p), rows_of(q_ref, p), NT, preferred_element_type=jnp.float32)
        for p in range(rows // 2)
    ]
    scores = jnp.stack([jnp.where(live, s, LOW) for s in scores])
    old_top = top_ref[...]
    top = jnp.maximum(old_top, jnp.max(scores, axis=1))
    expo = jnp.exp((scores - top[:, None, :]) * scale)
    back = jnp.exp((old_top - top) * scale)
    inverse = 1.0 / (back * total_ref[...] + jnp.sum(expo, axis=1))
    weights = (expo * inverse[:, None, :]).astype(jnp.bfloat16)
    back = back * inverse

    for n in range(2 * own):
        wide[pl.ds(n, rows * steps, stride=2 * own), :] = fresh[:, n * size : (n + 1) * size]
    fresh_ref.reshape(rows * steps * 2 * own, size)[...] = wide[...].astype(jnp.bfloat16)
    starts = list(range(0, rows // 2, group))

    def new_sums(at):
        pairs = range(at, at + group)
        values = jnp.concatenate(
            [
                jnp.concatenate([new_lines(1, p) if n == p else nothing for n in pairs], axis=1)
                for p in pairs
            ],
            axis=0,
        )
        return lax.dot_general(
            weights[at : at + group].reshape(group * keys, many), values, TN, preferred_element_type=jnp.float32
        )

    puts = []
    following = new_sums(starts[0])
    for at in starts:
        new = following
        if at != starts[-1]:
            following = new_sums(at + group)
        factors = back[at : at + group].T
        for n, p in enumerate(range(at, at + group)):
            both = new[:, n * size : (n + 1) * size] + factors[:, n : n + 1] * rows_of(old_ref, p)
            context_ref[2 * p : 2 * p + 2] = both.astype(jnp.bfloat16).reshape(2, queries, size)
        mine = pl.ds(2 * at, 2 * group)
        puts.append(pltpu.make_async_copy(context_ref.at[mine], context_hbm.at[mine], sems.at[1 + at // group]))
        puts[-1].start()
    puts.append(pltpu.make_async_copy(fresh_ref, fresh_hbm, sems.at[0]))
    puts[-1].start()
    for put in puts:
        put.wait()


def finish(parts, state, steps, own):
    rows, many, size = state[0].shape
    heads = many // steps
    groups = rows * own * steps // size
    fresh = (rows, steps, 2, own, size)
    fresh, context = pl.pallas_call(
        functools.partial(finish_kernel, steps, heads, size ** (-0.5), len(parts)),
        out_shape=(
            jax.ShapeDtypeStruct(fresh, jnp.bfloat16),
            jax.ShapeDtypeStruct((rows, many, size), jnp.bfloat16),
        ),
        in_specs=[VMEM] * (len(parts) + 4),
        out_specs=(pl.BlockSpec(memory_space=pltpu.HBM),) * 2,
        scratch_shapes=[
            pltpu.VMEM((rows * steps * 2 * own, size), jnp.float32),
            pltpu.VMEM(fresh, jnp.bfloat16),
            pltpu.VMEM((rows, many, size), jnp.bfloat16),
            pltpu.SemaphoreType.DMA((1 + groups,)),
        ],
        compiler_params=params(24),
        cost_estimate=cost(rows * many * size * size * 6, 8 * rows * many * size, rows * many * size * 2),
        name="finish",
    )(*parts, *state)
    return fresh, context.reshape(rows, steps, heads, size)


def join_kernel(*refs):
    blocks, out_ref = refs[:-1], refs[-1]
    at = 0
    for block in blocks:
        out_ref[at : at + block.shape[0], :] = block[...]
        at += block.shape[0]


def join(blocks):
    rows = sum(b.shape[0] for b in blocks)
    return pl.pallas_call(
        join_kernel,
        out_shape=pltpu.VMEM((rows, blocks[0].shape[1]), jnp.bfloat16),
        in_specs=[VMEM] * len(blocks),
        out_specs=VMEM,
        compiler_params=params(8),
        name="join",
    )(*blocks)


def gather_second(factor_a, factor_b, dp):
    count = dp // 2
    ranks = factor_b.shape[0]
    if ranks % 8 == 0 and count in (1, 2, 4):
        order = {1: (), 2: (1,), 4: (2, 3, 1)}[count]
        payload = make_payload(factor_a.T, factor_b)
        return [payload] + [lax.ppermute(payload, "dp", [(i, i ^ (2 * k)) for i in range(dp)]) for k in order]
    payload = jnp.concatenate([factor_a.T, factor_b.reshape(ranks, -1)], axis=1)
    groups = [[i for i in range(dp) if i % 2 == n] for n in range(2)]
    copies = jnp.broadcast_to(payload[None], (count,) + payload.shape)
    blocks = lax.all_to_all(copies, "dp", 0, 0, axis_index_groups=groups, tiled=True)
    return [blocks.reshape(count * ranks, payload.shape[1])]


def shards(dp, tp, hidden, base_weight, factor_a, factor_b, queries, cache, lengths):
    steps, own = queries.shape[1], cache.shape[3]
    assert dp % 2 == 0
    blocks = gather_second(factor_a, factor_b, dp)
    rows, steps, heads, size = queries.shape
    queries = queries.reshape(rows, steps * heads, size)
    chunk, early = 12, 2
    tokens, base, keys, values, scores = arrange(hidden, base_weight, cache, queries, chunk, early)
    blocks, tokens, base, keys, values, scores = lax.optimization_barrier((blocks, tokens, base, keys, values, scores))
    gathered = join(blocks) if len(blocks) > 1 else blocks[0]
    gathered = [gathered, lax.ppermute(gathered, "dp", [(i, i ^ 1) for i in range(dp)])]
    state = attend_cached(queries, cache, lengths, keys, values, scores, steps, chunk, early)
    gathered, state, tokens, base = lax.optimization_barrier((gathered, state, tokens, base))
    received = []
    for k in range(1, tp):
        other = project(k, tokens, base, gathered)
        received.append(lax.ppermute(other, "tp", [(i, i ^ k) for i in range(tp)]))
    mine = project(0, tokens, base, gathered)
    return finish([mine] + received, state, steps, own)


def solution(mesh):
    return jax.shard_map(
        functools.partial(shards, mesh.shape["dp"], mesh.shape["tp"]),
        mesh=mesh,
        in_specs=(
            P(("parts", "dp"), None, "tp"),
            P("tp", None, None, None),
            P(("parts", "tp"), "dp"),
            P(("parts", "dp"), None, None, None),
            P(("parts", "dp"), None, "tp", None),
            P(("parts", "dp"), None, None, "tp", None),
            P(("parts", "dp")),
        ),
        out_specs=(
            P(("parts", "dp"), None, None, "tp", None),
            P(("parts", "dp"), None, "tp", None),
        ),
        check_vma=False,
    )
```

```python
import functools

import jax
import jax.numpy as jnp
from jax import lax
from jax.experimental import pallas as pl
from jax.experimental.pallas import tpu as pltpu
from jax.sharding import PartitionSpec as P

LOW = -1e30
NT = (((1,), (1,)), ((), ()))
TN = (((0,), (0,)), ((), ()))
VMEM = pl.BlockSpec(memory_space=pltpu.VMEM)


def params(mib):
    return pltpu.CompilerParams(vmem_limit_bytes=mib * 1024 * 1024)


def in_hbm(x):
    return pltpu.with_memory_space_constraint(x, pltpu.HBM)


def in_vmem(x):
    return pltpu.with_memory_space_constraint(x, pltpu.VMEM)


def cost(flops, moved, exps=0):
    return pl.CostEstimate(flops=flops, bytes_accessed=moved, transcendentals=exps)


def payload_kernel(down_hbm, up_hbm, out_ref, ups, wide, sems):
    ranks, width = down_hbm.shape
    groups, size = ups.shape[1] * ups.shape[2], ups.shape[3]
    get_down = pltpu.make_async_copy(down_hbm, out_ref.at[:, pl.ds(0, width)], sems.at[0])
    get_up = pltpu.make_async_copy(up_hbm, ups, sems.at[1])
    get_up.start()
    get_down.start()
    get_up.wait()
    wide[...] = ups.reshape(ranks * groups, size)[...].astype(jnp.float32)
    for n in range(groups):
        out_ref[:, width + n * size : width + (n + 1) * size] = wide[pl.ds(n, ranks, stride=groups), :].astype(
            jnp.bfloat16
        )
    get_down.wait()


def make_payload(down, up):
    ranks, width = down.shape
    groups, size = up.shape[1] * up.shape[2], up.shape[3]
    return pl.pallas_call(
        payload_kernel,
        out_shape=pltpu.VMEM((ranks, width + groups * size), jnp.bfloat16),
        in_specs=[pl.BlockSpec(memory_space=pltpu.HBM)] * 2,
        out_specs=VMEM,
        scratch_shapes=[
            pltpu.VMEM(up.shape, jnp.bfloat16),
            pltpu.VMEM((ranks * groups, size), jnp.float32),
            pltpu.SemaphoreType.DMA((2,)),
        ],
        compiler_params=params(8),
        name="payload",
    )(in_hbm(down), in_hbm(up))


def cache_copies(cache_hbm, k, v, sems, i, chunk):
    mine = pl.ds(i * chunk, chunk)
    return [pltpu.make_async_copy(cache_hbm.at[mine, :, n], ref.at[mine], sems.at[i, n]) for n, ref in enumerate((k, v))]


def two_rows(ref, r):
    rows, slots, own, size = ref.shape
    flat = ref.reshape(rows, slots * own, size)
    return jnp.concatenate([flat[r], flat[r + 1]], axis=1)


def score_chunk(q_ref, k_ref, scores_ref, i, chunk):
    nothing = jnp.zeros(q_ref.shape[1:], jnp.bfloat16)
    for p in range(chunk // 2):
        r = i * chunk + 2 * p
        both_q = jnp.concatenate(
            [
                jnp.concatenate([q_ref[r], nothing], axis=1),
                jnp.concatenate([nothing, q_ref[r + 1]], axis=1),
            ],
            axis=0,
        )
        scores_ref[p] = lax.dot_general(two_rows(k_ref, r), both_q, NT, preferred_element_type=jnp.float32)


class Cached:
    def __init__(self, chunk, heads, scale, inputs, outputs, scratch):
        self.chunk, self.heads, self.scale = chunk, heads, scale
        self.lengths_hbm, self.cache_hbm, self.q = inputs
        self.k, self.v, first_scores, self.sums, self.tops, self.totals = outputs
        self.lengths, second_scores, *rest = scratch
        self.scores, self.weights = (first_scores, second_scores), rest[0:2]
        self.sems, self.length_sem = rest[2:]
        self.rows, self.queries, self.size = self.q.shape
        self.slots, self.own = self.k.shape[1:3]
        self.keys = self.slots * self.own
        own, queries = self.own, self.queries
        line = lax.broadcasted_iota(jnp.int32, (self.keys, 2 * queries), 0)
        query = lax.broadcasted_iota(jnp.int32, (self.keys, 2 * queries), 1)
        self.line = jnp.where(line % own == (query % heads) // (heads // own), line, self.keys)
        self.one = lax.broadcasted_iota(jnp.int32, (1, 2 * queries), 1) < queries

    def copies(self, i):
        return cache_copies(self.cache_hbm, self.k, self.v, self.sems, i, self.chunk)

    def lengths_copy(self):
        return pltpu.make_async_copy(self.lengths_hbm, self.lengths, self.length_sem)

    def start(self, i):
        for copy in self.copies(i):
            copy.start()

    def arrive(self, i):
        for copy in self.copies(i):
            copy.wait()

    def lines(self, ref, r):
        return two_rows(ref, r)

    def score(self, i, slot):
        score_chunk(self.q, self.k, self.scores[slot], i, self.chunk)

    def soften(self, i, slot):
        for p in range(self.chunk // 2):
            r = i * self.chunk + 2 * p
            limit = jnp.where(self.one, self.own * self.lengths[r], self.own * self.lengths[r + 1])
            scores = jnp.where(self.line < limit, self.scores[slot][p], LOW)
            top = jnp.max(scores, axis=0, keepdims=True)
            expo = jnp.exp((scores - top) * self.scale)
            self.weights[slot][p] = expo.astype(jnp.bfloat16)
            pair = pl.ds(i * (self.chunk // 2) + p, 1)
            self.tops[pair, :] = top
            self.totals[pair, :] = jnp.sum(expo, axis=0, keepdims=True)

    def collect(self, i, slot):
        queries, size = self.queries, self.size
        for p in range(self.chunk // 2):
            r = i * self.chunk + 2 * p
            both = lax.dot_general(
                self.weights[slot][p], self.lines(self.v, r), TN, preferred_element_type=jnp.float32
            )
            for h in range(2):
                self.sums[r + h] = both[h * queries : (h + 1) * queries, h * size : (h + 1) * size]


def cached_kernel(chunk, early, heads, scale, *refs):
    cached = Cached(chunk, heads, scale, refs[:3], refs[6:12], refs[12:])
    chunks = cached.rows // chunk
    cached.lengths_copy().start()
    for i in range(early, chunks):
        cached.start(i)
    cached.lengths_copy().wait()
    cached.score(1, 1)
    cached.soften(0, 0)

    @pl.loop(1, chunks // 2)
    def _(t):
        for slot in range(2):
            i = 2 * t + slot

            @pl.when(i >= early)
            def _():
                cached.arrive(i)

            cached.score(i, slot)
            cached.soften(i - 1, 1 - slot)
            cached.collect(i - 2, slot)

    cached.soften(chunks - 1, 1)
    cached.collect(chunks - 2, 0)
    cached.collect(chunks - 1, 1)


def attend_cached(queries, cache, lengths, keys, values, first_scores, steps, chunk, early):
    rows, many, size = queries.shape
    slots, own = cache.shape[1], cache.shape[3]
    heads = many // steps
    half = (rows, slots, own, size)
    scores = (chunk // 2, slots * own, 2 * many)
    line = (rows // 2, 2 * many)
    outs = (
        pltpu.VMEM(half, jnp.bfloat16),
        pltpu.VMEM(half, jnp.bfloat16),
        pltpu.VMEM(scores, jnp.float32),
        pltpu.VMEM((rows, many, size), jnp.float32),
        pltpu.VMEM(line, jnp.float32),
        pltpu.VMEM(line, jnp.float32),
    )
    _, _, _, *state = pl.pallas_call(
        functools.partial(cached_kernel, chunk, early, heads, size ** (-0.5)),
        out_shape=outs,
        in_specs=[pl.BlockSpec(memory_space=pltpu.HBM)] * 2 + [VMEM] * 4,
        out_specs=(VMEM,) * len(outs),
        scratch_shapes=[
            pltpu.SMEM(lengths.shape, jnp.int32),
            pltpu.VMEM(scores, jnp.float32),
            pltpu.VMEM(scores, jnp.bfloat16),
            pltpu.VMEM(scores, jnp.bfloat16),
            pltpu.SemaphoreType.DMA((rows // chunk, 2)),
            pltpu.SemaphoreType.DMA,
        ],
        input_output_aliases={3: 0, 4: 1, 5: 2},
        compiler_params=params(16),
        cost_estimate=cost(8 * rows * many * slots * size, 4 * rows * slots * own * size, rows * many * slots * own),
        name="attend_cached",
    )(in_hbm(lengths), in_hbm(cache), in_vmem(queries), keys, values, first_scores)
    return [queries, *state]


def arrange_kernel(chunks, chunk, early, *refs):
    cache_hbm, hidden_hbm, base_hbm, queries_hbm, tokens_ref, base_ref, k, v, scores_ref = refs[:9]
    hidden, base, q, base_sems, sems = refs[9:]
    width, two, kvh, size = base.shape
    own = k.shape[2]
    groups = two * kvh
    some_width = width // chunks
    copies = [copy for i in range(early) for copy in cache_copies(cache_hbm, k, v, sems, i, chunk)]
    get_hidden = pltpu.make_async_copy(hidden_hbm, hidden, base_sems.at[chunks])

    def get_base(i):
        features = pl.ds(i * some_width, some_width)
        return pltpu.make_async_copy(base_hbm.at[features], base.at[features], base_sems.at[i])

    for i in range(chunks):
        get_base(i).start()
    get_hidden.start()
    get_queries = pltpu.make_async_copy(queries_hbm.at[pl.ds(0, chunk)], q, base_sems.at[chunks + 1])
    get_queries.start()
    for copy in copies:
        copy.start()

    tile = 256
    some = tile // groups
    row = lax.broadcasted_iota(jnp.int32, (tile, tile), 0)
    place = lax.broadcasted_iota(jnp.int32, (tile, tile), 1)
    order = (place == (row % some) * groups + row // some).astype(jnp.float32).astype(jnp.bfloat16)
    flat_base = base.reshape(width * groups, size)

    def arrange(f):
        at = pl.multiple_of(f * groups, tile)
        pair = jnp.concatenate([flat_base[pl.ds(at + h * tile, tile), :] for h in range(2)], axis=1)
        moved = jnp.dot(order, pair, preferred_element_type=jnp.float32).astype(jnp.bfloat16)
        for n in range(groups):
            lanes = slice((n % own) * size, (n % own + 1) * size)
            for h in range(2):
                base_ref[n // own, pl.ds(pl.multiple_of(f + h * some, some), some), lanes] = moved[
                    n * some : (n + 1) * some, h * size : (h + 1) * size
                ]

    @pl.loop(0, chunks)
    def _(i):
        get_base(i).wait()
        for f in range(0, some_width, 2 * some):
            arrange(i * some_width + f)

    get_hidden.wait()
    tokens_ref[...] = hidden.reshape(tokens_ref.shape)[...]
    get_queries.wait()
    copies[0].wait()
    score_chunk(q, k, scores_ref, 0, chunk)
    for copy in copies[1:]:
        copy.wait()


def arrange(hidden, base, cache, queries, chunk, early):
    rows, steps, _ = hidden.shape
    slots, own = cache.shape[1], cache.shape[3]
    width, two, kvh, size = base.shape
    half = pltpu.VMEM((rows, slots, own, size), jnp.bfloat16)
    chunks = 4
    outs = (
        pltpu.VMEM((rows * steps, width), jnp.bfloat16),
        pltpu.VMEM((two * kvh // own, width, own * size), jnp.bfloat16),
        half,
        half,
        pltpu.VMEM((chunk // 2, slots * own, 2 * queries.shape[1]), jnp.float32),
    )
    return pl.pallas_call(
        functools.partial(arrange_kernel, chunks, chunk, early),
        out_shape=outs,
        in_specs=[pl.BlockSpec(memory_space=pltpu.HBM)] * 4,
        out_specs=(VMEM,) * len(outs),
        scratch_shapes=[
            pltpu.VMEM(hidden.shape, jnp.bfloat16),
            pltpu.VMEM(base.shape, jnp.bfloat16),
            pltpu.VMEM((chunk,) + queries.shape[1:], jnp.bfloat16),
            pltpu.SemaphoreType.DMA((chunks + 2,)),
            pltpu.SemaphoreType.DMA((early, 2)),
        ],
        compiler_params=params(16),
        cost_estimate=cost(512 * base.size, 4 * (base.size + hidden.size)),
        name="arrange",
    )(in_hbm(cache), in_hbm(hidden), in_hbm(base), in_hbm(queries))


def project_kernel(k, hidden_ref, base_ref, *refs):
    gathered, (out_ref, merged) = refs[:-2], refs[-2:]
    width, columns = merged.shape
    part = lax.axis_index("tp") ^ k
    parts = base_ref.shape[0] // 2
    half = columns // 2
    up = jnp.concatenate(
        [
            jnp.concatenate(
                [ref[:, pl.ds(pl.multiple_of(width + (c * parts + part) * half, 128), half)] for ref in gathered], axis=0
            )
            for c in range(2)
        ],
        axis=1,
    )
    step = 256

    def merge(first, last):
        for f in range(first, last, step):
            down = jnp.concatenate([ref[:, f : f + step] for ref in gathered], axis=0).T
            low_rank = jnp.dot(down, up, preferred_element_type=jnp.float32)
            for c in range(2):
                base = base_ref[c * parts + part, f : f + step, :].astype(jnp.float32)
                merged[f : f + step, c * half : (c + 1) * half] = (
                    base + low_rank[:, c * half : (c + 1) * half]
                ).astype(jnp.bfloat16)

    cuts = [0, width // 2, width]
    total = None
    for first, last in zip(cuts, cuts[1:]):
        merge(first, last)
        product = jnp.dot(hidden_ref[:, first:last], merged[first:last, :], preferred_element_type=jnp.float32)
        total = product if total is None else total + product
    out_ref[...] = total


def project(k, hidden, base, gathered):
    tokens, width = hidden.shape
    columns = 2 * base.shape[2]
    ranks = sum(g.shape[0] for g in gathered)
    return pl.pallas_call(
        functools.partial(project_kernel, k),
        out_shape=pltpu.VMEM((tokens, columns), jnp.float32),
        in_specs=[VMEM] * (2 + len(gathered)),
        out_specs=VMEM,
        scratch_shapes=[pltpu.VMEM((width, columns), jnp.bfloat16)],
        compiler_params=params(24),
        cost_estimate=cost(2 * width * columns * (tokens + ranks), 2 * width * columns + 2 * width * tokens),
        name="project",
    )(hidden, base, *gathered)


def finish_kernel(steps, heads, scale, terms, *refs):
    parts, refs = refs[:terms], refs[terms:]
    q_ref, old_ref, top_ref, total_ref = refs[:4]
    refs = refs[4:]
    fresh_hbm, context_hbm, wide, fresh_ref, context_ref, sems = refs
    rows, queries, size = context_ref.shape
    own = fresh_ref.shape[3]
    fresh = parts[0][...]
    for part in parts[1:]:
        fresh = fresh + part[...]
    for n in range(2 * own):
        wide[pl.ds(n, rows * steps, stride=2 * own), :] = fresh[:, n * size : (n + 1) * size]
    fresh_ref.reshape(rows * steps * 2 * own, size)[...] = wide[...].astype(jnp.bfloat16)
    puts = [pltpu.make_async_copy(fresh_ref, fresh_hbm, sems.at[0])]
    puts[0].start()
    keys, many = 2 * own * steps, 2 * queries
    group = size // keys
    key = lax.broadcasted_iota(jnp.int32, (keys, many), 0)
    query = lax.broadcasted_iota(jnp.int32, (keys, many), 1)
    same_head = (query % heads) // (heads // own) == key // (2 * steps)
    same_row = query // queries == (key // steps) % 2
    live = same_head & same_row & ((query % queries) // heads >= key % steps)
    nothing = jnp.zeros((keys, size), jnp.bfloat16)

    def new_lines(c, pair):
        tokens = slice(pair * 2 * steps, (pair + 1) * 2 * steps)
        lines = [fresh[tokens, (c * own + g) * size : (c * own + g + 1) * size] for g in range(own)]
        return jnp.concatenate(lines, axis=0).astype(jnp.bfloat16)

    def rows_of(ref, pair):
        return ref[2 * pair : 2 * pair + 2].reshape(many, size)

    scores = [
        lax.dot_general(new_lines(0, p), rows_of(q_ref, p), NT, preferred_element_type=jnp.float32)
        for p in range(rows // 2)
    ]
    scores = jnp.stack([jnp.where(live, s, LOW) for s in scores])
    old_top = top_ref[...]
    top = jnp.maximum(old_top, jnp.max(scores, axis=1))
    expo = jnp.exp((scores - top[:, None, :]) * scale)
    back = jnp.exp((old_top - top) * scale)
    inverse = 1.0 / (back * total_ref[...] + jnp.sum(expo, axis=1))
    weights = (expo * inverse[:, None, :]).astype(jnp.bfloat16)
    back = back * inverse

    for at in range(0, rows // 2, group):
        pairs = range(at, at + group)
        values = jnp.concatenate(
            [
                jnp.concatenate([new_lines(1, p) if n == p else nothing for n in pairs], axis=1)
                for p in pairs
            ],
            axis=0,
        )
        new = lax.dot_general(
            weights[at : at + group].reshape(group * keys, many), values, TN, preferred_element_type=jnp.float32
        )
        factors = back[at : at + group].T
        for n, p in enumerate(pairs):
            both = new[:, n * size : (n + 1) * size] + factors[:, n : n + 1] * rows_of(old_ref, p)
            context_ref[2 * p : 2 * p + 2] = both.astype(jnp.bfloat16).reshape(2, queries, size)
        mine = pl.ds(2 * at, 2 * group)
        puts.append(pltpu.make_async_copy(context_ref.at[mine], context_hbm.at[mine], sems.at[1 + at // group]))
        puts[-1].start()
    for put in puts:
        put.wait()


def finish(parts, state, steps, own):
    rows, many, size = state[0].shape
    heads = many // steps
    groups = rows * own * steps // size
    fresh = (rows, steps, 2, own, size)
    fresh, context = pl.pallas_call(
        functools.partial(finish_kernel, steps, heads, size ** (-0.5), len(parts)),
        out_shape=(
            jax.ShapeDtypeStruct(fresh, jnp.bfloat16),
            jax.ShapeDtypeStruct((rows, many, size), jnp.bfloat16),
        ),
        in_specs=[VMEM] * (len(parts) + 4),
        out_specs=(pl.BlockSpec(memory_space=pltpu.HBM),) * 2,
        scratch_shapes=[
            pltpu.VMEM((rows * steps * 2 * own, size), jnp.float32),
            pltpu.VMEM(fresh, jnp.bfloat16),
            pltpu.VMEM((rows, many, size), jnp.bfloat16),
            pltpu.SemaphoreType.DMA((1 + groups,)),
        ],
        compiler_params=params(24),
        cost_estimate=cost(rows * many * size * size * 6, 8 * rows * many * size, rows * many * size * 2),
        name="finish",
    )(*parts, *state)
    return fresh, context.reshape(rows, steps, heads, size)


def join_kernel(*refs):
    blocks, out_ref = refs[:-1], refs[-1]
    at = 0
    for block in blocks:
        out_ref[at : at + block.shape[0], :] = block[...]
        at += block.shape[0]


def join(blocks):
    rows = sum(b.shape[0] for b in blocks)
    return pl.pallas_call(
        join_kernel,
        out_shape=pltpu.VMEM((rows, blocks[0].shape[1]), jnp.bfloat16),
        in_specs=[VMEM] * len(blocks),
        out_specs=VMEM,
        compiler_params=params(8),
        name="join",
    )(*blocks)


def gather_second(factor_a, factor_b, dp):
    count = dp // 2
    ranks = factor_b.shape[0]
    if ranks % 8 == 0 and count in (1, 2, 4):
        order = {1: (), 2: (1,), 4: (2, 3, 1)}[count]
        payload = make_payload(factor_a.T, factor_b)
        return [payload] + [lax.ppermute(payload, "dp", [(i, i ^ (2 * k)) for i in range(dp)]) for k in order]
    payload = jnp.concatenate([factor_a.T, factor_b.reshape(ranks, -1)], axis=1)
    groups = [[i for i in range(dp) if i % 2 == n] for n in range(2)]
    copies = jnp.broadcast_to(payload[None], (count,) + payload.shape)
    blocks = lax.all_to_all(copies, "dp", 0, 0, axis_index_groups=groups, tiled=True)
    return [blocks.reshape(count * ranks, payload.shape[1])]


def shards(dp, tp, hidden, base_weight, factor_a, factor_b, queries, cache, lengths):
    steps, own = queries.shape[1], cache.shape[3]
    assert dp % 2 == 0
    blocks = gather_second(factor_a, factor_b, dp)
    rows, steps, heads, size = queries.shape
    queries = queries.reshape(rows, steps * heads, size)
    chunk, early = 12, 2
    tokens, base, keys, values, scores = arrange(hidden, base_weight, cache, queries, chunk, early)
    blocks, tokens, base, keys, values, scores = lax.optimization_barrier((blocks, tokens, base, keys, values, scores))
    gathered = join(blocks) if len(blocks) > 1 else blocks[0]
    gathered = [gathered, lax.ppermute(gathered, "dp", [(i, i ^ 1) for i in range(dp)])]
    state = attend_cached(queries, cache, lengths, keys, values, scores, steps, chunk, early)
    gathered, state, tokens, base = lax.optimization_barrier((gathered, state, tokens, base))
    received = []
    for k in range(1, tp):
        other = project(k, tokens, base, gathered)
        received.append(lax.ppermute(other, "tp", [(i, i ^ k) for i in range(tp)]))
    mine = project(0, tokens, base, gathered)
    return finish([mine] + received, state, steps, own)


def solution(mesh):
    return jax.shard_map(
        functools.partial(shards, mesh.shape["dp"], mesh.shape["tp"]),
        mesh=mesh,
        in_specs=(
            P(("parts", "dp"), None, "tp"),
            P("tp", None, None, None),
            P(("parts", "tp"), "dp"),
            P(("parts", "dp"), None, None, None),
            P(("parts", "dp"), None, "tp", None),
            P(("parts", "dp"), None, None, "tp", None),
            P(("parts", "dp")),
        ),
        out_specs=(
            P(("parts", "dp"), None, None, "tp", None),
            P(("parts", "dp"), None, "tp", None),
        ),
        check_vma=False,
    )
```

```python
import functools

import jax
import jax.numpy as jnp
from jax import lax
from jax.experimental import pallas as pl
from jax.experimental.pallas import tpu as pltpu
from jax.sharding import PartitionSpec as P

LOW = -1e30
NT = (((1,), (1,)), ((), ()))
TN = (((0,), (0,)), ((), ()))
VMEM = pl.BlockSpec(memory_space=pltpu.VMEM)


def params(mib):
    return pltpu.CompilerParams(vmem_limit_bytes=mib * 1024 * 1024)


def in_hbm(x):
    return pltpu.with_memory_space_constraint(x, pltpu.HBM)


def in_vmem(x):
    return pltpu.with_memory_space_constraint(x, pltpu.VMEM)


def cost(flops, moved, exps=0):
    return pl.CostEstimate(flops=flops, bytes_accessed=moved, transcendentals=exps)


def payload_kernel(down_hbm, up_hbm, out_ref, ups, wide, sems):
    ranks, width = down_hbm.shape
    groups, size = ups.shape[1] * ups.shape[2], ups.shape[3]
    get_down = pltpu.make_async_copy(down_hbm, out_ref.at[:, pl.ds(0, width)], sems.at[0])
    get_up = pltpu.make_async_copy(up_hbm, ups, sems.at[1])
    get_up.start()
    get_down.start()
    get_up.wait()
    wide[...] = ups.reshape(ranks * groups, size)[...].astype(jnp.float32)
    for n in range(groups):
        out_ref[:, width + n * size : width + (n + 1) * size] = wide[pl.ds(n, ranks, stride=groups), :].astype(
            jnp.bfloat16
        )
    get_down.wait()


def make_payload(down, up):
    ranks, width = down.shape
    groups, size = up.shape[1] * up.shape[2], up.shape[3]
    return pl.pallas_call(
        payload_kernel,
        out_shape=pltpu.VMEM((ranks, width + groups * size), jnp.bfloat16),
        in_specs=[pl.BlockSpec(memory_space=pltpu.HBM)] * 2,
        out_specs=VMEM,
        scratch_shapes=[
            pltpu.VMEM(up.shape, jnp.bfloat16),
            pltpu.VMEM((ranks * groups, size), jnp.float32),
            pltpu.SemaphoreType.DMA((2,)),
        ],
        compiler_params=params(8),
        name="payload",
    )(in_hbm(down), in_hbm(up))


def cache_copies(cache_hbm, k, v, sems, i, chunk):
    mine = pl.ds(i * chunk, chunk)
    return [pltpu.make_async_copy(cache_hbm.at[mine, :, n], ref.at[mine], sems.at[i, n]) for n, ref in enumerate((k, v))]


def two_rows(ref, r):
    rows, slots, own, size = ref.shape
    flat = ref.reshape(rows, slots * own, size)
    return jnp.concatenate([flat[r], flat[r + 1]], axis=1)


def score_chunk(q_ref, k_ref, scores_ref, i, chunk):
    nothing = jnp.zeros(q_ref.shape[1:], jnp.bfloat16)
    for p in range(chunk // 2):
        r = i * chunk + 2 * p
        both_q = jnp.concatenate(
            [
                jnp.concatenate([q_ref[r], nothing], axis=1),
                jnp.concatenate([nothing, q_ref[r + 1]], axis=1),
            ],
            axis=0,
        )
        scores_ref[p] = lax.dot_general(two_rows(k_ref, r), both_q, NT, preferred_element_type=jnp.float32)


class Cached:
    def __init__(self, chunk, heads, scale, inputs, outputs, scratch):
        self.chunk, self.heads, self.scale = chunk, heads, scale
        self.lengths_hbm, self.cache_hbm, self.q = inputs
        self.k, self.v, first_scores, self.sums, self.tops, self.totals = outputs
        self.lengths, second_scores, *rest = scratch
        self.scores, self.weights = (first_scores, second_scores), rest[0:2]
        self.sems, self.length_sem = rest[2:]
        self.rows, self.queries, self.size = self.q.shape
        self.slots, self.own = self.k.shape[1:3]
        self.keys = self.slots * self.own
        own, queries = self.own, self.queries
        line = lax.broadcasted_iota(jnp.int32, (self.keys, 2 * queries), 0)
        query = lax.broadcasted_iota(jnp.int32, (self.keys, 2 * queries), 1)
        self.line = jnp.where(line % own == (query % heads) // (heads // own), line, self.keys)
        self.one = lax.broadcasted_iota(jnp.int32, (1, 2 * queries), 1) < queries

    def copies(self, i):
        return cache_copies(self.cache_hbm, self.k, self.v, self.sems, i, self.chunk)

    def lengths_copy(self):
        return pltpu.make_async_copy(self.lengths_hbm, self.lengths, self.length_sem)

    def start(self, i):
        for copy in self.copies(i):
            copy.start()

    def arrive(self, i):
        for copy in self.copies(i):
            copy.wait()

    def lines(self, ref, r):
        return two_rows(ref, r)

    def score(self, i, slot):
        score_chunk(self.q, self.k, self.scores[slot], i, self.chunk)

    def soften(self, i, slot):
        for p in range(self.chunk // 2):
            r = i * self.chunk + 2 * p
            limit = jnp.where(self.one, self.own * self.lengths[r], self.own * self.lengths[r + 1])
            scores = jnp.where(self.line < limit, self.scores[slot][p], LOW)
            top = jnp.max(scores, axis=0, keepdims=True)
            expo = jnp.exp((scores - top) * self.scale)
            self.weights[slot][p] = expo.astype(jnp.bfloat16)
            pair = pl.ds(i * (self.chunk // 2) + p, 1)
            self.tops[pair, :] = top
            self.totals[pair, :] = jnp.sum(expo, axis=0, keepdims=True)

    def collect(self, i, slot):
        queries, size = self.queries, self.size
        for p in range(self.chunk // 2):
            r = i * self.chunk + 2 * p
            both = lax.dot_general(
                self.weights[slot][p], self.lines(self.v, r), TN, preferred_element_type=jnp.float32
            )
            for h in range(2):
                self.sums[r + h] = both[h * queries : (h + 1) * queries, h * size : (h + 1) * size]


def cached_kernel(chunk, early, heads, scale, *refs):
    cached = Cached(chunk, heads, scale, refs[:3], refs[6:12], refs[12:])
    chunks = cached.rows // chunk
    cached.lengths_copy().start()
    for i in range(early, chunks):
        cached.start(i)
    cached.lengths_copy().wait()
    cached.score(1, 1)
    cached.soften(0, 0)

    @pl.loop(1, chunks // 2)
    def _(t):
        for slot in range(2):
            i = 2 * t + slot

            @pl.when(i >= early)
            def _():
                cached.arrive(i)

            cached.score(i, slot)
            cached.soften(i - 1, 1 - slot)
            cached.collect(i - 2, slot)

    cached.soften(chunks - 1, 1)
    cached.collect(chunks - 2, 0)
    cached.collect(chunks - 1, 1)


def attend_cached(queries, cache, lengths, keys, values, first_scores, steps, chunk, early):
    rows, many, size = queries.shape
    slots, own = cache.shape[1], cache.shape[3]
    heads = many // steps
    half = (rows, slots, own, size)
    scores = (chunk // 2, slots * own, 2 * many)
    line = (rows // 2, 2 * many)
    outs = (
        pltpu.VMEM(half, jnp.bfloat16),
        pltpu.VMEM(half, jnp.bfloat16),
        pltpu.VMEM(scores, jnp.float32),
        pltpu.VMEM((rows, many, size), jnp.float32),
        pltpu.VMEM(line, jnp.float32),
        pltpu.VMEM(line, jnp.float32),
    )
    _, _, _, *state = pl.pallas_call(
        functools.partial(cached_kernel, chunk, early, heads, size ** (-0.5)),
        out_shape=outs,
        in_specs=[pl.BlockSpec(memory_space=pltpu.HBM)] * 2 + [VMEM] * 4,
        out_specs=(VMEM,) * len(outs),
        scratch_shapes=[
            pltpu.SMEM(lengths.shape, jnp.int32),
            pltpu.VMEM(scores, jnp.float32),
            pltpu.VMEM(scores, jnp.bfloat16),
            pltpu.VMEM(scores, jnp.bfloat16),
            pltpu.SemaphoreType.DMA((rows // chunk, 2)),
            pltpu.SemaphoreType.DMA,
        ],
        input_output_aliases={3: 0, 4: 1, 5: 2},
        compiler_params=params(16),
        cost_estimate=cost(8 * rows * many * slots * size, 4 * rows * slots * own * size, rows * many * slots * own),
        name="attend_cached",
    )(in_hbm(lengths), in_hbm(cache), in_vmem(queries), keys, values, first_scores)
    return [queries, *state]


def arrange_kernel(chunks, chunk, early, *refs):
    cache_hbm, hidden_hbm, base_hbm, queries_hbm, tokens_ref, base_ref, k, v, scores_ref = refs[:9]
    hidden, base, q, base_sems, sems = refs[9:]
    width, two, kvh, size = base.shape
    own = k.shape[2]
    groups = two * kvh
    some_width = width // chunks
    copies = [copy for i in range(early) for copy in cache_copies(cache_hbm, k, v, sems, i, chunk)]
    get_hidden = pltpu.make_async_copy(hidden_hbm, hidden, base_sems.at[chunks])

    def get_base(i):
        features = pl.ds(i * some_width, some_width)
        return pltpu.make_async_copy(base_hbm.at[features], base.at[features], base_sems.at[i])

    for i in range(chunks):
        get_base(i).start()
    get_hidden.start()
    get_queries = pltpu.make_async_copy(queries_hbm.at[pl.ds(0, chunk)], q, base_sems.at[chunks + 1])
    get_queries.start()
    for copy in copies:
        copy.start()

    tile = 256
    some = tile // groups
    row = lax.broadcasted_iota(jnp.int32, (tile, tile), 0)
    place = lax.broadcasted_iota(jnp.int32, (tile, tile), 1)
    order = (place == (row % some) * groups + row // some).astype(jnp.float32).astype(jnp.bfloat16)
    flat_base = base.reshape(width * groups, size)

    def arrange(f):
        at = pl.multiple_of(f * groups, tile)
        pair = jnp.concatenate([flat_base[pl.ds(at + h * tile, tile), :] for h in range(2)], axis=1)
        moved = jnp.dot(order, pair, preferred_element_type=jnp.float32).astype(jnp.bfloat16)
        for n in range(groups):
            lanes = slice((n % own) * size, (n % own + 1) * size)
            for h in range(2):
                base_ref[n // own, pl.ds(pl.multiple_of(f + h * some, some), some), lanes] = moved[
                    n * some : (n + 1) * some, h * size : (h + 1) * size
                ]

    @pl.loop(0, chunks)
    def _(i):
        get_base(i).wait()
        for f in range(0, some_width, 2 * some):
            arrange(i * some_width + f)

    get_hidden.wait()
    tokens_ref[...] = hidden.reshape(tokens_ref.shape)[...]
    get_queries.wait()
    copies[0].wait()
    score_chunk(q, k, scores_ref, 0, chunk)
    for copy in copies[1:]:
        copy.wait()


def arrange(hidden, base, cache, queries, chunk, early):
    rows, steps, _ = hidden.shape
    slots, own = cache.shape[1], cache.shape[3]
    width, two, kvh, size = base.shape
    half = pltpu.VMEM((rows, slots, own, size), jnp.bfloat16)
    chunks = 4
    outs = (
        pltpu.VMEM((rows * steps, width), jnp.bfloat16),
        pltpu.VMEM((two * kvh // own, width, own * size), jnp.bfloat16),
        half,
        half,
        pltpu.VMEM((chunk // 2, slots * own, 2 * queries.shape[1]), jnp.float32),
    )
    return pl.pallas_call(
        functools.partial(arrange_kernel, chunks, chunk, early),
        out_shape=outs,
        in_specs=[pl.BlockSpec(memory_space=pltpu.HBM)] * 4,
        out_specs=(VMEM,) * len(outs),
        scratch_shapes=[
            pltpu.VMEM(hidden.shape, jnp.bfloat16),
            pltpu.VMEM(base.shape, jnp.bfloat16),
            pltpu.VMEM((chunk,) + queries.shape[1:], jnp.bfloat16),
            pltpu.SemaphoreType.DMA((chunks + 2,)),
            pltpu.SemaphoreType.DMA((early, 2)),
        ],
        compiler_params=params(16),
        cost_estimate=cost(512 * base.size, 4 * (base.size + hidden.size)),
        name="arrange",
    )(in_hbm(cache), in_hbm(hidden), in_hbm(base), in_hbm(queries))


def project_kernel(k, hidden_ref, base_ref, *refs):
    gathered, (out_ref, merged) = refs[:-2], refs[-2:]
    width, columns = merged.shape
    part = lax.axis_index("tp") ^ k
    parts = base_ref.shape[0] // 2
    half = columns // 2
    up = jnp.concatenate(
        [
            jnp.concatenate(
                [ref[:, pl.ds(pl.multiple_of(width + (c * parts + part) * half, 128), half)] for ref in gathered], axis=0
            )
            for c in range(2)
        ],
        axis=1,
    )
    step = 640

    def merge(first, last):
        for f in range(first, last, step):
            down = jnp.concatenate([ref[:, f : f + step] for ref in gathered], axis=0).T
            low_rank = jnp.dot(down, up, preferred_element_type=jnp.float32)
            for c in range(2):
                base = base_ref[c * parts + part, f : f + step, :].astype(jnp.float32)
                merged[f : f + step, c * half : (c + 1) * half] = (
                    base + low_rank[:, c * half : (c + 1) * half]
                ).astype(jnp.bfloat16)

    cuts = [0, width // 2, width]
    total = None
    for first, last in zip(cuts, cuts[1:]):
        merge(first, last)
        product = jnp.dot(hidden_ref[:, first:last], merged[first:last, :], preferred_element_type=jnp.float32)
        total = product if total is None else total + product
    out_ref[...] = total


def project(k, hidden, base, gathered):
    tokens, width = hidden.shape
    columns = 2 * base.shape[2]
    ranks = sum(g.shape[0] for g in gathered)
    return pl.pallas_call(
        functools.partial(project_kernel, k),
        out_shape=pltpu.VMEM((tokens, columns), jnp.float32),
        in_specs=[VMEM] * (2 + len(gathered)),
        out_specs=VMEM,
        scratch_shapes=[pltpu.VMEM((width, columns), jnp.bfloat16)],
        compiler_params=params(24),
        cost_estimate=cost(2 * width * columns * (tokens + ranks), 2 * width * columns + 2 * width * tokens),
        name="project",
    )(hidden, base, *gathered)


def finish_kernel(steps, heads, scale, terms, *refs):
    parts, refs = refs[:terms], refs[terms:]
    q_ref, old_ref, top_ref, total_ref = refs[:4]
    refs = refs[4:]
    fresh_hbm, context_hbm, wide, fresh_ref, context_ref, sems = refs
    rows, queries, size = context_ref.shape
    own = fresh_ref.shape[3]
    fresh = parts[0][...]
    for part in parts[1:]:
        fresh = fresh + part[...]
    for n in range(2 * own):
        wide[pl.ds(n, rows * steps, stride=2 * own), :] = fresh[:, n * size : (n + 1) * size]
    fresh_ref.reshape(rows * steps * 2 * own, size)[...] = wide[...].astype(jnp.bfloat16)
    puts = [pltpu.make_async_copy(fresh_ref, fresh_hbm, sems.at[0])]
    puts[0].start()
    keys, many = 2 * own * steps, 2 * queries
    group = size // keys
    key = lax.broadcasted_iota(jnp.int32, (keys, many), 0)
    query = lax.broadcasted_iota(jnp.int32, (keys, many), 1)
    same_head = (query % heads) // (heads // own) == key // (2 * steps)
    same_row = query // queries == (key // steps) % 2
    live = same_head & same_row & ((query % queries) // heads >= key % steps)
    nothing = jnp.zeros((keys, size), jnp.bfloat16)

    def new_lines(c, pair):
        tokens = slice(pair * 2 * steps, (pair + 1) * 2 * steps)
        lines = [fresh[tokens, (c * own + g) * size : (c * own + g + 1) * size] for g in range(own)]
        return jnp.concatenate(lines, axis=0).astype(jnp.bfloat16)

    def rows_of(ref, pair):
        return ref[2 * pair : 2 * pair + 2].reshape(many, size)

    scores = [
        lax.dot_general(new_lines(0, p), rows_of(q_ref, p), NT, preferred_element_type=jnp.float32)
        for p in range(rows // 2)
    ]
    scores = jnp.stack([jnp.where(live, s, LOW) for s in scores])
    old_top = top_ref[...]
    top = jnp.maximum(old_top, jnp.max(scores, axis=1))
    expo = jnp.exp((scores - top[:, None, :]) * scale)
    back = jnp.exp((old_top - top) * scale)
    inverse = 1.0 / (back * total_ref[...] + jnp.sum(expo, axis=1))
    weights = (expo * inverse[:, None, :]).astype(jnp.bfloat16)
    back = back * inverse

    for at in range(0, rows // 2, group):
        pairs = range(at, at + group)
        values = jnp.concatenate(
            [
                jnp.concatenate([new_lines(1, p) if n == p else nothing for n in pairs], axis=1)
                for p in pairs
            ],
            axis=0,
        )
        new = lax.dot_general(
            weights[at : at + group].reshape(group * keys, many), values, TN, preferred_element_type=jnp.float32
        )
        factors = back[at : at + group].T
        for n, p in enumerate(pairs):
            both = new[:, n * size : (n + 1) * size] + factors[:, n : n + 1] * rows_of(old_ref, p)
            context_ref[2 * p : 2 * p + 2] = both.astype(jnp.bfloat16).reshape(2, queries, size)
        mine = pl.ds(2 * at, 2 * group)
        puts.append(pltpu.make_async_copy(context_ref.at[mine], context_hbm.at[mine], sems.at[1 + at // group]))
        puts[-1].start()
    for put in puts:
        put.wait()


def finish(parts, state, steps, own):
    rows, many, size = state[0].shape
    heads = many // steps
    groups = rows * own * steps // size
    fresh = (rows, steps, 2, own, size)
    fresh, context = pl.pallas_call(
        functools.partial(finish_kernel, steps, heads, size ** (-0.5), len(parts)),
        out_shape=(
            jax.ShapeDtypeStruct(fresh, jnp.bfloat16),
            jax.ShapeDtypeStruct((rows, many, size), jnp.bfloat16),
        ),
        in_specs=[VMEM] * (len(parts) + 4),
        out_specs=(pl.BlockSpec(memory_space=pltpu.HBM),) * 2,
        scratch_shapes=[
            pltpu.VMEM((rows * steps * 2 * own, size), jnp.float32),
            pltpu.VMEM(fresh, jnp.bfloat16),
            pltpu.VMEM((rows, many, size), jnp.bfloat16),
            pltpu.SemaphoreType.DMA((1 + groups,)),
        ],
        compiler_params=params(24),
        cost_estimate=cost(rows * many * size * size * 6, 8 * rows * many * size, rows * many * size * 2),
        name="finish",
    )(*parts, *state)
    return fresh, context.reshape(rows, steps, heads, size)


def join_kernel(*refs):
    blocks, out_ref = refs[:-1], refs[-1]
    at = 0
    for block in blocks:
        out_ref[at : at + block.shape[0], :] = block[...]
        at += block.shape[0]


def join(blocks):
    rows = sum(b.shape[0] for b in blocks)
    return pl.pallas_call(
        join_kernel,
        out_shape=pltpu.VMEM((rows, blocks[0].shape[1]), jnp.bfloat16),
        in_specs=[VMEM] * len(blocks),
        out_specs=VMEM,
        compiler_params=params(8),
        name="join",
    )(*blocks)


def gather_second(factor_a, factor_b, dp):
    count = dp // 2
    ranks = factor_b.shape[0]
    if ranks % 8 == 0 and count in (1, 2, 4):
        order = {1: (), 2: (1,), 4: (2, 3, 1)}[count]
        payload = make_payload(factor_a.T, factor_b)
        return [payload] + [lax.ppermute(payload, "dp", [(i, i ^ (2 * k)) for i in range(dp)]) for k in order]
    payload = jnp.concatenate([factor_a.T, factor_b.reshape(ranks, -1)], axis=1)
    groups = [[i for i in range(dp) if i % 2 == n] for n in range(2)]
    copies = jnp.broadcast_to(payload[None], (count,) + payload.shape)
    blocks = lax.all_to_all(copies, "dp", 0, 0, axis_index_groups=groups, tiled=True)
    return [blocks.reshape(count * ranks, payload.shape[1])]


def shards(dp, tp, hidden, base_weight, factor_a, factor_b, queries, cache, lengths):
    steps, own = queries.shape[1], cache.shape[3]
    assert dp % 2 == 0
    blocks = gather_second(factor_a, factor_b, dp)
    rows, steps, heads, size = queries.shape
    queries = queries.reshape(rows, steps * heads, size)
    chunk, early = 12, 2
    tokens, base, keys, values, scores = arrange(hidden, base_weight, cache, queries, chunk, early)
    blocks, tokens, base, keys, values, scores = lax.optimization_barrier((blocks, tokens, base, keys, values, scores))
    gathered = join(blocks) if len(blocks) > 1 else blocks[0]
    gathered = [gathered, lax.ppermute(gathered, "dp", [(i, i ^ 1) for i in range(dp)])]
    state = attend_cached(queries, cache, lengths, keys, values, scores, steps, chunk, early)
    gathered, state, tokens, base = lax.optimization_barrier((gathered, state, tokens, base))
    received = []
    for k in range(1, tp):
        other = project(k, tokens, base, gathered)
        received.append(lax.ppermute(other, "tp", [(i, i ^ k) for i in range(tp)]))
    mine = project(0, tokens, base, gathered)
    return finish([mine] + received, state, steps, own)


def solution(mesh):
    return jax.shard_map(
        functools.partial(shards, mesh.shape["dp"], mesh.shape["tp"]),
        mesh=mesh,
        in_specs=(
            P(("parts", "dp"), None, "tp"),
            P("tp", None, None, None),
            P(("parts", "tp"), "dp"),
            P(("parts", "dp"), None, None, None),
            P(("parts", "dp"), None, "tp", None),
            P(("parts", "dp"), None, None, "tp", None),
            P(("parts", "dp")),
        ),
        out_specs=(
            P(("parts", "dp"), None, None, "tp", None),
            P(("parts", "dp"), None, "tp", None),
        ),
        check_vma=False,
    )
```
